32 devices in a mesh: dp: 32 (over z, y, x, core).
Axes of the slice: x: 2, y: 2, z: 4, core: 2. Of those that a mesh axis runs over, the one named last changes fastest.
Arguments:
- tokens: bfloat16 [25600, 768], P('dp'), may hold values from -6 to 6
- mask_bits: int32 [25600], P('dp'), may hold values 0 or 1
- groups: int32 [256], P('dp'), may hold values from 0 to 2, as said below
- offsets: int32 [256], P('dp'), may hold values from 0 to 800, as said below
- mask_token: bfloat16 [768], P('dp'), may hold values from -5 to 5
- ln1_gain: bfloat16 [768], P('dp'), may hold values from 0.099609375 to 1.8984375
- ln1_bias: bfloat16 [768], P('dp'), may hold values from -1.5 to 1.5
- w_qkv: bfloat16 [768, 2304], P('dp'), may hold values from -0.21875 to 0.21875
- b_qv: bfloat16 [1536], P('dp'), may hold values from -1.5 to 1.5
- w_proj: bfloat16 [768, 768], P('dp'), may hold values from -0.875 to 0.875
- b_proj: bfloat16 [768], P('dp'), may hold values from -1.5 to 1.5
- ln2_gain: bfloat16 [768], P('dp'), may hold values from 0.099609375 to 1.8984375
- ln2_bias: bfloat16 [768], P('dp'), may hold values from -1.5 to 1.5
- w_fc1: bfloat16 [768, 3072], P('dp'), may hold values from -0.21875 to 0.21875
- b_fc1: bfloat16 [3072], P('dp'), may hold values from -1.5 to 1.5
- w_fc2: bfloat16 [3072, 768], P('dp'), may hold values from -0.109375 to 0.109375
- b_fc2: bfloat16 [768], P('dp'), may hold values from -1.5 to 1.5
- cotangent: bfloat16 [25600, 768], P('dp'), may hold values from -6 to 6
Outputs:
- output: bfloat16 [25600, 768], P('dp')
- grad_tokens: float32 [25600, 768], P('dp')
- grad_mask_token: float32 [768], P('dp')
- grad_ln1_gain: float32 [768], P('dp')
- grad_ln1_bias: float32 [768], P('dp')
- grad_w_qkv: float32 [768, 2304], P('dp')
- grad_b_qv: float32 [1536], P('dp')
- grad_w_proj: float32 [768, 768], P('dp')
- grad_b_proj: float32 [768], P('dp')
- grad_ln2_gain: float32 [768], P('dp')
- grad_ln2_bias: float32 [768], P('dp')
- grad_w_fc1: float32 [768, 3072], P('dp')
- grad_b_fc1: float32 [3072], P('dp')
- grad_w_fc2: float32 [3072, 768], P('dp')
- grad_b_fc2: float32 [768], P('dp')
The draws below stay inside these ranges and needn't reach their ends.
Inputs may be any that keep to these rules, and one draw needn't show every extreme that they name: `groups`: each device's 8 slots all carry one size group; which group a device gets varies with the seed, and every group occurs. `offsets`: each device's images lie back to back from its first local row, as many as fit in 800 rows; a slot without an image has offset 800.
All inputs are finite; a program needn't handle non-finite values. No bound on the sum of `mask_bits` on one device may be relied on, other than what follows from the above.
Results may differ from the reference program's by a relative error of at most 0.011.
Values may be sent and summed in bfloat16 or wider, within the bound.
A program may use at most 192 MiB of HBM per device.

```python
import jax
import jax.numpy as jnp
from jax import lax

D = 768
H = 12
DH = 64
FF = 3072
TOK_DEV = 800
P_SMALL = 100
P_MID = 196
P_LARGE = 400
IMG_DEV = 8
TOKENS = 25600
IMAGES = 256
N_DP = 32


def layout(key):
    devices_count = IMAGES // IMG_DEV
    order = jax.random.permutation(key, devices_count)
    devices = jnp.arange(IMAGES, dtype=jnp.int32) // IMG_DEV
    slots = jnp.arange(IMAGES, dtype=jnp.int32) % IMG_DEV
    group_ids = (order[devices] % 3).astype(jnp.int32)
    lengths = jnp.where(group_ids == 0, P_SMALL, jnp.where(group_ids == 1, P_MID, P_LARGE)).astype(jnp.int32)
    counts = TOK_DEV // lengths
    starts = jnp.where(slots < counts, slots * lengths, TOK_DEV).astype(jnp.int32)
    return (group_ids, starts)


def draw_groups(key, part):
    group_ids, starts = layout(key)
    return group_ids


def draw_offsets(key, part):
    group_ids, starts = layout(key)
    return starts


def with_ends(values, rng, least, high):
    index_at = [jax.random.randint(jax.random.fold_in(rng, axis), (), 0, length) for axis, length in enumerate(values.shape)]
    longest = values.shape.index(max(values.shape))
    beside = index_at[:longest] + [(index_at[longest] + 1) % values.shape[longest]] + index_at[longest + 1:]
    return values.at[tuple(index_at)].set(least).at[tuple(beside)].set(high)


def level_of(rng, extent, cuts, smallest, largest):
    factor_of, own = 1.0, jax.random.fold_in(rng, 6)
    for axis_at, blocks in cuts:
        draws = jnp.exp(jax.random.uniform(jax.random.fold_in(own, axis_at), (blocks,), jnp.float32, smallest / len(cuts), largest / len(cuts)))
        factor_of = factor_of * jnp.repeat(draws, extent[axis_at] // blocks).reshape([-1 if axis == axis_at else 1 for axis in range(len(extent))])
    return factor_of


def noise(key, extent, scale, limit, pieces=(), kind=jnp.bfloat16):
    values = scale * jax.random.normal(key, extent, jnp.float32)
    if pieces:
        values = values * level_of(key, extent, pieces, -0.22, 0.18)
    return jnp.clip(values, -limit, limit).astype(kind)


def setup_inputs(seed: int = 0) -> dict:
    streams_of = jax.random.split(jax.random.key(seed), 19)
    return {
        "tokens": noise(streams_of[0], (TOKENS, D), 1.0, 6.0, ((0, 32),)),
        "mask_bits": with_ends((jax.random.randint(streams_of[1], (TOKENS,), 0, 5) < 2).astype(jnp.int32), jax.random.fold_in(streams_of[1], 1), 0, 1),
        "groups": draw_groups(jax.random.fold_in(streams_of[18], 71), 0),
        "offsets": draw_offsets(jax.random.fold_in(streams_of[18], 71), 0),
        "mask_token": noise(streams_of[4], (D,), 1.0, 5.0, ((0, 32),)),
        "ln1_gain": jnp.clip(1.0 + 0.18 * jax.random.normal(streams_of[5], (D,), jnp.float32), 0.099609375, 1.8984375).astype(jnp.bfloat16),
        "ln1_bias": noise(streams_of[6], (D,), 0.3, 1.5, ((0, 32),)),
        "w_qkv": noise(streams_of[7], (D, 3 * D), D ** -0.5, 0.21875, ((0, 32),)),
        "b_qv": noise(streams_of[8], (2 * D,), 0.3, 1.5, ((0, 32),)),
        "w_proj": noise(streams_of[9], (D, D), (D // 16) ** -0.5, 0.875, ((0, 32),)),
        "b_proj": noise(streams_of[10], (D,), 0.3, 1.5, ((0, 32),)),
        "ln2_gain": jnp.clip(1.0 + 0.18 * jax.random.normal(streams_of[11], (D,), jnp.float32), 0.099609375, 1.8984375).astype(jnp.bfloat16),
        "ln2_bias": noise(streams_of[12], (D,), 0.3, 1.5, ((0, 32),)),
        "w_fc1": noise(streams_of[13], (D, FF), D ** -0.5, 0.21875, ((0, 32),)),
        "b_fc1": noise(streams_of[14], (FF,), 0.3, 1.5, ((0, 32),)),
        "w_fc2": noise(streams_of[15], (FF, D), FF ** -0.5, 0.109375, ((0, 32),)),
        "b_fc2": noise(streams_of[16], (D,), 0.3, 1.5, ((0, 32),)),
        "cotangent": noise(streams_of[17], (TOKENS, D), 1.0, 6.0, ((0, 32),)),
    }


@jax.custom_vjp
def low(v):
    return lax.optimization_barrier(v.astype(jnp.bfloat16)).astype(jnp.float32)

@jax.custom_vjp
def low_back(v):
    return v

def low_keep(v):
    return (low(v), None)

def low_pass(kept, grad):
    return (grad,)

def back_keep(v):
    return (v, None)

def back_low(kept, grad):
    return (low(grad),)
low.defvjp(low_keep, low_pass)
low_back.defvjp(back_keep, back_low)
eps_norm = 1e-06
score_scale = 0.125
neg_large = -1e+30

def matmul_high(left, right):
    return jnp.dot(left, right, precision=lax.Precision.HIGHEST, preferred_element_type=jnp.float32)

def normalize(values, gain, shift):
    center = values - lax.optimization_barrier(jnp.mean(values, axis=-1, keepdims=True))
    spread = lax.optimization_barrier(jnp.mean(center * center, axis=-1, keepdims=True))
    return center * lax.rsqrt(spread + eps_norm) * gain + shift

def segment_rows(groups, offsets, rows):
    lengths = jnp.where(groups == 0, P_SMALL, jnp.where(groups == 1, P_MID, P_LARGE)).astype(jnp.int32)
    positions = jnp.arange(rows, dtype=jnp.int32)
    inside = (positions[None, :] >= offsets[:, None]) & (positions[None, :] < offsets[:, None] + lengths[:, None])
    labels = jnp.arange(1, offsets.shape[0] + 1, dtype=jnp.int32)
    segment = lax.optimization_barrier(jnp.sum(jnp.where(inside, labels[:, None], 0), axis=0)).astype(jnp.int32) - 1
    return (segment, (segment >= 0).astype(jnp.float32))

def device_forward(block_rows, mask_rows, group_row, offset_row, params):
    token_mask, gain_one, shift_one, weight_qkv, bias_qv, weight_proj, bias_proj, gain_two, shift_two, weight_one, bias_one, weight_two, bias_two = params
    segment, valid = segment_rows(group_row, offset_row, TOK_DEV)
    valid_col = valid[:, None]
    start = jnp.where((mask_rows == 1)[:, None], token_mask[None, :], block_rows)
    normed_one = low(normalize(start, gain_one, shift_one))
    full_bias = jnp.concatenate([bias_qv[:D], jnp.zeros((D,), jnp.float32), bias_qv[D:]])
    projected = low_back(low(matmul_high(normed_one, weight_qkv) + full_bias))
    queries = projected[:, :D].reshape(TOK_DEV, H, DH)
    keys_all = projected[:, D:2 * D].reshape(TOK_DEV, H, DH)
    values_all = projected[:, 2 * D:].reshape(TOK_DEV, H, DH)
    scores = jnp.einsum('qhd,khd->hqk', queries, keys_all, precision=lax.Precision.HIGHEST) * score_scale
    scores = low_back(scores)
    same = segment[:, None] == segment[None, :]
    masked = jnp.where(same[None], scores, neg_large)
    attn_prob = jax.nn.softmax(masked, axis=-1)
    prob_low = low(attn_prob)
    context = jnp.einsum('hqk,khd->qhd', prob_low, values_all, precision=lax.Precision.HIGHEST).reshape(TOK_DEV, D)
    context = low_back(low(context))
    branch_one = low_back(matmul_high(context, weight_proj) + bias_proj)
    middle = start + valid_col * branch_one
    normed_two = low(normalize(middle, gain_two, shift_two))
    hidden_pre = low_back(matmul_high(normed_two, weight_one) + bias_one)
    hidden = low(jax.nn.gelu(hidden_pre, approximate=False))
    branch_two = low_back(matmul_high(hidden, weight_two) + bias_two)
    return middle + valid_col * branch_two

def reference(tokens, mask_bits, groups, offsets, mask_token, ln1_gain, ln1_bias, w_qkv, b_qv, w_proj, b_proj, ln2_gain, ln2_bias, w_fc1, b_fc1, w_fc2, b_fc2, cotangent):
    params = (mask_token.astype(jnp.float32), ln1_gain.astype(jnp.float32), ln1_bias.astype(jnp.float32), w_qkv.astype(jnp.float32), b_qv.astype(jnp.float32), w_proj.astype(jnp.float32), b_proj.astype(jnp.float32), ln2_gain.astype(jnp.float32), ln2_bias.astype(jnp.float32), w_fc1.astype(jnp.float32), b_fc1.astype(jnp.float32), w_fc2.astype(jnp.float32), b_fc2.astype(jnp.float32))
    inputs = tokens.astype(jnp.float32).reshape(N_DP, TOK_DEV, D)
    mask_blocks = mask_bits.reshape(N_DP, TOK_DEV)
    group_blocks = groups.reshape(N_DP, IMG_DEV)
    offset_blocks = offsets.reshape(N_DP, IMG_DEV)
    step_fn = jax.checkpoint(device_forward)

    def whole(inputs_all, params_all):

        def scan_step(carry, items):
            return (carry, step_fn(items[0], items[1], items[2], items[3], params_all))
        _, results = lax.scan(scan_step, jnp.zeros((), jnp.float32), (inputs_all, mask_blocks, group_blocks, offset_blocks))
        return results
    result, pullback = jax.vjp(whole, inputs, params)
    grad_inputs, grad_params = pullback(cotangent.astype(jnp.float32).reshape(N_DP, TOK_DEV, D))
    return (result.reshape(TOKENS, D).astype(jnp.bfloat16), grad_inputs.reshape(TOKENS, D), grad_params[0], grad_params[1], grad_params[2], grad_params[3], grad_params[4], grad_params[5], grad_params[6], grad_params[7], grad_params[8], grad_params[9], grad_params[10], grad_params[11], grad_params[12])
```

```python
import functools

import jax
import jax.numpy as jnp
from jax import lax
from jax.experimental import pallas as pl
from jax.experimental.pallas import tpu as pltpu
from jax.sharding import PartitionSpec as P

P_SMALL = 100
P_MID = 196
P_LARGE = 400
eps_norm = 1e-06

def nt(a,b): return lax.dot_general(a,b,(((1,),(1,)),((),())),preferred_element_type=jnp.float32)
def nn(a,b): return lax.dot_general(a,b,(((1,),(0,)),((),())),preferred_element_type=jnp.float32)
def tn(a,b): return lax.dot_general(a,b,(((0,),(0,)),((),())),preferred_element_type=jnp.float32)

def attn_fwd_kernel(bias_ref, q_ref, k_ref, v_ref, ctx_ref, p_ref):
    q=q_ref[...]; k=k_ref[...]; v=v_ref[...]
    rows,width=q.shape
    lane=lax.broadcasted_iota(jnp.int32,(rows,width),1)
    bias=bias_ref[0]
    outs=[]
    for j in range(2):
        mine=(lane>=64)==(j==1)
        qj=jnp.where(mine,q,jnp.zeros_like(q))
        s=nt(qj,k)*0.18033688011112042+bias
        m=jnp.max(s,axis=1,keepdims=True)
        e=jnp.exp2(s-m)
        l=jnp.sum(e,axis=1,keepdims=True)
        p=(e*(1.0/l)).astype(jnp.bfloat16)
        p_ref[0,0,j]=p
        outs.append(nn(p,v))
    ctx_ref[...]=jnp.where(lane<64,outs[0],outs[1]).astype(jnp.bfloat16)

def attn_fwd(proj,bias):
    rows=proj.shape[0]; half=rows//2; width=proj.shape[1]//3; pairs=width//128
    return pl.pallas_call(attn_fwd_kernel,grid=(2,pairs),
        in_specs=[pl.BlockSpec((1,half,half),lambda b,p:(b,0,0)),
                  pl.BlockSpec((half,128),lambda b,p:(b,p)),
                  pl.BlockSpec((half,128),lambda b,p:(b,p+pairs)),
                  pl.BlockSpec((half,128),lambda b,p:(b,p+2*pairs))],
        out_specs=[pl.BlockSpec((half,128),lambda b,p:(b,p)),
                   pl.BlockSpec((1,1,2,half,half),lambda b,p:(b,p,0,0,0))],
        out_shape=[jax.ShapeDtypeStruct((rows,width),jnp.bfloat16),
                   jax.ShapeDtypeStruct((2,pairs,2,half,half),jnp.bfloat16)],
        compiler_params=pltpu.CompilerParams(vmem_limit_bytes=40<<20),name="attn_fwd")(bias,proj,proj,proj)

def attn_bwd_kernel(q_ref,k_ref,v_ref,g_ref,c_ref,p_ref,dq_ref,dk_ref,dv_ref):
    q=q_ref[...]; k=k_ref[...]; v=v_ref[...]; g=g_ref[...]; c=c_ref[...]
    rows,width=q.shape
    lane=lax.broadcasted_iota(jnp.int32,(rows,width),1)
    gc=g.astype(jnp.float32)*c.astype(jnp.float32)
    dq=[];dk=[];dv=[]
    for j in range(2):
        mine=(lane>=64)==(j==1)
        zero=jnp.zeros_like(q)
        qj=jnp.where(mine,q,zero); gj=jnp.where(mine,g,zero)
        di=jnp.sum(jnp.where(mine,gc,0.0),axis=1,keepdims=True)
        p=p_ref[0,0,j]
        dp=nt(gj,v)
        ds=(p.astype(jnp.float32)*(dp-di)).astype(jnp.bfloat16)
        dq.append(nn(ds,k))
        dk.append(tn(ds,qj))
        dv.append(tn(p,gj))
    dq_ref[...]=(jnp.where(lane<64,dq[0],dq[1])*0.125).astype(jnp.bfloat16)
    dk_ref[...]=((dk[0]+dk[1])*0.125).astype(jnp.bfloat16)
    dv_ref[...]=(dv[0]+dv[1]).astype(jnp.bfloat16)

def attn_bwd(proj,gctx,ctx,p):
    rows=proj.shape[0]; half=rows//2; width=proj.shape[1]//3; pairs=width//128
    sp=lambda o: pl.BlockSpec((half,128),lambda b,p:(b,p+o*pairs))
    return pl.pallas_call(attn_bwd_kernel,grid=(2,pairs),
        in_specs=[sp(0),sp(1),sp(2),sp(0),sp(0),pl.BlockSpec((1,1,2,half,half),lambda b,p:(b,p,0,0,0))],
        out_specs=[sp(0)]*3,
        out_shape=[jax.ShapeDtypeStruct((rows,width),jnp.bfloat16)]*3,
        compiler_params=pltpu.CompilerParams(vmem_limit_bytes=40<<20),name="attn_bwd")(proj,proj,proj,gctx,ctx,p)
MESH=pl.DeviceIdType.MESH
F32=jnp.float32; BF=jnp.bfloat16

def place():
    me=lax.axis_index("dp")
    c=lax.rem(me,2); x=lax.rem(me//2,2); y=lax.rem(me//4,2); z=me//8
    return c,x,y,z
def dev(z,yx,c): return ((z*4+yx)*2+c,)

def greet():
    c,x,y,z=place(); yx=y*2+x
    bar=pltpu.get_barrier_semaphore()
    peers=[dev(z,yx,1-c),dev(z,y*2+1-x,c),dev(z,(1-y)*2+x,c)]+[dev(lax.rem(z+k,4),yx,c) for k in (1,2,3)]
    for p in peers: pl.semaphore_signal(bar,inc=1,device_id=p,device_id_type=MESH)
    pl.semaphore_wait(bar,len(peers))

class Gather:
    def __init__(self,view,ss,rs):
        self.view=view; self.ss=ss; self.rs=rs
        c,x,y,z=place()
        self.c=c; self.z=z; self.yx=y*2+x
        self.xn=y*2+1-x; self.yn=(1-y)*2+x; self.dg=(1-y)*2+1-x
        self.sends=[]
    def _cp(self,src,dst,slot,d):
        return pltpu.make_async_remote_copy(src_ref=src,dst_ref=dst,send_sem=self.ss.at[slot],recv_sem=self.rs.at[slot],device_id=d,device_id_type=MESH)
    def send(self,src,dst,slot,d):
        cp=self._cp(src,dst,slot,d); cp.start(); self.sends.append(cp)
    def got(self,dst,slot,d):
        self._cp(dst,dst,slot,d).wait_recv()
    def one(self,z): return self.view(pl.ds(z,1),self.yx,self.c)
    def z_send(self,src):
        for k in (1,2,3):
            self.send(src,self.one(self.z),k-1,dev(lax.rem(self.z+k,4),self.yx,self.c))
    def sib(self,ref,slot): self.send(ref,ref,slot,dev(self.z,self.yx,1-self.c))
    def z_recv(self):
        for k in (1,2,3):
            zz=lax.rem(self.z+4-k,4)
            self.got(self.one(zz),k-1,dev(zz,self.yx,self.c))
    def xy_send(self):
        r=self.view(pl.ds(0,4),self.yx,self.c)
        self.send(r,r,3,dev(self.z,self.xn,self.c))
        self.send(r,r,4,dev(self.z,self.yn,self.c))
        for k in (1,2,3): self.sib(self.one(lax.rem(self.z+4-k,4)),6+k)
    def xy_recv(self):
        rx=self.view(pl.ds(0,4),self.xn,self.c)
        self.got(rx,3,dev(self.z,self.xn,self.c))
        h=self.view(pl.ds(0,2),self.xn,self.c)
        self.send(h,h,5,dev(self.z,self.yn,self.c))
        ry=self.view(pl.ds(0,4),self.yn,self.c)
        self.got(ry,4,dev(self.z,self.yn,self.c))
        h=self.view(pl.ds(2,2),self.yn,self.c)
        self.send(h,h,6,dev(self.z,self.xn,self.c))
        self.sib(rx,10); self.sib(ry,11)
    def diag_recv(self):
        a=self.view(pl.ds(0,2),self.dg,self.c)
        self.got(a,5,dev(self.z,self.yn,self.c))
        self.sib(a,12)
        b=self.view(pl.ds(2,2),self.dg,self.c)
        self.got(b,6,dev(self.z,self.xn,self.c))
        self.sib(b,13)
    def finish(self):
        o=1-self.c; s=dev(self.z,self.yx,o)
        for k in (1,2,3): self.got(self.view(pl.ds(lax.rem(self.z+4-k,4),1),self.yx,o),6+k,s)
        self.got(self.view(pl.ds(0,4),self.xn,o),10,s)
        self.got(self.view(pl.ds(0,4),self.yn,o),11,s)
        self.got(self.view(pl.ds(0,2),self.dg,o),12,s)
        self.got(self.view(pl.ds(2,2),self.dg,o),13,s)
    def drain(self):
        for cp in self.sends: cp.wait_send()

def cols_view(ref):
    half=ref.shape[-1]//2
    def view(zs,yx,lane): return ref.at[zs,yx,:,pl.ds(pl.multiple_of(lane*half,128),half)]
    return view
def rows_view(ref):
    def view(zs,yx,lane): return ref.at[zs,yx,lane]
    return view

def join(c,own,sib):
    a=own.astype(F32); b=sib.astype(F32)
    return jnp.concatenate([jnp.where(c==0,a,b),jnp.where(c==0,b,a)],axis=0).astype(BF)

def gather_kernel(sm_ref,q_ref,p_ref,f1_ref,f2_ref,gs_ref,gq_ref,gp_ref,g1_ref,g2_ref,
        sq,sp,s1,bq,bp,b1,ss0,rs0,ssl,ss,rs):
    greet()
    c,x,y,z=place(); yx=y*2+x
    sibd=dev(z,yx,1-c)
    first=[]
    def swap(src,dst,i):
        cp=pltpu.make_async_remote_copy(src_ref=src,dst_ref=dst,send_sem=ss0.at[i],recv_sem=rs0.at[i],device_id=sibd,device_id_type=MESH)
        cp.start(); first.append(cp)
    swap(sm_ref,gs_ref.at[z,yx,c],0)
    swap(q_ref,sq,1); swap(p_ref,sp,2); swap(f1_ref,s1,3)
    swap(f2_ref,g2_ref.at[z,yx,c],4)
    gs=[Gather(rows_view(gs_ref),ss.at[0],rs.at[0]),Gather(cols_view(gq_ref),ss.at[1],rs.at[1]),Gather(cols_view(gp_ref),ss.at[2],rs.at[2]),
        Gather(cols_view(g1_ref),ss.at[3],rs.at[3]),Gather(rows_view(g2_ref),ss.at[4],rs.at[4])]
    local=[]
    def keep(src,dst,i):
        cp=pltpu.make_async_copy(src,dst,ssl.at[i]); cp.start(); local.append(cp)
    def half(b):
        h=b.shape[-1]//2
        return b.at[:,:,pl.ds(pl.multiple_of(c*h,128),h)]
    keep(sm_ref,gs_ref.at[z,yx,c],0)
    keep(f2_ref,g2_ref.at[z,yx,c],4)
    def begin(i):
        if i==0:
            local[0].wait(); gs[0].z_send(gs[0].one(z))
        elif i==4:
            local[1].wait(); gs[4].z_send(gs[4].one(z))
        else:
            own,sib,buf,dst={1:(q_ref,sq,bq,gq_ref),2:(p_ref,sp,bp,gp_ref),3:(f1_ref,s1,b1,g1_ref)}[i]
            first[i].wait_recv()
            buf[0]=join(c,own[...],sib[...])
            keep(buf,dst.at[pl.ds(z,1),yx],i)
            gs[i].z_send(half(buf))
    begin(0); begin(1)
    gs[0].z_recv(); gs[0].xy_send()
    begin(2)
    gs[1].z_recv(); local[2].wait(); gs[1].xy_send()
    begin(3)
    gs[0].xy_recv()
    gs[2].z_recv(); local[3].wait(); gs[2].xy_send()
    gs[0].diag_recv()
    gs[1].xy_recv()
    begin(4)
    gs[3].z_recv(); local[4].wait(); gs[3].xy_send()
    gs[2].xy_recv()
    gs[1].diag_recv()
    gs[2].diag_recv()
    gs[4].z_recv(); gs[4].xy_send()
    gs[3].xy_recv()
    gs[3].diag_recv()
    gs[4].xy_recv()
    gs[4].diag_recv()
    first[0].wait_recv(); first[4].wait_recv()
    for g in gs: g.finish()
    for cp in first: cp.wait_send()
    for g in gs: g.drain()

def gather_all(small,wq,wp,w1,w2):
    sds=jax.ShapeDtypeStruct
    nq,np_,n1,n2=wq.shape[1],wp.shape[1],w1.shape[1],w2.shape[1]
    r=wq.shape[0]; r2=w2.shape[0]
    V=pl.BlockSpec(memory_space=pltpu.VMEM); A=pl.BlockSpec(memory_space=pl.ANY)
    D=pltpu.SemaphoreType.DMA
    return pl.pallas_call(gather_kernel,
        in_specs=[V]*5,out_specs=[A]*5,
        out_shape=[sds((4,4,2)+small.shape,BF),sds((4,4,2*r,nq),BF),sds((4,4,2*r,np_),BF),sds((4,4,2*r,n1),BF),sds((4,4,2,r2,n2),BF)],
        scratch_shapes=[pltpu.VMEM((r,n),BF) for n in (nq,np_,n1)]+[pltpu.VMEM((1,2*r,n),BF) for n in (nq,np_,n1)]+
            [D((5,)),D((5,)),D((5,)),D((5,14)),D((5,14))],
        compiler_params=pltpu.CompilerParams(collective_id=0,has_side_effects=True,vmem_limit_bytes=16<<20),name="gather_all")(small,wq,wp,w1,w2)

class Scatter:
    def __init__(self,view,a,s,rxa,ryb,rx,ry,b,rz,ss,rs,ls):
        self.view=view; self.a=a; self.s=s; self.rxa=rxa; self.ryb=ryb; self.rx=rx; self.ry=ry; self.b=b; self.rz=rz
        self.ss=ss; self.rs=rs; self.ls=ls
        c,x,y,z=place()
        self.c=c; self.z=z; self.yx=y*2+x
        self.xn=y*2+1-x; self.yn=(1-y)*2+x; self.dg=(1-y)*2+1-x
        self.cps={}
    def send(self,src,dst,slot,d):
        cp=pltpu.make_async_remote_copy(src_ref=src,dst_ref=dst,send_sem=self.ss.at[slot],recv_sem=self.rs.at[slot],device_id=d,device_id_type=MESH)
        cp.start(); self.cps[slot]=cp
    def r0(self):
        self.send(self.view(1-self.c),self.s,0,dev(self.z,self.yx,1-self.c))
        self.loc=pltpu.make_async_copy(self.view(self.c),self.a,self.ls); self.loc.start()
    def r1(self):
        self.loc.wait(); self.cps[0].wait_recv()
        a,s=self.a,self.s
        def add(yx):
            def body(i,_):
                a[i,yx]=(a[i,yx].astype(F32)+s[i,yx].astype(F32)).astype(a.dtype)
                return 0
            lax.fori_loop(0,4,body,0)
        xd=dev(self.z,self.xn,self.c); yd=dev(self.z,self.yn,self.c)
        add(self.dg)
        self.send(a.at[pl.ds(0,2),self.dg],self.rxa,1,xd)
        self.send(a.at[pl.ds(2,2),self.dg],self.ryb,2,yd)
        add(self.xn)
        self.send(a.at[pl.ds(0,2),self.xn],self.rx.at[pl.ds(0,2)],3,xd)
        add(self.yn)
        self.send(a.at[pl.ds(2,2),self.yn],self.ry.at[pl.ds(2,2)],4,yd)
        add(self.yx)
    def r2(self):
        a=self.a
        xd=dev(self.z,self.xn,self.c); yd=dev(self.z,self.yn,self.c)
        self.cps[1].wait_recv()
        def body(i,_):
            a[i,self.yn]=(a[i,self.yn].astype(F32)+self.rxa[i].astype(F32)).astype(a.dtype)
            return 0
        lax.fori_loop(0,2,body,0)
        self.send(a.at[pl.ds(0,2),self.yn],self.ry.at[pl.ds(0,2)],6,yd)
        self.cps[2].wait_recv()
        def body(i,_):
            a[i+2,self.xn]=(a[i+2,self.xn].astype(F32)+self.ryb[i].astype(F32)).astype(a.dtype)
            return 0
        lax.fori_loop(0,2,body,0)
        self.send(a.at[pl.ds(2,2),self.xn],self.rx.at[pl.ds(2,2)],5,xd)
    def r3(self):
        for s in (3,4,5,6): self.cps[s].wait_recv()
        def body(i,_):
            self.b[i]=(self.a[i,self.yx].astype(F32)+self.rx[i].astype(F32)+self.ry[i].astype(F32)).astype(self.b.dtype)
            return 0
        lax.fori_loop(0,4,body,0)
        for k in (1,2,3):
            zz=lax.rem(self.z+k,4)
            self.send(self.b.at[zz],self.rz.at[k-1],6+k,dev(zz,self.yx,self.c))
    def r4(self):
        t=self.b[self.z].astype(F32)
        for k in (1,2,3):
            self.cps[6+k].wait_recv()
            t=t+self.rz[k-1].astype(F32)
        return t
    def drain(self):
        for cp in self.cps.values(): cp.wait_send()

def scatter_scratch(r,n,dt):
    V=pltpu.VMEM
    return [V((4,4,r,n),dt),V((4,4,r,n),dt),V((2,r,n),dt),V((2,r,n),dt),V((4,r,n),dt),V((4,r,n),dt),V((4,r,n),dt),V((3,r,n),dt)]

def scatter_kernel(sm_ref,q_ref,p_ref,f1_ref,f2_ref,os_ref,oq_ref,op_ref,o1_ref,o2_ref,*sc):
    bufs=[sc[8*i:8*i+8] for i in range(5)]
    fin=sc[40:46]; ss,rs,ls,fs,fr=sc[46:]
    greet()
    c,x,y,z=place(); yx=y*2+x
    def cv(ref):
        h=ref.shape[-1]//2
        return lambda lane: ref.at[:,:,:,pl.ds(pl.multiple_of(lane*h,128),h)]
    def rv(ref): return lambda lane: ref.at[:,:,lane]
    refs=[sm_ref,q_ref,p_ref,f1_ref,f2_ref]
    S=[Scatter((rv if i in (0,4) else cv)(refs[i]),*bufs[i],ss.at[i],rs.at[i],ls.at[i]) for i in range(5)]
    order=[4,3,2,1,0]
    sibd=dev(z,yx,1-c)
    ends=[]
    outs={1:oq_ref,2:op_ref,3:o1_ref}
    def end(i):
        t=S[i].r4()
        if i==0: os_ref[...]=t
        elif i==4: o2_ref[...]=t
        else:
            f,rf=fin[2*(i-1)],fin[2*(i-1)+1]
            r=t.shape[0]//2
            f[0]=t[:r]; f[1]=t[r:]
            cp=pltpu.make_async_remote_copy(src_ref=f.at[1-c],dst_ref=rf,send_sem=fs.at[i],recv_sem=fr.at[i],device_id=sibd,device_id_type=MESH)
            cp.start(); ends.append((i,cp))
    def close():
        for i,cp in ends:
            cp.wait_recv()
            f,rf=fin[2*(i-1)],fin[2*(i-1)+1]
            own=f[c]; oth=rf[...]
            o=outs[i]; h=own.shape[-1]
            o[:,:h]=jnp.where(c==0,own,oth); o[:,h:]=jnp.where(c==0,oth,own)
            cp.wait_send()
    for i in order: S[i].r0()
    n=len(order)
    stages=[lambda i:S[i].r1(),lambda i:S[i].r2(),lambda i:S[i].r3(),lambda i:end(i)]
    for t in range(n+3):
        for s in range(3,-1,-1):
            k=t-s
            if 0<=k<n: stages[s](order[k])
    close()
    for s in S: s.drain()

def scatter_all(sm,q,p,f1,f2):
    sds=jax.ShapeDtypeStruct
    V=pl.BlockSpec(memory_space=pltpu.VMEM); A=pl.BlockSpec(memory_space=pl.ANY)
    D=pltpu.SemaphoreType.DMA
    sc=[]
    for a,dt in ((sm,F32),(q,BF),(p,BF),(f1,BF),(f2,BF)):
        if a.ndim==5: sc+=scatter_scratch(a.shape[3],a.shape[4],dt)
        else: sc+=scatter_scratch(a.shape[2],a.shape[3]//2,dt)
    outs=[sds(sm.shape[3:],F32)]
    for a in (q,p,f1):
        r,n=a.shape[2]//2,a.shape[3]
        sc+=[pltpu.VMEM((2,r,n//2),F32),pltpu.VMEM((r,n//2),F32)]
        outs.append(sds((r,n),F32))
    outs.append(sds(f2.shape[3:],F32))
    return pl.pallas_call(scatter_kernel,in_specs=[A]*5,out_specs=[V]*5,out_shape=outs,
        scratch_shapes=sc+[D((5,10)),D((5,10)),D((5,)),D((5,)),D((5,))],
        compiler_params=pltpu.CompilerParams(collective_id=1,has_side_effects=True,vmem_limit_bytes=56<<20),name="scatter_all")(sm,q,p,f1,f2)

def normalize(values, gain, shift):
    center = values - jnp.mean(values, axis=-1, keepdims=True)
    spread = jnp.mean(center * center, axis=-1, keepdims=True)
    return center * lax.rsqrt(spread + eps_norm) * gain + shift

def activate(values):
    return jax.nn.gelu(values, approximate=False)

def segment_rows(groups, offsets, rows):
    lengths = jnp.where(groups == 0, P_SMALL, jnp.where(groups == 1, P_MID, P_LARGE)).astype(jnp.int32)
    positions = jnp.arange(rows, dtype=jnp.int32)
    inside = (positions[None, :] >= offsets[:, None]) & (positions[None, :] < offsets[:, None] + lengths[:, None])
    labels = jnp.arange(1, offsets.shape[0] + 1, dtype=jnp.int32)
    return jnp.sum(jnp.where(inside, labels[:, None], 0), axis=0) - 1

def settle(mid, rows):
    half = rows.shape[0] // 2
    cut = P_MID * (half // P_MID)
    gap = half - cut
    end = rows.shape[0] - gap
    moved = jnp.concatenate([rows[:cut], rows[end:], rows[cut:end]], axis=0)
    return jnp.where(mid, moved, rows)

def unsettle(mid, rows):
    half = rows.shape[0] // 2
    cut = P_MID * (half // P_MID)
    gap = half - cut
    moved = jnp.concatenate([rows[:cut], rows[half:], rows[cut:half]], axis=0)
    return jnp.where(mid, moved, rows)

def shards(n, tokens, mask_bits, groups, offsets, mask_token, ln1_gain, ln1_bias, w_qkv, b_qv, w_proj, b_proj,
           ln2_gain, ln2_bias, w_fc1, b_fc1, w_fc2, b_fc2, cotangent):
    vectors = (mask_token, ln1_gain, ln1_bias, b_qv, b_proj, ln2_gain, ln2_bias, b_fc1, b_fc2)
    sizes = [v.shape[0] for v in vectors]
    places = [sum(sizes[:i]) for i in range(len(sizes) + 1)]
    fits = n == 32 and places[-1] <= 1024
    packed = jnp.concatenate(vectors)
    if fits:
        small = jnp.pad(packed, (0, 2048 - places[-1])).reshape(16, 128)
        gathered = gather_all(small, w_qkv, w_proj, w_fc1, w_fc2)
        small_all = gathered[0].reshape(n, 2048)
        full_qkv, full_proj, full_fc1, full_fc2 = [
            g.reshape(-1, g.shape[-1]) for g in gathered[1:]]
    else:
        small_all = lax.all_gather(packed, "dp", axis=0, tiled=False)
        full_qkv, full_proj, full_fc1, full_fc2 = [
            lax.all_gather(w, "dp", axis=0, tiled=True) for w in (w_qkv, w_proj, w_fc1, w_fc2)]
    token_mask, gain_one, shift_one, bias_qv, bias_proj, gain_two, shift_two, bias_one, bias_two = [
        small_all[:, places[i]:places[i + 1]].reshape(-1).astype(F32) for i in range(len(sizes))]
    rows, width = tokens.shape
    half = rows // 2
    mid = groups[0] == 1
    tokens = settle(mid, tokens)
    cotangent = settle(mid, cotangent)
    mask_bits = settle(mid, mask_bits)
    segment = settle(mid, segment_rows(groups, offsets, rows))
    valid_col = (segment >= 0).astype(F32)[:, None]
    halves = segment.reshape(2, half)
    bias = jnp.where(halves[:, :, None] == halves[:, None, :], 0.0, -1e30).astype(F32)
    masked_rows = (mask_bits == 1)[:, None]
    start = jnp.where(masked_rows, token_mask[None, :], tokens.astype(F32))
    normed_one = normalize(start, gain_one, shift_one).astype(BF)
    full_bias = jnp.concatenate([bias_qv[:width], jnp.zeros((width,), F32), bias_qv[width:]])
    projected = (jnp.dot(normed_one, full_qkv, preferred_element_type=F32) + full_bias).astype(BF)
    context_low, probs = attn_fwd(projected, bias)
    middle = start + valid_col * (jnp.dot(context_low, full_proj, preferred_element_type=F32) + bias_proj)
    normed_two = normalize(middle, gain_two, shift_two).astype(BF)
    hidden_pre = jnp.dot(normed_two, full_fc1, preferred_element_type=F32) + bias_one
    hidden_low = activate(hidden_pre).astype(BF)
    result = middle + valid_col * (jnp.dot(hidden_low, full_fc2, preferred_element_type=F32) + bias_two)
    output = unsettle(mid, result.astype(BF))
    upstream = cotangent.astype(F32)
    grad_two = (valid_col * upstream).astype(BF)
    grad_wfc2 = tn(hidden_low, grad_two)
    grad_bfc2 = jnp.sum(grad_two.astype(F32), axis=0)
    grad_hidden = nt(grad_two, full_fc2)
    _, gelu_back = jax.vjp(activate, hidden_pre)
    grad_pre = gelu_back(grad_hidden)[0].astype(BF)
    grad_wfc1 = tn(normed_two, grad_pre)
    grad_bfc1 = jnp.sum(grad_pre.astype(F32), axis=0)
    grad_normed_two = nt(grad_pre, full_fc1)
    _, norm_back_two = jax.vjp(normalize, middle, gain_two, shift_two)
    grad_mid_part, grad_gain_two, grad_shift_two = norm_back_two(grad_normed_two)
    grad_middle = upstream + grad_mid_part
    grad_branch = (valid_col * grad_middle).astype(BF)
    grad_wproj = tn(context_low, grad_branch)
    grad_bproj = jnp.sum(grad_branch.astype(F32), axis=0)
    grad_context = nt(grad_branch, full_proj).astype(BF)
    dq, dk, dv = attn_bwd(projected, grad_context, context_low, probs)
    grad_projected = jnp.concatenate([dq, dk, dv], axis=1)
    grad_wqkv = tn(normed_one, grad_projected)
    grad_bqv = jnp.concatenate([jnp.sum(dq.astype(F32), axis=0), jnp.sum(dv.astype(F32), axis=0)])
    grad_normed_one = nt(grad_projected, full_qkv)
    _, norm_back_one = jax.vjp(normalize, start, gain_one, shift_one)
    grad_start_part, grad_gain_one, grad_shift_one = norm_back_one(grad_normed_one)
    grad_start = grad_middle + grad_start_part
    grad_token = jnp.sum(jnp.where(masked_rows, grad_start, 0.0), axis=0)
    grad_input = unsettle(mid, jnp.where(masked_rows, 0.0, grad_start))
    grad_vectors = (grad_token, grad_gain_one, grad_shift_one, grad_bqv, grad_bproj, grad_gain_two, grad_shift_two,
                    grad_bfc1, grad_bfc2)
    grad_small = jnp.concatenate([g.reshape(n, -1) for g in grad_vectors], axis=1)
    if fits:
        grad_small = jnp.pad(grad_small, ((0, 0), (0, 1024 - places[-1]))).reshape(4, 4, 2, 8, 128)
        shares = scatter_all(
            grad_small,
            *[g.astype(BF).reshape(4, 4, g.shape[0] // 16, g.shape[1]) for g in (grad_wqkv, grad_wproj, grad_wfc1)],
            grad_wfc2.astype(BF).reshape(4, 4, 2, grad_wfc2.shape[0] // 32, width))
        small_share = shares[0].reshape(1024)
        share_qkv, share_proj, share_fc1, share_fc2 = shares[1:]
    else:
        small_share = lax.psum_scatter(grad_small, "dp", scatter_dimension=0, tiled=False)
        share_qkv, share_proj, share_fc1, share_fc2 = [
            lax.psum_scatter(g, "dp", scatter_dimension=0, tiled=True)
            for g in (grad_wqkv, grad_wproj, grad_wfc1, grad_wfc2)]
    v = [small_share[places[i]:places[i + 1]] for i in range(len(sizes))]
    return (output, grad_input, v[0], v[1], v[2], share_qkv, v[3], share_proj, v[4], v[5], v[6], share_fc1, v[7],
            share_fc2, v[8])

def solution(mesh):
    row, flat = P("dp", None), P("dp")
    return jax.shard_map(
        functools.partial(shards, mesh.shape["dp"]),
        mesh=mesh,
        in_specs=(row, flat, flat, flat, flat, flat, flat, row, flat, row, flat, flat, flat, row, flat, row, flat, row),
        out_specs=(row, row, flat, flat, flat, row, flat, row, flat, flat, flat, row, flat, row, flat),
        check_vma=False,
    )
```

```python
import functools

import jax
import jax.numpy as jnp
from jax import lax
from jax.experimental import pallas as pl
from jax.experimental.pallas import tpu as pltpu
from jax.sharding import PartitionSpec as P

P_SMALL = 100
P_MID = 196
P_LARGE = 400
eps_norm = 1e-06

def nt(a,b): return lax.dot_general(a,b,(((1,),(1,)),((),())),preferred_element_type=jnp.float32)
def nn(a,b): return lax.dot_general(a,b,(((1,),(0,)),((),())),preferred_element_type=jnp.float32)
def tn(a,b): return lax.dot_general(a,b,(((0,),(0,)),((),())),preferred_element_type=jnp.float32)

def attn_fwd_kernel(bias_ref, q_ref, k_ref, v_ref, ctx_ref, p_ref):
    q=q_ref[...]; k=k_ref[...]; v=v_ref[...]
    rows,width=q.shape
    lane=lax.broadcasted_iota(jnp.int32,(rows,width),1)
    bias=bias_ref[0]
    outs=[]
    for j in range(2):
        mine=(lane>=64)==(j==1)
        qj=jnp.where(mine,q,jnp.zeros_like(q))
        s=nt(qj,k)*0.18033688011112042+bias
        m=jnp.max(s,axis=1,keepdims=True)
        e=jnp.exp2(s-m)
        l=jnp.sum(e,axis=1,keepdims=True)
        p=(e*(1.0/l)).astype(jnp.bfloat16)
        p_ref[0,0,j]=p
        outs.append(nn(p,v))
    ctx_ref[...]=jnp.where(lane<64,outs[0],outs[1]).astype(jnp.bfloat16)

def attn_fwd(proj,bias):
    rows=proj.shape[0]; half=rows//2; width=proj.shape[1]//3; pairs=width//128
    return pl.pallas_call(attn_fwd_kernel,grid=(2,pairs),
        in_specs=[pl.BlockSpec((1,half,half),lambda b,p:(b,0,0)),
                  pl.BlockSpec((half,128),lambda b,p:(b,p)),
                  pl.BlockSpec((half,128),lambda b,p:(b,p+pairs)),
                  pl.BlockSpec((half,128),lambda b,p:(b,p+2*pairs))],
        out_specs=[pl.BlockSpec((half,128),lambda b,p:(b,p)),
                   pl.BlockSpec((1,1,2,half,half),lambda b,p:(b,p,0,0,0))],
        out_shape=[jax.ShapeDtypeStruct((rows,width),jnp.bfloat16),
                   jax.ShapeDtypeStruct((2,pairs,2,half,half),jnp.bfloat16)],
        compiler_params=pltpu.CompilerParams(vmem_limit_bytes=40<<20),name="attn_fwd")(bias,proj,proj,proj)

def attn_bwd_kernel(q_ref,k_ref,v_ref,g_ref,c_ref,p_ref,dq_ref,dk_ref,dv_ref):
    q=q_ref[...]; k=k_ref[...]; v=v_ref[...]; g=g_ref[...]; c=c_ref[...]
    rows,width=q.shape
    lane=lax.broadcasted_iota(jnp.int32,(rows,width),1)
    gc=g.astype(jnp.float32)*c.astype(jnp.float32)
    dq=[];dk=[];dv=[]
    for j in range(2):
        mine=(lane>=64)==(j==1)
        zero=jnp.zeros_like(q)
        qj=jnp.where(mine,q,zero); gj=jnp.where(mine,g,zero)
        di=jnp.sum(jnp.where(mine,gc,0.0),axis=1,keepdims=True)
        p=p_ref[0,0,j]
        dp=nt(gj,v)
        ds=(p.astype(jnp.float32)*(dp-di)).astype(jnp.bfloat16)
        dq.append(nn(ds,k))
        dk.append(tn(ds,qj))
        dv.append(tn(p,gj))
    dq_ref[...]=(jnp.where(lane<64,dq[0],dq[1])*0.125).astype(jnp.bfloat16)
    dk_ref[...]=((dk[0]+dk[1])*0.125).astype(jnp.bfloat16)
    dv_ref[...]=(dv[0]+dv[1]).astype(jnp.bfloat16)

def attn_bwd(proj,gctx,ctx,p):
    rows=proj.shape[0]; half=rows//2; width=proj.shape[1]//3; pairs=width//128
    sp=lambda o: pl.BlockSpec((half,128),lambda b,p:(b,p+o*pairs))
    return pl.pallas_call(attn_bwd_kernel,grid=(2,pairs),
        in_specs=[sp(0),sp(1),sp(2),sp(0),sp(0),pl.BlockSpec((1,1,2,half,half),lambda b,p:(b,p,0,0,0))],
        out_specs=[sp(0)]*3,
        out_shape=[jax.ShapeDtypeStruct((rows,width),jnp.bfloat16)]*3,
        compiler_params=pltpu.CompilerParams(vmem_limit_bytes=40<<20),name="attn_bwd")(proj,proj,proj,gctx,ctx,p)
MESH=pl.DeviceIdType.MESH
F32=jnp.float32; BF=jnp.bfloat16

def place():
    me=lax.axis_index("dp")
    c=lax.rem(me,2); x=lax.rem(me//2,2); y=lax.rem(me//4,2); z=me//8
    return c,x,y,z
def dev(z,yx,c): return ((z*4+yx)*2+c,)

def greet():
    c,x,y,z=place(); yx=y*2+x
    bar=pltpu.get_barrier_semaphore()
    peers=[dev(z,yx,1-c),dev(z,y*2+1-x,c),dev(z,(1-y)*2+x,c)]+[dev(lax.rem(z+k,4),yx,c) for k in (1,2,3)]
    for p in peers: pl.semaphore_signal(bar,inc=1,device_id=p,device_id_type=MESH)
    pl.semaphore_wait(bar,len(peers))

class Gather:
    def __init__(self,view,ss,rs):
        self.view=view; self.ss=ss; self.rs=rs
        c,x,y,z=place()
        self.c=c; self.z=z; self.yx=y*2+x
        self.xn=y*2+1-x; self.yn=(1-y)*2+x; self.dg=(1-y)*2+1-x
        self.sends=[]
    def _cp(self,src,dst,slot,d):
        return pltpu.make_async_remote_copy(src_ref=src,dst_ref=dst,send_sem=self.ss.at[slot],recv_sem=self.rs.at[slot],device_id=d,device_id_type=MESH)
    def send(self,src,dst,slot,d):
        cp=self._cp(src,dst,slot,d); cp.start(); self.sends.append(cp)
    def got(self,dst,slot,d):
        self._cp(dst,dst,slot,d).wait_recv()
    def one(self,z): return self.view(pl.ds(z,1),self.yx,self.c)
    def z_send(self,src):
        for k in (1,2,3):
            self.send(src,self.one(self.z),k-1,dev(lax.rem(self.z+k,4),self.yx,self.c))
    def sib(self,ref,slot): self.send(ref,ref,slot,dev(self.z,self.yx,1-self.c))
    def z_recv(self):
        for k in (1,2,3):
            zz=lax.rem(self.z+4-k,4)
            self.got(self.one(zz),k-1,dev(zz,self.yx,self.c))
    def xy_send(self):
        r=self.view(pl.ds(0,4),self.yx,self.c)
        self.send(r,r,3,dev(self.z,self.xn,self.c))
        self.send(r,r,4,dev(self.z,self.yn,self.c))
        for k in (1,2,3): self.sib(self.one(lax.rem(self.z+4-k,4)),6+k)
    def xy_recv(self):
        rx=self.view(pl.ds(0,4),self.xn,self.c)
        self.got(rx,3,dev(self.z,self.xn,self.c))
        h=self.view(pl.ds(0,2),self.xn,self.c)
        self.send(h,h,5,dev(self.z,self.yn,self.c))
        ry=self.view(pl.ds(0,4),self.yn,self.c)
        self.got(ry,4,dev(self.z,self.yn,self.c))
        h=self.view(pl.ds(2,2),self.yn,self.c)
        self.send(h,h,6,dev(self.z,self.xn,self.c))
        self.sib(rx,10); self.sib(ry,11)
    def diag_recv(self):
        a=self.view(pl.ds(0,2),self.dg,self.c)
        self.got(a,5,dev(self.z,self.yn,self.c))
        self.sib(a,12)
        b=self.view(pl.ds(2,2),self.dg,self.c)
        self.got(b,6,dev(self.z,self.xn,self.c))
        self.sib(b,13)
    def finish(self):
        o=1-self.c; s=dev(self.z,self.yx,o)
        for k in (1,2,3): self.got(self.view(pl.ds(lax.rem(self.z+4-k,4),1),self.yx,o),6+k,s)
        self.got(self.view(pl.ds(0,4),self.xn,o),10,s)
        self.got(self.view(pl.ds(0,4),self.yn,o),11,s)
        self.got(self.view(pl.ds(0,2),self.dg,o),12,s)
        self.got(self.view(pl.ds(2,2),self.dg,o),13,s)
    def drain(self):
        for cp in self.sends: cp.wait_send()

def cols_view(ref):
    half=ref.shape[-1]//2
    def view(zs,yx,lane): return ref.at[zs,yx,:,pl.ds(pl.multiple_of(lane*half,128),half)]
    return view
def rows_view(ref):
    def view(zs,yx,lane): return ref.at[zs,yx,lane]
    return view

def join(c,own,sib):
    a=own.astype(F32); b=sib.astype(F32)
    return jnp.concatenate([jnp.where(c==0,a,b),jnp.where(c==0,b,a)],axis=0).astype(BF)

def gather_kernel(sm_ref,q_ref,p_ref,f1_ref,f2_ref,gs_ref,gq_ref,gp_ref,g1_ref,g2_ref,
        sq,sp,s1,bq,bp,b1,ss0,rs0,ssl,ss,rs):
    greet()
    c,x,y,z=place(); yx=y*2+x
    sibd=dev(z,yx,1-c)
    first=[]
    def swap(src,dst,i):
        cp=pltpu.make_async_remote_copy(src_ref=src,dst_ref=dst,send_sem=ss0.at[i],recv_sem=rs0.at[i],device_id=sibd,device_id_type=MESH)
        cp.start(); first.append(cp)
    swap(sm_ref,gs_ref.at[z,yx,c],0)
    swap(q_ref,sq,1); swap(p_ref,sp,2); swap(f1_ref,s1,3)
    swap(f2_ref,g2_ref.at[z,yx,c],4)
    gs=[Gather(rows_view(gs_ref),ss.at[0],rs.at[0]),Gather(cols_view(gq_ref),ss.at[1],rs.at[1]),Gather(cols_view(gp_ref),ss.at[2],rs.at[2]),
        Gather(cols_view(g1_ref),ss.at[3],rs.at[3]),Gather(rows_view(g2_ref),ss.at[4],rs.at[4])]
    local=[]
    def keep(src,dst,i):
        cp=pltpu.make_async_copy(src,dst,ssl.at[i]); cp.start(); local.append(cp)
    def half(b):
        h=b.shape[-1]//2
        return b.at[:,:,pl.ds(pl.multiple_of(c*h,128),h)]
    keep(sm_ref,gs_ref.at[z,yx,c],0)
    keep(f2_ref,g2_ref.at[z,yx,c],4)
    def begin(i):
        if i==0:
            local[0].wait(); gs[0].z_send(gs[0].one(z))
        elif i==4:
            local[1].wait(); gs[4].z_send(gs[4].one(z))
        else:
            own,sib,buf,dst={1:(q_ref,sq,bq,gq_ref),2:(p_ref,sp,bp,gp_ref),3:(f1_ref,s1,b1,g1_ref)}[i]
            first[i].wait_recv()
            buf[0]=join(c,own[...],sib[...])
            keep(buf,dst.at[pl.ds(z,1),yx],i)
            gs[i].z_send(half(buf))
    begin(0); begin(1)
    gs[0].z_recv(); gs[0].xy_send()
    begin(2)
    gs[1].z_recv(); local[2].wait(); gs[1].xy_send()
    begin(3)
    gs[0].xy_recv()
    gs[2].z_recv(); local[3].wait(); gs[2].xy_send()
    gs[0].diag_recv()
    gs[1].xy_recv()
    begin(4)
    gs[3].z_recv(); local[4].wait(); gs[3].xy_send()
    gs[2].xy_recv()
    gs[1].diag_recv()
    gs[2].diag_recv()
    gs[4].z_recv(); gs[4].xy_send()
    gs[3].xy_recv()
    gs[3].diag_recv()
    gs[4].xy_recv()
    gs[4].diag_recv()
    first[0].wait_recv(); first[4].wait_recv()
    for g in gs: g.finish()
    for cp in first: cp.wait_send()
    for g in gs: g.drain()

def gather_all(small,wq,wp,w1,w2):
    sds=jax.ShapeDtypeStruct
    nq,np_,n1,n2=wq.shape[1],wp.shape[1],w1.shape[1],w2.shape[1]
    r=wq.shape[0]; r2=w2.shape[0]
    V=pl.BlockSpec(memory_space=pltpu.VMEM); A=pl.BlockSpec(memory_space=pl.ANY)
    D=pltpu.SemaphoreType.DMA
    return pl.pallas_call(gather_kernel,
        in_specs=[V]*5,out_specs=[A]*5,
        out_shape=[sds((4,4,2)+small.shape,BF),sds((4,4,2*r,nq),BF),sds((4,4,2*r,np_),BF),sds((4,4,2*r,n1),BF),sds((4,4,2,r2,n2),BF)],
        scratch_shapes=[pltpu.VMEM((r,n),BF) for n in (nq,np_,n1)]+[pltpu.VMEM((1,2*r,n),BF) for n in (nq,np_,n1)]+
            [D((5,)),D((5,)),D((5,)),D((5,14)),D((5,14))],
        compiler_params=pltpu.CompilerParams(collective_id=0,has_side_effects=True,vmem_limit_bytes=16<<20),name="gather_all")(small,wq,wp,w1,w2)

class Scatter:
    def __init__(self,view,a,s,rxa,ryb,rx,ry,b,rz,ss,rs,ls):
        self.view=view; self.a=a; self.s=s; self.rxa=rxa; self.ryb=ryb; self.rx=rx; self.ry=ry; self.b=b; self.rz=rz
        self.ss=ss; self.rs=rs; self.ls=ls
        c,x,y,z=place()
        self.c=c; self.z=z; self.yx=y*2+x
        self.xn=y*2+1-x; self.yn=(1-y)*2+x; self.dg=(1-y)*2+1-x
        self.cps={}
    def send(self,src,dst,slot,d):
        cp=pltpu.make_async_remote_copy(src_ref=src,dst_ref=dst,send_sem=self.ss.at[slot],recv_sem=self.rs.at[slot],device_id=d,device_id_type=MESH)
        cp.start(); self.cps[slot]=cp
    def r0(self):
        self.send(self.view(1-self.c),self.s,0,dev(self.z,self.yx,1-self.c))
        self.loc=pltpu.make_async_copy(self.view(self.c),self.a,self.ls); self.loc.start()
    def r1(self):
        self.loc.wait(); self.cps[0].wait_recv()
        a,s=self.a,self.s
        def add(yx):
            def body(i,_):
                a[i,yx]=(a[i,yx].astype(F32)+s[i,yx].astype(F32)).astype(a.dtype)
                return 0
            lax.fori_loop(0,4,body,0)
        xd=dev(self.z,self.xn,self.c); yd=dev(self.z,self.yn,self.c)
        add(self.dg)
        self.send(a.at[pl.ds(0,2),self.dg],self.rxa,1,xd)
        self.send(a.at[pl.ds(2,2),self.dg],self.ryb,2,yd)
        add(self.xn)
        self.send(a.at[pl.ds(0,2),self.xn],self.rx.at[pl.ds(0,2)],3,xd)
        add(self.yn)
        self.send(a.at[pl.ds(2,2),self.yn],self.ry.at[pl.ds(2,2)],4,yd)
        add(self.yx)
    def r2(self):
        a=self.a
        xd=dev(self.z,self.xn,self.c); yd=dev(self.z,self.yn,self.c)
        self.cps[1].wait_recv()
        def body(i,_):
            a[i,self.yn]=(a[i,self.yn].astype(F32)+self.rxa[i].astype(F32)).astype(a.dtype)
            return 0
        lax.fori_loop(0,2,body,0)
        self.send(a.at[pl.ds(0,2),self.yn],self.ry.at[pl.ds(0,2)],6,yd)
        self.cps[2].wait_recv()
        def body(i,_):
            a[i+2,self.xn]=(a[i+2,self.xn].astype(F32)+self.ryb[i].astype(F32)).astype(a.dtype)
            return 0
        lax.fori_loop(0,2,body,0)
        self.send(a.at[pl.ds(2,2),self.xn],self.rx.at[pl.ds(2,2)],5,xd)
    def r3(self):
        for s in (3,4,5,6): self.cps[s].wait_recv()
        def body(i,_):
            self.b[i]=(self.a[i,self.yx].astype(F32)+self.rx[i].astype(F32)+self.ry[i].astype(F32)).astype(self.b.dtype)
            return 0
        lax.fori_loop(0,4,body,0)
        for k in (1,2,3):
            zz=lax.rem(self.z+k,4)
            self.send(self.b.at[zz],self.rz.at[k-1],6+k,dev(zz,self.yx,self.c))
    def r4(self):
        t=self.b[self.z].astype(F32)
        for k in (1,2,3):
            self.cps[6+k].wait_recv()
            t=t+self.rz[k-1].astype(F32)
        return t
    def drain(self):
        for cp in self.cps.values(): cp.wait_send()

def scatter_scratch(r,n,dt):
    V=pltpu.VMEM
    return [V((4,4,r,n),dt),V((4,4,r,n),dt),V((2,r,n),dt),V((2,r,n),dt),V((4,r,n),dt),V((4,r,n),dt),V((4,r,n),dt),V((3,r,n),dt)]

def scatter_kernel(sm_ref,q_ref,p_ref,f1_ref,f2_ref,os_ref,oq_ref,op_ref,o1_ref,o2_ref,*sc):
    bufs=[sc[8*i:8*i+8] for i in range(5)]
    fin=sc[40:46]; ss,rs,ls,fs,fr=sc[46:]
    greet()
    c,x,y,z=place(); yx=y*2+x
    def cv(ref):
        h=ref.shape[-1]//2
        return lambda lane: ref.at[:,:,:,pl.ds(pl.multiple_of(lane*h,128),h)]
    def rv(ref): return lambda lane: ref.at[:,:,lane]
    refs=[sm_ref,q_ref,p_ref,f1_ref,f2_ref]
    S=[Scatter((rv if i in (0,4) else cv)(refs[i]),*bufs[i],ss.at[i],rs.at[i],ls.at[i]) for i in range(5)]
    order=[4,3,2,1,0]
    sibd=dev(z,yx,1-c)
    ends=[]
    outs={1:oq_ref,2:op_ref,3:o1_ref}
    def end(i):
        t=S[i].r4()
        if i==0: os_ref[...]=t
        elif i==4: o2_ref[...]=t
        else:
            f,rf=fin[2*(i-1)],fin[2*(i-1)+1]
            r=t.shape[0]//2
            f[0]=t[:r]; f[1]=t[r:]
            cp=pltpu.make_async_remote_copy(src_ref=f.at[1-c],dst_ref=rf,send_sem=fs.at[i],recv_sem=fr.at[i],device_id=sibd,device_id_type=MESH)
            cp.start(); ends.append((i,cp))
    def close():
        for i,cp in ends:
            cp.wait_recv()
            f,rf=fin[2*(i-1)],fin[2*(i-1)+1]
            own=f[c]; oth=rf[...]
            o=outs[i]; h=own.shape[-1]
            o[:,:h]=jnp.where(c==0,own,oth); o[:,h:]=jnp.where(c==0,oth,own)
            cp.wait_send()
    for i in order: S[i].r0()
    n=len(order)
    stages=[lambda i:S[i].r1(),lambda i:S[i].r2(),lambda i:S[i].r3(),lambda i:end(i)]
    for t in range(n+3):
        for s in range(3,-1,-1):
            k=t-s
            if 0<=k<n: stages[s](order[k])
    close()
    for s in S: s.drain()

def scatter_all(sm,q,p,f1,f2):
    sds=jax.ShapeDtypeStruct
    V=pl.BlockSpec(memory_space=pltpu.VMEM); A=pl.BlockSpec(memory_space=pl.ANY)
    D=pltpu.SemaphoreType.DMA
    sc=[]
    for a,dt in ((sm,F32),(q,BF),(p,BF),(f1,BF),(f2,BF)):
        if a.ndim==5: sc+=scatter_scratch(a.shape[3],a.shape[4],dt)
        else: sc+=scatter_scratch(a.shape[2],a.shape[3]//2,dt)
    outs=[sds(sm.shape[3:],F32)]
    for a in (q,p,f1):
        r,n=a.shape[2]//2,a.shape[3]
        sc+=[pltpu.VMEM((2,r,n//2),F32),pltpu.VMEM((r,n//2),F32)]
        outs.append(sds((r,n),F32))
    outs.append(sds(f2.shape[3:],F32))
    return pl.pallas_call(scatter_kernel,in_specs=[A]*5,out_specs=[V]*5,out_shape=outs,
        scratch_shapes=sc+[D((5,10)),D((5,10)),D((5,)),D((5,)),D((5,))],
        compiler_params=pltpu.CompilerParams(collective_id=1,has_side_effects=True,vmem_limit_bytes=56<<20),name="scatter_all")(sm,q,p,f1,f2)
class Gather2:
    def __init__(self,view,ss,rs):
        self.view=view; self.ss=ss; self.rs=rs
        c,x,y,z=place()
        self.c=c; self.z=z; self.yx=y*2+x
        self.xn=y*2+1-x; self.yn=(1-y)*2+x; self.dg=(1-y)*2+1-x
        self.xd=dev(z,self.xn,c); self.yd=dev(z,self.yn,c); self.sd=dev(z,self.yx,1-c)
        self.sends=[]
    def at(self,k,yx,lane=None): return self.view(pl.ds(lax.rem(self.z+4-k,4),1),yx,self.c if lane is None else lane)
    def all(self,yx,lane=None): return self.view(pl.ds(0,4),yx,self.c if lane is None else lane)
    def _cp(self,src,dst,slot,d):
        return pltpu.make_async_remote_copy(src_ref=src,dst_ref=dst,send_sem=self.ss.at[slot],recv_sem=self.rs.at[slot],device_id=d,device_id_type=MESH)
    def send(self,src,dst,slot,d):
        cp=self._cp(src,dst,slot,d); cp.start(); self.sends.append(cp)
    def got(self,dst,slot,d): self._cp(dst,dst,slot,d).wait_recv()
    def near(self,src):
        self.send(src,self.at(0,self.yx),3,self.xd)
        self.send(src,self.at(0,self.yx),7,self.yd)
    def far(self,src):
        for k in (1,2,3): self.send(src,self.at(0,self.yx),k-1,dev(lax.rem(self.z+k,4),self.yx,self.c))
    def X0(self):
        r=self.at(0,self.xn); self.got(r,3,self.xd)
        self.send(r,r,11,self.yd)
        self.got(self.at(0,self.yn),7,self.yd)
    def Z(self):
        for k in (1,3,2):
            r=self.at(k,self.yx)
            self.got(r,k-1,dev(lax.rem(self.z+4-k,4),self.yx,self.c))
            self.send(r,r,3+k,self.xd); self.send(r,r,7+k,self.yd)
        for k in (1,3,2):
            r=self.at(k,self.yx); self.send(r,r,14+k,self.sd)
    def X(self):
        for k in (1,3,2):
            a=self.at(k,self.xn); b=self.at(k,self.yn)
            self.got(a,3+k,self.xd)
            if k==1: self.send(a,a,11+k,self.yd)
            self.got(b,7+k,self.yd)
            if k!=1: self.send(b,b,11+k,self.xd)
        for yx,s in ((self.xn,18),(self.yn,19)):
            r=self.all(yx); self.send(r,r,s,self.sd)
    def D(self):
        for k in (0,1,3,2):
            self.got(self.at(k,self.dg),11+k,self.yd if k<2 else self.xd)
        r=self.all(self.dg); self.send(r,r,20,self.sd)
    def F(self):
        o=1-self.c
        for k in (1,2,3): self.got(self.at(k,self.yx,o),14+k,self.sd)
        for yx,s in ((self.xn,18),(self.yn,19),(self.dg,20)): self.got(self.all(yx,o),s,self.sd)
    def drain(self):
        for cp in self.sends: cp.wait_send()

def gelu_parts(x):
    d=1.0+0.23164189*jnp.abs(x)
    t=pl.reciprocal(d,approx=True)
    t=t*(2.0-d*t)
    e=jnp.exp2(x*x*(-0.5*1.4426950408889634))
    q=((((0.5*1.061405429*t-0.5*1.453152027)*t+0.5*1.421413741)*t-0.5*0.284496736)*t+0.5*0.254829592)*t*e
    cdf=jnp.where(x>=0,1.0-q,q)
    return x*cdf, cdf+x*e*0.3989422804014327

def row_stats(x):
    inv=1.0/x.shape[1]
    mean=jnp.sum(x,axis=1,keepdims=True)*inv
    c=x-mean
    var=jnp.sum(c*c,axis=1,keepdims=True)*inv
    return c,lax.rsqrt(var+eps_norm)

def spread(each,total,cols):
    j=lax.broadcasted_iota(jnp.int32,(128,total),1); l=lax.broadcasted_iota(jnp.int32,(128,total),0)
    return jnp.where(j-cols*each==l,1.0,0.0).astype(BF)

def over(each,shape):
    j=lax.broadcasted_iota(jnp.int32,shape,1)
    return (j*((1<<22)//each+1))>>22

def settled(g1,r):
    return r+jnp.where(r>=400,-8*g1,jnp.where(r>=392,400*g1,0))

def segments(groups,offsets,pos):
    g=groups[0]
    length=jnp.where(g==0,P_SMALL,jnp.where(g==1,P_MID,P_LARGE))
    seg=jnp.full(pos.shape,-1,jnp.int32)
    for s in range(8):
        o=offsets[s]
        seg=jnp.where((pos>=o)&(pos<o+length),s,seg)
    return seg

def settle_rows(g1,read,write):
    def either(a,b): return [jnp.where(g1==1,u,w) for u,w in zip(a,b)]
    def body(i,_):
        r=pl.multiple_of(i*56,8)
        write(r,56,read(r,56)); return 0
    lax.fori_loop(0,7,body,0)
    write(392,8,either(read(792,8),read(392,8)))
    def body2(i,_):
        r=pl.multiple_of(400+i*40,8)
        write(r,40,either(read(pl.multiple_of(392+i*40,8),40),read(r,40))); return 0
    lax.fori_loop(0,10,body2,0)

def forward_kernel(groups,offsets,sm_ref,q_ref,p_ref,f1_ref,f2_ref,tok_ref,cot_ref,mask_ref,
        wq_o,wp_o,w1_o,w2_o,pr_o,n1_o,n2_o,ctx_o,pj_o,hid_o,dg_o,st_o,mid_o,pt2_o,gt_o,cs_o,vec_o,meta_o,
        gs,gq,gp,g1w,sq,sp,s1,bq,bp,b1,raw,mid,st,n1,pj,bias,ctx,n2,hid,dg,gt,cs,pt2,pst,bqv,bf1,
        ss0,rs0,ssl,sss,srs,ss,rs,psem,osem):
    greet()
    c,x,y,z=place(); yx=y*2+x
    sibd=dev(z,yx,1-c)
    first=[]
    def swap(src,dst,i):
        cp=pltpu.make_async_remote_copy(src_ref=src,dst_ref=dst,send_sem=ss0.at[i],recv_sem=rs0.at[i],device_id=sibd,device_id_type=MESH)
        cp.start(); first.append(cp)
    swap(sm_ref,gs.at[z,yx,c],0)
    swap(q_ref,sq,1); swap(p_ref,sp,2); swap(f1_ref,s1,3)
    swap(f2_ref,w2_o.at[z,yx,c],4)
    gs[z,yx,c]=sm_ref[...]
    own2=pltpu.make_async_copy(f2_ref,w2_o.at[z,yx,c],ssl.at[0]); own2.start()
    S=Gather(rows_view(gs),sss,srs)
    Q,Pj,F1=[Gather2(cols_view(r),ss.at[i],rs.at[i]) for i,r in enumerate((gq,gp,g1w))]
    F2=Gather2(rows_view(w2_o),ss.at[3],rs.at[3])
    outs=[]
    def put(src,dst):
        cp=pltpu.make_async_copy(src,dst,osem.at[len(outs)]); cp.start(); outs.append(cp)
    def build(i):
        own,sib,buf,dst={1:(q_ref,sq,bq,gq),2:(p_ref,sp,bp,gp),3:(f1_ref,s1,b1,g1w)}[i]
        first[i].wait_recv()
        j=join(c,own[...],sib[...])
        buf[0]=j; dst[z,yx]=j
    def half(b):
        h=b.shape[-1]//2
        return b.at[:,:,pl.ds(pl.multiple_of(c*h,128),h)]
    S.z_send(S.one(z))
    build(1); Q.far(half(bq)); Q.near(half(bq))
    S.z_recv(); S.xy_send()
    build(2); Pj.near(half(bp))
    build(3); F1.near(half(b1))
    S.xy_recv()
    own2.wait(); F2.near(F2.at(0,yx))
    Q.X0()
    g1=jnp.where(groups[0]==1,1,0)
    raw[...]=tok_ref[...].astype(F32)
    segc=segments(groups,offsets,settled(g1,lax.broadcasted_iota(jnp.int32,(800,1),0)))
    meta_o[:,0:1]=jnp.where(segc>=0,1.0,0.0)
    for b in range(2):
        segr=segments(groups,offsets,settled(g1,lax.broadcasted_iota(jnp.int32,(1,400),1)+400*b))
        bias[b]=jnp.where(segc[400*b:400*b+400]==segr,0.0,-1e30)
    S.diag_recv(); first[0].wait_recv(); S.finish()
    Pj.far(half(bp)); Pj.X0()
    X=gs[...].reshape(512,128)
    E=nn(X,spread(24,768,over(24,(128,768))))
    E=jnp.where(lax.broadcasted_iota(jnp.int32,(512,768),0)>>4==over(24,(512,768)),E,0.0).reshape(32,16,768)
    vec_o[...]=jnp.sum(E,axis=0)
    def wide(row,each,total):
        sel=jnp.where(lax.broadcasted_iota(jnp.int32,(32,512),1)==lax.broadcasted_iota(jnp.int32,(32,512),0)*16+row,1.0,0.0).astype(BF)
        e=nn(nn(sel,X).astype(BF),spread(each,total,over(each,(128,total))))
        e=jnp.where(lax.broadcasted_iota(jnp.int32,(32,total),0)==over(each,(32,total)),e,0.0)
        return jnp.sum(e,axis=0,keepdims=True)
    bqv[...]=wide(3,48,1536); bf1[...]=wide(7,96,3072)
    Q.Z(); F1.far(half(b1))
    F1.X0(); F2.X0()
    def write(r,n,v):
        t,m=v
        meta_o[pl.ds(r,n),1:2]=m
        mid[pl.ds(r,n),:]=jnp.where(m>0.0,vec_o[0:1,:],t)
    settle_rows(g1,lambda r,n:(raw[pl.ds(r,n),:],mask_ref[pl.ds(r,n),:]),write)
    def body(i,_):
        r=pl.ds(pl.multiple_of(i*80,16),80)
        s=mid[r,:]
        st[r,:]=s.astype(BF)
        cc,rstd=row_stats(s)
        n1[r,:]=(cc*rstd*vec_o[1:2,:]+vec_o[2:3,:]).astype(BF)
        return 0
    lax.fori_loop(0,10,body,0)
    put(st,st_o); put(n1,n1_o)
    Pj.Z(); F2.far(F2.at(0,yx))
    raw[...]=cot_ref[...].astype(F32)
    def write2(r,n,v): mid[pl.ds(r,n),:]=v[0]
    settle_rows(g1,lambda r,n:(raw[pl.ds(r,n),:],),write2)
    def body(i,_):
        r=pl.ds(pl.multiple_of(i*80,16),80)
        v=mid[r,:]
        cs[r,:]=v.astype(BF); gt[r,:]=(v*meta_o[r,0:1]).astype(BF)
        return 0
    lax.fori_loop(0,10,body,0)
    put(cs,cs_o); put(gt,gt_o)
    Q.X(); Pj.X(); Q.D(); Q.F()
    def qkv(j):
        r=nn(n1[...],gq[:,:,:,768*j:768*j+768].reshape(768,768))
        if j==0: r=r+bqv[:,:768]
        if j==2: r=r+bqv[:,768:]
        pj[:,768*j:768*j+768]=r.astype(BF)
    qkv(0); qkv(1); F1.Z(); Pj.D(); qkv(2)
    put(gq,wq_o); put(pj,pj_o)
    lane=lax.broadcasted_iota(jnp.int32,(400,128),1)
    def pcopy(it):
        return pltpu.make_async_copy(pst.at[lax.rem(it,2)],pr_o.at[it],psem.at[lax.rem(it,2)])
    def attend(it,_):
        b=it//6; p=lax.rem(it,6); s=lax.rem(it,2)
        r=pl.ds(pl.multiple_of(b*400,16),400)
        cc=lambda o: pl.ds(pl.multiple_of(o+p*128,128),128)
        @pl.when(it>=2)
        def _(): pcopy(it-2).wait()
        q=pj[r,cc(0)]; k=pj[r,cc(768)]; v=pj[r,cc(1536)]
        res=[]
        for j in range(2):
            qj=jnp.where((lane>=64)==(j==1),q,jnp.zeros_like(q))
            t=nt(qj,k)*0.18033688011112042+bias[b]
            e=jnp.exp2(t-jnp.max(t,axis=1,keepdims=True))
            pr=(e*(1.0/jnp.sum(e,axis=1,keepdims=True))).astype(BF)
            pst[s,j]=pr
            res.append(nn(pr,v))
        ctx[r,cc(0)]=jnp.where(lane<64,res[0],res[1]).astype(BF)
        pcopy(it).start()
        return 0
    lax.fori_loop(0,3,attend,0)
    Pj.F(); put(gp,wp_o)
    lax.fori_loop(3,6,attend,0)
    F1.X()
    lax.fori_loop(6,9,attend,0)
    F2.Z()
    lax.fori_loop(9,12,attend,0)
    put(ctx,ctx_o)
    wpv=gp[...].reshape(768,768)
    def body(i,_):
        r=pl.ds(pl.multiple_of(i*400,16),400)
        mid[r,:]=st[r,:].astype(F32)+meta_o[r,0:1]*(nn(ctx[r,:],wpv)+vec_o[4:5,:])
        return 0
    lax.fori_loop(0,2,body,0)
    def body(i,_):
        r=pl.ds(pl.multiple_of(i*80,16),80)
        cc,rstd=row_stats(mid[r,:])
        n2[r,:]=(cc*rstd*vec_o[5:6,:]+vec_o[6:7,:]).astype(BF)
        return 0
    lax.fori_loop(0,10,body,0)
    put(mid,mid_o); put(n2,n2_o)
    F1.D(); F1.F(); put(g1w,w1_o)
    def mlp(i,_):
        cc=pl.ds(pl.multiple_of(i*512,128),512)
        a,d=gelu_parts(nn(n2[...],g1w[:,:,:,cc].reshape(768,512))+bf1[:,cc])
        hid[:,cc]=a.astype(BF); dg[:,cc]=d.astype(BF)
        return 0
    lax.fori_loop(0,3,mlp,0)
    F2.X()
    lax.fori_loop(3,6,mlp,0)
    put(hid,hid_o); put(dg,dg_o)
    F2.D()
    def grads(i,_):
        cc=pl.ds(pl.multiple_of(i*768,128),768)
        pt2[i]=tn(hid[:,cc],gt[...]).astype(BF).reshape(4,2,96,768)
        return 0
    lax.fori_loop(0,2,grads,0)
    put(pt2.at[pl.ds(0,2)],pt2_o.at[pl.ds(0,2)])
    lax.fori_loop(2,4,grads,0)
    put(pt2.at[pl.ds(2,2)],pt2_o.at[pl.ds(2,2)])
    first[4].wait_recv(); F2.F()
    pcopy(10).wait(); pcopy(11).wait()
    for cp in outs: cp.wait()
    for cp in first: cp.wait_send()
    for g in (S,Q,Pj,F1,F2): g.drain()

def forward(groups,offsets,small,wq,wp,w1,w2,tok,cot,mask):
    sds=jax.ShapeDtypeStruct
    V=pl.BlockSpec(memory_space=pltpu.VMEM); A=pl.BlockSpec(memory_space=pl.ANY); M=pl.BlockSpec(memory_space=pltpu.SMEM)
    D=pltpu.SemaphoreType.DMA
    v=pltpu.VMEM
    R,W=tok.shape
    outs=[((4,4,48,2304),BF),((4,4,48,768),BF),((4,4,48,3072),BF),((4,4,2,96,768),BF),((12,2,400,400),BF)]+[((R,W),BF)]*4+[((R,3*W),BF),((R,4*W),BF),((R,4*W),BF)]
    outs=[((4,4,48,2304),BF),((4,4,48,768),BF),((4,4,48,3072),BF),((4,4,2,96,768),BF),((12,2,400,400),BF),
        ((R,W),BF),((R,W),BF),((R,W),BF),((R,3*W),BF),((R,4*W),BF),((R,4*W),BF),((R,W),BF),((R,W),F32),((4,4,2,96,768),BF),((R,W),BF),((R,W),BF),
        ((16,W),F32),((R,2),F32)]
    return pl.pallas_call(forward_kernel,
        in_specs=[M,M]+[V]*8,out_specs=[A]*16+[V,V],out_shape=[sds(*o) for o in outs],
        scratch_shapes=[v((4,4,2,16,128),BF),v((4,4,48,2304),BF),v((4,4,48,768),BF),v((4,4,48,3072),BF),
            v((24,2304),BF),v((24,768),BF),v((24,3072),BF),v((1,48,2304),BF),v((1,48,768),BF),v((1,48,3072),BF),
            v((R,W),F32),v((R,W),F32),v((R,W),BF),v((R,W),BF),v((R,3*W),BF),v((2,400,400),F32),v((R,W),BF),v((R,W),BF),
            v((R,4*W),BF),v((R,4*W),BF),v((R,W),BF),v((R,W),BF),v((4,4,2,96,768),BF),v((2,2,400,400),BF),v((1,2*W),F32),v((1,4*W),F32),
            D((5,)),D((5,)),D((1,)),D((14,)),D((14,)),D((4,21)),D((4,21)),D((2,)),D((16,))],
        compiler_params=pltpu.CompilerParams(collective_id=0,has_side_effects=True,vmem_limit_bytes=60<<20),name="forward")(
        groups,offsets,small,wq,wp,w1,w2,tok,cot,mask)

def normalize(values, gain, shift):
    center = values - jnp.mean(values, axis=-1, keepdims=True)
    spread = jnp.mean(center * center, axis=-1, keepdims=True)
    return center * lax.rsqrt(spread + eps_norm) * gain + shift

def activate(values):
    return jax.nn.gelu(values, approximate=False)

def segment_rows(groups, offsets, rows):
    lengths = jnp.where(groups == 0, P_SMALL, jnp.where(groups == 1, P_MID, P_LARGE)).astype(jnp.int32)
    positions = jnp.arange(rows, dtype=jnp.int32)
    inside = (positions[None, :] >= offsets[:, None]) & (positions[None, :] < offsets[:, None] + lengths[:, None])
    labels = jnp.arange(1, offsets.shape[0] + 1, dtype=jnp.int32)
    return jnp.sum(jnp.where(inside, labels[:, None], 0), axis=0) - 1

def settle(mid, rows):
    half = rows.shape[0] // 2
    cut = P_MID * (half // P_MID)
    gap = half - cut
    end = rows.shape[0] - gap
    moved = jnp.concatenate([rows[:cut], rows[end:], rows[cut:end]], axis=0)
    return jnp.where(mid, moved, rows)

def unsettle(mid, rows):
    half = rows.shape[0] // 2
    cut = P_MID * (half // P_MID)
    gap = half - cut
    moved = jnp.concatenate([rows[:cut], rows[half:], rows[cut:half]], axis=0)
    return jnp.where(mid, moved, rows)

def shards(n, tokens, mask_bits, groups, offsets, mask_token, ln1_gain, ln1_bias, w_qkv, b_qv, w_proj, b_proj,
           ln2_gain, ln2_bias, w_fc1, b_fc1, w_fc2, b_fc2, cotangent):
    vectors = (mask_token, ln1_gain, ln1_bias, b_qv, b_proj, ln2_gain, ln2_bias, b_fc1, b_fc2)
    sizes = [v.shape[0] for v in vectors]
    places = [sum(sizes[:i]) for i in range(len(sizes) + 1)]
    fits = n == 32 and places[-1] <= 1024
    packed = jnp.concatenate(vectors)
    if fits:
        small = jnp.pad(packed, (0, 2048 - places[-1])).reshape(16, 128)
        gathered = gather_all(small, w_qkv, w_proj, w_fc1, w_fc2)
        small_all = gathered[0].reshape(n, 2048)
        full_qkv, full_proj, full_fc1, full_fc2 = [
            g.reshape(-1, g.shape[-1]) for g in gathered[1:]]
    else:
        small_all = lax.all_gather(packed, "dp", axis=0, tiled=False)
        full_qkv, full_proj, full_fc1, full_fc2 = [
            lax.all_gather(w, "dp", axis=0, tiled=True) for w in (w_qkv, w_proj, w_fc1, w_fc2)]
    token_mask, gain_one, shift_one, bias_qv, bias_proj, gain_two, shift_two, bias_one, bias_two = [
        small_all[:, places[i]:places[i + 1]].reshape(-1).astype(F32) for i in range(len(sizes))]
    rows, width = tokens.shape
    half = rows // 2
    mid = groups[0] == 1
    tokens = settle(mid, tokens)
    cotangent = settle(mid, cotangent)
    mask_bits = settle(mid, mask_bits)
    segment = settle(mid, segment_rows(groups, offsets, rows))
    valid_col = (segment >= 0).astype(F32)[:, None]
    halves = segment.reshape(2, half)
    bias = jnp.where(halves[:, :, None] == halves[:, None, :], 0.0, -1e30).astype(F32)
    masked_rows = (mask_bits == 1)[:, None]
    start = jnp.where(masked_rows, token_mask[None, :], tokens.astype(F32))
    normed_one = normalize(start, gain_one, shift_one).astype(BF)
    full_bias = jnp.concatenate([bias_qv[:width], jnp.zeros((width,), F32), bias_qv[width:]])
    projected = (jnp.dot(normed_one, full_qkv, preferred_element_type=F32) + full_bias).astype(BF)
    context_low, probs = attn_fwd(projected, bias)
    middle = start + valid_col * (jnp.dot(context_low, full_proj, preferred_element_type=F32) + bias_proj)
    normed_two = normalize(middle, gain_two, shift_two).astype(BF)
    hidden_pre = jnp.dot(normed_two, full_fc1, preferred_element_type=F32) + bias_one
    hidden_low = activate(hidden_pre).astype(BF)
    result = middle + valid_col * (jnp.dot(hidden_low, full_fc2, preferred_element_type=F32) + bias_two)
    output = unsettle(mid, result.astype(BF))
    upstream = cotangent.astype(F32)
    grad_two = (valid_col * upstream).astype(BF)
    grad_wfc2 = tn(hidden_low, grad_two)
    grad_bfc2 = jnp.sum(grad_two.astype(F32), axis=0)
    grad_hidden = nt(grad_two, full_fc2)
    _, gelu_back = jax.vjp(activate, hidden_pre)
    grad_pre = gelu_back(grad_hidden)[0].astype(BF)
    grad_wfc1 = tn(normed_two, grad_pre)
    grad_bfc1 = jnp.sum(grad_pre.astype(F32), axis=0)
    grad_normed_two = nt(grad_pre, full_fc1)
    _, norm_back_two = jax.vjp(normalize, middle, gain_two, shift_two)
    grad_mid_part, grad_gain_two, grad_shift_two = norm_back_two(grad_normed_two)
    grad_middle = upstream + grad_mid_part
    grad_branch = (valid_col * grad_middle).astype(BF)
    grad_wproj = tn(context_low, grad_branch)
    grad_bproj = jnp.sum(grad_branch.astype(F32), axis=0)
    grad_context = nt(grad_branch, full_proj).astype(BF)
    dq, dk, dv = attn_bwd(projected, grad_context, context_low, probs)
    grad_projected = jnp.concatenate([dq, dk, dv], axis=1)
    grad_wqkv = tn(normed_one, grad_projected)
    grad_bqv = jnp.concatenate([jnp.sum(dq.astype(F32), axis=0), jnp.sum(dv.astype(F32), axis=0)])
    grad_normed_one = nt(grad_projected, full_qkv)
    _, norm_back_one = jax.vjp(normalize, start, gain_one, shift_one)
    grad_start_part, grad_gain_one, grad_shift_one = norm_back_one(grad_normed_one)
    grad_start = grad_middle + grad_start_part
    grad_token = jnp.sum(jnp.where(masked_rows, grad_start, 0.0), axis=0)
    grad_input = unsettle(mid, jnp.where(masked_rows, 0.0, grad_start))
    grad_vectors = (grad_token, grad_gain_one, grad_shift_one, grad_bqv, grad_bproj, grad_gain_two, grad_shift_two,
                    grad_bfc1, grad_bfc2)
    grad_small = jnp.concatenate([g.reshape(n, -1) for g in grad_vectors], axis=1)
    if fits:
        grad_small = jnp.pad(grad_small, ((0, 0), (0, 1024 - places[-1]))).reshape(4, 4, 2, 8, 128)
        shares = scatter_all(
            grad_small,
            *[g.astype(BF).reshape(4, 4, g.shape[0] // 16, g.shape[1]) for g in (grad_wqkv, grad_wproj, grad_wfc1)],
            grad_wfc2.astype(BF).reshape(4, 4, 2, grad_wfc2.shape[0] // 32, width))
        small_share = shares[0].reshape(1024)
        share_qkv, share_proj, share_fc1, share_fc2 = shares[1:]
    else:
        small_share = lax.psum_scatter(grad_small, "dp", scatter_dimension=0, tiled=False)
        share_qkv, share_proj, share_fc1, share_fc2 = [
            lax.psum_scatter(g, "dp", scatter_dimension=0, tiled=True)
            for g in (grad_wqkv, grad_wproj, grad_wfc1, grad_wfc2)]
    v = [small_share[places[i]:places[i + 1]] for i in range(len(sizes))]
    return (output, grad_input, v[0], v[1], v[2], share_qkv, v[3], share_proj, v[4], v[5], v[6], share_fc1, v[7],
            share_fc2, v[8])


def pack_small(vectors):
    total = jnp.zeros((16, 128), F32)
    for i, v in enumerate(vectors):
        total = total + jnp.pad(v.astype(F32)[None, :], ((i, 15 - i), (0, 128 - v.shape[0])))
    return total.astype(BF)

def shards_fast(n, tokens, mask_bits, groups, offsets, mask_token, ln1_gain, ln1_bias, w_qkv, b_qv, w_proj, b_proj,
           ln2_gain, ln2_bias, w_fc1, b_fc1, w_fc2, b_fc2, cotangent):
    vectors = (mask_token, ln1_gain, ln1_bias, b_qv, b_proj, ln2_gain, ln2_bias, b_fc1, b_fc2)
    sizes = [v.shape[0] for v in vectors]
    places = [sum(sizes[:i]) for i in range(len(sizes) + 1)]
    small = pack_small(vectors)
    mask_col = mask_bits.astype(F32)[:, None]
    (gq, gp, g1, g2, probs, normed_one, normed_two, context_low, projected, hidden_low, dgelu, start, middle, part2,
     grad_two, cots, vec, meta) = forward(groups, offsets, small, w_qkv, w_proj, w_fc1, w_fc2, tokens, cotangent, mask_col)
    full_qkv, full_proj, full_fc1, full_fc2 = [g.reshape(-1, g.shape[-1]) for g in (gq, gp, g1, g2)]
    rows, width = tokens.shape
    mid = groups[0] == 1
    valid_col = meta[:, 0:1]
    masked_rows = meta[:, 1:2] > 0
    gain_one, shift_one, gain_two, shift_two, bias_two = vec[1], vec[2], vec[5], vec[6], vec[8]
    start = start.astype(F32)
    result = middle + valid_col * (jnp.dot(hidden_low, full_fc2, preferred_element_type=F32) + bias_two)
    output = unsettle(mid, result.astype(BF))
    upstream = cots.astype(F32)
    grad_bfc2 = jnp.sum(grad_two.astype(F32), axis=0)
    grad_pre = (nt(grad_two, full_fc2) * dgelu.astype(F32)).astype(BF)
    grad_wfc1 = tn(normed_two, grad_pre)
    grad_bfc1 = jnp.sum(grad_pre.astype(F32), axis=0)
    grad_normed_two = nt(grad_pre, full_fc1)
    _, norm_back_two = jax.vjp(normalize, middle, gain_two, shift_two)
    grad_mid_part, grad_gain_two, grad_shift_two = norm_back_two(grad_normed_two)
    grad_middle = upstream + grad_mid_part
    grad_branch = (valid_col * grad_middle).astype(BF)
    grad_wproj = tn(context_low, grad_branch)
    grad_bproj = jnp.sum(grad_branch.astype(F32), axis=0)
    grad_context = nt(grad_branch, full_proj).astype(BF)
    dq, dk, dv = attn_bwd(projected, grad_context, context_low, probs.reshape(2, 6, 2, 400, 400))
    grad_projected = jnp.concatenate([dq, dk, dv], axis=1)
    grad_wqkv = tn(normed_one, grad_projected)
    grad_bqv = jnp.concatenate([jnp.sum(dq.astype(F32), axis=0), jnp.sum(dv.astype(F32), axis=0)])
    grad_normed_one = nt(grad_projected, full_qkv)
    _, norm_back_one = jax.vjp(normalize, start, gain_one, shift_one)
    grad_start_part, grad_gain_one, grad_shift_one = norm_back_one(grad_normed_one)
    grad_start = grad_middle + grad_start_part
    grad_token = jnp.sum(jnp.where(masked_rows, grad_start, 0.0), axis=0)
    grad_input = unsettle(mid, jnp.where(masked_rows, 0.0, grad_start))
    grad_vectors = (grad_token, grad_gain_one, grad_shift_one, grad_bqv, grad_bproj, grad_gain_two, grad_shift_two,
                    grad_bfc1, grad_bfc2)
    grad_small = jnp.concatenate([g.reshape(n, -1) for g in grad_vectors], axis=1)
    if True:
        grad_small = jnp.pad(grad_small, ((0, 0), (0, 1024 - places[-1]))).reshape(4, 4, 2, 8, 128)
        shares = scatter_all(
            grad_small,
            *[g.astype(BF).reshape(4, 4, g.shape[0] // 16, g.shape[1]) for g in (grad_wqkv, grad_wproj, grad_wfc1)],
            part2)
        small_share = shares[0].reshape(1024)
        share_qkv, share_proj, share_fc1, share_fc2 = shares[1:]
    v = [small_share[places[i]:places[i + 1]] for i in range(len(sizes))]
    return (output, grad_input, v[0], v[1], v[2], share_qkv, v[3], share_proj, v[4], v[5], v[6], share_fc1, v[7],
            share_fc2, v[8])

def solution(mesh):
    row, flat = P("dp", None), P("dp")
    return jax.shard_map(
        functools.partial(shards_fast if mesh.shape["dp"] == 32 else shards, mesh.shape["dp"]),
        mesh=mesh,
        in_specs=(row, flat, flat, flat, flat, flat, flat, row, flat, row, flat, flat, flat, row, flat, row, flat, row),
        out_specs=(row, row, flat, flat, flat, row, flat, row, flat, flat, flat, row, flat, row, flat),
        check_vma=False,
    )
```

```python
import functools

import jax
import jax.numpy as jnp
from jax import lax
from jax.experimental import pallas as pl
from jax.experimental.pallas import tpu as pltpu
from jax.sharding import PartitionSpec as P

P_SMALL = 100
P_MID = 196
P_LARGE = 400
eps_norm = 1e-06

def nt(a,b): return lax.dot_general(a,b,(((1,),(1,)),((),())),preferred_element_type=jnp.float32)
def nn(a,b): return lax.dot_general(a,b,(((1,),(0,)),((),())),preferred_element_type=jnp.float32)
def tn(a,b): return lax.dot_general(a,b,(((0,),(0,)),((),())),preferred_element_type=jnp.float32)

def attn_fwd_kernel(bias_ref, q_ref, k_ref, v_ref, ctx_ref, p_ref):
    q=q_ref[...]; k=k_ref[...]; v=v_ref[...]
    rows,width=q.shape
    lane=lax.broadcasted_iota(jnp.int32,(rows,width),1)
    bias=bias_ref[0]
    outs=[]
    for j in range(2):
        mine=(lane>=64)==(j==1)
        qj=jnp.where(mine,q,jnp.zeros_like(q))
        s=nt(qj,k)*0.18033688011112042+bias
        m=jnp.max(s,axis=1,keepdims=True)
        e=jnp.exp2(s-m)
        l=jnp.sum(e,axis=1,keepdims=True)
        p=(e*(1.0/l)).astype(jnp.bfloat16)
        p_ref[0,0,j]=p
        outs.append(nn(p,v))
    ctx_ref[...]=jnp.where(lane<64,outs[0],outs[1]).astype(jnp.bfloat16)

def attn_fwd(proj,bias):
    rows=proj.shape[0]; half=rows//2; width=proj.shape[1]//3; pairs=width//128
    return pl.pallas_call(attn_fwd_kernel,grid=(2,pairs),
        in_specs=[pl.BlockSpec((1,half,half),lambda b,p:(b,0,0)),
                  pl.BlockSpec((half,128),lambda b,p:(b,p)),
                  pl.BlockSpec((half,128),lambda b,p:(b,p+pairs)),
                  pl.BlockSpec((half,128),lambda b,p:(b,p+2*pairs))],
        out_specs=[pl.BlockSpec((half,128),lambda b,p:(b,p)),
                   pl.BlockSpec((1,1,2,half,half),lambda b,p:(b,p,0,0,0))],
        out_shape=[jax.ShapeDtypeStruct((rows,width),jnp.bfloat16),
                   jax.ShapeDtypeStruct((2,pairs,2,half,half),jnp.bfloat16)],
        compiler_params=pltpu.CompilerParams(vmem_limit_bytes=40<<20),name="attn_fwd")(bias,proj,proj,proj)

def attn_bwd_kernel(q_ref,k_ref,v_ref,g_ref,c_ref,p_ref,dq_ref,dk_ref,dv_ref):
    q=q_ref[...]; k=k_ref[...]; v=v_ref[...]; g=g_ref[...]; c=c_ref[...]
    rows,width=q.shape
    lane=lax.broadcasted_iota(jnp.int32,(rows,width),1)
    gc=g.astype(jnp.float32)*c.astype(jnp.float32)
    dq=[];dk=[];dv=[]
    for j in range(2):
        mine=(lane>=64)==(j==1)
        zero=jnp.zeros_like(q)
        qj=jnp.where(mine,q,zero); gj=jnp.where(mine,g,zero)
        di=jnp.sum(jnp.where(mine,gc,0.0),axis=1,keepdims=True)
        p=p_ref[0,0,j]
        dp=nt(gj,v)
        ds=(p.astype(jnp.float32)*(dp-di)).astype(jnp.bfloat16)
        dq.append(nn(ds,k))
        dk.append(tn(ds,qj))
        dv.append(tn(p,gj))
    dq_ref[...]=(jnp.where(lane<64,dq[0],dq[1])*0.125).astype(jnp.bfloat16)
    dk_ref[...]=((dk[0]+dk[1])*0.125).astype(jnp.bfloat16)
    dv_ref[...]=(dv[0]+dv[1]).astype(jnp.bfloat16)

def attn_bwd(proj,gctx,ctx,p):
    rows=proj.shape[0]; half=rows//2; width=proj.shape[1]//3; pairs=width//128
    sp=lambda o: pl.BlockSpec((half,128),lambda b,p:(b,p+o*pairs))
    return pl.pallas_call(attn_bwd_kernel,grid=(2,pairs),
        in_specs=[sp(0),sp(1),sp(2),sp(0),sp(0),pl.BlockSpec((1,1,2,half,half),lambda b,p:(b,p,0,0,0))],
        out_specs=[sp(0)]*3,
        out_shape=[jax.ShapeDtypeStruct((rows,width),jnp.bfloat16)]*3,
        compiler_params=pltpu.CompilerParams(vmem_limit_bytes=40<<20),name="attn_bwd")(proj,proj,proj,gctx,ctx,p)
MESH=pl.DeviceIdType.MESH
F32=jnp.float32; BF=jnp.bfloat16

def place():
    me=lax.axis_index("dp")
    c=lax.rem(me,2); x=lax.rem(me//2,2); y=lax.rem(me//4,2); z=me//8
    return c,x,y,z
def dev(z,yx,c): return ((z*4+yx)*2+c,)

def greet():
    c,x,y,z=place(); yx=y*2+x
    bar=pltpu.get_barrier_semaphore()
    peers=[dev(z,yx,1-c),dev(z,y*2+1-x,c),dev(z,(1-y)*2+x,c)]+[dev(lax.rem(z+k,4),yx,c) for k in (1,2,3)]
    for p in peers: pl.semaphore_signal(bar,inc=1,device_id=p,device_id_type=MESH)
    pl.semaphore_wait(bar,len(peers))

class Gather:
    def __init__(self,view,ss,rs):
        self.view=view; self.ss=ss; self.rs=rs
        c,x,y,z=place()
        self.c=c; self.z=z; self.yx=y*2+x
        self.xn=y*2+1-x; self.yn=(1-y)*2+x; self.dg=(1-y)*2+1-x
        self.sends=[]
    def _cp(self,src,dst,slot,d):
        return pltpu.make_async_remote_copy(src_ref=src,dst_ref=dst,send_sem=self.ss.at[slot],recv_sem=self.rs.at[slot],device_id=d,device_id_type=MESH)
    def send(self,src,dst,slot,d):
        cp=self._cp(src,dst,slot,d); cp.start(); self.sends.append(cp)
    def got(self,dst,slot,d):
        self._cp(dst,dst,slot,d).wait_recv()
    def one(self,z): return self.view(pl.ds(z,1),self.yx,self.c)
    def z_send(self,src):
        for k in (1,2,3):
            self.send(src,self.one(self.z),k-1,dev(lax.rem(self.z+k,4),self.yx,self.c))
    def sib(self,ref,slot): self.send(ref,ref,slot,dev(self.z,self.yx,1-self.c))
    def z_recv(self):
        for k in (1,2,3):
            zz=lax.rem(self.z+4-k,4)
            self.got(self.one(zz),k-1,dev(zz,self.yx,self.c))
    def xy_send(self):
        r=self.view(pl.ds(0,4),self.yx,self.c)
        self.send(r,r,3,dev(self.z,self.xn,self.c))
        self.send(r,r,4,dev(self.z,self.yn,self.c))
        for k in (1,2,3): self.sib(self.one(lax.rem(self.z+4-k,4)),6+k)
    def xy_recv(self):
        rx=self.view(pl.ds(0,4),self.xn,self.c)
        self.got(rx,3,dev(self.z,self.xn,self.c))
        h=self.view(pl.ds(0,2),self.xn,self.c)
        self.send(h,h,5,dev(self.z,self.yn,self.c))
        ry=self.view(pl.ds(0,4),self.yn,self.c)
        self.got(ry,4,dev(self.z,self.yn,self.c))
        h=self.view(pl.ds(2,2),self.yn,self.c)
        self.send(h,h,6,dev(self.z,self.xn,self.c))
        self.sib(rx,10); self.sib(ry,11)
    def diag_recv(self):
        a=self.view(pl.ds(0,2),self.dg,self.c)
        self.got(a,5,dev(self.z,self.yn,self.c))
        self.sib(a,12)
        b=self.view(pl.ds(2,2),self.dg,self.c)
        self.got(b,6,dev(self.z,self.xn,self.c))
        self.sib(b,13)
    def finish(self):
        o=1-self.c; s=dev(self.z,self.yx,o)
        for k in (1,2,3): self.got(self.view(pl.ds(lax.rem(self.z+4-k,4),1),self.yx,o),6+k,s)
        self.got(self.view(pl.ds(0,4),self.xn,o),10,s)
        self.got(self.view(pl.ds(0,4),self.yn,o),11,s)
        self.got(self.view(pl.ds(0,2),self.dg,o),12,s)
        self.got(self.view(pl.ds(2,2),self.dg,o),13,s)
    def drain(self):
        for cp in self.sends: cp.wait_send()

def cols_view(ref):
    half=ref.shape[-1]//2
    def view(zs,yx,lane): return ref.at[zs,yx,:,pl.ds(pl.multiple_of(lane*half,128),half)]
    return view
def rows_view(ref):
    def view(zs,yx,lane): return ref.at[zs,yx,lane]
    return view

def join(c,own,sib):
    a=own.astype(F32); b=sib.astype(F32)
    return jnp.concatenate([jnp.where(c==0,a,b),jnp.where(c==0,b,a)],axis=0).astype(BF)

def gather_kernel(sm_ref,q_ref,p_ref,f1_ref,f2_ref,gs_ref,gq_ref,gp_ref,g1_ref,g2_ref,
        sq,sp,s1,bq,bp,b1,ss0,rs0,ssl,ss,rs):
    greet()
    c,x,y,z=place(); yx=y*2+x
    sibd=dev(z,yx,1-c)
    first=[]
    def swap(src,dst,i):
        cp=pltpu.make_async_remote_copy(src_ref=src,dst_ref=dst,send_sem=ss0.at[i],recv_sem=rs0.at[i],device_id=sibd,device_id_type=MESH)
        cp.start(); first.append(cp)
    swap(sm_ref,gs_ref.at[z,yx,c],0)
    swap(q_ref,sq,1); swap(p_ref,sp,2); swap(f1_ref,s1,3)
    swap(f2_ref,g2_ref.at[z,yx,c],4)
    gs=[Gather(rows_view(gs_ref),ss.at[0],rs.at[0]),Gather(cols_view(gq_ref),ss.at[1],rs.at[1]),Gather(cols_view(gp_ref),ss.at[2],rs.at[2]),
        Gather(cols_view(g1_ref),ss.at[3],rs.at[3]),Gather(rows_view(g2_ref),ss.at[4],rs.at[4])]
    local=[]
    def keep(src,dst,i):
        cp=pltpu.make_async_copy(src,dst,ssl.at[i]); cp.start(); local.append(cp)
    def half(b):
        h=b.shape[-1]//2
        return b.at[:,:,pl.ds(pl.multiple_of(c*h,128),h)]
    keep(sm_ref,gs_ref.at[z,yx,c],0)
    keep(f2_ref,g2_ref.at[z,yx,c],4)
    def begin(i):
        if i==0:
            local[0].wait(); gs[0].z_send(gs[0].one(z))
        elif i==4:
            local[1].wait(); gs[4].z_send(gs[4].one(z))
        else:
            own,sib,buf,dst={1:(q_ref,sq,bq,gq_ref),2:(p_ref,sp,bp,gp_ref),3:(f1_ref,s1,b1,g1_ref)}[i]
            first[i].wait_recv()
            buf[0]=join(c,own[...],sib[...])
            keep(buf,dst.at[pl.ds(z,1),yx],i)
            gs[i].z_send(half(buf))
    begin(0); begin(1)
    gs[0].z_recv(); gs[0].xy_send()
    begin(2)
    gs[1].z_recv(); local[2].wait(); gs[1].xy_send()
    begin(3)
    gs[0].xy_recv()
    gs[2].z_recv(); local[3].wait(); gs[2].xy_send()
    gs[0].diag_recv()
    gs[1].xy_recv()
    begin(4)
    gs[3].z_recv(); local[4].wait(); gs[3].xy_send()
    gs[2].xy_recv()
    gs[1].diag_recv()
    gs[2].diag_recv()
    gs[4].z_recv(); gs[4].xy_send()
    gs[3].xy_recv()
    gs[3].diag_recv()
    gs[4].xy_recv()
    gs[4].diag_recv()
    first[0].wait_recv(); first[4].wait_recv()
    for g in gs: g.finish()
    for cp in first: cp.wait_send()
    for g in gs: g.drain()

def gather_all(small,wq,wp,w1,w2):
    sds=jax.ShapeDtypeStruct
    nq,np_,n1,n2=wq.shape[1],wp.shape[1],w1.shape[1],w2.shape[1]
    r=wq.shape[0]; r2=w2.shape[0]
    V=pl.BlockSpec(memory_space=pltpu.VMEM); A=pl.BlockSpec(memory_space=pl.ANY)
    D=pltpu.SemaphoreType.DMA
    return pl.pallas_call(gather_kernel,
        in_specs=[V]*5,out_specs=[A]*5,
        out_shape=[sds((4,4,2)+small.shape,BF),sds((4,4,2*r,nq),BF),sds((4,4,2*r,np_),BF),sds((4,4,2*r,n1),BF),sds((4,4,2,r2,n2),BF)],
        scratch_shapes=[pltpu.VMEM((r,n),BF) for n in (nq,np_,n1)]+[pltpu.VMEM((1,2*r,n),BF) for n in (nq,np_,n1)]+
            [D((5,)),D((5,)),D((5,)),D((5,14)),D((5,14))],
        compiler_params=pltpu.CompilerParams(collective_id=0,has_side_effects=True,vmem_limit_bytes=16<<20),name="gather_all")(small,wq,wp,w1,w2)

class Scatter:
    def __init__(self,view,a,s,rxa,ryb,rx,ry,b,rz,ss,rs,ls):
        self.view=view; self.a=a; self.s=s; self.rxa=rxa; self.ryb=ryb; self.rx=rx; self.ry=ry; self.b=b; self.rz=rz
        self.ss=ss; self.rs=rs; self.ls=ls
        c,x,y,z=place()
        self.c=c; self.z=z; self.yx=y*2+x
        self.xn=y*2+1-x; self.yn=(1-y)*2+x; self.dg=(1-y)*2+1-x
        self.cps={}
    def send(self,src,dst,slot,d):
        cp=pltpu.make_async_remote_copy(src_ref=src,dst_ref=dst,send_sem=self.ss.at[slot],recv_sem=self.rs.at[slot],device_id=d,device_id_type=MESH)
        cp.start(); self.cps[slot]=cp
    def r0(self):
        self.send(self.view(1-self.c),self.s,0,dev(self.z,self.yx,1-self.c))
        self.loc=pltpu.make_async_copy(self.view(self.c),self.a,self.ls); self.loc.start()
    def r1(self):
        self.loc.wait(); self.cps[0].wait_recv()
        a,s=self.a,self.s
        def add(yx):
            def body(i,_):
                a[i,yx]=(a[i,yx].astype(F32)+s[i,yx].astype(F32)).astype(a.dtype)
                return 0
            lax.fori_loop(0,4,body,0)
        xd=dev(self.z,self.xn,self.c); yd=dev(self.z,self.yn,self.c)
        add(self.dg)
        self.send(a.at[pl.ds(0,2),self.dg],self.rxa,1,xd)
        self.send(a.at[pl.ds(2,2),self.dg],self.ryb,2,yd)
        add(self.xn)
        self.send(a.at[pl.ds(0,2),self.xn],self.rx.at[pl.ds(0,2)],3,xd)
        add(self.yn)
        self.send(a.at[pl.ds(2,2),self.yn],self.ry.at[pl.ds(2,2)],4,yd)
        add(self.yx)
    def r2(self):
        a=self.a
        xd=dev(self.z,self.xn,self.c); yd=dev(self.z,self.yn,self.c)
        self.cps[1].wait_recv()
        def body(i,_):
            a[i,self.yn]=(a[i,self.yn].astype(F32)+self.rxa[i].astype(F32)).astype(a.dtype)
            return 0
        lax.fori_loop(0,2,body,0)
        self.send(a.at[pl.ds(0,2),self.yn],self.ry.at[pl.ds(0,2)],6,yd)
        self.cps[2].wait_recv()
        def body(i,_):
            a[i+2,self.xn]=(a[i+2,self.xn].astype(F32)+self.ryb[i].astype(F32)).astype(a.dtype)
            return 0
        lax.fori_loop(0,2,body,0)
        self.send(a.at[pl.ds(2,2),self.xn],self.rx.at[pl.ds(2,2)],5,xd)
    def r3(self):
        for s in (3,4,5,6): self.cps[s].wait_recv()
        def body(i,_):
            self.b[i]=(self.a[i,self.yx].astype(F32)+self.rx[i].astype(F32)+self.ry[i].astype(F32)).astype(self.b.dtype)
            return 0
        lax.fori_loop(0,4,body,0)
        for k in (1,2,3):
            zz=lax.rem(self.z+k,4)
            self.send(self.b.at[zz],self.rz.at[k-1],6+k,dev(zz,self.yx,self.c))
    def r4(self):
        t=self.b[self.z].astype(F32)
        for k in (1,2,3):
            self.cps[6+k].wait_recv()
            t=t+self.rz[k-1].astype(F32)
        return t
    def drain(self):
        for cp in self.cps.values(): cp.wait_send()

def scatter_scratch(r,n,dt):
    V=pltpu.VMEM
    return [V((4,4,r,n),dt),V((4,4,r,n),dt),V((2,r,n),dt),V((2,r,n),dt),V((4,r,n),dt),V((4,r,n),dt),V((4,r,n),dt),V((3,r,n),dt)]

def scatter_kernel(sm_ref,q_ref,p_ref,f1_ref,f2_ref,os_ref,oq_ref,op_ref,o1_ref,o2_ref,*sc):
    bufs=[sc[8*i:8*i+8] for i in range(5)]
    fin=sc[40:46]; ss,rs,ls,fs,fr=sc[46:]
    greet()
    c,x,y,z=place(); yx=y*2+x
    def cv(ref):
        h=ref.shape[-1]//2
        return lambda lane: ref.at[:,:,:,pl.ds(pl.multiple_of(lane*h,128),h)]
    def rv(ref): return lambda lane: ref.at[:,:,lane]
    refs=[sm_ref,q_ref,p_ref,f1_ref,f2_ref]
    S=[Scatter((rv if i in (0,4) else cv)(refs[i]),*bufs[i],ss.at[i],rs.at[i],ls.at[i]) for i in range(5)]
    order=[4,3,2,1,0]
    sibd=dev(z,yx,1-c)
    ends=[]
    outs={1:oq_ref,2:op_ref,3:o1_ref}
    def end(i):
        t=S[i].r4()
        if i==0: os_ref[...]=t
        elif i==4: o2_ref[...]=t
        else:
            f,rf=fin[2*(i-1)],fin[2*(i-1)+1]
            r=t.shape[0]//2
            f[0]=t[:r]; f[1]=t[r:]
            cp=pltpu.make_async_remote_copy(src_ref=f.at[1-c],dst_ref=rf,send_sem=fs.at[i],recv_sem=fr.at[i],device_id=sibd,device_id_type=MESH)
            cp.start(); ends.append((i,cp))
    def close():
        for i,cp in ends:
            cp.wait_recv()
            f,rf=fin[2*(i-1)],fin[2*(i-1)+1]
            own=f[c]; oth=rf[...]
            o=outs[i]; h=own.shape[-1]
            o[:,:h]=jnp.where(c==0,own,oth); o[:,h:]=jnp.where(c==0,oth,own)
            cp.wait_send()
    for i in order: S[i].r0()
    n=len(order)
    stages=[lambda i:S[i].r1(),lambda i:S[i].r2(),lambda i:S[i].r3(),lambda i:end(i)]
    for t in range(n+3):
        for s in range(3,-1,-1):
            k=t-s
            if 0<=k<n: stages[s](order[k])
    close()
    for s in S: s.drain()

def scatter_all(sm,q,p,f1,f2):
    sds=jax.ShapeDtypeStruct
    V=pl.BlockSpec(memory_space=pltpu.VMEM); A=pl.BlockSpec(memory_space=pl.ANY)
    D=pltpu.SemaphoreType.DMA
    sc=[]
    for a,dt in ((sm,F32),(q,BF),(p,BF),(f1,BF),(f2,BF)):
        if a.ndim==5: sc+=scatter_scratch(a.shape[3],a.shape[4],dt)
        else: sc+=scatter_scratch(a.shape[2],a.shape[3]//2,dt)
    outs=[sds(sm.shape[3:],F32)]
    for a in (q,p,f1):
        r,n=a.shape[2]//2,a.shape[3]
        sc+=[pltpu.VMEM((2,r,n//2),F32),pltpu.VMEM((r,n//2),F32)]
        outs.append(sds((r,n),F32))
    outs.append(sds(f2.shape[3:],F32))
    return pl.pallas_call(scatter_kernel,in_specs=[A]*5,out_specs=[V]*5,out_shape=outs,
        scratch_shapes=sc+[D((5,10)),D((5,10)),D((5,)),D((5,)),D((5,))],
        compiler_params=pltpu.CompilerParams(collective_id=1,has_side_effects=True,vmem_limit_bytes=56<<20),name="scatter_all")(sm,q,p,f1,f2)
class Gather2:
    def __init__(self,view,ss,rs):
        self.view=view; self.ss=ss; self.rs=rs
        c,x,y,z=place()
        self.c=c; self.z=z; self.yx=y*2+x
        self.xn=y*2+1-x; self.yn=(1-y)*2+x; self.dg=(1-y)*2+1-x
        self.xd=dev(z,self.xn,c); self.yd=dev(z,self.yn,c); self.sd=dev(z,self.yx,1-c)
        self.sends=[]
    def at(self,k,yx,lane=None): return self.view(pl.ds(lax.rem(self.z+4-k,4),1),yx,self.c if lane is None else lane)
    def all(self,yx,lane=None): return self.view(pl.ds(0,4),yx,self.c if lane is None else lane)
    def _cp(self,src,dst,slot,d):
        return pltpu.make_async_remote_copy(src_ref=src,dst_ref=dst,send_sem=self.ss.at[slot],recv_sem=self.rs.at[slot],device_id=d,device_id_type=MESH)
    def send(self,src,dst,slot,d):
        cp=self._cp(src,dst,slot,d); cp.start(); self.sends.append(cp)
    def got(self,dst,slot,d): self._cp(dst,dst,slot,d).wait_recv()
    def near(self,src):
        self.send(src,self.at(0,self.yx),3,self.xd)
        self.send(src,self.at(0,self.yx),7,self.yd)
    def far(self,src):
        for k in (1,2,3): self.send(src,self.at(0,self.yx),k-1,dev(lax.rem(self.z+k,4),self.yx,self.c))
    def X0(self):
        r=self.at(0,self.xn); self.got(r,3,self.xd)
        self.send(r,r,11,self.yd)
        self.got(self.at(0,self.yn),7,self.yd)
    def Z(self):
        for k in (1,3,2):
            r=self.at(k,self.yx)
            self.got(r,k-1,dev(lax.rem(self.z+4-k,4),self.yx,self.c))
            self.send(r,r,3+k,self.xd); self.send(r,r,7+k,self.yd)
        for k in (1,3,2):
            r=self.at(k,self.yx); self.send(r,r,14+k,self.sd)
    def X(self):
        for k in (1,3,2):
            a=self.at(k,self.xn); b=self.at(k,self.yn)
            self.got(a,3+k,self.xd)
            if k==1: self.send(a,a,11+k,self.yd)
            self.got(b,7+k,self.yd)
            if k!=1: self.send(b,b,11+k,self.xd)
        for yx,s in ((self.xn,18),(self.yn,19)):
            r=self.all(yx); self.send(r,r,s,self.sd)
    def D(self):
        for k in (0,1,3,2):
            self.got(self.at(k,self.dg),11+k,self.yd if k<2 else self.xd)
        r=self.all(self.dg); self.send(r,r,20,self.sd)
    def F(self):
        o=1-self.c
        for k in (1,2,3): self.got(self.at(k,self.yx,o),14+k,self.sd)
        for yx,s in ((self.xn,18),(self.yn,19),(self.dg,20)): self.got(self.all(yx,o),s,self.sd)
    def drain(self):
        for cp in self.sends: cp.wait_send()

def gelu_parts(x):
    d=1.0+0.23164189*jnp.abs(x)
    t=pl.reciprocal(d,approx=True)
    t=t*(2.0-d*t)
    e=jnp.exp2(x*x*(-0.5*1.4426950408889634))
    q=((((0.5*1.061405429*t-0.5*1.453152027)*t+0.5*1.421413741)*t-0.5*0.284496736)*t+0.5*0.254829592)*t*e
    cdf=jnp.where(x>=0,1.0-q,q)
    return x*cdf, cdf+x*e*0.3989422804014327

def row_stats(x):
    inv=1.0/x.shape[1]
    mean=jnp.sum(x,axis=1,keepdims=True)*inv
    c=x-mean
    var=jnp.sum(c*c,axis=1,keepdims=True)*inv
    return c,lax.rsqrt(var+eps_norm)

def spread(each,total,cols):
    j=lax.broadcasted_iota(jnp.int32,(128,total),1); l=lax.broadcasted_iota(jnp.int32,(128,total),0)
    return jnp.where(j-cols*each==l,1.0,0.0).astype(BF)

def over(each,shape):
    j=lax.broadcasted_iota(jnp.int32,shape,1)
    return (j*((1<<22)//each+1))>>22

def settled(g1,r):
    return r+jnp.where(r>=400,-8*g1,jnp.where(r>=392,400*g1,0))

def segments(groups,offsets,pos):
    g=groups[0]
    length=jnp.where(g==0,P_SMALL,jnp.where(g==1,P_MID,P_LARGE))
    seg=jnp.full(pos.shape,-1,jnp.int32)
    for s in range(8):
        o=offsets[s]
        seg=jnp.where((pos>=o)&(pos<o+length),s,seg)
    return seg

def settle_rows(g1,read,write):
    def either(a,b): return [jnp.where(g1==1,u,w) for u,w in zip(a,b)]
    def body(i,_):
        r=pl.multiple_of(i*56,8)
        write(r,56,read(r,56)); return 0
    lax.fori_loop(0,7,body,0)
    write(392,8,either(read(792,8),read(392,8)))
    def body2(i,_):
        r=pl.multiple_of(400+i*40,8)
        write(r,40,either(read(pl.multiple_of(392+i*40,8),40),read(r,40))); return 0
    lax.fori_loop(0,10,body2,0)

def forward_kernel(groups,offsets,sm_ref,q_ref,p_ref,f1_ref,f2_ref,tok_ref,cot_ref,mask_ref,
        wq_o,wp_o,w1_o,w2_o,pr_o,n1_o,n2_o,ctx_o,pj_o,hid_o,dg_o,st_o,mid_o,pt2_o,gt_o,cs_o,vec_o,meta_o,
        gs,gq,gp,g1w,sq,sp,s1,bq,bp,b1,raw,mid,st,n1,pj,bias,ctx,n2,hid,dg,gt,cs,pt2,pst,bqv,bf1,
        ss0,rs0,ssl,sss,srs,ss,rs,psem,osem):
    greet()
    c,x,y,z=place(); yx=y*2+x
    sibd=dev(z,yx,1-c)
    first=[]
    def swap(src,dst,i):
        cp=pltpu.make_async_remote_copy(src_ref=src,dst_ref=dst,send_sem=ss0.at[i],recv_sem=rs0.at[i],device_id=sibd,device_id_type=MESH)
        cp.start(); first.append(cp)
    swap(sm_ref,gs.at[z,yx,c],0)
    swap(q_ref,sq,1); swap(p_ref,sp,2); swap(f1_ref,s1,3)
    swap(f2_ref,w2_o.at[z,yx,c],4)
    gs[z,yx,c]=sm_ref[...]
    own2=pltpu.make_async_copy(f2_ref,w2_o.at[z,yx,c],ssl.at[0]); own2.start()
    S=Gather(rows_view(gs),sss,srs)
    Q,Pj,F1=[Gather2(cols_view(r),ss.at[i],rs.at[i]) for i,r in enumerate((gq,gp,g1w))]
    F2=Gather2(rows_view(w2_o),ss.at[3],rs.at[3])
    outs=[]
    def put(src,dst):
        cp=pltpu.make_async_copy(src,dst,osem.at[len(outs)]); cp.start(); outs.append(cp)
    def build(i):
        own,sib,buf,dst={1:(q_ref,sq,bq,gq),2:(p_ref,sp,bp,gp),3:(f1_ref,s1,b1,g1w)}[i]
        first[i].wait_recv()
        j=join(c,own[...],sib[...])
        buf[0]=j; dst[z,yx]=j
    def half(b):
        h=b.shape[-1]//2
        return b.at[:,:,pl.ds(pl.multiple_of(c*h,128),h)]
    S.z_send(S.one(z))
    build(1); Q.far(half(bq)); Q.near(half(bq))
    S.z_recv(); S.xy_send()
    build(2); Pj.near(half(bp))
    build(3); F1.near(half(b1))
    S.xy_recv()
    own2.wait(); F2.near(F2.at(0,yx))
    Q.X0()
    g1=jnp.where(groups[0]==1,1,0)
    raw[...]=tok_ref[...].astype(F32)
    segc=segments(groups,offsets,settled(g1,lax.broadcasted_iota(jnp.int32,(800,1),0)))
    meta_o[:,0:1]=jnp.where(segc>=0,1.0,0.0)
    for b in range(2):
        segr=segments(groups,offsets,settled(g1,lax.broadcasted_iota(jnp.int32,(1,400),1)+400*b))
        bias[b]=jnp.where(segc[400*b:400*b+400]==segr,0.0,-1e30)
    S.diag_recv(); first[0].wait_recv(); S.finish()
    Pj.far(half(bp)); Pj.X0()
    X=gs[...].reshape(512,128)
    E=nn(X,spread(24,768,over(24,(128,768))))
    E=jnp.where(lax.broadcasted_iota(jnp.int32,(512,768),0)>>4==over(24,(512,768)),E,0.0).reshape(32,16,768)
    vec_o[...]=jnp.sum(E,axis=0)
    def wide(row,each,total):
        sel=jnp.where(lax.broadcasted_iota(jnp.int32,(32,512),1)==lax.broadcasted_iota(jnp.int32,(32,512),0)*16+row,1.0,0.0).astype(BF)
        e=nn(nn(sel,X).astype(BF),spread(each,total,over(each,(128,total))))
        e=jnp.where(lax.broadcasted_iota(jnp.int32,(32,total),0)==over(each,(32,total)),e,0.0)
        return jnp.sum(e,axis=0,keepdims=True)
    bqv[...]=wide(3,48,1536); bf1[...]=wide(7,96,3072)
    Q.Z(); F1.far(half(b1))
    F1.X0(); F2.X0()
    def write(r,n,v):
        t,m=v
        meta_o[pl.ds(r,n),1:2]=m
        mid[pl.ds(r,n),:]=jnp.where(m>0.0,vec_o[0:1,:],t)
    settle_rows(g1,lambda r,n:(raw[pl.ds(r,n),:],mask_ref[pl.ds(r,n),:]),write)
    def body(i,_):
        r=pl.ds(pl.multiple_of(i*80,16),80)
        s=mid[r,:]
        st[r,:]=s.astype(BF)
        cc,rstd=row_stats(s)
        n1[r,:]=(cc*rstd*vec_o[1:2,:]+vec_o[2:3,:]).astype(BF)
        return 0
    lax.fori_loop(0,10,body,0)
    put(st,st_o); put(n1,n1_o)
    Pj.Z(); F2.far(F2.at(0,yx))
    raw[...]=cot_ref[...].astype(F32)
    def write2(r,n,v): mid[pl.ds(r,n),:]=v[0]
    settle_rows(g1,lambda r,n:(raw[pl.ds(r,n),:],),write2)
    def body(i,_):
        r=pl.ds(pl.multiple_of(i*80,16),80)
        v=mid[r,:]
        cs[r,:]=v.astype(BF); gt[r,:]=(v*meta_o[r,0:1]).astype(BF)
        return 0
    lax.fori_loop(0,10,body,0)
    put(cs,cs_o); put(gt,gt_o)
    Q.X(); Pj.X(); Q.D(); Q.F()
    def qkv(j):
        r=nn(n1[...],gq[:,:,:,768*j:768*j+768].reshape(768,768))
        if j==0: r=r+bqv[:,:768]
        if j==2: r=r+bqv[:,768:]
        pj[:,768*j:768*j+768]=r.astype(BF)
    qkv(0); qkv(1); F1.Z(); Pj.D(); qkv(2)
    put(gq,wq_o); put(pj,pj_o)
    lane=lax.broadcasted_iota(jnp.int32,(400,128),1)
    def pcopy(it):
        return pltpu.make_async_copy(pst.at[lax.rem(it,2)],pr_o.at[it],psem.at[lax.rem(it,2)])
    def attend(it,_):
        b=it//6; p=lax.rem(it,6); s=lax.rem(it,2)
        r=pl.ds(pl.multiple_of(b*400,16),400)
        cc=lambda o: pl.ds(pl.multiple_of(o+p*128,128),128)
        @pl.when(it>=2)
        def _(): pcopy(it-2).wait()
        q=pj[r,cc(0)]; k=pj[r,cc(768)]; v=pj[r,cc(1536)]
        res=[]
        for j in range(2):
            qj=jnp.where((lane>=64)==(j==1),q,jnp.zeros_like(q))
            t=nt(qj,k)*0.18033688011112042+bias[b]
            e=jnp.exp2(t-jnp.max(t,axis=1,keepdims=True))
            pr=(e*(1.0/jnp.sum(e,axis=1,keepdims=True))).astype(BF)
            pst[s,j]=pr
            res.append(nn(pr,v))
        ctx[r,cc(0)]=jnp.where(lane<64,res[0],res[1]).astype(BF)
        pcopy(it).start()
        return 0
    lax.fori_loop(0,3,attend,0)
    Pj.F(); put(gp,wp_o)
    lax.fori_loop(3,6,attend,0)
    F1.X()
    lax.fori_loop(6,9,attend,0)
    F2.Z()
    lax.fori_loop(9,12,attend,0)
    put(ctx,ctx_o)
    wpv=gp[...].reshape(768,768)
    def body(i,_):
        r=pl.ds(pl.multiple_of(i*400,16),400)
        mid[r,:]=st[r,:].astype(F32)+meta_o[r,0:1]*(nn(ctx[r,:],wpv)+vec_o[4:5,:])
        return 0
    lax.fori_loop(0,2,body,0)
    def body(i,_):
        r=pl.ds(pl.multiple_of(i*80,16),80)
        cc,rstd=row_stats(mid[r,:])
        n2[r,:]=(cc*rstd*vec_o[5:6,:]+vec_o[6:7,:]).astype(BF)
        return 0
    lax.fori_loop(0,10,body,0)
    put(mid,mid_o); put(n2,n2_o)
    F1.D(); F1.F(); put(g1w,w1_o)
    def mlp(i,_):
        cc=pl.ds(pl.multiple_of(i*512,128),512)
        a,d=gelu_parts(nn(n2[...],g1w[:,:,:,cc].reshape(768,512))+bf1[:,cc])
        hid[:,cc]=a.astype(BF); dg[:,cc]=d.astype(BF)
        return 0
    lax.fori_loop(0,3,mlp,0)
    F2.X()
    lax.fori_loop(3,6,mlp,0)
    put(hid,hid_o); put(dg,dg_o)
    F2.D()
    def grads(i,_):
        cc=pl.ds(pl.multiple_of(i*768,128),768)
        pt2[i]=tn(hid[:,cc],gt[...]).astype(BF).reshape(4,2,96,768)
        return 0
    lax.fori_loop(0,2,grads,0)
    put(pt2.at[pl.ds(0,2)],pt2_o.at[pl.ds(0,2)])
    lax.fori_loop(2,4,grads,0)
    put(pt2.at[pl.ds(2,2)],pt2_o.at[pl.ds(2,2)])
    first[4].wait_recv(); F2.F()
    pcopy(10).wait(); pcopy(11).wait()
    for cp in outs: cp.wait()
    for cp in first: cp.wait_send()
    for g in (S,Q,Pj,F1,F2): g.drain()

def forward(groups,offsets,small,wq,wp,w1,w2,tok,cot,mask):
    sds=jax.ShapeDtypeStruct
    V=pl.BlockSpec(memory_space=pltpu.VMEM); A=pl.BlockSpec(memory_space=pl.ANY); M=pl.BlockSpec(memory_space=pltpu.SMEM)
    D=pltpu.SemaphoreType.DMA
    v=pltpu.VMEM
    R,W=tok.shape
    outs=[((4,4,48,2304),BF),((4,4,48,768),BF),((4,4,48,3072),BF),((4,4,2,96,768),BF),((12,2,400,400),BF)]+[((R,W),BF)]*4+[((R,3*W),BF),((R,4*W),BF),((R,4*W),BF)]
    outs=[((4,4,48,2304),BF),((4,4,48,768),BF),((4,4,48,3072),BF),((4,4,2,96,768),BF),((12,2,400,400),BF),
        ((R,W),BF),((R,W),BF),((R,W),BF),((R,3*W),BF),((R,4*W),BF),((R,4*W),BF),((R,W),BF),((R,W),F32),((4,4,2,96,768),BF),((R,W),BF),((R,W),BF),
        ((16,W),F32),((R,2),F32)]
    return pl.pallas_call(forward_kernel,
        in_specs=[M,M]+[V]*8,out_specs=[A]*16+[V,V],out_shape=[sds(*o) for o in outs],
        scratch_shapes=[v((4,4,2,16,128),BF),v((4,4,48,2304),BF),v((4,4,48,768),BF),v((4,4,48,3072),BF),
            v((24,2304),BF),v((24,768),BF),v((24,3072),BF),v((1,48,2304),BF),v((1,48,768),BF),v((1,48,3072),BF),
            v((R,W),F32),v((R,W),F32),v((R,W),BF),v((R,W),BF),v((R,3*W),BF),v((2,400,400),F32),v((R,W),BF),v((R,W),BF),
            v((R,4*W),BF),v((R,4*W),BF),v((R,W),BF),v((R,W),BF),v((4,4,2,96,768),BF),v((2,2,400,400),BF),v((1,2*W),F32),v((1,4*W),F32),
            D((5,)),D((5,)),D((1,)),D((14,)),D((14,)),D((4,21)),D((4,21)),D((2,)),D((16,))],
        compiler_params=pltpu.CompilerParams(collective_id=0,has_side_effects=True,vmem_limit_bytes=60<<20),name="forward")(
        groups,offsets,small,wq,wp,w1,w2,tok,cot,mask)
class Reduce:
    def __init__(self,give,a,s,rxa,ryb,rx,ry,b,rz,ss,rs):
        self.give=give; self.a=a; self.s=s; self.rxa=rxa; self.ryb=ryb; self.rx=rx; self.ry=ry; self.b=b; self.rz=rz
        self.ss=ss; self.rs=rs
        c,x,y,z=place()
        self.c=c; self.z=z; self.yx=y*2+x
        self.xn=y*2+1-x; self.yn=(1-y)*2+x; self.dg=(1-y)*2+1-x
        self.xd=dev(z,self.xn,c); self.yd=dev(z,self.yn,c); self.sd=dev(z,self.yx,1-c)
        self.cps={}
    def send(self,src,dst,slot,d):
        cp=pltpu.make_async_remote_copy(src_ref=src,dst_ref=dst,send_sem=self.ss.at[slot],recv_sem=self.rs.at[slot],device_id=d,device_id_type=MESH)
        cp.start(); self.cps[slot]=cp
    def r0(self): self.send(self.give,self.s,0,self.sd)
    def add(self,n,z0,yx,other):
        def body(i,_):
            t=self.a(pl.ds(i+z0,1),yx)
            t[...]=(t[...].astype(F32)+other(i)[...].astype(F32)).astype(BF)
            return 0
        lax.fori_loop(0,n,body,0)
    def r1(self):
        self.cps[0].wait_recv()
        def own(yx): self.add(4,0,yx,lambda i: self.s.at[pl.ds(i,1),yx])
        own(self.dg)
        self.send(self.a(pl.ds(0,2),self.dg),self.rxa,1,self.xd)
        self.send(self.a(pl.ds(2,2),self.dg),self.ryb,2,self.yd)
        own(self.xn)
        self.send(self.a(pl.ds(0,2),self.xn),self.rx.at[pl.ds(0,2)],3,self.xd)
        own(self.yn)
        self.send(self.a(pl.ds(2,2),self.yn),self.ry.at[pl.ds(2,2)],4,self.yd)
        own(self.yx)
    def r2(self):
        self.cps[1].wait_recv()
        self.add(2,0,self.yn,lambda i: self.rxa.at[pl.ds(i,1)])
        self.send(self.a(pl.ds(0,2),self.yn),self.ry.at[pl.ds(0,2)],6,self.yd)
        self.cps[2].wait_recv()
        self.add(2,2,self.xn,lambda i: self.ryb.at[pl.ds(i,1)])
        self.send(self.a(pl.ds(2,2),self.xn),self.rx.at[pl.ds(2,2)],5,self.xd)
    def r3(self):
        for s in (3,4,5,6): self.cps[s].wait_recv()
        def body(i,_):
            k=pl.ds(i,1)
            self.b[k]=(self.a(k,self.yx)[...].astype(F32)+self.rx[k].astype(F32)+self.ry[k].astype(F32)).astype(BF)
            return 0
        lax.fori_loop(0,4,body,0)
        for k in (1,2,3):
            zz=lax.rem(self.z+k,4)
            self.send(self.b.at[zz],self.rz.at[k-1],6+k,dev(zz,self.yx,self.c))
    def total(self):
        t=self.b[self.z].astype(F32)
        for k in (1,2,3):
            self.cps[6+k].wait_recv()
            t=t+self.rz[k-1].astype(F32)
        return t
    def drain(self):
        for cp in self.cps.values(): cp.wait_send()

def eights(v):
    return jnp.sum(v.reshape(v.shape[0]//8,8,v.shape[1]),axis=0)

def backward_kernel(w2_r,w1_r,wp_r,wq_r,pr_r,n1_r,n2_r,ctx_r,pj_r,hid_r,dg_r,st_r,mid_r,pt2_r,gt_r,cs_r,vec,meta,
        out_o,tok_o,sm_o,oq,op,o1,o2,
        w2,w1,wp,gp,pj,mid,gf,nt_,tmp,ctx,gt,gb,pst,acc,accb,
        a2,s2,xa2,yb2,x2,y2,b2,z2,part,sb,xab,ybb,xb,yb,bb,zb,fb,frb,vs,vr,
        lsem,psem,osem,rss,rrs,fss,frs,vss,vrs):
    greet()
    c,x,y,z=place(); yx=y*2+x
    sibd=dev(z,yx,1-c)
    loads={}
    def get(name,src,dst):
        cp=pltpu.make_async_copy(src,dst,lsem.at[len(loads)]); cp.start(); loads[name]=cp
    def have(*names):
        for n in names: loads[n].wait()
    C2=[Reduce(pt2_r.at[:,:,1-c,h],lambda zs,q,h=h: a2.at[h,zs,q],s2.at[h],xa2.at[h],yb2.at[h],x2.at[h],y2.at[h],b2.at[h],z2.at[h],rss.at[h],rrs.at[h]) for h in range(2)]
    def sib_at(i): return sb.at[i] if i<5 else s2.at[(i-5)//2,:,:,:,pl.ds(384*((i-5)%2),384)]
    mine=pl.ds(pl.multiple_of(c*384,128),384); theirs=pl.ds(pl.multiple_of((1-c)*384,128),384)
    CH=[Reduce(part.at[i,:,:,:,theirs],lambda zs,q,i=i: part.at[i,zs,q,:,mine],sib_at(i),xab.at[i],ybb.at[i],xb.at[i],yb.at[i],bb.at[i],zb.at[i],rss.at[2+i],rrs.at[2+i]) for i in range(8)]
    F=CH[0:4]; PJ=CH[4]; QK=CH[5:8]
    get("gt",gt_r,gt)
    get("w2a",w2_r.at[pl.ds(0,32)],w2.at[pl.ds(0,32)]); get("dga",dg_r.at[:,pl.ds(0,1536)],gp.at[:,pl.ds(0,1536)])
    C2[0].r0()
    get("w2b",w2_r.at[pl.ds(32,32)],w2.at[pl.ds(32,32)]); get("dgb",dg_r.at[:,pl.ds(1536,1536)],gp.at[:,pl.ds(1536,1536)])
    get("a2a",pt2_r.at[:,:,c,0],a2.at[0])
    C2[1].r0()
    get("a2b",pt2_r.at[:,:,c,1],a2.at[1])
    get("n2",n2_r,tmp)
    get("w1",w1_r,w1); get("mid",mid_r,mid); get("ctx",ctx_r,ctx); get("wp",wp_r,wp); get("pj",pj_r,pj)
    acc[...]=jnp.zeros_like(acc)
    ends=[]
    def end(i):
        t=CH[i].total()
        fb[i,0]=t[:24]; fb[i,1]=t[24:]
        cp=pltpu.make_async_remote_copy(src_ref=fb.at[i,1-c],dst_ref=frb.at[i],send_sem=fss.at[i],recv_sem=frs.at[i],device_id=sibd,device_id_type=MESH)
        cp.start(); ends.append((i,cp))
    def end2(h): o2[48*h:48*h+48,:]=C2[h].total()
    def mlp(i,_):
        cc=pl.ds(pl.multiple_of(i*768,128),768)
        g=(nt(gt[...],w2[pl.ds(16*i,16)].reshape(768,768))*gp[:,cc].astype(F32)).astype(BF)
        gp[:,cc]=g
        accb[:,cc]=eights(g.astype(F32))
        return 0
    have("gt","w2a","dga")
    lax.fori_loop(0,2,mlp,0)
    have("a2a"); C2[0].r1()
    have("w2b","dgb")
    lax.fori_loop(2,4,mlp,0)
    have("a2b"); C2[1].r1()
    have("n2"); nt_[...]=tmp[...].T
    get("cs",cs_r,tmp)
    def w1grad(i):
        part[i]=nn(nt_[...],gp[:,768*i:768*i+768]).astype(BF).reshape(4,4,48,768)
        F[i].r0()
    w1grad(0); w1grad(1)
    C2[0].r2(); F[0].r1()
    w1grad(2)
    w1grad(3); F[1].r1()
    def norm_back(i0,rows,gain,ka,kb,finish):
        def body(i,_):
            r=pl.ds(pl.multiple_of(i0+i*80,16),80)
            g,m=gf[r,:],rows(r)
            cc,rstd=row_stats(m)
            xh=cc*rstd
            acc[ka]+=eights(g*xh); acc[kb]+=eights(g)
            gx=g*gain
            m1=jnp.sum(gx,axis=1,keepdims=True)*(1.0/768); m2=jnp.sum(gx*xh,axis=1,keepdims=True)*(1.0/768)
            finish(r,rstd*(gx-m1-xh*m2))
            return 0
        lax.fori_loop(0,5,body,0)
    def finish2(r,d):
        gm=tmp[r,:].astype(F32)+d
        mid[r,:]=gm
        v=(meta[r,0:1]*gm).astype(BF)
        gb[r,:]=v
        acc[4]+=eights(v.astype(F32))
        acc[8]+=eights(gt[r,:].astype(F32))
    have("w1","cs","mid")
    gf[0:400,:]=nt(gp[0:400,:],w1[...].reshape(768,3072))
    norm_back(0,lambda r: mid[r,:],vec[5:6,:],5,6,finish2)
    F[2].r1(); C2[1].r2()
    gf[400:800,:]=nt(gp[400:800,:],w1[...].reshape(768,3072))
    norm_back(400,lambda r: mid[r,:],vec[5:6,:],5,6,finish2)
    get("hid",hid_r,gp)
    get("n1",n1_r,tmp)
    C2[0].r3(); F[3].r1()
    have("ctx","wp")
    gc=gt
    gc[...]=nt(gb[...],wp[...].reshape(768,768)).astype(BF)
    part[4]=tn(ctx[...],gb[...]).astype(BF).reshape(4,4,48,768)
    PJ.r0()
    have("n1"); nt_[...]=tmp[...].T
    get("st",st_r,tmp)
    F[0].r2()
    have("pj")
    lane=lax.broadcasted_iota(jnp.int32,(400,128),1)
    def where_of(t):
        g=t//4; b=lax.rem(t,4)//2; p=2*g+lax.rem(t,2)
        return b,p
    def pcopy(t):
        b,p=where_of(t)
        return pltpu.make_async_copy(pr_r.at[b*6+p],pst.at[lax.rem(t,2)],psem.at[lax.rem(t,2)])
    def attend(t,_):
        b,p=where_of(t); s=lax.rem(t,2)
        r=pl.ds(pl.multiple_of(b*400,16),400)
        cc=lambda o: pl.ds(pl.multiple_of(o+p*128,128),128)
        pcopy(t).wait()
        @pl.when(t<11)
        def _(): pcopy(t+1).start()
        q=pj[r,cc(0)]; k=pj[r,cc(768)]; v=pj[r,cc(1536)]; g=gc[r,cc(0)]
        gx=g.astype(F32)*ctx[r,cc(0)].astype(F32)
        dq=[];dk=[];dv=[]
        for j in range(2):
            own=(lane>=64)==(j==1)
            zero=jnp.zeros_like(q)
            qj=jnp.where(own,q,zero); gj=jnp.where(own,g,zero)
            di=jnp.sum(jnp.where(own,gx,0.0),axis=1,keepdims=True)
            pr=pst[s,j]
            ds=(pr.astype(F32)*(nt(gj,v)-di)).astype(BF)
            dq.append(nn(ds,k)); dk.append(tn(ds,qj)); dv.append(tn(pr,gj))
        pj[r,cc(0)]=(jnp.where(lane<64,dq[0],dq[1])*0.125).astype(BF)
        pj[r,cc(768)]=((dk[0]+dk[1])*0.125).astype(BF)
        pj[r,cc(1536)]=(dv[0]+dv[1]).astype(BF)
        return 0
    def qkvgrad(g):
        cols=[pj[:,o+256*g:o+256*g+256] for o in (0,768,1536)]
        for o,k in ((0,3),(2,7)): acc[k,:,256*g:256*g+256]=eights(cols[o].astype(F32))
        part[5+g]=nn(nt_[...],jnp.concatenate(cols,axis=1)).astype(BF).reshape(4,4,48,768)
        QK[g].r0()
    def steps(a,b): lax.fori_loop(a,b,attend,0)
    pcopy(0).start()
    steps(0,2); C2[1].r3(); PJ.r1()
    steps(2,4); qkvgrad(0); F[0].r3(); F[1].r2(); end2(0)
    steps(4,6); QK[0].r1(); F[1].r3(); F[2].r2()
    steps(6,8); qkvgrad(1); end2(1); end(0)
    steps(8,10); QK[1].r1(); F[2].r3(); F[3].r2(); end(1)
    steps(10,12); qkvgrad(2); F[3].r3(); PJ.r2(); end(2)
    have("hid","st")
    get("mid2",mid_r,gf)
    have("mid2")
    def outp(i):
        r=slice(400*i,400*i+400)
        gf[r,:]=gf[r,:]+meta[r,0:1]*(nn(gp[r,:],w2[...].reshape(3072,768))+vec[8:9,:])
    outp(0); QK[2].r1(); PJ.r3(); QK[0].r2(); end(3)
    outp(1)
    get("wq0",wq_r.at[:,:,pl.ds(0,768)],w2.at[pl.ds(0,16)]); get("wq1",wq_r.at[:,:,pl.ds(768,768)],w2.at[pl.ds(16,16)]); get("wq2",wq_r.at[:,:,pl.ds(1536,768)],w2.at[pl.ds(32,16)])
    stores=[]
    def put(src,dst):
        cp=pltpu.make_async_copy(src,dst,osem.at[len(stores)]); cp.start(); stores.append(cp)
    put(gf,out_o)
    have("wq0","wq1","wq2")
    QK[0].r3(); end(4); QK[1].r2()
    put_done=stores[0]; put_done.wait()
    def back(i):
        r=slice(400*i,400*i+400)
        gf[r,:]=sum(nt(pj[r,768*j:768*j+768],w2[16*j:16*j+16].reshape(768,768)) for j in range(3))
    def finish1(r,d):
        gs=mid[r,:]+d
        m=meta[r,1:2]>0.0
        acc[0]+=eights(jnp.where(m,gs,0.0))
        mid[r,:]=jnp.where(m,0.0,gs)
    back(0); norm_back(0,lambda r: tmp[r,:].astype(F32),vec[1:2,:],1,2,finish1)
    QK[2].r2(); QK[1].r3(); end(5)
    back(1); norm_back(400,lambda r: tmp[r,:].astype(F32),vec[1:2,:],1,2,finish1)
    put(mid,tok_o)
    vs[0]=jnp.zeros((16,768),F32)
    for k in range(9): vs[0,k:k+1,:]=jnp.sum(acc[k],axis=0,keepdims=True)
    for k in range(4): vs[0,9+k:10+k,:]=jnp.sum(accb[:,768*k:768*k+768],axis=0,keepdims=True)
    vc=[]
    def vsend(a,slot,d):
        cp=pltpu.make_async_remote_copy(src_ref=vs.at[a],dst_ref=vr.at[slot],send_sem=vss.at[slot],recv_sem=vrs.at[slot],device_id=d,device_id_type=MESH)
        cp.start(); vc.append(cp)
    vsend(0,0,sibd)
    QK[2].r3()
    vc[0].wait_recv(); vs[1]=vs[0]+vr[0]
    vsend(1,1,dev(z,y*2+1-x,c))
    end(6)
    vc[1].wait_recv(); vs[2]=vs[1]+vr[1]
    vsend(2,2,dev(z,(1-y)*2+x,c))
    vc[2].wait_recv(); vs[3]=vs[2]+vr[2]
    for k in (1,2,3): vsend(3,2+k,dev(lax.rem(z+k,4),yx,c))
    for k in (1,2,3): vc[2+k].wait_recv()
    tot=vs[3]+vr[3]+vr[4]+vr[5]
    me=lax.axis_index("dp")
    def turn(v,by): return pltpu.roll(v,lax.rem(768-by,768),1)[:,:128]
    sm_o[...]=turn(tot,24*me)

    pick=jnp.where(me>=16,tot[7:8],tot[3:4])
    sm_o[3:4,:]=turn(jnp.concatenate([pick]*8,axis=0),48*lax.rem(me,16))[0:1]
    k8=me//8
    pick=jnp.where(k8==0,tot[9:10],jnp.where(k8==1,tot[10:11],jnp.where(k8==2,tot[11:12],tot[12:13])))
    sm_o[7:8,:]=turn(jnp.concatenate([pick]*8,axis=0),96*lax.rem(me,8))[0:1]
    end(7)
    for i,cp in ends:
        cp.wait_recv()
        own=fb[i,c]; oth=frb[i]
        lo=jnp.where(c==0,own,oth); hi=jnp.where(c==0,oth,own)
        if i<4: o1[:,768*i:768*i+384]=lo; o1[:,768*i+384:768*i+768]=hi
        elif i==4: op[:,:384]=lo; op[:,384:]=hi
        else:
            g=256*(i-5)
            oq[:,g:g+256]=lo[:,:256]; oq[:,768+g:768+g+128]=lo[:,256:]
            oq[:,768+g+128:768+g+256]=hi[:,:128]; oq[:,1536+g:1536+g+256]=hi[:,128:]
        cp.wait_send()
    stores[1].wait()
    for cp in vc: cp.wait_send()
    for q in C2+CH: q.drain()

def backward(w2,w1,wp,wq,pr,n1,n2,ctx,pj,hid,dg,st,mid,pt2,gt,cs,vec,meta):
    sds=jax.ShapeDtypeStruct
    V=pl.BlockSpec(memory_space=pltpu.VMEM); A=pl.BlockSpec(memory_space=pl.ANY)
    D=pltpu.SemaphoreType.DMA
    v=pltpu.VMEM
    R,W=n1.shape
    scr=[v((64,48,W),BF),v((4,4,48,4*W),BF),v((4,4,48,W),BF),v((R,4*W),BF),v((R,3*W),BF),v((R,W),F32),v((R,W),F32),v((W,R),BF),
        v((R,W),BF),v((R,W),BF),v((R,W),BF),v((R,W),BF),v((2,2,400,400),BF),v((9,8,W),F32),v((8,4*W),F32)]
    def rs(n,r,w,own):
        o=[v((n,4,4,r,own),BF),v((min(n,5),4,4,r,w),BF),v((n,2,r,w),BF),v((n,2,r,w),BF),v((n,4,r,w),BF),v((n,4,r,w),BF),v((n,4,r,w),BF),v((n,3,r,w),BF)]
        return o
    scr+=rs(2,48,W,W)+rs(8,48,W//2,W)
    scr+=[v((8,2,24,W//2),F32),v((8,24,W//2),F32),v((4,16,W),F32),v((6,16,W),F32)]
    scr+=[D((24,)),D((2,)),D((2,)),D((10,10)),D((10,10)),D((8,)),D((8,)),D((6,)),D((6,))]
    outs=[((R,W),F32),((R,W),F32),((16,128),F32),((24,3*W),F32),((24,W),F32),((24,4*W),F32),((96,W),F32)]
    return pl.pallas_call(backward_kernel,in_specs=[A]*16+[V]*2,out_specs=[A,A]+[V]*5,out_shape=[sds(*o) for o in outs],scratch_shapes=scr,
        compiler_params=pltpu.CompilerParams(collective_id=1,has_side_effects=True,vmem_limit_bytes=63<<20),name="backward")(
        w2,w1,wp,wq,pr,n1,n2,ctx,pj,hid,dg,st,mid,pt2,gt,cs,vec,meta)

def normalize(values, gain, shift):
    center = values - jnp.mean(values, axis=-1, keepdims=True)
    spread = jnp.mean(center * center, axis=-1, keepdims=True)
    return center * lax.rsqrt(spread + eps_norm) * gain + shift

def activate(values):
    return jax.nn.gelu(values, approximate=False)

def segment_rows(groups, offsets, rows):
    lengths = jnp.where(groups == 0, P_SMALL, jnp.where(groups == 1, P_MID, P_LARGE)).astype(jnp.int32)
    positions = jnp.arange(rows, dtype=jnp.int32)
    inside = (positions[None, :] >= offsets[:, None]) & (positions[None, :] < offsets[:, None] + lengths[:, None])
    labels = jnp.arange(1, offsets.shape[0] + 1, dtype=jnp.int32)
    return jnp.sum(jnp.where(inside, labels[:, None], 0), axis=0) - 1

def settle(mid, rows):
    half = rows.shape[0] // 2
    cut = P_MID * (half // P_MID)
    gap = half - cut
    end = rows.shape[0] - gap
    moved = jnp.concatenate([rows[:cut], rows[end:], rows[cut:end]], axis=0)
    return jnp.where(mid, moved, rows)

def unsettle(mid, rows):
    half = rows.shape[0] // 2
    cut = P_MID * (half // P_MID)
    gap = half - cut
    moved = jnp.concatenate([rows[:cut], rows[half:], rows[cut:half]], axis=0)
    return jnp.where(mid, moved, rows)

def shards(n, tokens, mask_bits, groups, offsets, mask_token, ln1_gain, ln1_bias, w_qkv, b_qv, w_proj, b_proj,
           ln2_gain, ln2_bias, w_fc1, b_fc1, w_fc2, b_fc2, cotangent):
    vectors = (mask_token, ln1_gain, ln1_bias, b_qv, b_proj, ln2_gain, ln2_bias, b_fc1, b_fc2)
    sizes = [v.shape[0] for v in vectors]
    places = [sum(sizes[:i]) for i in range(len(sizes) + 1)]
    fits = n == 32 and places[-1] <= 1024
    packed = jnp.concatenate(vectors)
    if fits:
        small = jnp.pad(packed, (0, 2048 - places[-1])).reshape(16, 128)
        gathered = gather_all(small, w_qkv, w_proj, w_fc1, w_fc2)
        small_all = gathered[0].reshape(n, 2048)
        full_qkv, full_proj, full_fc1, full_fc2 = [
            g.reshape(-1, g.shape[-1]) for g in gathered[1:]]
    else:
        small_all = lax.all_gather(packed, "dp", axis=0, tiled=False)
        full_qkv, full_proj, full_fc1, full_fc2 = [
            lax.all_gather(w, "dp", axis=0, tiled=True) for w in (w_qkv, w_proj, w_fc1, w_fc2)]
    token_mask, gain_one, shift_one, bias_qv, bias_proj, gain_two, shift_two, bias_one, bias_two = [
        small_all[:, places[i]:places[i + 1]].reshape(-1).astype(F32) for i in range(len(sizes))]
    rows, width = tokens.shape
    half = rows // 2
    mid = groups[0] == 1
    tokens = settle(mid, tokens)
    cotangent = settle(mid, cotangent)
    mask_bits = settle(mid, mask_bits)
    segment = settle(mid, segment_rows(groups, offsets, rows))
    valid_col = (segment >= 0).astype(F32)[:, None]
    halves = segment.reshape(2, half)
    bias = jnp.where(halves[:, :, None] == halves[:, None, :], 0.0, -1e30).astype(F32)
    masked_rows = (mask_bits == 1)[:, None]
    start = jnp.where(masked_rows, token_mask[None, :], tokens.astype(F32))
    normed_one = normalize(start, gain_one, shift_one).astype(BF)
    full_bias = jnp.concatenate([bias_qv[:width], jnp.zeros((width,), F32), bias_qv[width:]])
    projected = (jnp.dot(normed_one, full_qkv, preferred_element_type=F32) + full_bias).astype(BF)
    context_low, probs = attn_fwd(projected, bias)
    middle = start + valid_col * (jnp.dot(context_low, full_proj, preferred_element_type=F32) + bias_proj)
    normed_two = normalize(middle, gain_two, shift_two).astype(BF)
    hidden_pre = jnp.dot(normed_two, full_fc1, preferred_element_type=F32) + bias_one
    hidden_low = activate(hidden_pre).astype(BF)
    result = middle + valid_col * (jnp.dot(hidden_low, full_fc2, preferred_element_type=F32) + bias_two)
    output = unsettle(mid, result.astype(BF))
    upstream = cotangent.astype(F32)
    grad_two = (valid_col * upstream).astype(BF)
    grad_wfc2 = tn(hidden_low, grad_two)
    grad_bfc2 = jnp.sum(grad_two.astype(F32), axis=0)
    grad_hidden = nt(grad_two, full_fc2)
    _, gelu_back = jax.vjp(activate, hidden_pre)
    grad_pre = gelu_back(grad_hidden)[0].astype(BF)
    grad_wfc1 = tn(normed_two, grad_pre)
    grad_bfc1 = jnp.sum(grad_pre.astype(F32), axis=0)
    grad_normed_two = nt(grad_pre, full_fc1)
    _, norm_back_two = jax.vjp(normalize, middle, gain_two, shift_two)
    grad_mid_part, grad_gain_two, grad_shift_two = norm_back_two(grad_normed_two)
    grad_middle = upstream + grad_mid_part
    grad_branch = (valid_col * grad_middle).astype(BF)
    grad_wproj = tn(context_low, grad_branch)
    grad_bproj = jnp.sum(grad_branch.astype(F32), axis=0)
    grad_context = nt(grad_branch, full_proj).astype(BF)
    dq, dk, dv = attn_bwd(projected, grad_context, context_low, probs)
    grad_projected = jnp.concatenate([dq, dk, dv], axis=1)
    grad_wqkv = tn(normed_one, grad_projected)
    grad_bqv = jnp.concatenate([jnp.sum(dq.astype(F32), axis=0), jnp.sum(dv.astype(F32), axis=0)])
    grad_normed_one = nt(grad_projected, full_qkv)
    _, norm_back_one = jax.vjp(normalize, start, gain_one, shift_one)
    grad_start_part, grad_gain_one, grad_shift_one = norm_back_one(grad_normed_one)
    grad_start = grad_middle + grad_start_part
    grad_token = jnp.sum(jnp.where(masked_rows, grad_start, 0.0), axis=0)
    grad_input = unsettle(mid, jnp.where(masked_rows, 0.0, grad_start))
    grad_vectors = (grad_token, grad_gain_one, grad_shift_one, grad_bqv, grad_bproj, grad_gain_two, grad_shift_two,
                    grad_bfc1, grad_bfc2)
    grad_small = jnp.concatenate([g.reshape(n, -1) for g in grad_vectors], axis=1)
    if fits:
        grad_small = jnp.pad(grad_small, ((0, 0), (0, 1024 - places[-1]))).reshape(4, 4, 2, 8, 128)
        shares = scatter_all(
            grad_small,
            *[g.astype(BF).reshape(4, 4, g.shape[0] // 16, g.shape[1]) for g in (grad_wqkv, grad_wproj, grad_wfc1)],
            grad_wfc2.astype(BF).reshape(4, 4, 2, grad_wfc2.shape[0] // 32, width))
        small_share = shares[0].reshape(1024)
        share_qkv, share_proj, share_fc1, share_fc2 = shares[1:]
    else:
        small_share = lax.psum_scatter(grad_small, "dp", scatter_dimension=0, tiled=False)
        share_qkv, share_proj, share_fc1, share_fc2 = [
            lax.psum_scatter(g, "dp", scatter_dimension=0, tiled=True)
            for g in (grad_wqkv, grad_wproj, grad_wfc1, grad_wfc2)]
    v = [small_share[places[i]:places[i + 1]] for i in range(len(sizes))]
    return (output, grad_input, v[0], v[1], v[2], share_qkv, v[3], share_proj, v[4], v[5], v[6], share_fc1, v[7],
            share_fc2, v[8])


def pack_small(vectors):
    total = jnp.zeros((16, 128), F32)
    for i, v in enumerate(vectors):
        total = total + jnp.pad(v.astype(F32)[None, :], ((i, 15 - i), (0, 128 - v.shape[0])))
    return total.astype(BF)

def shards_fast(n, tokens, mask_bits, groups, offsets, mask_token, ln1_gain, ln1_bias, w_qkv, b_qv, w_proj, b_proj,
           ln2_gain, ln2_bias, w_fc1, b_fc1, w_fc2, b_fc2, cotangent):
    vectors = (mask_token, ln1_gain, ln1_bias, b_qv, b_proj, ln2_gain, ln2_bias, b_fc1, b_fc2)
    sizes = [v.shape[0] for v in vectors]
    places = [sum(sizes[:i]) for i in range(len(sizes) + 1)]
    small = pack_small(vectors)
    mask_col = mask_bits.astype(F32)[:, None]
    (gq, gp, g1, g2, probs, normed_one, normed_two, context_low, projected, hidden_low, dgelu, start, middle, part2,
     grad_two, cots, vec, meta) = forward(groups, offsets, small, w_qkv, w_proj, w_fc1, w_fc2, tokens, cotangent, mask_col)
    rows, width = tokens.shape
    mid = groups[0] == 1
    result, grad_start, small_share, share_qkv, share_proj, share_fc1, share_fc2 = backward(
        g2.reshape(64, 48, width), g1, gp, gq.reshape(16, 48, 3 * width), probs, normed_one, normed_two, context_low,
        projected, hidden_low, dgelu, start, middle, part2.reshape(4, 4, 2, 2, 48, width), grad_two, cots, vec, meta)
    output = unsettle(mid, result).astype(BF)
    grad_input = unsettle(mid, grad_start)
    v = [small_share[i, :sizes[i]] for i in range(len(sizes))]
    return (output, grad_input, v[0], v[1], v[2], share_qkv, v[3], share_proj, v[4], v[5], v[6], share_fc1, v[7],
            share_fc2, v[8])

def solution(mesh):
    row, flat = P("dp", None), P("dp")
    return jax.shard_map(
        functools.partial(shards_fast if mesh.shape["dp"] == 32 else shards, mesh.shape["dp"]),
        mesh=mesh,
        in_specs=(row, flat, flat, flat, flat, flat, flat, row, flat, row, flat, flat, flat, row, flat, row, flat, row),
        out_specs=(row, row, flat, flat, flat, row, flat, row, flat, flat, flat, row, flat, row, flat),
        check_vma=False,
    )
```

```python
import functools

import jax
import jax.numpy as jnp
from jax import lax
from jax.experimental import pallas as pl
from jax.experimental.pallas import tpu as pltpu
from jax.sharding import PartitionSpec as P

P_SMALL = 100
P_MID = 196
P_LARGE = 400
eps_norm = 1e-06

def nt(a,b): return lax.dot_general(a,b,(((1,),(1,)),((),())),preferred_element_type=jnp.float32)
def nn(a,b): return lax.dot_general(a,b,(((1,),(0,)),((),())),preferred_element_type=jnp.float32)
def tn(a,b): return lax.dot_general(a,b,(((0,),(0,)),((),())),preferred_element_type=jnp.float32)

def attn_fwd_kernel(bias_ref, q_ref, k_ref, v_ref, ctx_ref, p_ref):
    q=q_ref[...]; k=k_ref[...]; v=v_ref[...]
    rows,width=q.shape
    lane=lax.broadcasted_iota(jnp.int32,(rows,width),1)
    bias=bias_ref[0]
    outs=[]
    for j in range(2):
        mine=(lane>=64)==(j==1)
        qj=jnp.where(mine,q,jnp.zeros_like(q))
        s=nt(qj,k)*0.18033688011112042+bias
        m=jnp.max(s,axis=1,keepdims=True)
        e=jnp.exp2(s-m)
        l=jnp.sum(e,axis=1,keepdims=True)
        p=(e*(1.0/l)).astype(jnp.bfloat16)
        p_ref[0,0,j]=p
        outs.append(nn(p,v))
    ctx_ref[...]=jnp.where(lane<64,outs[0],outs[1]).astype(jnp.bfloat16)

def attn_fwd(proj,bias):
    rows=proj.shape[0]; half=rows//2; width=proj.shape[1]//3; pairs=width//128
    return pl.pallas_call(attn_fwd_kernel,grid=(2,pairs),
        in_specs=[pl.BlockSpec((1,half,half),lambda b,p:(b,0,0)),
                  pl.BlockSpec((half,128),lambda b,p:(b,p)),
                  pl.BlockSpec((half,128),lambda b,p:(b,p+pairs)),
                  pl.BlockSpec((half,128),lambda b,p:(b,p+2*pairs))],
        out_specs=[pl.BlockSpec((half,128),lambda b,p:(b,p)),
                   pl.BlockSpec((1,1,2,half,half),lambda b,p:(b,p,0,0,0))],
        out_shape=[jax.ShapeDtypeStruct((rows,width),jnp.bfloat16),
                   jax.ShapeDtypeStruct((2,pairs,2,half,half),jnp.bfloat16)],
        compiler_params=pltpu.CompilerParams(vmem_limit_bytes=40<<20),name="attn_fwd")(bias,proj,proj,proj)

def attn_bwd_kernel(q_ref,k_ref,v_ref,g_ref,c_ref,p_ref,dq_ref,dk_ref,dv_ref):
    q=q_ref[...]; k=k_ref[...]; v=v_ref[...]; g=g_ref[...]; c=c_ref[...]
    rows,width=q.shape
    lane=lax.broadcasted_iota(jnp.int32,(rows,width),1)
    gc=g.astype(jnp.float32)*c.astype(jnp.float32)
    dq=[];dk=[];dv=[]
    for j in range(2):
        mine=(lane>=64)==(j==1)
        zero=jnp.zeros_like(q)
        qj=jnp.where(mine,q,zero); gj=jnp.where(mine,g,zero)
        di=jnp.sum(jnp.where(mine,gc,0.0),axis=1,keepdims=True)
        p=p_ref[0,0,j]
        dp=nt(gj,v)
        ds=(p.astype(jnp.float32)*(dp-di)).astype(jnp.bfloat16)
        dq.append(nn(ds,k))
        dk.append(tn(ds,qj))
        dv.append(tn(p,gj))
    dq_ref[...]=(jnp.where(lane<64,dq[0],dq[1])*0.125).astype(jnp.bfloat16)
    dk_ref[...]=((dk[0]+dk[1])*0.125).astype(jnp.bfloat16)
    dv_ref[...]=(dv[0]+dv[1]).astype(jnp.bfloat16)

def attn_bwd(proj,gctx,ctx,p):
    rows=proj.shape[0]; half=rows//2; width=proj.shape[1]//3; pairs=width//128
    sp=lambda o: pl.BlockSpec((half,128),lambda b,p:(b,p+o*pairs))
    return pl.pallas_call(attn_bwd_kernel,grid=(2,pairs),
        in_specs=[sp(0),sp(1),sp(2),sp(0),sp(0),pl.BlockSpec((1,1,2,half,half),lambda b,p:(b,p,0,0,0))],
        out_specs=[sp(0)]*3,
        out_shape=[jax.ShapeDtypeStruct((rows,width),jnp.bfloat16)]*3,
        compiler_params=pltpu.CompilerParams(vmem_limit_bytes=40<<20),name="attn_bwd")(proj,proj,proj,gctx,ctx,p)
MESH=pl.DeviceIdType.MESH
F32=jnp.float32; BF=jnp.bfloat16

def place():
    me=lax.axis_index("dp")
    c=lax.rem(me,2); x=lax.rem(me//2,2); y=lax.rem(me//4,2); z=me//8
    return c,x,y,z
def dev(z,yx,c): return ((z*4+yx)*2+c,)

def greet():
    c,x,y,z=place(); yx=y*2+x
    bar=pltpu.get_barrier_semaphore()
    peers=[dev(z,yx,1-c),dev(z,y*2+1-x,c),dev(z,(1-y)*2+x,c)]+[dev(lax.rem(z+k,4),yx,c) for k in (1,2,3)]
    for p in peers: pl.semaphore_signal(bar,inc=1,device_id=p,device_id_type=MESH)
    pl.semaphore_wait(bar,len(peers))

class Gather:
    def __init__(self,view,ss,rs):
        self.view=view; self.ss=ss; self.rs=rs
        c,x,y,z=place()
        self.c=c; self.z=z; self.yx=y*2+x
        self.xn=y*2+1-x; self.yn=(1-y)*2+x; self.dg=(1-y)*2+1-x
        self.sends=[]
    def _cp(self,src,dst,slot,d):
        return pltpu.make_async_remote_copy(src_ref=src,dst_ref=dst,send_sem=self.ss.at[slot],recv_sem=self.rs.at[slot],device_id=d,device_id_type=MESH)
    def send(self,src,dst,slot,d):
        cp=self._cp(src,dst,slot,d); cp.start(); self.sends.append(cp)
    def got(self,dst,slot,d):
        self._cp(dst,dst,slot,d).wait_recv()
    def one(self,z): return self.view(pl.ds(z,1),self.yx,self.c)
    def z_send(self,src):
        for k in (1,2,3):
            self.send(src,self.one(self.z),k-1,dev(lax.rem(self.z+k,4),self.yx,self.c))
    def sib(self,ref,slot): self.send(ref,ref,slot,dev(self.z,self.yx,1-self.c))
    def z_recv(self):
        for k in (1,2,3):
            zz=lax.rem(self.z+4-k,4)
            self.got(self.one(zz),k-1,dev(zz,self.yx,self.c))
    def xy_send(self):
        r=self.view(pl.ds(0,4),self.yx,self.c)
        self.send(r,r,3,dev(self.z,self.xn,self.c))
        self.send(r,r,4,dev(self.z,self.yn,self.c))
        for k in (1,2,3): self.sib(self.one(lax.rem(self.z+4-k,4)),6+k)
    def xy_recv(self):
        rx=self.view(pl.ds(0,4),self.xn,self.c)
        self.got(rx,3,dev(self.z,self.xn,self.c))
        h=self.view(pl.ds(0,2),self.xn,self.c)
        self.send(h,h,5,dev(self.z,self.yn,self.c))
        ry=self.view(pl.ds(0,4),self.yn,self.c)
        self.got(ry,4,dev(self.z,self.yn,self.c))
        h=self.view(pl.ds(2,2),self.yn,self.c)
        self.send(h,h,6,dev(self.z,self.xn,self.c))
        self.sib(rx,10); self.sib(ry,11)
    def diag_recv(self):
        a=self.view(pl.ds(0,2),self.dg,self.c)
        self.got(a,5,dev(self.z,self.yn,self.c))
        self.sib(a,12)
        b=self.view(pl.ds(2,2),self.dg,self.c)
        self.got(b,6,dev(self.z,self.xn,self.c))
        self.sib(b,13)
    def finish(self):
        o=1-self.c; s=dev(self.z,self.yx,o)
        for k in (1,2,3): self.got(self.view(pl.ds(lax.rem(self.z+4-k,4),1),self.yx,o),6+k,s)
        self.got(self.view(pl.ds(0,4),self.xn,o),10,s)
        self.got(self.view(pl.ds(0,4),self.yn,o),11,s)
        self.got(self.view(pl.ds(0,2),self.dg,o),12,s)
        self.got(self.view(pl.ds(2,2),self.dg,o),13,s)
    def drain(self):
        for cp in self.sends: cp.wait_send()

def cols_view(ref):
    half=ref.shape[-1]//2
    def view(zs,yx,lane): return ref.at[zs,yx,:,pl.ds(pl.multiple_of(lane*half,128),half)]
    return view
def rows_view(ref):
    def view(zs,yx,lane): return ref.at[zs,yx,lane]
    return view

def join(c,own,sib):
    a=own.astype(F32); b=sib.astype(F32)
    return jnp.concatenate([jnp.where(c==0,a,b),jnp.where(c==0,b,a)],axis=0).astype(BF)

def gather_kernel(sm_ref,q_ref,p_ref,f1_ref,f2_ref,gs_ref,gq_ref,gp_ref,g1_ref,g2_ref,
        sq,sp,s1,bq,bp,b1,ss0,rs0,ssl,ss,rs):
    greet()
    c,x,y,z=place(); yx=y*2+x
    sibd=dev(z,yx,1-c)
    first=[]
    def swap(src,dst,i):
        cp=pltpu.make_async_remote_copy(src_ref=src,dst_ref=dst,send_sem=ss0.at[i],recv_sem=rs0.at[i],device_id=sibd,device_id_type=MESH)
        cp.start(); first.append(cp)
    swap(sm_ref,gs_ref.at[z,yx,c],0)
    swap(q_ref,sq,1); swap(p_ref,sp,2); swap(f1_ref,s1,3)
    swap(f2_ref,g2_ref.at[z,yx,c],4)
    gs=[Gather(rows_view(gs_ref),ss.at[0],rs.at[0]),Gather(cols_view(gq_ref),ss.at[1],rs.at[1]),Gather(cols_view(gp_ref),ss.at[2],rs.at[2]),
        Gather(cols_view(g1_ref),ss.at[3],rs.at[3]),Gather(rows_view(g2_ref),ss.at[4],rs.at[4])]
    local=[]
    def keep(src,dst,i):
        cp=pltpu.make_async_copy(src,dst,ssl.at[i]); cp.start(); local.append(cp)
    def half(b):
        h=b.shape[-1]//2
        return b.at[:,:,pl.ds(pl.multiple_of(c*h,128),h)]
    keep(sm_ref,gs_ref.at[z,yx,c],0)
    keep(f2_ref,g2_ref.at[z,yx,c],4)
    def begin(i):
        if i==0:
            local[0].wait(); gs[0].z_send(gs[0].one(z))
        elif i==4:
            local[1].wait(); gs[4].z_send(gs[4].one(z))
        else:
            own,sib,buf,dst={1:(q_ref,sq,bq,gq_ref),2:(p_ref,sp,bp,gp_ref),3:(f1_ref,s1,b1,g1_ref)}[i]
            first[i].wait_recv()
            buf[0]=join(c,own[...],sib[...])
            keep(buf,dst.at[pl.ds(z,1),yx],i)
            gs[i].z_send(half(buf))
    begin(0); begin(1)
    gs[0].z_recv(); gs[0].xy_send()
    begin(2)
    gs[1].z_recv(); local[2].wait(); gs[1].xy_send()
    begin(3)
    gs[0].xy_recv()
    gs[2].z_recv(); local[3].wait(); gs[2].xy_send()
    gs[0].diag_recv()
    gs[1].xy_recv()
    begin(4)
    gs[3].z_recv(); local[4].wait(); gs[3].xy_send()
    gs[2].xy_recv()
    gs[1].diag_recv()
    gs[2].diag_recv()
    gs[4].z_recv(); gs[4].xy_send()
    gs[3].xy_recv()
    gs[3].diag_recv()
    gs[4].xy_recv()
    gs[4].diag_recv()
    first[0].wait_recv(); first[4].wait_recv()
    for g in gs: g.finish()
    for cp in first: cp.wait_send()
    for g in gs: g.drain()

def gather_all(small,wq,wp,w1,w2):
    sds=jax.ShapeDtypeStruct
    nq,np_,n1,n2=wq.shape[1],wp.shape[1],w1.shape[1],w2.shape[1]
    r=wq.shape[0]; r2=w2.shape[0]
    V=pl.BlockSpec(memory_space=pltpu.VMEM); A=pl.BlockSpec(memory_space=pl.ANY)
    D=pltpu.SemaphoreType.DMA
    return pl.pallas_call(gather_kernel,
        in_specs=[V]*5,out_specs=[A]*5,
        out_shape=[sds((4,4,2)+small.shape,BF),sds((4,4,2*r,nq),BF),sds((4,4,2*r,np_),BF),sds((4,4,2*r,n1),BF),sds((4,4,2,r2,n2),BF)],
        scratch_shapes=[pltpu.VMEM((r,n),BF) for n in (nq,np_,n1)]+[pltpu.VMEM((1,2*r,n),BF) for n in (nq,np_,n1)]+
            [D((5,)),D((5,)),D((5,)),D((5,14)),D((5,14))],
        compiler_params=pltpu.CompilerParams(collective_id=0,has_side_effects=True,vmem_limit_bytes=16<<20),name="gather_all")(small,wq,wp,w1,w2)

class Scatter:
    def __init__(self,view,a,s,rxa,ryb,rx,ry,b,rz,ss,rs,ls):
        self.view=view; self.a=a; self.s=s; self.rxa=rxa; self.ryb=ryb; self.rx=rx; self.ry=ry; self.b=b; self.rz=rz
        self.ss=ss; self.rs=rs; self.ls=ls
        c,x,y,z=place()
        self.c=c; self.z=z; self.yx=y*2+x
        self.xn=y*2+1-x; self.yn=(1-y)*2+x; self.dg=(1-y)*2+1-x
        self.cps={}
    def send(self,src,dst,slot,d):
        cp=pltpu.make_async_remote_copy(src_ref=src,dst_ref=dst,send_sem=self.ss.at[slot],recv_sem=self.rs.at[slot],device_id=d,device_id_type=MESH)
        cp.start(); self.cps[slot]=cp
    def r0(self):
        self.send(self.view(1-self.c),self.s,0,dev(self.z,self.yx,1-self.c))
        self.loc=pltpu.make_async_copy(self.view(self.c),self.a,self.ls); self.loc.start()
    def r1(self):
        self.loc.wait(); self.cps[0].wait_recv()
        a,s=self.a,self.s
        def add(yx):
            def body(i,_):
                a[i,yx]=(a[i,yx].astype(F32)+s[i,yx].astype(F32)).astype(a.dtype)
                return 0
            lax.fori_loop(0,4,body,0)
        xd=dev(self.z,self.xn,self.c); yd=dev(self.z,self.yn,self.c)
        add(self.dg)
        self.send(a.at[pl.ds(0,2),self.dg],self.rxa,1,xd)
        self.send(a.at[pl.ds(2,2),self.dg],self.ryb,2,yd)
        add(self.xn)
        self.send(a.at[pl.ds(0,2),self.xn],self.rx.at[pl.ds(0,2)],3,xd)
        add(self.yn)
        self.send(a.at[pl.ds(2,2),self.yn],self.ry.at[pl.ds(2,2)],4,yd)
        add(self.yx)
    def r2(self):
        a=self.a
        xd=dev(self.z,self.xn,self.c); yd=dev(self.z,self.yn,self.c)
        self.cps[1].wait_recv()
        def body(i,_):
            a[i,self.yn]=(a[i,self.yn].astype(F32)+self.rxa[i].astype(F32)).astype(a.dtype)
            return 0
        lax.fori_loop(0,2,body,0)
        self.send(a.at[pl.ds(0,2),self.yn],self.ry.at[pl.ds(0,2)],6,yd)
        self.cps[2].wait_recv()
        def body(i,_):
            a[i+2,self.xn]=(a[i+2,self.xn].astype(F32)+self.ryb[i].astype(F32)).astype(a.dtype)
            return 0
        lax.fori_loop(0,2,body,0)
        self.send(a.at[pl.ds(2,2),self.xn],self.rx.at[pl.ds(2,2)],5,xd)
    def r3(self):
        for s in (3,4,5,6): self.cps[s].wait_recv()
        def body(i,_):
            self.b[i]=(self.a[i,self.yx].astype(F32)+self.rx[i].astype(F32)+self.ry[i].astype(F32)).astype(self.b.dtype)
            return 0
        lax.fori_loop(0,4,body,0)
        for k in (1,2,3):
            zz=lax.rem(self.z+k,4)
            self.send(self.b.at[zz],self.rz.at[k-1],6+k,dev(zz,self.yx,self.c))
    def r4(self):
        t=self.b[self.z].astype(F32)
        for k in (1,2,3):
            self.cps[6+k].wait_recv()
            t=t+self.rz[k-1].astype(F32)
        return t
    def drain(self):
        for cp in self.cps.values(): cp.wait_send()

def scatter_scratch(r,n,dt):
    V=pltpu.VMEM
    return [V((4,4,r,n),dt),V((4,4,r,n),dt),V((2,r,n),dt),V((2,r,n),dt),V((4,r,n),dt),V((4,r,n),dt),V((4,r,n),dt),V((3,r,n),dt)]

def scatter_kernel(sm_ref,q_ref,p_ref,f1_ref,f2_ref,os_ref,oq_ref,op_ref,o1_ref,o2_ref,*sc):
    bufs=[sc[8*i:8*i+8] for i in range(5)]
    fin=sc[40:46]; ss,rs,ls,fs,fr=sc[46:]
    greet()
    c,x,y,z=place(); yx=y*2+x
    def cv(ref):
        h=ref.shape[-1]//2
        return lambda lane: ref.at[:,:,:,pl.ds(pl.multiple_of(lane*h,128),h)]
    def rv(ref): return lambda lane: ref.at[:,:,lane]
    refs=[sm_ref,q_ref,p_ref,f1_ref,f2_ref]
    S=[Scatter((rv if i in (0,4) else cv)(refs[i]),*bufs[i],ss.at[i],rs.at[i],ls.at[i]) for i in range(5)]
    order=[4,3,2,1,0]
    sibd=dev(z,yx,1-c)
    ends=[]
    outs={1:oq_ref,2:op_ref,3:o1_ref}
    def end(i):
        t=S[i].r4()
        if i==0: os_ref[...]=t
        elif i==4: o2_ref[...]=t
        else:
            f,rf=fin[2*(i-1)],fin[2*(i-1)+1]
            r=t.shape[0]//2
            f[0]=t[:r]; f[1]=t[r:]
            cp=pltpu.make_async_remote_copy(src_ref=f.at[1-c],dst_ref=rf,send_sem=fs.at[i],recv_sem=fr.at[i],device_id=sibd,device_id_type=MESH)
            cp.start(); ends.append((i,cp))
    def close():
        for i,cp in ends:
            cp.wait_recv()
            f,rf=fin[2*(i-1)],fin[2*(i-1)+1]
            own=f[c]; oth=rf[...]
            o=outs[i]; h=own.shape[-1]
            o[:,:h]=jnp.where(c==0,own,oth); o[:,h:]=jnp.where(c==0,oth,own)
            cp.wait_send()
    for i in order: S[i].r0()
    n=len(order)
    stages=[lambda i:S[i].r1(),lambda i:S[i].r2(),lambda i:S[i].r3(),lambda i:end(i)]
    for t in range(n+3):
        for s in range(3,-1,-1):
            k=t-s
            if 0<=k<n: stages[s](order[k])
    close()
    for s in S: s.drain()

def scatter_all(sm,q,p,f1,f2):
    sds=jax.ShapeDtypeStruct
    V=pl.BlockSpec(memory_space=pltpu.VMEM); A=pl.BlockSpec(memory_space=pl.ANY)
    D=pltpu.SemaphoreType.DMA
    sc=[]
    for a,dt in ((sm,F32),(q,BF),(p,BF),(f1,BF),(f2,BF)):
        if a.ndim==5: sc+=scatter_scratch(a.shape[3],a.shape[4],dt)
        else: sc+=scatter_scratch(a.shape[2],a.shape[3]//2,dt)
    outs=[sds(sm.shape[3:],F32)]
    for a in (q,p,f1):
        r,n=a.shape[2]//2,a.shape[3]
        sc+=[pltpu.VMEM((2,r,n//2),F32),pltpu.VMEM((r,n//2),F32)]
        outs.append(sds((r,n),F32))
    outs.append(sds(f2.shape[3:],F32))
    return pl.pallas_call(scatter_kernel,in_specs=[A]*5,out_specs=[V]*5,out_shape=outs,
        scratch_shapes=sc+[D((5,10)),D((5,10)),D((5,)),D((5,)),D((5,))],
        compiler_params=pltpu.CompilerParams(collective_id=1,has_side_effects=True,vmem_limit_bytes=56<<20),name="scatter_all")(sm,q,p,f1,f2)
class Gather2:
    def __init__(self,view,ss,rs):
        self.view=view; self.ss=ss; self.rs=rs
        c,x,y,z=place()
        self.c=c; self.z=z; self.yx=y*2+x
        self.xn=y*2+1-x; self.yn=(1-y)*2+x; self.dg=(1-y)*2+1-x
        self.xd=dev(z,self.xn,c); self.yd=dev(z,self.yn,c); self.sd=dev(z,self.yx,1-c)
        self.sends=[]
    def at(self,k,yx,lane=None): return self.view(pl.ds(lax.rem(self.z+4-k,4),1),yx,self.c if lane is None else lane)
    def all(self,yx,lane=None): return self.view(pl.ds(0,4),yx,self.c if lane is None else lane)
    def _cp(self,src,dst,slot,d):
        return pltpu.make_async_remote_copy(src_ref=src,dst_ref=dst,send_sem=self.ss.at[slot],recv_sem=self.rs.at[slot],device_id=d,device_id_type=MESH)
    def send(self,src,dst,slot,d):
        cp=self._cp(src,dst,slot,d); cp.start(); self.sends.append(cp)
    def got(self,dst,slot,d): self._cp(dst,dst,slot,d).wait_recv()
    def near(self,src):
        self.send(src,self.at(0,self.yx),3,self.xd)
        self.send(src,self.at(0,self.yx),7,self.yd)
    def far(self,src):
        for k in (1,2,3): self.send(src,self.at(0,self.yx),k-1,dev(lax.rem(self.z+k,4),self.yx,self.c))
    def X0(self):
        r=self.at(0,self.xn); self.got(r,3,self.xd)
        self.send(r,r,11,self.yd)
        self.got(self.at(0,self.yn),7,self.yd)
    def Z(self,k):
        r=self.at(k,self.yx)
        self.got(r,k-1,dev(lax.rem(self.z+4-k,4),self.yx,self.c))
        self.send(r,r,3+k,self.xd); self.send(r,r,7+k,self.yd); self.send(r,r,14+k,self.sd)
    def X(self,k):
        a=self.at(k,self.xn); b=self.at(k,self.yn)
        self.got(a,3+k,self.xd)
        if k==1: self.send(a,a,11+k,self.yd)
        self.got(b,7+k,self.yd)
        if k!=1: self.send(b,b,11+k,self.xd)
        if k==2:
            for yx,s in ((self.xn,18),(self.yn,19)):
                r=self.all(yx); self.send(r,r,s,self.sd)
    def D(self):
        for k in (0,1,3,2):
            self.got(self.at(k,self.dg),11+k,self.yd if k<2 else self.xd)
        r=self.all(self.dg); self.send(r,r,20,self.sd)
    def F(self):
        o=1-self.c
        for k in (1,2,3): self.got(self.at(k,self.yx,o),14+k,self.sd)
        for yx,s in ((self.xn,18),(self.yn,19),(self.dg,20)): self.got(self.all(yx,o),s,self.sd)
    def drain(self):
        for cp in self.sends: cp.wait_send()

def gelu_parts(x):
    d=1.0+0.23164189*jnp.abs(x)
    t=pl.reciprocal(d,approx=True)
    t=t*(2.0-d*t)
    e=jnp.exp2(x*x*(-0.5*1.4426950408889634))
    q=((((0.5*1.061405429*t-0.5*1.453152027)*t+0.5*1.421413741)*t-0.5*0.284496736)*t+0.5*0.254829592)*t*e
    cdf=jnp.where(x>=0,1.0-q,q)
    return x*cdf, cdf+x*e*0.3989422804014327

def row_stats(x):
    inv=1.0/x.shape[1]
    mean=jnp.sum(x,axis=1,keepdims=True)*inv
    c=x-mean
    var=jnp.sum(c*c,axis=1,keepdims=True)*inv
    return c,lax.rsqrt(var+eps_norm)

def spread(each,total,cols):
    j=lax.broadcasted_iota(jnp.int32,(128,total),1); l=lax.broadcasted_iota(jnp.int32,(128,total),0)
    return jnp.where(j-cols*each==l,1.0,0.0).astype(BF)

def over(each,shape):
    j=lax.broadcasted_iota(jnp.int32,shape,1)
    return (j*((1<<22)//each+1))>>22

def settled(g1,r):
    return r+jnp.where(r>=400,-8*g1,jnp.where(r>=392,400*g1,0))

def segments(groups,offsets,pos):
    g=groups[0]
    length=jnp.where(g==0,P_SMALL,jnp.where(g==1,P_MID,P_LARGE))
    seg=jnp.full(pos.shape,-1,jnp.int32)
    for s in range(8):
        o=offsets[s]
        seg=jnp.where((pos>=o)&(pos<o+length),s,seg)
    return seg

def settle_rows(g1,read,write):
    def either(a,b): return [jnp.where(g1==1,u,w) for u,w in zip(a,b)]
    def body(i,_):
        r=pl.multiple_of(i*56,8)
        write(r,56,read(r,56)); return 0
    lax.fori_loop(0,7,body,0)
    write(392,8,either(read(792,8),read(392,8)))
    def body2(i,_):
        r=pl.multiple_of(400+i*40,8)
        write(r,40,either(read(pl.multiple_of(392+i*40,8),40),read(r,40))); return 0
    lax.fori_loop(0,10,body2,0)

FORWARD_ORDER=(
    96, 0, 1, 16, 48, 97, 17, 64, 200, 49, 98, 32, 3, 5, 4, 20, 19, 99, 33, 21, 201, 65, 52, 2, 53, 8, 100, 6, 18,
    51, 202, 7, 24, 203, 22, 37, 36, 56, 50, 23, 35, 9, 34, 204, 10, 220, 40, 54, 55, 25, 38, 39, 80, 230, 26, 81,
    57, 41, 69, 67, 231, 68, 221, 232, 42, 66, 58, 72, 233, 222, 70, 71, 234, 85, 84, 235, 83, 82, 73, 205, 74,
    240, 241, 88, 242, 243, 86, 244, 87, 245, 250, 251, 89, 252, 253, 90,
)

def forward_kernel(groups,offsets,v0,v1,v2,v3,v4,v5,v6,v7,v8,q_ref,p_ref,f1_ref,f2_ref,tok_ref,cot_ref,mask_ref,
        wq_o,wp_o,w1_o,w2_o,pr_o,n1_o,n2_o,ctx_o,pj_o,hid_o,dg_o,st_o,mid_o,pt2_o,gt_o,cs_o,vec_o,meta_o,
        gs,gq,gp,g1w,sq,sp,s1,bq,bp,b1,raw,mid,st,n1,nt_,pj,bias,ctx,n2,hid,dg,gt,cs,pt2,pst,sc,sm_ref,smf,mk,bqv,bf1,
        ss0,rs0,ssl,sss,srs,ss,rs,psem,osem):
    smf[...]=jnp.zeros_like(smf)
    for i,r in enumerate((v0,v1,v2,v3,v4,v5,v6,v7,v8)):
        m=r.shape[0]
        smf[i:i+1,0:m]=r[...].astype(F32).reshape(1,m)
    sm_ref[...]=smf[...].astype(BF)
    greet()
    c,x,y,z=place(); yx=y*2+x
    sibd=dev(z,yx,1-c)
    first=[]
    def swap(src,dst,i):
        cp=pltpu.make_async_remote_copy(src_ref=src,dst_ref=dst,send_sem=ss0.at[i],recv_sem=rs0.at[i],device_id=sibd,device_id_type=MESH)
        cp.start(); first.append(cp)
    swap(sm_ref,gs.at[z,yx,c],0)
    swap(q_ref,sq,1); swap(p_ref,sp,2); swap(f1_ref,s1,3)
    swap(f2_ref,w2_o.at[z,yx,c],4)
    gs[z,yx,c]=sm_ref[...]
    own2=pltpu.make_async_copy(f2_ref,w2_o.at[z,yx,c],ssl.at[0]); own2.start()
    S=Gather(rows_view(gs),sss,srs)
    QA,QB,QC,Pj,F1=[Gather2(cols_view(r),ss.at[i],rs.at[i]) for i,r in enumerate((gq.at[0],gq.at[1],gq.at[2],gp,g1w))]
    F2=Gather2(rows_view(w2_o),ss.at[5],rs.at[5])
    outs=[]; lag=[]; used=[0]
    def put(src,dst):
        cp=pltpu.make_async_copy(src,dst,osem.at[used[0]]); cp.start(); outs.append(cp); used[0]+=1
    waited=set()
    def swapped(i):
        if i not in waited: waited.add(i); first[i].wait_recv()
    def build(own,sib,buf,dst):
        j=join(c,own,sib)
        buf[0]=j; dst[z,yx]=j
    def parts(ref,g): return jnp.concatenate([ref[:,o+256*g:o+256*g+256] for o in (0,768,1536)],axis=1)
    def half(b):
        h=b.shape[-1]//2
        return b.at[:,:,pl.ds(pl.multiple_of(c*h,128),h)]
    def near(n):
        if n=="F2": own2.wait(); F2.near(F2.at(0,yx)); return
        if n[0]=="Q":
            g="ABC".index(n[1]); swapped(1); build(parts(q_ref,g),parts(sq,g),bq.at[g],gq.at[g]); G[n].near(half(bq.at[g]))
        elif n=="P": swapped(2); build(p_ref[...],sp[...],bp,gp); Pj.near(half(bp))
        else: swapped(3); build(f1_ref[...],s1[...],b1,g1w); F1.near(half(b1))
    def far(n):
        if n=="F2": F2.far(F2.at(0,yx))
        elif n[0]=="Q": G[n].far(half(bq.at["ABC".index(n[1])]))
        else: G[n].far(half(bp if n=="P" else b1))
    G={"QA":QA,"QB":QB,"QC":QC,"P":Pj,"F1":F1,"F2":F2}
    def finish(n):
        if n=="F2": first[4].wait_recv()
        G[n].F()
        if n[0]=="Q": g="ABC".index(n[1]); put(gq.at[g],wq_o.at[g])
        elif n=="P": put(gp,wp_o)
        elif n=="F1": put(g1w,w1_o)
    def small(k):
        if k=="s": S.z_send(S.one(z))
        elif k=="Z": S.z_recv(); S.xy_send()
        elif k=="X": S.xy_recv()
        elif k=="D": S.diag_recv()
        else: first[0].wait_recv(); S.finish()
    g1=jnp.where(groups[0]==1,1,0)
    def setup(k):
        if k==0:
            raw[...]=tok_ref[...].astype(F32)
        segc=segments(groups,offsets,settled(g1,lax.broadcasted_iota(jnp.int32,(400,1),0)+400*k))
        meta_o[400*k:400*k+400,0:1]=jnp.where(segc>=0,1.0,0.0)
        segr=segments(groups,offsets,settled(g1,lax.broadcasted_iota(jnp.int32,(1,400),1)+400*k))
        bias[k]=jnp.where(segc==segr,0.0,-1e30)
    def vectors():
        X=gs[...].reshape(512,128)
        E=nn(X,spread(24,768,over(24,(128,768))))
        E=jnp.where(lax.broadcasted_iota(jnp.int32,(512,768),0)>>4==over(24,(512,768)),E,0.0).reshape(32,16,768)
        vec_o[...]=jnp.sum(E,axis=0)
        def wide(row,each,total):
            sel=jnp.where(lax.broadcasted_iota(jnp.int32,(32,512),1)==lax.broadcasted_iota(jnp.int32,(32,512),0)*16+row,1.0,0.0).astype(BF)
            e=nn(nn(sel,X).astype(BF),spread(each,total,over(each,(128,total))))
            e=jnp.where(lax.broadcasted_iota(jnp.int32,(32,total),0)==over(each,(32,total)),e,0.0)
            return jnp.sum(e,axis=0,keepdims=True)
        bqv[...]=wide(3,48,1536); bf1[...]=wide(7,96,3072)
    def norm_one():
        mask=jnp.broadcast_to(mask_ref[...].astype(F32).reshape(1,800),(8,800)).T
        mk[...]=mask[:,0:1]
        def write(r,n,v):
            t,m=v
            meta_o[pl.ds(r,n),1:2]=m
            mid[pl.ds(r,n),:]=jnp.where(m>0.0,vec_o[0:1,:],t)
        settle_rows(g1,lambda r,n:(raw[pl.ds(r,n),:],mk[pl.ds(r,n),:]),write)
        def body(i,_):
            r=pl.ds(pl.multiple_of(i*80,16),80)
            s=mid[r,:]
            st[r,:]=s.astype(BF)
            cc,rstd=row_stats(s)
            n1[r,:]=(cc*rstd*vec_o[1:2,:]+vec_o[2:3,:]).astype(BF)
            return 0
        lax.fori_loop(0,10,body,0)
        put(st,st_o)
    def cotangents():
        raw[...]=cot_ref[...].astype(F32)
        def write2(r,n,v): mid[pl.ds(r,n),:]=v[0]
        settle_rows(g1,lambda r,n:(raw[pl.ds(r,n),:],),write2)
        def body(i,_):
            r=pl.ds(pl.multiple_of(i*80,16),80)
            v=mid[r,:]
            cs[r,:]=v.astype(BF); gt[r,:]=(v*meta_o[r,0:1]).astype(BF)
            return 0
        lax.fori_loop(0,10,body,0)
        put(cs,cs_o); put(gt,gt_o)
        nt_[...]=n1[...].T
        put(nt_,n1_o)
        lag.append(outs[-1])
    def qkv(g):
        r=nn(n1[...],gq[g].reshape(768,768))
        for k,o in enumerate((0,768,1536)):
            t=r[:,256*k:256*k+256]
            if k!=1: t=t+bqv[:,384*k+256*g:384*k+256*g+256]
            pj[:,o+256*g:o+256*g+256]=t.astype(BF)
        if g==2: put(pj,pj_o)
    lane=lax.broadcasted_iota(jnp.int32,(400,128),1)
    def where_of(t):
        return lax.rem(t,4)//2,2*(t//4)+lax.rem(t,2)
    def pcopy(t):
        b,p=where_of(t)
        return pltpu.make_async_copy(pst.at[lax.rem(t,2)],pr_o.at[b*6+p],psem.at[lax.rem(t,2)])
    def attend(t,_):
        b,p=where_of(t); s=lax.rem(t,2)
        r=pl.ds(pl.multiple_of(b*400,16),400)
        cc=lambda o: pl.ds(pl.multiple_of(o+p*128,128),128)
        @pl.when(t>=2)
        def _(): pcopy(t-2).wait()
        q=pj[r,cc(0)]; k=pj[r,cc(768)]; v=pj[r,cc(1536)]
        res=[]
        for j in range(2):
            qj=jnp.where((lane>=64)==(j==1),q,jnp.zeros_like(q))
            sc[j]=nt(qj,k)
        for j in range(2):
            for i in range(10):
                u=slice(40*i,40*i+40)
                t_=sc[j,u]*0.18033688011112042+bias[b,u]
                e=jnp.exp2(t_-jnp.max(t_,axis=1,keepdims=True))
                sc[j,u]=e*(1.0/jnp.sum(e,axis=1,keepdims=True))
        for j in range(2):
            pr=sc[j].astype(BF)
            pst[s,j]=pr
            res.append(nn(pr,v))
        ctx[r,cc(0)]=jnp.where(lane<64,res[0],res[1]).astype(BF)
        pcopy(t).start()
        return 0
    def proj():
        put(ctx,ctx_o)
        wpv=gp[...].reshape(768,768)
        def body(i,_):
            r=pl.ds(pl.multiple_of(i*400,16),400)
            mid[r,:]=st[r,:].astype(F32)+meta_o[r,0:1]*(nn(ctx[r,:],wpv)+vec_o[4:5,:])
            return 0
        lax.fori_loop(0,2,body,0)
        def body(i,_):
            r=pl.ds(pl.multiple_of(i*80,16),80)
            cc,rstd=row_stats(mid[r,:])
            n2[r,:]=(cc*rstd*vec_o[5:6,:]+vec_o[6:7,:]).astype(BF)
            return 0
        lax.fori_loop(0,10,body,0)
        put(mid,mid_o)
        lag[0].wait(); outs[:]=[o for o in outs if o is not lag[0]]
        nt_[...]=n2[...].T
        put(nt_,n2_o)
    def mlp(i,_):
        cc=pl.ds(pl.multiple_of(i*512,128),512)
        a,d=gelu_parts(nn(n2[...],g1w[:,:,:,cc].reshape(768,512))+bf1[:,cc])
        hid[:,cc]=a.astype(BF); dg[:,cc]=d.astype(BF)
        return 0
    def grads(i,_):
        cc=pl.ds(pl.multiple_of(i*768,128),768)
        pt2[i]=tn(hid[:,cc],gt[...]).astype(BF).reshape(4,2,96,768)
        return 0
    chunks=("QA","QB","QC","P","F1","F2")
    k=0
    while k<len(FORWARD_ORDER):
        op=FORWARD_ORDER[k]; k+=1
        if op>=96 and op<200: small("sZXDF"[op-96])
        elif op<96:
            n=chunks[op//16]; g=G[n]; t=op%16
            if t==0: near(n)
            elif t==1: far(n)
            elif t==2: g.X0()
            elif t<6: g.Z(t-2)
            elif t<9: g.X(t-5)
            elif t==9: g.D()
            else: finish(n)
        elif op<220: (lambda:setup(0),lambda:setup(1),vectors,norm_one,cotangents,proj)[op-200]()
        elif op<230: qkv(op-220)
        else:
            a=b=op%10
            while k<len(FORWARD_ORDER) and FORWARD_ORDER[k]==op-a+b+1: b+=1; k+=1
            if op>=250:
                lax.fori_loop(a,b+1,grads,0)
                put(pt2.at[pl.ds(a,b+1-a)],pt2_o.at[pl.ds(a,b+1-a)])
            elif op<240: lax.fori_loop(2*a,2*b+2,attend,0)
            else:
                lax.fori_loop(a,b+1,mlp,0)
                if b==5:
                    put(hid,hid_o); put(dg,dg_o)
    pcopy(10).wait(); pcopy(11).wait()
    for cp in outs: cp.wait()
    for cp in first: cp.wait_send()
    for g in [S]+list(G.values()): g.drain()

def forward(groups,offsets,vectors,wq,wp,w1,w2,tok,cot,mask):
    sds=jax.ShapeDtypeStruct
    V=pl.BlockSpec(memory_space=pltpu.VMEM); A=pl.BlockSpec(memory_space=pl.ANY); M=pl.BlockSpec(memory_space=pltpu.SMEM)
    D=pltpu.SemaphoreType.DMA
    v=pltpu.VMEM
    R,W=tok.shape
    outs=[((3,4,4,48,768),BF),((4,4,48,768),BF),((4,4,48,3072),BF),((4,4,2,96,768),BF),((12,2,400,400),BF),
        ((W,R),BF),((W,R),BF),((R,W),BF),((R,3*W),BF),((R,4*W),BF),((R,4*W),BF),((R,W),BF),((R,W),F32),((4,4,2,96,768),BF),((R,W),BF),((R,W),BF),
        ((16,W),F32),((R,2),F32)]
    return pl.pallas_call(forward_kernel,
        in_specs=[M,M]+[V]*16,out_specs=[A]*16+[V,V],out_shape=[sds(*o) for o in outs],
        scratch_shapes=[v((4,4,2,16,128),BF),v((3,4,4,48,768),BF),v((4,4,48,768),BF),v((4,4,48,3072),BF),
            v((24,2304),BF),v((24,768),BF),v((24,3072),BF),v((3,1,48,768),BF),v((1,48,768),BF),v((1,48,3072),BF),
            v((R,W),F32),v((R,W),F32),v((R,W),BF),v((R,W),BF),v((W,R),BF),v((R,3*W),BF),v((2,400,400),F32),v((R,W),BF),v((R,W),BF),
            v((R,4*W),BF),v((R,4*W),BF),v((R,W),BF),v((R,W),BF),v((4,4,2,96,768),BF),v((2,2,400,400),BF),v((2,400,400),F32),v((16,128),BF),v((16,128),F32),v((800,1),F32),v((1,2*W),F32),v((1,4*W),F32),
            D((5,)),D((5,)),D((1,)),D((14,)),D((14,)),D((6,21)),D((6,21)),D((2,)),D((24,))],
        compiler_params=pltpu.CompilerParams(collective_id=0,has_side_effects=True,vmem_limit_bytes=60<<20),name="forward")(
        groups,offsets,*vectors,wq,wp,w1,w2,tok,cot,mask)

class Reduce:
    def __init__(self,give,a,s,rxa,ryb,rx,ry,b,rz,ss,rs):
        self.give=give; self.a=a; self.s=s; self.rxa=rxa; self.ryb=ryb; self.rx=rx; self.ry=ry; self.b=b; self.rz=rz
        self.ss=ss; self.rs=rs
        c,x,y,z=place()
        self.c=c; self.z=z; self.yx=y*2+x
        self.xn=y*2+1-x; self.yn=(1-y)*2+x; self.dg=(1-y)*2+1-x
        self.xd=dev(z,self.xn,c); self.yd=dev(z,self.yn,c); self.sd=dev(z,self.yx,1-c)
        self.cps={}
    def send(self,src,dst,slot,d):
        cp=pltpu.make_async_remote_copy(src_ref=src,dst_ref=dst,send_sem=self.ss.at[slot],recv_sem=self.rs.at[slot],device_id=d,device_id_type=MESH)
        cp.start(); self.cps[slot]=cp
    def r0(self): self.send(self.give,self.s,0,self.sd)
    def add(self,n,z0,yx,other):
        def body(i,_):
            t=self.a(pl.ds(i+z0,1),yx)
            t[...]=t[...]+other(i)[...]
            return 0
        lax.fori_loop(0,n,body,0)
    def r1(self):
        self.cps[0].wait_recv()
        def own(yx): self.add(4,0,yx,lambda i: self.s.at[pl.ds(i,1),yx])
        own(self.dg)
        self.send(self.a(pl.ds(0,2),self.dg),self.rxa,1,self.xd)
        self.send(self.a(pl.ds(2,2),self.dg),self.ryb,2,self.yd)
        own(self.xn)
        self.send(self.a(pl.ds(0,2),self.xn),self.rx.at[pl.ds(0,2)],3,self.xd)
        own(self.yn)
        self.send(self.a(pl.ds(2,2),self.yn),self.ry.at[pl.ds(2,2)],4,self.yd)
        own(self.yx)
    def r2(self):
        self.cps[1].wait_recv()
        self.add(2,0,self.yn,lambda i: self.rxa.at[pl.ds(i,1)])
        self.send(self.a(pl.ds(0,2),self.yn),self.ry.at[pl.ds(0,2)],6,self.yd)
        self.cps[2].wait_recv()
        self.add(2,2,self.xn,lambda i: self.ryb.at[pl.ds(i,1)])
        self.send(self.a(pl.ds(2,2),self.xn),self.rx.at[pl.ds(2,2)],5,self.xd)
    def r3(self):
        for s in (3,4,5,6): self.cps[s].wait_recv()
        def body(i,_):
            k=pl.ds(i,1)
            self.b[k]=(self.a(k,self.yx)[...].astype(F32)+self.rx[k].astype(F32)+self.ry[k].astype(F32)).astype(BF)
            return 0
        lax.fori_loop(0,4,body,0)
        for k in (1,2,3):
            zz=lax.rem(self.z+k,4)
            self.send(self.b.at[zz],self.rz.at[k-1],6+k,dev(zz,self.yx,self.c))
    def total(self):
        t=self.b[self.z].astype(F32)
        for k in (1,2,3):
            self.cps[6+k].wait_recv()
            t=t+self.rz[k-1].astype(F32)
        return t
    def drain(self):
        for cp in self.cps.values(): cp.wait_send()

def eights(v):
    return jnp.sum(v.reshape(v.shape[0]//8,8,v.shape[1]),axis=0)

class Total:
    def __init__(self,v,r,ss,rs):
        self.v=v; self.r=r; self.ss=ss; self.rs=rs; self.cps=[]
    def send(self,a,slot,d):
        cp=pltpu.make_async_remote_copy(src_ref=self.v.at[a],dst_ref=self.r.at[slot],send_sem=self.ss.at[slot],recv_sem=self.rs.at[slot],device_id=d,device_id_type=MESH)
        cp.start(); self.cps.append(cp)
    def stage(self,k):
        c,x,y,z=place(); yx=y*2+x
        if k:
            if k<4: self.cps[k-1].wait_recv(); self.v[k]=self.v[k-1]+self.r[k-1]
        if k==0: self.send(0,0,dev(z,yx,1-c))
        elif k==1: self.send(1,1,dev(z,y*2+1-x,c))
        elif k==2: self.send(2,2,dev(z,(1-y)*2+x,c))
        elif k==3:
            for h in (1,2,3): self.send(3,2+h,dev(lax.rem(z+h,4),yx,c))
        else:
            for h in (1,2,3): self.cps[2+h].wait_recv()
            self.sum=self.v[3]+self.r[3]+self.r[4]+self.r[5]
    def drain(self):
        for cp in self.cps: cp.wait_send()

BACKWARD_ORDER=(
    0, 200, 16, 240, 1, 241, 242, 243, 2, 220, 221, 32, 17, 48, 222, 223, 49, 201, 64, 33, 18, 3, 80, 202, 50, 203,
    204, 65, 96, 250, 81, 19, 34, 97, 251, 230, 112, 66, 252, 113, 51, 253, 35, 98, 67, 82, 231, 114, 128, 254,
    129, 83, 99, 255, 130, 232, 176, 144, 36, 52, 4, 115, 131, 177, 205, 178, 145, 206, 179, 207, 160, 146, 132,
    161, 116, 147, 162, 208, 163, 84, 20, 209, 100, 68, 180, 148, 164,
)

def backward_kernel(w2_r,w1_r,wp_r,wq_r,pr_r,n1_r,n2_r,ctx_r,pj_r,hid_r,dg_r,st_r,mid_r,pt2_r,gt_r,cs_r,vec,meta,
        out_o,tok_o,sm_o,oq,op_,o1,o2,
        w2,w1,wp,gp,pj,mid,gf,nt_,tmp,ctx,gt,gb,pst,acc,accb,
        a2,s2,xa2,yb2,x2,y2,b2,z2,part,sb,xab,ybb,xb,yb,bb,zb,fb,frb,vs,vr,us,ur,
        lsem,psem,osem,rss,rrs,fss,frs,vss,vrs,uss,urs):
    greet()
    c,x,y,z=place(); yx=y*2+x
    sibd=dev(z,yx,1-c)
    loads={}; held=set()
    def get(name,src,dst):
        cp=pltpu.make_async_copy(src,dst,lsem.at[len(loads)]); cp.start(); loads[name]=cp
    def have(*names):
        for n in names:
            if n not in held: held.add(n); loads[n].wait()
    C2=[Reduce(pt2_r.at[:,:,1-c,h],lambda zs,q,h=h: a2.at[h,zs,q],s2.at[h],xa2.at[h],yb2.at[h],x2.at[h],y2.at[h],b2.at[h],z2.at[h],rss.at[h],rrs.at[h]) for h in range(2)]
    def sib_at(i): return sb.at[i] if i<5 else s2.at[(i-5)//2,:,:,:,pl.ds(384*((i-5)%2),384)]
    mine=pl.ds(pl.multiple_of(c*384,128),384); theirs=pl.ds(pl.multiple_of((1-c)*384,128),384)
    CH=[Reduce(part.at[i,:,:,:,theirs],lambda zs,q,i=i: part.at[i,zs,q,:,mine],sib_at(i),xab.at[i],ybb.at[i],xb.at[i],yb.at[i],bb.at[i],zb.at[i],rss.at[2+i],rrs.at[2+i]) for i in range(8)]
    F=CH[0:4]; PJ=CH[4]; QK=CH[5:8]
    get("gt",gt_r,gt)
    get("w2a",w2_r.at[pl.ds(0,32)],w2.at[pl.ds(0,32)]); get("dga",dg_r.at[:,pl.ds(0,1536)],gp.at[:,pl.ds(0,1536)])
    get("a2a",pt2_r.at[:,:,c,0],a2.at[0])
    get("w2b",w2_r.at[pl.ds(32,32)],w2.at[pl.ds(32,32)]); get("dgb",dg_r.at[:,pl.ds(1536,1536)],gp.at[:,pl.ds(1536,1536)])
    get("a2b",pt2_r.at[:,:,c,1],a2.at[1])
    get("n2",n2_r,nt_); get("cs",cs_r,tmp)
    get("w1",w1_r,w1); get("mid",mid_r,mid); get("wp",wp_r,wp); get("ctx",ctx_r,ctx); get("pj",pj_r,pj)
    acc[...]=jnp.zeros_like(acc)
    ends=[]
    def end(i):
        t=CH[i].total()
        fb[i,0]=t[:24]; fb[i,1]=t[24:]
        cp=pltpu.make_async_remote_copy(src_ref=fb.at[i,1-c],dst_ref=frb.at[i],send_sem=fss.at[i],recv_sem=frs.at[i],device_id=sibd,device_id_type=MESH)
        cp.start(); ends.append((i,cp))
    def end2(h): o2[48*h:48*h+48,:]=C2[h].total()
    def mlp(i,_):
        cc=pl.ds(pl.multiple_of(i*768,128),768)
        g=(nt(gt[...],w2[pl.ds(16*i,16)].reshape(768,768))*gp[:,cc].astype(F32)).astype(BF)
        gp[:,cc]=g
        accb[:,cc]=eights(g.astype(F32))
        return 0
    def w1grad(i):
        have("n2")
        part[i]=nn(nt_[...],gp[:,768*i:768*i+768]).astype(BF).reshape(4,4,48,768)
        if i==3: get("n1",n1_r,nt_)
    def norm_back(i0,rows,gain,ka,kb,finish):
        def body(i,_):
            r=pl.ds(pl.multiple_of(i0+i*80,16),80)
            g,m=gf[r,:],rows(r)
            cc,rstd=row_stats(m)
            xh=cc*rstd
            acc[ka]+=eights(g*xh); acc[kb]+=eights(g)
            gx=g*gain
            m1=jnp.sum(gx,axis=1,keepdims=True)*(1.0/768); m2=jnp.sum(gx*xh,axis=1,keepdims=True)*(1.0/768)
            finish(r,rstd*(gx-m1-xh*m2))
            return 0
        lax.fori_loop(0,5,body,0)
    def finish2(r,d):
        gm=tmp[r,:].astype(F32)+d
        mid[r,:]=gm
        v=(meta[r,0:1]*gm).astype(BF)
        gb[r,:]=v
        acc[4]+=eights(v.astype(F32))
        acc[8]+=eights(gt[r,:].astype(F32))
    def p10(k):
        have("w1","cs","mid")
        r=slice(400*k,400*k+400)
        gf[r,:]=nt(gp[r,:],w1[...].reshape(768,3072))
        norm_back(400*k,lambda r: mid[r,:],vec[5:6,:],5,6,finish2)
        if k==1:
            get("hid",hid_r,gp); get("st",st_r,tmp)
            for g in range(3): get("wq%d"%g,wq_r.at[g],w1.at[:,:,:,pl.ds(768*g,768)])
    gc=gt
    def gctx():
        have("wp")
        gc[...]=nt(gb[...],wp[...].reshape(768,768)).astype(BF)
        pcopy(0).start()
    def wpgrad():
        have("ctx")
        part[4]=tn(ctx[...],gb[...]).astype(BF).reshape(4,4,48,768)
    lane=lax.broadcasted_iota(jnp.int32,(400,128),1)
    def where_of(t):
        return lax.rem(t,4)//2,2*(t//4)+lax.rem(t,2)
    def pcopy(t):
        b,p=where_of(t)
        return pltpu.make_async_copy(pr_r.at[b*6+p],pst.at[lax.rem(t,2)],psem.at[lax.rem(t,2)])
    def attend(t,_):
        b,p=where_of(t); s=lax.rem(t,2)
        r=pl.ds(pl.multiple_of(b*400,16),400)
        cc=lambda o: pl.ds(pl.multiple_of(o+p*128,128),128)
        pcopy(t).wait()
        @pl.when(t<11)
        def _(): pcopy(t+1).start()
        q=pj[r,cc(0)]; k=pj[r,cc(768)]; v=pj[r,cc(1536)]; g=gc[r,cc(0)]
        gx=g.astype(F32)*ctx[r,cc(0)].astype(F32)
        dq=[];dk=[];dv=[]
        for j in range(2):
            own=(lane>=64)==(j==1)
            zero=jnp.zeros_like(q)
            qj=jnp.where(own,q,zero); gj=jnp.where(own,g,zero)
            di=jnp.sum(jnp.where(own,gx,0.0),axis=1,keepdims=True)
            pr=pst[s,j]
            ds=(pr.astype(F32)*(nt(gj,v)-di)).astype(BF)
            dq.append(nn(ds,k)); dk.append(tn(ds,qj)); dv.append(tn(pr,gj))
        pj[r,cc(0)]=(jnp.where(lane<64,dq[0],dq[1])*0.125).astype(BF)
        pj[r,cc(768)]=((dk[0]+dk[1])*0.125).astype(BF)
        pj[r,cc(1536)]=(dv[0]+dv[1]).astype(BF)
        return 0
    def group(r,g): return jnp.concatenate([pj[r,o+256*g:o+256*g+256] for o in (0,768,1536)],axis=1)
    def qkvgrad(g):
        if g==0: have("n1")
        cols=group(slice(None),g)
        acc[3,:,256*g:256*g+256]=eights(cols[:,:256].astype(F32)); acc[7,:,256*g:256*g+256]=eights(cols[:,512:].astype(F32))
        part[5+g]=nn(nt_[...],cols).astype(BF).reshape(4,4,48,768)
        if g==2:
            for k in range(6): us[0,k:k+1,:]=jnp.sum(acc[3+k],axis=0,keepdims=True)
            for k in range(4): us[0,6+k:7+k,:]=jnp.sum(accb[:,768*k:768*k+768],axis=0,keepdims=True)
            us[0,10:16,:]=jnp.zeros((6,768),F32)
    def finish1(r,d):
        gs=mid[r,:]+d
        m=meta[r,1:2]>0.0
        acc[0]+=eights(jnp.where(m,gs,0.0))
        mid[r,:]=jnp.where(m,0.0,gs)
    stores=[]
    def put(src,dst):
        cp=pltpu.make_async_copy(src,dst,osem.at[len(stores)]); cp.start(); stores.append(cp)
    def back(i):
        if i==0: have("st","wq0","wq1","wq2")
        r=slice(400*i,400*i+400)
        gf[r,:]=sum(nt(group(r,g),w1[:,:,:,768*g:768*g+768].reshape(768,768)) for g in range(3))
        norm_back(400*i,lambda r: tmp[r,:].astype(F32),vec[1:2,:],1,2,finish1)
        if i==1: put(mid,tok_o); get("mid2",mid_r,gf)
    def fin():
        for k in range(3): vs[0,k:k+1,:]=jnp.sum(acc[k],axis=0,keepdims=True)
        vs[0,3:8,:]=jnp.zeros((5,768),F32)
    def outp(i):
        if i==0: have("hid","mid2")
        r=slice(400*i,400*i+400)
        gf[r,:]=gf[r,:]+meta[r,0:1]*(nn(gp[r,:],w2[...].reshape(3072,768))+vec[8:9,:])
        put(gf.at[pl.ds(400*i,400)],out_o.at[pl.ds(400*i,400)])
    sums=[Total(vs,vr,vss,vrs),Total(us,ur,uss,urs)]
    plain=(lambda:None,lambda:p10(0),lambda:p10(1),gctx,wpgrad,lambda:back(0),lambda:back(1),fin,lambda:outp(0),lambda:outp(1))
    k=0
    while k<len(BACKWARD_ORDER):
        op=BACKWARD_ORDER[k]; k+=1
        i,t=op//16,op%16
        if i<10:
            if t==4:
                if i<2: end2(i)
                else: end(i-2)
            else:
                if i<2 and t==1: have(("a2a","a2b")[i])
                r=(C2+CH)[i]
                (r.r0,r.r1,r.r2,r.r3)[t]()
        elif i<12: sums[i-10].stage(t)
        elif op<220: plain[op-200]()
        elif op<230: w1grad(op-220)
        elif op<240: qkvgrad(op-230)
        else:
            a=b=op%10
            while k<len(BACKWARD_ORDER) and BACKWARD_ORDER[k]==op-a+b+1: b+=1; k+=1
            if op<250:
                for i in range(a,b+1):
                    if i==0: have("gt","w2a","dga")
                    if i==2: have("w2b","dgb")
                for lo,hi in ((a,min(b+1,2)),(max(a,2),b+1)):
                    if lo<hi: lax.fori_loop(lo,hi,mlp,0)
            else:
                if a==0: have("pj")
                lax.fori_loop(2*a,2*b+2,attend,0)
    vt,ut=sums[0].sum,sums[1].sum
    me=lax.axis_index("dp")
    def turn(v,by): return pltpu.roll(v,lax.rem(768-by,768),1)[:,:128]
    eight=lambda v: jnp.concatenate([v]*8,axis=0)
    sm_o[0:8,:]=turn(vt,24*me)
    t=turn(ut,24*me)
    sm_o[4:7,:]=t[1:4]; sm_o[8:9,:]=t[5:6]
    sm_o[3:4,:]=turn(eight(jnp.where(me>=16,ut[4:5],ut[0:1])),48*lax.rem(me,16))[0:1]
    k8=me//8
    pick=jnp.where(k8==0,ut[6:7],jnp.where(k8==1,ut[7:8],jnp.where(k8==2,ut[8:9],ut[9:10])))
    sm_o[7:8,:]=turn(eight(pick),96*lax.rem(me,8))[0:1]
    for i,cp in ends:
        cp.wait_recv()
        own=fb[i,c]; oth=frb[i]
        lo=jnp.where(c==0,own,oth); hi=jnp.where(c==0,oth,own)
        if i<4: o1[:,768*i:768*i+384]=lo; o1[:,768*i+384:768*i+768]=hi
        elif i==4: op_[:,:384]=lo; op_[:,384:]=hi
        else:
            g=256*(i-5)
            oq[:,g:g+256]=lo[:,:256]; oq[:,768+g:768+g+128]=lo[:,256:]
            oq[:,768+g+128:768+g+256]=hi[:,:128]; oq[:,1536+g:1536+g+256]=hi[:,128:]
        cp.wait_send()
    for cp in stores: cp.wait()
    for q in C2+CH+sums: q.drain()

def backward(w2,w1,wp,wq,pr,n1,n2,ctx,pj,hid,dg,st,mid,pt2,gt,cs,vec,meta):
    sds=jax.ShapeDtypeStruct
    V=pl.BlockSpec(memory_space=pltpu.VMEM); A=pl.BlockSpec(memory_space=pl.ANY)
    D=pltpu.SemaphoreType.DMA
    v=pltpu.VMEM
    W,R=n1.shape
    scr=[v((64,48,W),BF),v((4,4,48,4*W),BF),v((4,4,48,W),BF),v((R,4*W),BF),v((R,3*W),BF),v((R,W),F32),v((R,W),F32),v((W,R),BF),
        v((R,W),BF),v((R,W),BF),v((R,W),BF),v((R,W),BF),v((2,2,400,400),BF),v((9,8,W),F32),v((8,4*W),F32)]
    def rs(n,r,w,own):
        o=[v((n,4,4,r,own),BF),v((min(n,5),4,4,r,w),BF),v((n,2,r,w),BF),v((n,2,r,w),BF),v((n,4,r,w),BF),v((n,4,r,w),BF),v((n,4,r,w),BF),v((n,3,r,w),BF)]
        return o
    scr+=rs(2,48,W,W)+rs(8,48,W//2,W)
    scr+=[v((8,2,24,W//2),F32),v((8,24,W//2),F32),v((4,8,W),F32),v((6,8,W),F32),v((4,16,W),F32),v((6,16,W),F32)]
    scr+=[D((24,)),D((2,)),D((3,)),D((10,10)),D((10,10)),D((8,)),D((8,))]+[D((6,))]*4
    outs=[((R,W),F32),((R,W),F32),((16,128),F32),((24,3*W),F32),((24,W),F32),((24,4*W),F32),((96,W),F32)]
    return pl.pallas_call(backward_kernel,in_specs=[A]*16+[V]*2,out_specs=[A,A]+[V]*5,out_shape=[sds(*o) for o in outs],scratch_shapes=scr,
        compiler_params=pltpu.CompilerParams(collective_id=1,has_side_effects=True,vmem_limit_bytes=63<<20),name="backward")(
        w2,w1,wp,wq,pr,n1,n2,ctx,pj,hid,dg,st,mid,pt2,gt,cs,vec,meta)

def settle_back_kernel(groups,out_r,tok_r,sm,q_r,p_r,w1_r,w2_r,out_o,tok_o,q_o,p_o,w1_o,w2_o,v0,v1,v2,v3,v4,v5,v6,v7,v8,buf,sem):
    cps=[pltpu.make_async_copy(a,b,sem.at[i]) for i,(a,b) in enumerate(((out_r,buf),(q_r,q_o),(p_r,p_o),(w1_r,w1_o),(w2_r,w2_o)))]
    for cp in cps: cp.start()
    moved=groups[0]==1
    one=[pltpu.make_async_copy(tok_r,tok_o,sem.at[5])]
    three=[pltpu.make_async_copy(tok_r.at[pl.ds(a,n)],tok_o.at[pl.ds(b,n)],sem.at[6+i]) for i,(a,b,n) in enumerate(((0,0,392),(400,392,400),(392,792,8)))]
    @pl.when(moved)
    def _():
        for cp in three: cp.start()
    @pl.when(jnp.logical_not(moved))
    def _():
        for cp in one: cp.start()
    for i,v in enumerate((v0,v1,v2,v3,v4,v5,v6,v7,v8)):
        m=v.shape[0]
        v[...]=sm[i:i+1,0:m].reshape(m)
    cps[0].wait()
    out_o[0:384]=buf[0:384].astype(BF)
    a=buf[384:800]
    b=jnp.concatenate([buf[384:392],buf[400:800],buf[392:400]],axis=0)
    out_o[384:800]=jnp.where(moved,b,a).astype(BF)
    for cp in cps[1:]: cp.wait()
    @pl.when(moved)
    def _():
        for cp in three: cp.wait()
    @pl.when(jnp.logical_not(moved))
    def _():
        for cp in one: cp.wait()

def settle_back(groups,sizes,out,tok,sm,q,p,w1,w2):
    sds=jax.ShapeDtypeStruct
    V=pl.BlockSpec(memory_space=pltpu.VMEM); A=pl.BlockSpec(memory_space=pl.ANY); M=pl.BlockSpec(memory_space=pltpu.SMEM)
    return pl.pallas_call(settle_back_kernel,in_specs=[M,A,A,V,A,A,A,A],out_specs=[V]+[A]*5+[V]*len(sizes),
        out_shape=[sds(out.shape,BF)]+[sds(a.shape,F32) for a in (tok,q,p,w1,w2)]+[sds((m,),F32) for m in sizes],
        scratch_shapes=[pltpu.VMEM(out.shape,F32),pltpu.SemaphoreType.DMA((9,))],
        compiler_params=pltpu.CompilerParams(vmem_limit_bytes=60<<20),name="settle_back")(groups,out,tok,sm,q,p,w1,w2)

def normalize(values, gain, shift):
    center = values - jnp.mean(values, axis=-1, keepdims=True)
    spread = jnp.mean(center * center, axis=-1, keepdims=True)
    return center * lax.rsqrt(spread + eps_norm) * gain + shift

def activate(values):
    return jax.nn.gelu(values, approximate=False)

def segment_rows(groups, offsets, rows):
    lengths = jnp.where(groups == 0, P_SMALL, jnp.where(groups == 1, P_MID, P_LARGE)).astype(jnp.int32)
    positions = jnp.arange(rows, dtype=jnp.int32)
    inside = (positions[None, :] >= offsets[:, None]) & (positions[None, :] < offsets[:, None] + lengths[:, None])
    labels = jnp.arange(1, offsets.shape[0] + 1, dtype=jnp.int32)
    return jnp.sum(jnp.where(inside, labels[:, None], 0), axis=0) - 1

def settle(mid, rows):
    half = rows.shape[0] // 2
    cut = P_MID * (half // P_MID)
    gap = half - cut
    end = rows.shape[0] - gap
    moved = jnp.concatenate([rows[:cut], rows[end:], rows[cut:end]], axis=0)
    return jnp.where(mid, moved, rows)

def unsettle(mid, rows):
    half = rows.shape[0] // 2
    cut = P_MID * (half // P_MID)
    gap = half - cut
    moved = jnp.concatenate([rows[:cut], rows[half:], rows[cut:half]], axis=0)
    return jnp.where(mid, moved, rows)

def shards(n, tokens, mask_bits, groups, offsets, mask_token, ln1_gain, ln1_bias, w_qkv, b_qv, w_proj, b_proj,
           ln2_gain, ln2_bias, w_fc1, b_fc1, w_fc2, b_fc2, cotangent):
    vectors = (mask_token, ln1_gain, ln1_bias, b_qv, b_proj, ln2_gain, ln2_bias, b_fc1, b_fc2)
    sizes = [v.shape[0] for v in vectors]
    places = [sum(sizes[:i]) for i in range(len(sizes) + 1)]
    small_all = lax.all_gather(jnp.concatenate(vectors), "dp", axis=0, tiled=False)
    full_qkv, full_proj, full_fc1, full_fc2 = [
        lax.all_gather(w, "dp", axis=0, tiled=True) for w in (w_qkv, w_proj, w_fc1, w_fc2)]
    token_mask, gain_one, shift_one, bias_qv, bias_proj, gain_two, shift_two, bias_one, bias_two = [
        small_all[:, places[i]:places[i + 1]].reshape(-1).astype(F32) for i in range(len(sizes))]
    rows, width = tokens.shape
    half = rows // 2
    mid = groups[0] == 1
    tokens = settle(mid, tokens)
    cotangent = settle(mid, cotangent)
    mask_bits = settle(mid, mask_bits)
    segment = settle(mid, segment_rows(groups, offsets, rows))
    valid_col = (segment >= 0).astype(F32)[:, None]
    halves = segment.reshape(2, half)
    bias = jnp.where(halves[:, :, None] == halves[:, None, :], 0.0, -1e30).astype(F32)
    masked_rows = (mask_bits == 1)[:, None]
    start = jnp.where(masked_rows, token_mask[None, :], tokens.astype(F32))
    normed_one = normalize(start, gain_one, shift_one).astype(BF)
    full_bias = jnp.concatenate([bias_qv[:width], jnp.zeros((width,), F32), bias_qv[width:]])
    projected = (jnp.dot(normed_one, full_qkv, preferred_element_type=F32) + full_bias).astype(BF)
    context_low, probs = attn_fwd(projected, bias)
    middle = start + valid_col * (jnp.dot(context_low, full_proj, preferred_element_type=F32) + bias_proj)
    normed_two = normalize(middle, gain_two, shift_two).astype(BF)
    hidden_pre = jnp.dot(normed_two, full_fc1, preferred_element_type=F32) + bias_one
    hidden_low = activate(hidden_pre).astype(BF)
    result = middle + valid_col * (jnp.dot(hidden_low, full_fc2, preferred_element_type=F32) + bias_two)
    output = unsettle(mid, result.astype(BF))
    upstream = cotangent.astype(F32)
    grad_two = (valid_col * upstream).astype(BF)
    grad_wfc2 = tn(hidden_low, grad_two)
    grad_bfc2 = jnp.sum(grad_two.astype(F32), axis=0)
    grad_hidden = nt(grad_two, full_fc2)
    _, gelu_back = jax.vjp(activate, hidden_pre)
    grad_pre = gelu_back(grad_hidden)[0].astype(BF)
    grad_wfc1 = tn(normed_two, grad_pre)
    grad_bfc1 = jnp.sum(grad_pre.astype(F32), axis=0)
    grad_normed_two = nt(grad_pre, full_fc1)
    _, norm_back_two = jax.vjp(normalize, middle, gain_two, shift_two)
    grad_mid_part, grad_gain_two, grad_shift_two = norm_back_two(grad_normed_two)
    grad_middle = upstream + grad_mid_part
    grad_branch = (valid_col * grad_middle).astype(BF)
    grad_wproj = tn(context_low, grad_branch)
    grad_bproj = jnp.sum(grad_branch.astype(F32), axis=0)
    grad_context = nt(grad_branch, full_proj).astype(BF)
    dq, dk, dv = attn_bwd(projected, grad_context, context_low, probs)
    grad_projected = jnp.concatenate([dq, dk, dv], axis=1)
    grad_wqkv = tn(normed_one, grad_projected)
    grad_bqv = jnp.concatenate([jnp.sum(dq.astype(F32), axis=0), jnp.sum(dv.astype(F32), axis=0)])
    grad_normed_one = nt(grad_projected, full_qkv)
    _, norm_back_one = jax.vjp(normalize, start, gain_one, shift_one)
    grad_start_part, grad_gain_one, grad_shift_one = norm_back_one(grad_normed_one)
    grad_start = grad_middle + grad_start_part
    grad_token = jnp.sum(jnp.where(masked_rows, grad_start, 0.0), axis=0)
    grad_input = unsettle(mid, jnp.where(masked_rows, 0.0, grad_start))
    grad_vectors = (grad_token, grad_gain_one, grad_shift_one, grad_bqv, grad_bproj, grad_gain_two, grad_shift_two,
                    grad_bfc1, grad_bfc2)
    grad_small = jnp.concatenate([g.reshape(n, -1) for g in grad_vectors], axis=1)
    small_share = lax.psum_scatter(grad_small, "dp", scatter_dimension=0, tiled=False)
    share_qkv, share_proj, share_fc1, share_fc2 = [
        lax.psum_scatter(g, "dp", scatter_dimension=0, tiled=True)
        for g in (grad_wqkv, grad_wproj, grad_wfc1, grad_wfc2)]
    v = [small_share[places[i]:places[i + 1]] for i in range(len(sizes))]
    return (output, grad_input, v[0], v[1], v[2], share_qkv, v[3], share_proj, v[4], v[5], v[6], share_fc1, v[7],
            share_fc2, v[8])


def shards_fast(n, tokens, mask_bits, groups, offsets, mask_token, ln1_gain, ln1_bias, w_qkv, b_qv, w_proj, b_proj,
           ln2_gain, ln2_bias, w_fc1, b_fc1, w_fc2, b_fc2, cotangent):
    vectors = (mask_token, ln1_gain, ln1_bias, b_qv, b_proj, ln2_gain, ln2_bias, b_fc1, b_fc2)
    sizes = [v.shape[0] for v in vectors]
    (gq, gp, g1, g2, probs, normed_one, normed_two, context_low, projected, hidden_low, dgelu, start, middle, part2,
     grad_two, cots, vec, meta) = forward(groups, offsets, vectors, w_qkv, w_proj, w_fc1, w_fc2, tokens, cotangent, mask_bits)
    width = tokens.shape[1]
    shares = backward(
        g2.reshape(64, 48, width), g1, gp, gq, probs, normed_one, normed_two, context_low,
        projected, hidden_low, dgelu, start, middle, part2.reshape(4, 4, 2, 2, 48, width), grad_two, cots, vec, meta)
    output, grad_input, share_qkv, share_proj, share_fc1, share_fc2, *v = settle_back(groups, sizes, *shares)
    return (output, grad_input, v[0], v[1], v[2], share_qkv, v[3], share_proj, v[4], v[5], v[6], share_fc1, v[7],
            share_fc2, v[8])

def solution(mesh):
    row, flat = P("dp", None), P("dp")
    return jax.shard_map(
        functools.partial(shards_fast if mesh.shape["dp"] == 32 else shards, mesh.shape["dp"]),
        mesh=mesh,
        in_specs=(row, flat, flat, flat, flat, flat, flat, row, flat, row, flat, flat, flat, row, flat, row, flat, row),
        out_specs=(row, row, flat, flat, flat, row, flat, row, flat, flat, flat, row, flat, row, flat),
        check_vma=False,
    )
```

```python
import functools

import jax
import jax.numpy as jnp
from jax import lax
from jax.experimental import pallas as pl
from jax.experimental.pallas import tpu as pltpu
from jax.sharding import PartitionSpec as P

P_SMALL = 100
P_MID = 196
P_LARGE = 400
eps_norm = 1e-06

def nt(a,b): return lax.dot_general(a,b,(((1,),(1,)),((),())),preferred_element_type=jnp.float32)
def nn(a,b): return lax.dot_general(a,b,(((1,),(0,)),((),())),preferred_element_type=jnp.float32)
def tn(a,b): return lax.dot_general(a,b,(((0,),(0,)),((),())),preferred_element_type=jnp.float32)

def attn_fwd_kernel(bias_ref, q_ref, k_ref, v_ref, ctx_ref, p_ref):
    q=q_ref[...]; k=k_ref[...]; v=v_ref[...]
    rows,width=q.shape
    lane=lax.broadcasted_iota(jnp.int32,(rows,width),1)
    bias=bias_ref[0]
    outs=[]
    for j in range(2):
        mine=(lane>=64)==(j==1)
        qj=jnp.where(mine,q,jnp.zeros_like(q))
        s=nt(qj,k)*0.18033688011112042+bias
        m=jnp.max(s,axis=1,keepdims=True)
        e=jnp.exp2(s-m)
        l=jnp.sum(e,axis=1,keepdims=True)
        p=(e*(1.0/l)).astype(jnp.bfloat16)
        p_ref[0,0,j]=p
        outs.append(nn(p,v))
    ctx_ref[...]=jnp.where(lane<64,outs[0],outs[1]).astype(jnp.bfloat16)

def attn_fwd(proj,bias):
    rows=proj.shape[0]; half=rows//2; width=proj.shape[1]//3; pairs=width//128
    return pl.pallas_call(attn_fwd_kernel,grid=(2,pairs),
        in_specs=[pl.BlockSpec((1,half,half),lambda b,p:(b,0,0)),
                  pl.BlockSpec((half,128),lambda b,p:(b,p)),
                  pl.BlockSpec((half,128),lambda b,p:(b,p+pairs)),
                  pl.BlockSpec((half,128),lambda b,p:(b,p+2*pairs))],
        out_specs=[pl.BlockSpec((half,128),lambda b,p:(b,p)),
                   pl.BlockSpec((1,1,2,half,half),lambda b,p:(b,p,0,0,0))],
        out_shape=[jax.ShapeDtypeStruct((rows,width),jnp.bfloat16),
                   jax.ShapeDtypeStruct((2,pairs,2,half,half),jnp.bfloat16)],
        compiler_params=pltpu.CompilerParams(vmem_limit_bytes=40<<20),name="attn_fwd")(bias,proj,proj,proj)

def attn_bwd_kernel(q_ref,k_ref,v_ref,g_ref,c_ref,p_ref,dq_ref,dk_ref,dv_ref):
    q=q_ref[...]; k=k_ref[...]; v=v_ref[...]; g=g_ref[...]; c=c_ref[...]
    rows,width=q.shape
    lane=lax.broadcasted_iota(jnp.int32,(rows,width),1)
    gc=g.astype(jnp.float32)*c.astype(jnp.float32)
    dq=[];dk=[];dv=[]
    for j in range(2):
        mine=(lane>=64)==(j==1)
        zero=jnp.zeros_like(q)
        qj=jnp.where(mine,q,zero); gj=jnp.where(mine,g,zero)
        di=jnp.sum(jnp.where(mine,gc,0.0),axis=1,keepdims=True)
        p=p_ref[0,0,j]
        dp=nt(gj,v)
        ds=(p.astype(jnp.float32)*(dp-di)).astype(jnp.bfloat16)
        dq.append(nn(ds,k))
        dk.append(tn(ds,qj))
        dv.append(tn(p,gj))
    dq_ref[...]=(jnp.where(lane<64,dq[0],dq[1])*0.125).astype(jnp.bfloat16)
    dk_ref[...]=((dk[0]+dk[1])*0.125).astype(jnp.bfloat16)
    dv_ref[...]=(dv[0]+dv[1]).astype(jnp.bfloat16)

def attn_bwd(proj,gctx,ctx,p):
    rows=proj.shape[0]; half=rows//2; width=proj.shape[1]//3; pairs=width//128
    sp=lambda o: pl.BlockSpec((half,128),lambda b,p:(b,p+o*pairs))
    return pl.pallas_call(attn_bwd_kernel,grid=(2,pairs),
        in_specs=[sp(0),sp(1),sp(2),sp(0),sp(0),pl.BlockSpec((1,1,2,half,half),lambda b,p:(b,p,0,0,0))],
        out_specs=[sp(0)]*3,
        out_shape=[jax.ShapeDtypeStruct((rows,width),jnp.bfloat16)]*3,
        compiler_params=pltpu.CompilerParams(vmem_limit_bytes=40<<20),name="attn_bwd")(proj,proj,proj,gctx,ctx,p)
MESH=pl.DeviceIdType.MESH
F32=jnp.float32; BF=jnp.bfloat16

def place():
    me=lax.axis_index("dp")
    c=lax.rem(me,2); x=lax.rem(me//2,2); y=lax.rem(me//4,2); z=me//8
    return c,x,y,z
def dev(z,yx,c): return ((z*4+yx)*2+c,)

def greet():
    c,x,y,z=place(); yx=y*2+x
    bar=pltpu.get_barrier_semaphore()
    peers=[dev(z,yx,1-c),dev(z,y*2+1-x,c),dev(z,(1-y)*2+x,c)]+[dev(lax.rem(z+k,4),yx,c) for k in (1,2,3)]
    for p in peers: pl.semaphore_signal(bar,inc=1,device_id=p,device_id_type=MESH)
    pl.semaphore_wait(bar,len(peers))

class Gather:
    def __init__(self,view,ss,rs):
        self.view=view; self.ss=ss; self.rs=rs
        c,x,y,z=place()
        self.c=c; self.z=z; self.yx=y*2+x
        self.xn=y*2+1-x; self.yn=(1-y)*2+x; self.dg=(1-y)*2+1-x
        self.sends=[]
    def _cp(self,src,dst,slot,d):
        return pltpu.make_async_remote_copy(src_ref=src,dst_ref=dst,send_sem=self.ss.at[slot],recv_sem=self.rs.at[slot],device_id=d,device_id_type=MESH)
    def send(self,src,dst,slot,d):
        cp=self._cp(src,dst,slot,d); cp.start(); self.sends.append(cp)
    def got(self,dst,slot,d):
        self._cp(dst,dst,slot,d).wait_recv()
    def one(self,z): return self.view(pl.ds(z,1),self.yx,self.c)
    def z_send(self,src):
        for k in (1,2,3):
            self.send(src,self.one(self.z),k-1,dev(lax.rem(self.z+k,4),self.yx,self.c))
    def sib(self,ref,slot): self.send(ref,ref,slot,dev(self.z,self.yx,1-self.c))
    def z_recv(self):
        for k in (1,2,3):
            zz=lax.rem(self.z+4-k,4)
            self.got(self.one(zz),k-1,dev(zz,self.yx,self.c))
    def xy_send(self):
        r=self.view(pl.ds(0,4),self.yx,self.c)
        self.send(r,r,3,dev(self.z,self.xn,self.c))
        self.send(r,r,4,dev(self.z,self.yn,self.c))
        for k in (1,2,3): self.sib(self.one(lax.rem(self.z+4-k,4)),6+k)
    def xy_recv(self):
        rx=self.view(pl.ds(0,4),self.xn,self.c)
        self.got(rx,3,dev(self.z,self.xn,self.c))
        h=self.view(pl.ds(0,2),self.xn,self.c)
        self.send(h,h,5,dev(self.z,self.yn,self.c))
        ry=self.view(pl.ds(0,4),self.yn,self.c)
        self.got(ry,4,dev(self.z,self.yn,self.c))
        h=self.view(pl.ds(2,2),self.yn,self.c)
        self.send(h,h,6,dev(self.z,self.xn,self.c))
        self.sib(rx,10); self.sib(ry,11)
    def diag_recv(self):
        a=self.view(pl.ds(0,2),self.dg,self.c)
        self.got(a,5,dev(self.z,self.yn,self.c))
        self.sib(a,12)
        b=self.view(pl.ds(2,2),self.dg,self.c)
        self.got(b,6,dev(self.z,self.xn,self.c))
        self.sib(b,13)
    def finish(self):
        o=1-self.c; s=dev(self.z,self.yx,o)
        for k in (1,2,3): self.got(self.view(pl.ds(lax.rem(self.z+4-k,4),1),self.yx,o),6+k,s)
        self.got(self.view(pl.ds(0,4),self.xn,o),10,s)
        self.got(self.view(pl.ds(0,4),self.yn,o),11,s)
        self.got(self.view(pl.ds(0,2),self.dg,o),12,s)
        self.got(self.view(pl.ds(2,2),self.dg,o),13,s)
    def drain(self):
        for cp in self.sends: cp.wait_send()

def cols_view(ref):
    half=ref.shape[-1]//2
    def view(zs,yx,lane): return ref.at[zs,yx,:,pl.ds(pl.multiple_of(lane*half,128),half)]
    return view
def rows_view(ref):
    def view(zs,yx,lane): return ref.at[zs,yx,lane]
    return view

def join(c,own,sib):
    a=own.astype(F32); b=sib.astype(F32)
    return jnp.concatenate([jnp.where(c==0,a,b),jnp.where(c==0,b,a)],axis=0).astype(BF)

def gather_kernel(sm_ref,q_ref,p_ref,f1_ref,f2_ref,gs_ref,gq_ref,gp_ref,g1_ref,g2_ref,
        sq,sp,s1,bq,bp,b1,ss0,rs0,ssl,ss,rs):
    greet()
    c,x,y,z=place(); yx=y*2+x
    sibd=dev(z,yx,1-c)
    first=[]
    def swap(src,dst,i):
        cp=pltpu.make_async_remote_copy(src_ref=src,dst_ref=dst,send_sem=ss0.at[i],recv_sem=rs0.at[i],device_id=sibd,device_id_type=MESH)
        cp.start(); first.append(cp)
    swap(sm_ref,gs_ref.at[z,yx,c],0)
    swap(q_ref,sq,1); swap(p_ref,sp,2); swap(f1_ref,s1,3)
    swap(f2_ref,g2_ref.at[z,yx,c],4)
    gs=[Gather(rows_view(gs_ref),ss.at[0],rs.at[0]),Gather(cols_view(gq_ref),ss.at[1],rs.at[1]),Gather(cols_view(gp_ref),ss.at[2],rs.at[2]),
        Gather(cols_view(g1_ref),ss.at[3],rs.at[3]),Gather(rows_view(g2_ref),ss.at[4],rs.at[4])]
    local=[]
    def keep(src,dst,i):
        cp=pltpu.make_async_copy(src,dst,ssl.at[i]); cp.start(); local.append(cp)
    def half(b):
        h=b.shape[-1]//2
        return b.at[:,:,pl.ds(pl.multiple_of(c*h,128),h)]
    keep(sm_ref,gs_ref.at[z,yx,c],0)
    keep(f2_ref,g2_ref.at[z,yx,c],4)
    def begin(i):
        if i==0:
            local[0].wait(); gs[0].z_send(gs[0].one(z))
        elif i==4:
            local[1].wait(); gs[4].z_send(gs[4].one(z))
        else:
            own,sib,buf,dst={1:(q_ref,sq,bq,gq_ref),2:(p_ref,sp,bp,gp_ref),3:(f1_ref,s1,b1,g1_ref)}[i]
            first[i].wait_recv()
            buf[0]=join(c,own[...],sib[...])
            keep(buf,dst.at[pl.ds(z,1),yx],i)
            gs[i].z_send(half(buf))
    begin(0); begin(1)
    gs[0].z_recv(); gs[0].xy_send()
    begin(2)
    gs[1].z_recv(); local[2].wait(); gs[1].xy_send()
    begin(3)
    gs[0].xy_recv()
    gs[2].z_recv(); local[3].wait(); gs[2].xy_send()
    gs[0].diag_recv()
    gs[1].xy_recv()
    begin(4)
    gs[3].z_recv(); local[4].wait(); gs[3].xy_send()
    gs[2].xy_recv()
    gs[1].diag_recv()
    gs[2].diag_recv()
    gs[4].z_recv(); gs[4].xy_send()
    gs[3].xy_recv()
    gs[3].diag_recv()
    gs[4].xy_recv()
    gs[4].diag_recv()
    first[0].wait_recv(); first[4].wait_recv()
    for g in gs: g.finish()
    for cp in first: cp.wait_send()
    for g in gs: g.drain()

def gather_all(small,wq,wp,w1,w2):
    sds=jax.ShapeDtypeStruct
    nq,np_,n1,n2=wq.shape[1],wp.shape[1],w1.shape[1],w2.shape[1]
    r=wq.shape[0]; r2=w2.shape[0]
    V=pl.BlockSpec(memory_space=pltpu.VMEM); A=pl.BlockSpec(memory_space=pl.ANY)
    D=pltpu.SemaphoreType.DMA
    return pl.pallas_call(gather_kernel,
        in_specs=[V]*5,out_specs=[A]*5,
        out_shape=[sds((4,4,2)+small.shape,BF),sds((4,4,2*r,nq),BF),sds((4,4,2*r,np_),BF),sds((4,4,2*r,n1),BF),sds((4,4,2,r2,n2),BF)],
        scratch_shapes=[pltpu.VMEM((r,n),BF) for n in (nq,np_,n1)]+[pltpu.VMEM((1,2*r,n),BF) for n in (nq,np_,n1)]+
            [D((5,)),D((5,)),D((5,)),D((5,14)),D((5,14))],
        compiler_params=pltpu.CompilerParams(collective_id=0,has_side_effects=True,vmem_limit_bytes=16<<20),name="gather_all")(small,wq,wp,w1,w2)

class Scatter:
    def __init__(self,view,a,s,rxa,ryb,rx,ry,b,rz,ss,rs,ls):
        self.view=view; self.a=a; self.s=s; self.rxa=rxa; self.ryb=ryb; self.rx=rx; self.ry=ry; self.b=b; self.rz=rz
        self.ss=ss; self.rs=rs; self.ls=ls
        c,x,y,z=place()
        self.c=c; self.z=z; self.yx=y*2+x
        self.xn=y*2+1-x; self.yn=(1-y)*2+x; self.dg=(1-y)*2+1-x
        self.cps={}
    def send(self,src,dst,slot,d):
        cp=pltpu.make_async_remote_copy(src_ref=src,dst_ref=dst,send_sem=self.ss.at[slot],recv_sem=self.rs.at[slot],device_id=d,device_id_type=MESH)
        cp.start(); self.cps[slot]=cp
    def r0(self):
        self.send(self.view(1-self.c),self.s,0,dev(self.z,self.yx,1-self.c))
        self.loc=pltpu.make_async_copy(self.view(self.c),self.a,self.ls); self.loc.start()
    def r1(self):
        self.loc.wait(); self.cps[0].wait_recv()
        a,s=self.a,self.s
        def add(yx):
            def body(i,_):
                a[i,yx]=(a[i,yx].astype(F32)+s[i,yx].astype(F32)).astype(a.dtype)
                return 0
            lax.fori_loop(0,4,body,0)
        xd=dev(self.z,self.xn,self.c); yd=dev(self.z,self.yn,self.c)
        add(self.dg)
        self.send(a.at[pl.ds(0,2),self.dg],self.rxa,1,xd)
        self.send(a.at[pl.ds(2,2),self.dg],self.ryb,2,yd)
        add(self.xn)
        self.send(a.at[pl.ds(0,2),self.xn],self.rx.at[pl.ds(0,2)],3,xd)
        add(self.yn)
        self.send(a.at[pl.ds(2,2),self.yn],self.ry.at[pl.ds(2,2)],4,yd)
        add(self.yx)
    def r2(self):
        a=self.a
        xd=dev(self.z,self.xn,self.c); yd=dev(self.z,self.yn,self.c)
        self.cps[1].wait_recv()
        def body(i,_):
            a[i,self.yn]=(a[i,self.yn].astype(F32)+self.rxa[i].astype(F32)).astype(a.dtype)
            return 0
        lax.fori_loop(0,2,body,0)
        self.send(a.at[pl.ds(0,2),self.yn],self.ry.at[pl.ds(0,2)],6,yd)
        self.cps[2].wait_recv()
        def body(i,_):
            a[i+2,self.xn]=(a[i+2,self.xn].astype(F32)+self.ryb[i].astype(F32)).astype(a.dtype)
            return 0
        lax.fori_loop(0,2,body,0)
        self.send(a.at[pl.ds(2,2),self.xn],self.rx.at[pl.ds(2,2)],5,xd)
    def r3(self):
        for s in (3,4,5,6): self.cps[s].wait_recv()
        def body(i,_):
            self.b[i]=(self.a[i,self.yx].astype(F32)+self.rx[i].astype(F32)+self.ry[i].astype(F32)).astype(self.b.dtype)
            return 0
        lax.fori_loop(0,4,body,0)
        for k in (1,2,3):
            zz=lax.rem(self.z+k,4)
            self.send(self.b.at[zz],self.rz.at[k-1],6+k,dev(zz,self.yx,self.c))
    def r4(self):
        t=self.b[self.z].astype(F32)
        for k in (1,2,3):
            self.cps[6+k].wait_recv()
            t=t+self.rz[k-1].astype(F32)
        return t
    def drain(self):
        for cp in self.cps.values(): cp.wait_send()

def scatter_scratch(r,n,dt):
    V=pltpu.VMEM
    return [V((4,4,r,n),dt),V((4,4,r,n),dt),V((2,r,n),dt),V((2,r,n),dt),V((4,r,n),dt),V((4,r,n),dt),V((4,r,n),dt),V((3,r,n),dt)]

def scatter_kernel(sm_ref,q_ref,p_ref,f1_ref,f2_ref,os_ref,oq_ref,op_ref,o1_ref,o2_ref,*sc):
    bufs=[sc[8*i:8*i+8] for i in range(5)]
    fin=sc[40:46]; ss,rs,ls,fs,fr=sc[46:]
    greet()
    c,x,y,z=place(); yx=y*2+x
    def cv(ref):
        h=ref.shape[-1]//2
        return lambda lane: ref.at[:,:,:,pl.ds(pl.multiple_of(lane*h,128),h)]
    def rv(ref): return lambda lane: ref.at[:,:,lane]
    refs=[sm_ref,q_ref,p_ref,f1_ref,f2_ref]
    S=[Scatter((rv if i in (0,4) else cv)(refs[i]),*bufs[i],ss.at[i],rs.at[i],ls.at[i]) for i in range(5)]
    order=[4,3,2,1,0]
    sibd=dev(z,yx,1-c)
    ends=[]
    outs={1:oq_ref,2:op_ref,3:o1_ref}
    def end(i):
        t=S[i].r4()
        if i==0: os_ref[...]=t
        elif i==4: o2_ref[...]=t
        else:
            f,rf=fin[2*(i-1)],fin[2*(i-1)+1]
            r=t.shape[0]//2
            f[0]=t[:r]; f[1]=t[r:]
            cp=pltpu.make_async_remote_copy(src_ref=f.at[1-c],dst_ref=rf,send_sem=fs.at[i],recv_sem=fr.at[i],device_id=sibd,device_id_type=MESH)
            cp.start(); ends.append((i,cp))
    def close():
        for i,cp in ends:
            cp.wait_recv()
            f,rf=fin[2*(i-1)],fin[2*(i-1)+1]
            own=f[c]; oth=rf[...]
            o=outs[i]; h=own.shape[-1]
            o[:,:h]=jnp.where(c==0,own,oth); o[:,h:]=jnp.where(c==0,oth,own)
            cp.wait_send()
    for i in order: S[i].r0()
    n=len(order)
    stages=[lambda i:S[i].r1(),lambda i:S[i].r2(),lambda i:S[i].r3(),lambda i:end(i)]
    for t in range(n+3):
        for s in range(3,-1,-1):
            k=t-s
            if 0<=k<n: stages[s](order[k])
    close()
    for s in S: s.drain()

def scatter_all(sm,q,p,f1,f2):
    sds=jax.ShapeDtypeStruct
    V=pl.BlockSpec(memory_space=pltpu.VMEM); A=pl.BlockSpec(memory_space=pl.ANY)
    D=pltpu.SemaphoreType.DMA
    sc=[]
    for a,dt in ((sm,F32),(q,BF),(p,BF),(f1,BF),(f2,BF)):
        if a.ndim==5: sc+=scatter_scratch(a.shape[3],a.shape[4],dt)
        else: sc+=scatter_scratch(a.shape[2],a.shape[3]//2,dt)
    outs=[sds(sm.shape[3:],F32)]
    for a in (q,p,f1):
        r,n=a.shape[2]//2,a.shape[3]
        sc+=[pltpu.VMEM((2,r,n//2),F32),pltpu.VMEM((r,n//2),F32)]
        outs.append(sds((r,n),F32))
    outs.append(sds(f2.shape[3:],F32))
    return pl.pallas_call(scatter_kernel,in_specs=[A]*5,out_specs=[V]*5,out_shape=outs,
        scratch_shapes=sc+[D((5,10)),D((5,10)),D((5,)),D((5,)),D((5,))],
        compiler_params=pltpu.CompilerParams(collective_id=1,has_side_effects=True,vmem_limit_bytes=56<<20),name="scatter_all")(sm,q,p,f1,f2)
class Gather2:
    def __init__(self,view,ss,rs):
        self.view=view; self.ss=ss; self.rs=rs
        c,x,y,z=place()
        self.c=c; self.z=z; self.yx=y*2+x
        self.xn=y*2+1-x; self.yn=(1-y)*2+x; self.dg=(1-y)*2+1-x
        self.xd=dev(z,self.xn,c); self.yd=dev(z,self.yn,c); self.sd=dev(z,self.yx,1-c)
        self.sends=[]
    def at(self,k,yx,lane=None): return self.view(pl.ds(lax.rem(self.z+4-k,4),1),yx,self.c if lane is None else lane)
    def all(self,yx,lane=None): return self.view(pl.ds(0,4),yx,self.c if lane is None else lane)
    def _cp(self,src,dst,slot,d):
        return pltpu.make_async_remote_copy(src_ref=src,dst_ref=dst,send_sem=self.ss.at[slot],recv_sem=self.rs.at[slot],device_id=d,device_id_type=MESH)
    def send(self,src,dst,slot,d):
        cp=self._cp(src,dst,slot,d); cp.start(); self.sends.append(cp)
    def got(self,dst,slot,d): self._cp(dst,dst,slot,d).wait_recv()
    def near(self,src):
        self.send(src,self.at(0,self.yx),3,self.xd)
        self.send(src,self.at(0,self.yx),7,self.yd)
    def far(self,src):
        for k in (1,2,3): self.send(src,self.at(0,self.yx),k-1,dev(lax.rem(self.z+k,4),self.yx,self.c))
    def X0(self):
        r=self.at(0,self.xn); self.got(r,3,self.xd)
        self.send(r,r,11,self.yd)
        self.got(self.at(0,self.yn),7,self.yd)
    def Z(self,k):
        r=self.at(k,self.yx)
        self.got(r,k-1,dev(lax.rem(self.z+4-k,4),self.yx,self.c))
        self.send(r,r,3+k,self.xd); self.send(r,r,7+k,self.yd); self.send(r,r,14+k,self.sd)
    def X(self,k):
        a=self.at(k,self.xn); b=self.at(k,self.yn)
        self.got(a,3+k,self.xd)
        if k==1: self.send(a,a,11+k,self.yd)
        self.got(b,7+k,self.yd)
        if k!=1: self.send(b,b,11+k,self.xd)
        if k==2:
            for yx,s in ((self.xn,18),(self.yn,19)):
                r=self.all(yx); self.send(r,r,s,self.sd)
    def D(self):
        for k in (0,1,3,2):
            self.got(self.at(k,self.dg),11+k,self.yd if k<2 else self.xd)
        r=self.all(self.dg); self.send(r,r,20,self.sd)
    def F(self):
        o=1-self.c
        for k in (1,2,3): self.got(self.at(k,self.yx,o),14+k,self.sd)
        for yx,s in ((self.xn,18),(self.yn,19),(self.dg,20)): self.got(self.all(yx,o),s,self.sd)
    def drain(self):
        for cp in self.sends: cp.wait_send()

def gelu_parts(x):
    cdf=0.5+0.5*lax.erf(x*0.7071067811865476)
    e=jnp.exp2(x*x*(-0.5*1.4426950408889634))
    return x*cdf, cdf+x*e*0.3989422804014327

def row_stats(x):
    inv=1.0/x.shape[1]
    mean=jnp.sum(x,axis=1,keepdims=True)*inv
    c=x-mean
    var=jnp.sum(c*c,axis=1,keepdims=True)*inv
    return c,lax.rsqrt(var+eps_norm)

def by_sixteen(first,last,rows):
    step=next(k for k in (200,160,80) if k%16==0 and (last-first)%k==0)
    def body(i,_):
        for u in range(step//16): rows(pl.ds(pl.multiple_of(first+i*step+16*u,16),16))
        return 0
    lax.fori_loop(0,(last-first)//step,body,0)

def spread(each,total,cols):
    j=lax.broadcasted_iota(jnp.int32,(128,total),1); l=lax.broadcasted_iota(jnp.int32,(128,total),0)
    return jnp.where(j-cols*each==l,1.0,0.0).astype(BF)

def over(each,shape):
    j=lax.broadcasted_iota(jnp.int32,shape,1)
    return (j*((1<<22)//each+1))>>22

def settled(g1,r):
    return r+jnp.where(r>=400,-8*g1,jnp.where(r>=392,400*g1,0))

def segments(groups,offsets,pos):
    g=groups[0]
    length=jnp.where(g==0,P_SMALL,jnp.where(g==1,P_MID,P_LARGE))
    seg=jnp.full(pos.shape,-1,jnp.int32)
    for s in range(8):
        o=offsets[s]
        seg=jnp.where((pos>=o)&(pos<o+length),s,seg)
    return seg

def settle_rows(g1,read,write):
    def either(a,b): return [jnp.where(g1==1,u,w) for u,w in zip(a,b)]
    def body(i,_):
        r=pl.multiple_of(i*56,8)
        write(r,56,read(r,56)); return 0
    lax.fori_loop(0,7,body,0)
    write(392,8,either(read(792,8),read(392,8)))
    def body2(i,_):
        r=pl.multiple_of(400+i*40,8)
        write(r,40,either(read(pl.multiple_of(392+i*40,8),40),read(r,40))); return 0
    lax.fori_loop(0,10,body2,0)

FORWARD_ORDER=(
    96, 0, 1, 16, 32, 48, 17, 97, 200, 80, 4, 201, 98, 3, 21, 49, 5, 64, 33, 65, 99, 6, 50, 100, 2, 8, 7, 53, 20,
    81, 202, 51, 19, 203, 24, 37, 52, 9, 35, 204, 54, 36, 56, 34, 22, 40, 18, 55, 23, 10, 220, 230, 38, 39, 69,
    25, 231, 41, 26, 67, 68, 221, 72, 42, 66, 57, 232, 233, 222, 70, 71, 234, 85, 58, 83, 235, 84, 82, 73, 205,
    74, 240, 88, 241, 86, 242, 243, 87, 244, 245, 250, 251, 89, 252, 253, 90,
)

def forward_kernel(groups,offsets,v0,v1,v2,v3,v4,v5,v6,v7,v8,q_ref,p_ref,f1_ref,f2_ref,tok_r,cot_r,mask_ref,
        wq_o,wp_o,w1_o,w2_o,pr_o,n1_o,n2_o,ctx_o,pj_o,hid_o,dg_o,xa_o,xb_o,mid_o,pt2_o,gt_o,cs_o,vec_o,meta_o,
        gs,gq,gp,g1w,sq,sp,s1,bq,bp,b1,raw,mid,st,xa,xb,n1,nt_,pj,bias,ctx,n2,hid,dg,gt,cs,pt2,pst,sc,sm_ref,smf,mk,tok_ref,cot_ref,bqv,bf1,
        ss0,rs0,ssl,sss,srs,ss,rs,psem,osem,lsem):
    loads=[pltpu.make_async_copy(a,b,lsem.at[i]) for i,(a,b) in enumerate(((tok_r,tok_ref),(cot_r,cot_ref)))]
    for cp in loads: cp.start()
    smf[...]=jnp.zeros_like(smf)
    for i,r in enumerate((v0,v1,v2,v3,v4,v5,v6,v7,v8)):
        m=r.shape[0]
        smf[i:i+1,0:m]=r[...].astype(F32).reshape(1,m)
    sm_ref[...]=smf[...].astype(BF)
    greet()
    c,x,y,z=place(); yx=y*2+x
    sibd=dev(z,yx,1-c)
    first=[]
    def swap(src,dst,i):
        cp=pltpu.make_async_remote_copy(src_ref=src,dst_ref=dst,send_sem=ss0.at[i],recv_sem=rs0.at[i],device_id=sibd,device_id_type=MESH)
        cp.start(); first.append(cp)
    swap(sm_ref,gs.at[z,yx,c],0)
    swap(q_ref,sq,1); swap(p_ref,sp,2); swap(f1_ref,s1,3)
    swap(f2_ref,w2_o.at[z,yx,c],4)
    gs[z,yx,c]=sm_ref[...]
    own2=pltpu.make_async_copy(f2_ref,w2_o.at[z,yx,c],ssl.at[0]); own2.start()
    S=Gather(rows_view(gs),sss,srs)
    QA,QB,QC,Pj,F1=[Gather2(cols_view(r),ss.at[i],rs.at[i]) for i,r in enumerate((gq.at[0],gq.at[1],gq.at[2],gp,g1w))]
    F2=Gather2(rows_view(w2_o),ss.at[5],rs.at[5])
    outs=[]; lag=[]; used=[0]
    def put(src,dst):
        cp=pltpu.make_async_copy(src,dst,osem.at[used[0]]); cp.start(); outs.append(cp); used[0]+=1
    waited=set()
    def swapped(i):
        if i not in waited: waited.add(i); first[i].wait_recv()
    def build(own,sib,buf,dst):
        j=join(c,own,sib)
        buf[0]=j; dst[z,yx]=j
    def parts(ref,g): return jnp.concatenate([ref[:,o+256*g:o+256*g+256] for o in (0,768,1536)],axis=1)
    def half(b):
        h=b.shape[-1]//2
        return b.at[:,:,pl.ds(pl.multiple_of(c*h,128),h)]
    def near(n):
        if n=="F2": own2.wait(); F2.near(F2.at(0,yx)); return
        if n[0]=="Q":
            g="ABC".index(n[1]); swapped(1); build(parts(q_ref,g),parts(sq,g),bq.at[g],gq.at[g]); G[n].near(half(bq.at[g]))
        elif n=="P": swapped(2); build(p_ref[...],sp[...],bp,gp); Pj.near(half(bp))
        else: swapped(3); build(f1_ref[...],s1[...],b1,g1w); F1.near(half(b1))
    def far(n):
        if n=="F2": F2.far(F2.at(0,yx))
        elif n[0]=="Q": G[n].far(half(bq.at["ABC".index(n[1])]))
        else: G[n].far(half(bp if n=="P" else b1))
    G={"QA":QA,"QB":QB,"QC":QC,"P":Pj,"F1":F1,"F2":F2}
    def finish(n):
        if n=="F2": first[4].wait_recv()
        G[n].F()
        if n[0]=="Q": g="ABC".index(n[1]); put(gq.at[g],wq_o.at[g])
        elif n=="P": put(gp,wp_o)
        elif n=="F1": put(g1w,w1_o)
    def small(k):
        if k=="s": S.z_send(S.one(z))
        elif k=="Z": S.z_recv(); S.xy_send()
        elif k=="X": S.xy_recv()
        elif k=="D": S.diag_recv()
        else: first[0].wait_recv(); S.finish()
    g1=jnp.where(groups[0]==1,1,0)
    def setup(k):
        if k==0:
            loads[0].wait()
            raw[...]=tok_ref[...].astype(F32)
        segc=segments(groups,offsets,settled(g1,lax.broadcasted_iota(jnp.int32,(400,1),0)+400*k))
        meta_o[400*k:400*k+400,0:1]=jnp.where(segc>=0,1.0,0.0)
        segr=segments(groups,offsets,settled(g1,lax.broadcasted_iota(jnp.int32,(1,400),1)+400*k))
        bias[k]=jnp.where(segc==segr,0.0,-1e30)
    def vectors():
        X=gs[...].reshape(512,128)
        E=nn(X,spread(24,768,over(24,(128,768))))
        E=jnp.where(lax.broadcasted_iota(jnp.int32,(512,768),0)>>4==over(24,(512,768)),E,0.0).reshape(32,16,768)
        vec_o[...]=jnp.sum(E,axis=0)
        def wide(row,each,total):
            sel=jnp.where(lax.broadcasted_iota(jnp.int32,(32,512),1)==lax.broadcasted_iota(jnp.int32,(32,512),0)*16+row,1.0,0.0).astype(BF)
            e=nn(nn(sel,X).astype(BF),spread(each,total,over(each,(128,total))))
            e=jnp.where(lax.broadcasted_iota(jnp.int32,(32,total),0)==over(each,(32,total)),e,0.0)
            return jnp.sum(e,axis=0,keepdims=True)
        bqv[...]=wide(3,48,1536); bf1[...]=wide(7,96,3072)
    def norm_one():
        mask=jnp.broadcast_to(mask_ref[...].astype(F32).reshape(1,800),(8,800)).T
        mk[...]=mask[:,0:1]
        def write(r,n,v):
            t,m=v
            meta_o[pl.ds(r,n),1:2]=m
            mid[pl.ds(r,n),:]=jnp.where(m>0.0,vec_o[0:1,:],t)
        settle_rows(g1,lambda r,n:(raw[pl.ds(r,n),:],mk[pl.ds(r,n),:]),write)
        def rows(r):
            s=mid[r,:]
            st[r,:]=s.astype(BF)
            cc,rstd=row_stats(s)
            xh=cc*rstd
            xa[r,:]=xh.astype(BF); meta_o[r,2:3]=rstd
            n1[r,:]=(xh*vec_o[1:2,:]+vec_o[2:3,:]).astype(BF)
        by_sixteen(0,800,rows)
        put(xa,xa_o)
    def cotangents():
        loads[1].wait()
        raw[...]=cot_ref[...].astype(F32)
        def write2(r,n,v): mid[pl.ds(r,n),:]=v[0]
        settle_rows(g1,lambda r,n:(raw[pl.ds(r,n),:],),write2)
        def body(i,_):
            r=pl.ds(pl.multiple_of(i*80,16),80)
            v=mid[r,:]
            cs[r,:]=v.astype(BF); gt[r,:]=(v*meta_o[r,0:1]).astype(BF)
            return 0
        lax.fori_loop(0,10,body,0)
        put(cs,cs_o); put(gt,gt_o)
        nt_[...]=n1[...].T
        put(nt_,n1_o)
        lag.append(outs[-1])
    def qkv(g):
        r=nn(n1[...],gq[g].reshape(768,768))
        for k,o in enumerate((0,768,1536)):
            t=r[:,256*k:256*k+256]
            if k!=1: t=t+bqv[:,384*k+256*g:384*k+256*g+256]
            pj[:,o+256*g:o+256*g+256]=t.astype(BF)
        if g==2: put(pj,pj_o)
    lane=lax.broadcasted_iota(jnp.int32,(400,128),1)
    def where_of(t):
        return lax.rem(t,4)//2,2*(t//4)+lax.rem(t,2)
    def pcopy(t):
        b,p=where_of(t)
        return pltpu.make_async_copy(pst.at[lax.rem(t,2)],pr_o.at[b*6+p],psem.at[lax.rem(t,2)])
    def attend(t,_):
        b,p=where_of(t); s=lax.rem(t,2)
        r=pl.ds(pl.multiple_of(b*400,16),400)
        cc=lambda o: pl.ds(pl.multiple_of(o+p*128,128),128)
        @pl.when(t>=2)
        def _(): pcopy(t-2).wait()
        q=pj[r,cc(0)]; k=pj[r,cc(768)]; v=pj[r,cc(1536)]
        res=[]
        for j in range(2):
            qj=jnp.where((lane>=64)==(j==1),q,jnp.zeros_like(q))
            sc[j]=nt(qj,k)
        for j in range(2):
            for i in range(10):
                u=slice(40*i,40*i+40)
                t_=sc[j,u]*0.18033688011112042+bias[b,u]
                e=jnp.exp2(t_-jnp.max(t_,axis=1,keepdims=True))
                sc[j,u]=e*(1.0/jnp.sum(e,axis=1,keepdims=True))
        for j in range(2):
            pr=sc[j].astype(BF)
            pst[s,j]=pr
            res.append(nn(pr,v))
        ctx[r,cc(0)]=jnp.where(lane<64,res[0],res[1]).astype(BF)
        pcopy(t).start()
        return 0
    def proj():
        put(ctx,ctx_o)
        wpv=gp[...].reshape(768,768)
        def body(i,_):
            r=pl.ds(pl.multiple_of(i*400,16),400)
            mid[r,:]=st[r,:].astype(F32)+meta_o[r,0:1]*(nn(ctx[r,:],wpv)+vec_o[4:5,:])
            return 0
        lax.fori_loop(0,2,body,0)
        def rows(r):
            cc,rstd=row_stats(mid[r,:])
            xh=cc*rstd
            xb[r,:]=xh.astype(BF); meta_o[r,3:4]=rstd
            n2[r,:]=(xh*vec_o[5:6,:]+vec_o[6:7,:]).astype(BF)
        by_sixteen(0,800,rows)
        put(mid,mid_o); put(xb,xb_o)
        lag[0].wait(); outs[:]=[o for o in outs if o is not lag[0]]
        nt_[...]=n2[...].T
        put(nt_,n2_o)
    def mlp(i,_):
        cc=pl.ds(pl.multiple_of(i*512,128),512)
        a,d=gelu_parts(nn(n2[...],g1w[:,:,:,cc].reshape(768,512))+bf1[:,cc])
        hid[:,cc]=a.astype(BF); dg[:,cc]=d.astype(BF)
        return 0
    def grads(i,_):
        cc=pl.ds(pl.multiple_of(i*768,128),768)
        pt2[i]=tn(hid[:,cc],gt[...]).astype(BF).reshape(4,2,96,768)
        return 0
    chunks=("QA","QB","QC","P","F1","F2")
    k=0
    while k<len(FORWARD_ORDER):
        op=FORWARD_ORDER[k]; k+=1
        if op>=96 and op<200: small("sZXDF"[op-96])
        elif op<96:
            n=chunks[op//16]; g=G[n]; t=op%16
            if t==0: near(n)
            elif t==1: far(n)
            elif t==2: g.X0()
            elif t<6: g.Z(t-2)
            elif t<9: g.X(t-5)
            elif t==9: g.D()
            else: finish(n)
        elif op<220: (lambda:setup(0),lambda:setup(1),vectors,norm_one,cotangents,proj)[op-200]()
        elif op<230: qkv(op-220)
        else:
            a=b=op%10
            while k<len(FORWARD_ORDER) and FORWARD_ORDER[k]==op-a+b+1: b+=1; k+=1
            if op>=250:
                lax.fori_loop(a,b+1,grads,0)
                put(pt2.at[pl.ds(a,b+1-a)],pt2_o.at[pl.ds(a,b+1-a)])
            elif op<240: lax.fori_loop(2*a,2*b+2,attend,0)
            else:
                lax.fori_loop(a,b+1,mlp,0)
                if b==5:
                    put(hid,hid_o); put(dg,dg_o)
    pcopy(10).wait(); pcopy(11).wait()
    for cp in outs: cp.wait()
    for cp in first: cp.wait_send()
    for g in [S]+list(G.values()): g.drain()

def forward(groups,offsets,vectors,wq,wp,w1,w2,tok,cot,mask):
    sds=jax.ShapeDtypeStruct
    V=pl.BlockSpec(memory_space=pltpu.VMEM); A=pl.BlockSpec(memory_space=pl.ANY); M=pl.BlockSpec(memory_space=pltpu.SMEM)
    D=pltpu.SemaphoreType.DMA
    v=pltpu.VMEM
    R,W=tok.shape
    outs=[((3,4,4,48,768),BF),((4,4,48,768),BF),((4,4,48,3072),BF),((4,4,2,96,768),BF),((12,2,400,400),BF),
        ((W,R),BF),((W,R),BF),((R,W),BF),((R,3*W),BF),((R,4*W),BF),((R,4*W),BF),((R,W),BF),((R,W),BF),((R,W),F32),((4,4,2,96,768),BF),((R,W),BF),((R,W),BF),
        ((16,W),F32),((R,4),F32)]
    return pl.pallas_call(forward_kernel,
        in_specs=[M,M]+[V]*13+[A,A,V],out_specs=[A]*17+[V,V],out_shape=[sds(*o) for o in outs],
        scratch_shapes=[v((4,4,2,16,128),BF),v((3,4,4,48,768),BF),v((4,4,48,768),BF),v((4,4,48,3072),BF),
            v((24,2304),BF),v((24,768),BF),v((24,3072),BF),v((3,1,48,768),BF),v((1,48,768),BF),v((1,48,3072),BF),
            v((R,W),F32),v((R,W),F32),v((R,W),BF),v((R,W),BF),v((R,W),BF),v((R,W),BF),v((W,R),BF),v((R,3*W),BF),v((2,400,400),F32),v((R,W),BF),v((R,W),BF),
            v((R,4*W),BF),v((R,4*W),BF),v((R,W),BF),v((R,W),BF),v((4,4,2,96,768),BF),v((2,2,400,400),BF),v((2,400,400),F32),v((16,128),BF),v((16,128),F32),v((800,1),F32),v((R,W),BF),v((R,W),BF),v((1,2*W),F32),v((1,4*W),F32),
            D((5,)),D((5,)),D((1,)),D((14,)),D((14,)),D((6,21)),D((6,21)),D((2,)),D((24,)),D((2,))],
        compiler_params=pltpu.CompilerParams(collective_id=0,has_side_effects=True,vmem_limit_bytes=60<<20),name="forward")(
        groups,offsets,*vectors,wq,wp,w1,w2,tok,cot,mask)

class Reduce:
    def __init__(self,give,a,s,rxa,ryb,rx,ry,b,rz,ss,rs):
        self.give=give; self.a=a; self.s=s; self.rxa=rxa; self.ryb=ryb; self.rx=rx; self.ry=ry; self.b=b; self.rz=rz
        self.ss=ss; self.rs=rs
        c,x,y,z=place()
        self.c=c; self.z=z; self.yx=y*2+x
        self.xn=y*2+1-x; self.yn=(1-y)*2+x; self.dg=(1-y)*2+1-x
        self.xd=dev(z,self.xn,c); self.yd=dev(z,self.yn,c); self.sd=dev(z,self.yx,1-c)
        self.cps={}
    def send(self,src,dst,slot,d):
        cp=pltpu.make_async_remote_copy(src_ref=src,dst_ref=dst,send_sem=self.ss.at[slot],recv_sem=self.rs.at[slot],device_id=d,device_id_type=MESH)
        cp.start(); self.cps[slot]=cp
    def r0(self): self.send(self.give,self.s,0,self.sd)
    def add(self,n,z0,yx,other):
        def body(i,_):
            t=self.a(pl.ds(i+z0,1),yx)
            t[...]=t[...]+other(i)[...]
            return 0
        lax.fori_loop(0,n,body,0)
    def r1(self):
        self.cps[0].wait_recv()
        def own(yx): self.add(4,0,yx,lambda i: self.s.at[pl.ds(i,1),yx])
        own(self.dg)
        self.send(self.a(pl.ds(0,2),self.dg),self.rxa,1,self.xd)
        self.send(self.a(pl.ds(2,2),self.dg),self.ryb,2,self.yd)
        own(self.xn)
        self.send(self.a(pl.ds(0,2),self.xn),self.rx.at[pl.ds(0,2)],3,self.xd)
        own(self.yn)
        self.send(self.a(pl.ds(2,2),self.yn),self.ry.at[pl.ds(2,2)],4,self.yd)
        own(self.yx)
    def r2(self):
        self.cps[1].wait_recv()
        self.add(2,0,self.yn,lambda i: self.rxa.at[pl.ds(i,1)])
        self.send(self.a(pl.ds(0,2),self.yn),self.ry.at[pl.ds(0,2)],6,self.yd)
        self.cps[2].wait_recv()
        self.add(2,2,self.xn,lambda i: self.ryb.at[pl.ds(i,1)])
        self.send(self.a(pl.ds(2,2),self.xn),self.rx.at[pl.ds(2,2)],5,self.xd)
    def r3(self):
        for s in (3,4,5,6): self.cps[s].wait_recv()
        def body(i,_):
            k=pl.ds(i,1)
            self.b[k]=(self.a(k,self.yx)[...].astype(F32)+self.rx[k].astype(F32)+self.ry[k].astype(F32)).astype(BF)
            return 0
        lax.fori_loop(0,4,body,0)
        for k in (1,2,3):
            zz=lax.rem(self.z+k,4)
            self.send(self.b.at[zz],self.rz.at[k-1],6+k,dev(zz,self.yx,self.c))
    def total(self):
        t=self.b[self.z].astype(F32)
        for k in (1,2,3):
            self.cps[6+k].wait_recv()
            t=t+self.rz[k-1].astype(F32)
        return t
    def drain(self):
        for cp in self.cps.values(): cp.wait_send()

def eights(v):
    return jnp.sum(v.reshape(v.shape[0]//8,8,v.shape[1]),axis=0)

class Total:
    def __init__(self,v,r,ss,rs):
        self.v=v; self.r=r; self.ss=ss; self.rs=rs; self.cps=[]
    def send(self,a,slot,d):
        cp=pltpu.make_async_remote_copy(src_ref=self.v.at[a],dst_ref=self.r.at[slot],send_sem=self.ss.at[slot],recv_sem=self.rs.at[slot],device_id=d,device_id_type=MESH)
        cp.start(); self.cps.append(cp)
    def stage(self,k):
        c,x,y,z=place(); yx=y*2+x
        if k:
            if k<4: self.cps[k-1].wait_recv(); self.v[k]=self.v[k-1]+self.r[k-1]
        if k==0: self.send(0,0,dev(z,yx,1-c))
        elif k==1: self.send(1,1,dev(z,y*2+1-x,c))
        elif k==2: self.send(2,2,dev(z,(1-y)*2+x,c))
        elif k==3:
            for h in (1,2,3): self.send(3,2+h,dev(lax.rem(z+h,4),yx,c))
        else:
            for h in (1,2,3): self.cps[2+h].wait_recv()
            self.sum=self.v[3]+self.r[3]+self.r[4]+self.r[5]
    def drain(self):
        for cp in self.cps: cp.wait_send()

BACKWARD_ORDER=(
    0, 200, 240, 241, 242, 16, 1, 243, 220, 221, 17, 222, 64, 32, 48, 223, 2, 201, 33, 65, 18, 202, 80, 49, 203,
    3, 34, 204, 250, 251, 81, 96, 19, 230, 112, 50, 252, 66, 35, 82, 97, 253, 231, 83, 113, 51, 254, 67, 128, 98,
    114, 255, 129, 232, 176, 99, 115, 4, 36, 144, 130, 177, 205, 131, 178, 145, 206, 179, 207, 160, 146, 161, 147,
    84, 162, 208, 163, 68, 20, 100, 52, 116, 132, 148, 209, 180, 164,
)

def backward_kernel(w2_r,w1_r,wp_r,wq_r,pr_r,n1_r,n2_r,ctx_r,pj_r,hid_r,dg_r,xa_r,xb_r,mid_r,pt2_r,gt_r,cs_r,vec,meta,
        out_o,tok_o,sm_o,oq,op_,o1,o2,
        w2,w1,wp,gp,pj,mid,gf,nt_,tmp,ctx,gt,gb,pst,acc,accb,
        a2,s2,xa2,yb2,x2,y2,b2,z2,part,sb,xab,ybb,xb,yb,bb,zb,fb,frb,vs,vr,us,ur,
        lsem,psem,osem,rss,rrs,fss,frs,vss,vrs,uss,urs):
    greet()
    c,x,y,z=place(); yx=y*2+x
    sibd=dev(z,yx,1-c)
    loads={}; held=set()
    def get(name,src,dst):
        cp=pltpu.make_async_copy(src,dst,lsem.at[len(loads)]); cp.start(); loads[name]=cp
    def have(*names):
        for n in names:
            if n not in held: held.add(n); loads[n].wait()
    C2=[Reduce(pt2_r.at[:,:,1-c,h],lambda zs,q,h=h: a2.at[h,zs,q],s2.at[h],xa2.at[h],yb2.at[h],x2.at[h],y2.at[h],b2.at[h],z2.at[h],rss.at[h],rrs.at[h]) for h in range(2)]
    def sib_at(i): return sb.at[i] if i<5 else s2.at[(i-5)//2,:,:,:,pl.ds(384*((i-5)%2),384)]
    mine=pl.ds(pl.multiple_of(c*384,128),384); theirs=pl.ds(pl.multiple_of((1-c)*384,128),384)
    CH=[Reduce(part.at[i,:,:,:,theirs],lambda zs,q,i=i: part.at[i,zs,q,:,mine],sib_at(i),xab.at[i],ybb.at[i],xb.at[i],yb.at[i],bb.at[i],zb.at[i],rss.at[2+i],rrs.at[2+i]) for i in range(8)]
    F=CH[0:4]; PJ=CH[4]; QK=CH[5:8]
    get("gt",gt_r,gt)
    def tile(i):
        get("t%d"%i,w2_r.at[pl.ds(16*i,16)],w2.at[pl.ds(16*i,16)]); get("d%d"%i,dg_r.at[:,pl.ds(768*i,768)],gp.at[:,pl.ds(768*i,768)])
    tile(0); tile(1)
    ahead={240:lambda:(get("a2a",pt2_r.at[:,:,c,0],a2.at[0]),tile(2)),241:lambda:(tile(3),get("a2b",pt2_r.at[:,:,c,1],a2.at[1])),
        242:lambda:get("n2",n2_r,nt_),243:lambda:(get("cs",cs_r,tmp),get("w1",w1_r,w1)),220:lambda:(get("xb",xb_r,gb),get("wp",wp_r,wp)),
        221:lambda:get("ctx",ctx_r,ctx),222:lambda:get("pj",pj_r,pj)}
    acc[...]=jnp.zeros_like(acc)
    ends=[]
    def end(i):
        t=CH[i].total()
        fb[i,0]=t[:24]; fb[i,1]=t[24:]
        cp=pltpu.make_async_remote_copy(src_ref=fb.at[i,1-c],dst_ref=frb.at[i],send_sem=fss.at[i],recv_sem=frs.at[i],device_id=sibd,device_id_type=MESH)
        cp.start(); ends.append((i,cp))
    def end2(h): o2[48*h:48*h+48,:]=C2[h].total()
    def mlp(i,_):
        cc=pl.ds(pl.multiple_of(i*768,128),768)
        g=(nt(gt[...],w2[pl.ds(16*i,16)].reshape(768,768))*gp[:,cc].astype(F32)).astype(BF)
        gp[:,cc]=g
        accb[:,cc]=eights(g.astype(F32))
        return 0
    def w1grad(i):
        have("n2")
        if 220+i in ahead: ahead[220+i]()
        part[i]=nn(nt_[...],gp[:,768*i:768*i+768]).astype(BF).reshape(4,4,48,768)
        if i==3: get("n1",n1_r,nt_)
    def norm_back(i0,rows,col,gain,ka,kb,finish):
        def body(i,_):
            sums={}; later=[]
            def add(k,v): sums[k]=sums[k]+eights(v) if k in sums else eights(v)
            for u in range(5):
                r=pl.ds(pl.multiple_of(i0+(i*5+u)*16,16),16)
                g,xh,rstd=gf[r,:],rows[r,:].astype(F32),meta[r,col:col+1]
                add(ka,g*xh); add(kb,g)
                gx=g*gain
                m1=jnp.sum(gx,axis=1,keepdims=True)*(1.0/768); m2=jnp.sum(gx*xh,axis=1,keepdims=True)*(1.0/768)
                later+=finish(r,rstd*(gx-m1-xh*m2),add)
            for ref,r,v in later: ref[r,:]=v
            for k,v in sums.items(): acc[k]+=v
            return 0
        lax.fori_loop(0,25//5,body,0)
    def finish2(r,d,add):
        gm=tmp[r,:].astype(F32)+d
        v=(meta[r,0:1]*gm).astype(BF)
        add(4,v.astype(F32)); add(8,gt[r,:].astype(F32))
        return [(mid,r,gm),(gb,r,v)]
    def p10(k):
        have("w1","cs","xb")
        r=slice(400*k,400*k+400)
        gf[r,:]=nt(gp[r,:],w1[...].reshape(768,3072))
        norm_back(400*k,gb,3,vec[5:6,:],5,6,finish2)
        if k==1:
            get("hid",hid_r,gp); get("xa",xa_r,tmp)
            for g in range(3): get("wq%d"%g,wq_r.at[g],w1.at[:,:,:,pl.ds(768*g,768)])
    gc=gt
    def gctx():
        have("wp")
        gc[...]=nt(gb[...],wp[...].reshape(768,768)).astype(BF)
        pcopy(0).start()
    def wpgrad():
        have("ctx")
        part[4]=tn(ctx[...],gb[...]).astype(BF).reshape(4,4,48,768)
    lane=lax.broadcasted_iota(jnp.int32,(400,128),1)
    def where_of(t):
        return lax.rem(t,4)//2,2*(t//4)+lax.rem(t,2)
    def pcopy(t):
        b,p=where_of(t)
        return pltpu.make_async_copy(pr_r.at[b*6+p],pst.at[lax.rem(t,2)],psem.at[lax.rem(t,2)])
    def attend(t,_):
        b,p=where_of(t); s=lax.rem(t,2)
        r=pl.ds(pl.multiple_of(b*400,16),400)
        cc=lambda o: pl.ds(pl.multiple_of(o+p*128,128),128)
        pcopy(t).wait()
        @pl.when(t<11)
        def _(): pcopy(t+1).start()
        q=pj[r,cc(0)]; k=pj[r,cc(768)]; v=pj[r,cc(1536)]; g=gc[r,cc(0)]
        gx=g.astype(F32)*ctx[r,cc(0)].astype(F32)
        dq=[];dk=[];dv=[]
        for j in range(2):
            own=(lane>=64)==(j==1)
            zero=jnp.zeros_like(q)
            qj=jnp.where(own,q,zero); gj=jnp.where(own,g,zero)
            di=jnp.sum(jnp.where(own,gx,0.0),axis=1,keepdims=True)
            pr=pst[s,j]
            ds=(pr.astype(F32)*(nt(gj,v)-di)).astype(BF)
            dq.append(nn(ds,k)); dk.append(tn(ds,qj)); dv.append(tn(pr,gj))
        pj[r,cc(0)]=(jnp.where(lane<64,dq[0],dq[1])*0.125).astype(BF)
        pj[r,cc(768)]=((dk[0]+dk[1])*0.125).astype(BF)
        pj[r,cc(1536)]=(dv[0]+dv[1]).astype(BF)
        return 0
    def group(r,g): return jnp.concatenate([pj[r,o+256*g:o+256*g+256] for o in (0,768,1536)],axis=1)
    def qkvgrad(g):
        if g==0: have("n1")
        cols=group(slice(None),g)
        acc[3,:,256*g:256*g+256]=eights(cols[:,:256].astype(F32)); acc[7,:,256*g:256*g+256]=eights(cols[:,512:].astype(F32))
        part[5+g]=nn(nt_[...],cols).astype(BF).reshape(4,4,48,768)
        if g==2:
            for k in range(6): us[0,k:k+1,:]=jnp.sum(acc[3+k],axis=0,keepdims=True)
            for k in range(4): us[0,6+k:7+k,:]=jnp.sum(accb[:,768*k:768*k+768],axis=0,keepdims=True)
            us[0,10:16,:]=jnp.zeros((6,768),F32)
    def finish1(r,d,add):
        gs=mid[r,:]+d
        m=meta[r,1:2]>0.0
        add(0,jnp.where(m,gs,0.0))
        return [(mid,r,jnp.where(m,0.0,gs))]
    stores=[]
    def put(src,dst):
        cp=pltpu.make_async_copy(src,dst,osem.at[len(stores)]); cp.start(); stores.append(cp)
    def back(i):
        if i==0: have("xa","wq0","wq1","wq2")
        r=slice(400*i,400*i+400)
        gf[r,:]=sum(nt(group(r,g),w1[:,:,:,768*g:768*g+768].reshape(768,768)) for g in range(3))
        norm_back(400*i,tmp,2,vec[1:2,:],1,2,finish1)
        if i==1: put(mid,tok_o); get("mid2",mid_r,gf)
    def fin():
        for k in range(3): vs[0,k:k+1,:]=jnp.sum(acc[k],axis=0,keepdims=True)
        vs[0,3:8,:]=jnp.zeros((5,768),F32)
    def outp(i):
        if i==0: have("hid","mid2")
        r=slice(400*i,400*i+400)
        gf[r,:]=gf[r,:]+meta[r,0:1]*(nn(gp[r,:],w2[...].reshape(3072,768))+vec[8:9,:])
        put(gf.at[pl.ds(400*i,400)],out_o.at[pl.ds(400*i,400)])
    sums=[Total(vs,vr,vss,vrs),Total(us,ur,uss,urs)]
    plain=(lambda:None,lambda:p10(0),lambda:p10(1),gctx,wpgrad,lambda:back(0),lambda:back(1),fin,lambda:outp(0),lambda:outp(1))
    k=0
    while k<len(BACKWARD_ORDER):
        op=BACKWARD_ORDER[k]; k+=1
        i,t=op//16,op%16
        if i<10:
            if t==4:
                if i<2: end2(i)
                else: end(i-2)
            else:
                if i<2 and t==1: have(("a2a","a2b")[i])
                r=(C2+CH)[i]
                (r.r0,r.r1,r.r2,r.r3)[t]()
        elif i<12: sums[i-10].stage(t)
        elif op<220: plain[op-200]()
        elif op<230: w1grad(op-220)
        elif op<240: qkvgrad(op-230)
        else:
            a=b=op%10
            while k<len(BACKWARD_ORDER) and BACKWARD_ORDER[k]==op-a+b+1: b+=1; k+=1
            if op<250:
                have("gt")
                for i in range(a,b+1):
                    have("t%d"%i,"d%d"%i); ahead[240+i]()
                    lax.fori_loop(i,i+1,mlp,0)
            else:
                if a==0: have("pj")
                lax.fori_loop(2*a,2*b+2,attend,0)
    vt,ut=sums[0].sum,sums[1].sum
    me=lax.axis_index("dp")
    def turn(v,by): return pltpu.roll(v,lax.rem(768-by,768),1)[:,:128]
    eight=lambda v: jnp.concatenate([v]*8,axis=0)
    sm_o[0:8,:]=turn(vt,24*me)
    t=turn(ut,24*me)
    sm_o[4:7,:]=t[1:4]; sm_o[8:9,:]=t[5:6]
    sm_o[3:4,:]=turn(eight(jnp.where(me>=16,ut[4:5],ut[0:1])),48*lax.rem(me,16))[0:1]
    k8=me//8
    pick=jnp.where(k8==0,ut[6:7],jnp.where(k8==1,ut[7:8],jnp.where(k8==2,ut[8:9],ut[9:10])))
    sm_o[7:8,:]=turn(eight(pick),96*lax.rem(me,8))[0:1]
    for i,cp in ends:
        cp.wait_recv()
        own=fb[i,c]; oth=frb[i]
        lo=jnp.where(c==0,own,oth); hi=jnp.where(c==0,oth,own)
        if i<4: o1[:,768*i:768*i+384]=lo; o1[:,768*i+384:768*i+768]=hi
        elif i==4: op_[:,:384]=lo; op_[:,384:]=hi
        else:
            g=256*(i-5)
            oq[:,g:g+256]=lo[:,:256]; oq[:,768+g:768+g+128]=lo[:,256:]
            oq[:,768+g+128:768+g+256]=hi[:,:128]; oq[:,1536+g:1536+g+256]=hi[:,128:]
        cp.wait_send()
    for cp in stores: cp.wait()
    for q in C2+CH+sums: q.drain()

def backward(w2,w1,wp,wq,pr,n1,n2,ctx,pj,hid,dg,xa,xb,mid,pt2,gt,cs,vec,meta):
    sds=jax.ShapeDtypeStruct
    V=pl.BlockSpec(memory_space=pltpu.VMEM); A=pl.BlockSpec(memory_space=pl.ANY)
    D=pltpu.SemaphoreType.DMA
    v=pltpu.VMEM
    W,R=n1.shape
    scr=[v((64,48,W),BF),v((4,4,48,4*W),BF),v((4,4,48,W),BF),v((R,4*W),BF),v((R,3*W),BF),v((R,W),F32),v((R,W),F32),v((W,R),BF),
        v((R,W),BF),v((R,W),BF),v((R,W),BF),v((R,W),BF),v((2,2,400,400),BF),v((9,8,W),F32),v((8,4*W),F32)]
    def rs(n,r,w,own):
        o=[v((n,4,4,r,own),BF),v((min(n,5),4,4,r,w),BF),v((n,2,r,w),BF),v((n,2,r,w),BF),v((n,4,r,w),BF),v((n,4,r,w),BF),v((n,4,r,w),BF),v((n,3,r,w),BF)]
        return o
    scr+=rs(2,48,W,W)+rs(8,48,W//2,W)
    scr+=[v((8,2,24,W//2),F32),v((8,24,W//2),F32),v((4,8,W),F32),v((6,8,W),F32),v((4,16,W),F32),v((6,16,W),F32)]
    scr+=[D((28,)),D((2,)),D((3,)),D((10,10)),D((10,10)),D((8,)),D((8,))]+[D((6,))]*4
    outs=[((R,W),F32),((R,W),F32),((16,128),F32),((24,3*W),F32),((24,W),F32),((24,4*W),F32),((96,W),F32)]
    return pl.pallas_call(backward_kernel,in_specs=[A]*17+[V]*2,out_specs=[A,A]+[V]*5,out_shape=[sds(*o) for o in outs],scratch_shapes=scr,
        compiler_params=pltpu.CompilerParams(collective_id=1,has_side_effects=True,vmem_limit_bytes=63<<20),name="backward")(
        w2,w1,wp,wq,pr,n1,n2,ctx,pj,hid,dg,xa,xb,mid,pt2,gt,cs,vec,meta)

def settle_back_kernel(groups,out_r,tok_r,sm,q_r,p_r,w1_r,w2_r,out_o,tok_o,q_o,p_o,w1_o,w2_o,v0,v1,v2,v3,v4,v5,v6,v7,v8,buf,ob,tb,qb,pb,b1,b2,sem):
    pairs=((tok_r,tb),(out_r,buf),(w1_r,b1),(q_r,qb),(w2_r,b2),(p_r,pb))
    loads=[pltpu.make_async_copy(a,b,sem.at[i]) for i,(a,b) in enumerate(pairs)]
    for cp in loads: cp.start()
    moved=groups[0]==1
    one=[pltpu.make_async_copy(tb,tok_o,sem.at[6])]
    three=[pltpu.make_async_copy(tb.at[pl.ds(a,n)],tok_o.at[pl.ds(b,n)],sem.at[7+i]) for i,(a,b,n) in enumerate(((0,0,392),(400,392,400),(392,792,8)))]
    for i,v in enumerate((v0,v1,v2,v3,v4,v5,v6,v7,v8)):
        m=v.shape[0]
        v[...]=sm[i:i+1,0:m].reshape(m)
    loads[0].wait()
    @pl.when(moved)
    def _():
        for cp in three: cp.start()
    @pl.when(jnp.logical_not(moved))
    def _():
        for cp in one: cp.start()
    loads[1].wait()
    ob[0:384]=buf[0:384].astype(BF)
    a=buf[384:800]
    b=jnp.concatenate([buf[384:392],buf[400:800],buf[392:400]],axis=0)
    ob[384:800]=jnp.where(moved,b,a).astype(BF)
    stores=[pltpu.make_async_copy(ob,out_o,sem.at[10])]
    stores[0].start()
    for i,(b,o) in enumerate(((b1,w1_o),(qb,q_o),(b2,w2_o),(pb,p_o))):
        loads[2+i].wait()
        cp=pltpu.make_async_copy(b,o,sem.at[11+i]); cp.start(); stores.append(cp)
    for cp in stores: cp.wait()
    @pl.when(moved)
    def _():
        for cp in three: cp.wait()
    @pl.when(jnp.logical_not(moved))
    def _():
        for cp in one: cp.wait()

def settle_back(groups,sizes,out,tok,sm,q,p,w1,w2):
    sds=jax.ShapeDtypeStruct
    V=pl.BlockSpec(memory_space=pltpu.VMEM); A=pl.BlockSpec(memory_space=pl.ANY); M=pl.BlockSpec(memory_space=pltpu.SMEM)
    v=pltpu.VMEM
    return pl.pallas_call(settle_back_kernel,in_specs=[M,A,A,V,A,A,A,A],out_specs=[A]*6+[V]*len(sizes),
        out_shape=[sds(out.shape,BF)]+[sds(a.shape,F32) for a in (tok,q,p,w1,w2)]+[sds((m,),F32) for m in sizes],
        scratch_shapes=[v(out.shape,F32),v(out.shape,BF)]+[v(a.shape,F32) for a in (tok,q,p,w1,w2)]+[pltpu.SemaphoreType.DMA((15,))],
        compiler_params=pltpu.CompilerParams(vmem_limit_bytes=60<<20),name="settle_back")(groups,out,tok,sm,q,p,w1,w2)

def normalize(values, gain, shift):
    center = values - jnp.mean(values, axis=-1, keepdims=True)
    spread = jnp.mean(center * center, axis=-1, keepdims=True)
    return center * lax.rsqrt(spread + eps_norm) * gain + shift

def activate(values):
    return jax.nn.gelu(values, approximate=False)

def segment_rows(groups, offsets, rows):
    lengths = jnp.where(groups == 0, P_SMALL, jnp.where(groups == 1, P_MID, P_LARGE)).astype(jnp.int32)
    positions = jnp.arange(rows, dtype=jnp.int32)
    inside = (positions[None, :] >= offsets[:, None]) & (positions[None, :] < offsets[:, None] + lengths[:, None])
    labels = jnp.arange(1, offsets.shape[0] + 1, dtype=jnp.int32)
    return jnp.sum(jnp.where(inside, labels[:, None], 0), axis=0) - 1

def settle(mid, rows):
    half = rows.shape[0] // 2
    cut = P_MID * (half // P_MID)
    gap = half - cut
    end = rows.shape[0] - gap
    moved = jnp.concatenate([rows[:cut], rows[end:], rows[cut:end]], axis=0)
    return jnp.where(mid, moved, rows)

def unsettle(mid, rows):
    half = rows.shape[0] // 2
    cut = P_MID * (half // P_MID)
    gap = half - cut
    moved = jnp.concatenate([rows[:cut], rows[half:], rows[cut:half]], axis=0)
    return jnp.where(mid, moved, rows)

def shards(n, tokens, mask_bits, groups, offsets, mask_token, ln1_gain, ln1_bias, w_qkv, b_qv, w_proj, b_proj,
           ln2_gain, ln2_bias, w_fc1, b_fc1, w_fc2, b_fc2, cotangent):
    vectors = (mask_token, ln1_gain, ln1_bias, b_qv, b_proj, ln2_gain, ln2_bias, b_fc1, b_fc2)
    sizes = [v.shape[0] for v in vectors]
    places = [sum(sizes[:i]) for i in range(len(sizes) + 1)]
    small_all = lax.all_gather(jnp.concatenate(vectors), "dp", axis=0, tiled=False)
    full_qkv, full_proj, full_fc1, full_fc2 = [
        lax.all_gather(w, "dp", axis=0, tiled=True) for w in (w_qkv, w_proj, w_fc1, w_fc2)]
    token_mask, gain_one, shift_one, bias_qv, bias_proj, gain_two, shift_two, bias_one, bias_two = [
        small_all[:, places[i]:places[i + 1]].reshape(-1).astype(F32) for i in range(len(sizes))]
    rows, width = tokens.shape
    half = rows // 2
    mid = groups[0] == 1
    tokens = settle(mid, tokens)
    cotangent = settle(mid, cotangent)
    mask_bits = settle(mid, mask_bits)
    segment = settle(mid, segment_rows(groups, offsets, rows))
    valid_col = (segment >= 0).astype(F32)[:, None]
    halves = segment.reshape(2, half)
    bias = jnp.where(halves[:, :, None] == halves[:, None, :], 0.0, -1e30).astype(F32)
    masked_rows = (mask_bits == 1)[:, None]
    start = jnp.where(masked_rows, token_mask[None, :], tokens.astype(F32))
    normed_one = normalize(start, gain_one, shift_one).astype(BF)
    full_bias = jnp.concatenate([bias_qv[:width], jnp.zeros((width,), F32), bias_qv[width:]])
    projected = (jnp.dot(normed_one, full_qkv, preferred_element_type=F32) + full_bias).astype(BF)
    context_low, probs = attn_fwd(projected, bias)
    middle = start + valid_col * (jnp.dot(context_low, full_proj, preferred_element_type=F32) + bias_proj)
    normed_two = normalize(middle, gain_two, shift_two).astype(BF)
    hidden_pre = jnp.dot(normed_two, full_fc1, preferred_element_type=F32) + bias_one
    hidden_low = activate(hidden_pre).astype(BF)
    result = middle + valid_col * (jnp.dot(hidden_low, full_fc2, preferred_element_type=F32) + bias_two)
    output = unsettle(mid, result.astype(BF))
    upstream = cotangent.astype(F32)
    grad_two = (valid_col * upstream).astype(BF)
    grad_wfc2 = tn(hidden_low, grad_two)
    grad_bfc2 = jnp.sum(grad_two.astype(F32), axis=0)
    grad_hidden = nt(grad_two, full_fc2)
    _, gelu_back = jax.vjp(activate, hidden_pre)
    grad_pre = gelu_back(grad_hidden)[0].astype(BF)
    grad_wfc1 = tn(normed_two, grad_pre)
    grad_bfc1 = jnp.sum(grad_pre.astype(F32), axis=0)
    grad_normed_two = nt(grad_pre, full_fc1)
    _, norm_back_two = jax.vjp(normalize, middle, gain_two, shift_two)
    grad_mid_part, grad_gain_two, grad_shift_two = norm_back_two(grad_normed_two)
    grad_middle = upstream + grad_mid_part
    grad_branch = (valid_col * grad_middle).astype(BF)
    grad_wproj = tn(context_low, grad_branch)
    grad_bproj = jnp.sum(grad_branch.astype(F32), axis=0)
    grad_context = nt(grad_branch, full_proj).astype(BF)
    dq, dk, dv = attn_bwd(projected, grad_context, context_low, probs)
    grad_projected = jnp.concatenate([dq, dk, dv], axis=1)
    grad_wqkv = tn(normed_one, grad_projected)
    grad_bqv = jnp.concatenate([jnp.sum(dq.astype(F32), axis=0), jnp.sum(dv.astype(F32), axis=0)])
    grad_normed_one = nt(grad_projected, full_qkv)
    _, norm_back_one = jax.vjp(normalize, start, gain_one, shift_one)
    grad_start_part, grad_gain_one, grad_shift_one = norm_back_one(grad_normed_one)
    grad_start = grad_middle + grad_start_part
    grad_token = jnp.sum(jnp.where(masked_rows, grad_start, 0.0), axis=0)
    grad_input = unsettle(mid, jnp.where(masked_rows, 0.0, grad_start))
    grad_vectors = (grad_token, grad_gain_one, grad_shift_one, grad_bqv, grad_bproj, grad_gain_two, grad_shift_two,
                    grad_bfc1, grad_bfc2)
    grad_small = jnp.concatenate([g.reshape(n, -1) for g in grad_vectors], axis=1)
    small_share = lax.psum_scatter(grad_small, "dp", scatter_dimension=0, tiled=False)
    share_qkv, share_proj, share_fc1, share_fc2 = [
        lax.psum_scatter(g, "dp", scatter_dimension=0, tiled=True)
        for g in (grad_wqkv, grad_wproj, grad_wfc1, grad_wfc2)]
    v = [small_share[places[i]:places[i + 1]] for i in range(len(sizes))]
    return (output, grad_input, v[0], v[1], v[2], share_qkv, v[3], share_proj, v[4], v[5], v[6], share_fc1, v[7],
            share_fc2, v[8])


def shards_fast(n, tokens, mask_bits, groups, offsets, mask_token, ln1_gain, ln1_bias, w_qkv, b_qv, w_proj, b_proj,
           ln2_gain, ln2_bias, w_fc1, b_fc1, w_fc2, b_fc2, cotangent):
    vectors = (mask_token, ln1_gain, ln1_bias, b_qv, b_proj, ln2_gain, ln2_bias, b_fc1, b_fc2)
    sizes = [v.shape[0] for v in vectors]
    (gq, gp, g1, g2, probs, normed_one, normed_two, context_low, projected, hidden_low, dgelu, rows_one, rows_two, middle, part2,
     grad_two, cots, vec, meta) = forward(groups, offsets, vectors, w_qkv, w_proj, w_fc1, w_fc2, tokens, cotangent, mask_bits)
    width = tokens.shape[1]
    shares = backward(
        g2.reshape(64, 48, width), g1, gp, gq, probs, normed_one, normed_two, context_low,
        projected, hidden_low, dgelu, rows_one, rows_two, middle, part2.reshape(4, 4, 2, 2, 48, width), grad_two, cots, vec, meta)
    output, grad_input, share_qkv, share_proj, share_fc1, share_fc2, *v = settle_back(groups, sizes, *shares)
    return (output, grad_input, v[0], v[1], v[2], share_qkv, v[3], share_proj, v[4], v[5], v[6], share_fc1, v[7],
            share_fc2, v[8])

def solution(mesh):
    row, flat = P("dp", None), P("dp")
    return jax.shard_map(
        functools.partial(shards_fast if mesh.shape["dp"] == 32 else shards, mesh.shape["dp"]),
        mesh=mesh,
        in_specs=(row, flat, flat, flat, flat, flat, flat, row, flat, row, flat, flat, flat, row, flat, row, flat, row),
        out_specs=(row, row, flat, flat, flat, row, flat, row, flat, flat, flat, row, flat, row, flat),
        check_vma=False,
    )
```

```python
import functools

import jax
import jax.numpy as jnp
from jax import lax
from jax.experimental import pallas as pl
from jax.experimental.pallas import tpu as pltpu
from jax.sharding import PartitionSpec as P

P_SMALL = 100
P_MID = 196
P_LARGE = 400
eps_norm = 1e-06

def nt(a,b): return lax.dot_general(a,b,(((1,),(1,)),((),())),preferred_element_type=jnp.float32)
def nn(a,b): return lax.dot_general(a,b,(((1,),(0,)),((),())),preferred_element_type=jnp.float32)
def tn(a,b): return lax.dot_general(a,b,(((0,),(0,)),((),())),preferred_element_type=jnp.float32)

def attn_fwd_kernel(bias_ref, q_ref, k_ref, v_ref, ctx_ref, p_ref):
    q=q_ref[...]; k=k_ref[...]; v=v_ref[...]
    rows,width=q.shape
    lane=lax.broadcasted_iota(jnp.int32,(rows,width),1)
    bias=bias_ref[0]
    outs=[]
    for j in range(2):
        mine=(lane>=64)==(j==1)
        qj=jnp.where(mine,q,jnp.zeros_like(q))
        s=nt(qj,k)*0.18033688011112042+bias
        m=jnp.max(s,axis=1,keepdims=True)
        e=jnp.exp2(s-m)
        l=jnp.sum(e,axis=1,keepdims=True)
        p=(e*(1.0/l)).astype(jnp.bfloat16)
        p_ref[0,0,j]=p
        outs.append(nn(p,v))
    ctx_ref[...]=jnp.where(lane<64,outs[0],outs[1]).astype(jnp.bfloat16)

def attn_fwd(proj,bias):
    rows=proj.shape[0]; half=rows//2; width=proj.shape[1]//3; pairs=width//128
    return pl.pallas_call(attn_fwd_kernel,grid=(2,pairs),
        in_specs=[pl.BlockSpec((1,half,half),lambda b,p:(b,0,0)),
                  pl.BlockSpec((half,128),lambda b,p:(b,p)),
                  pl.BlockSpec((half,128),lambda b,p:(b,p+pairs)),
                  pl.BlockSpec((half,128),lambda b,p:(b,p+2*pairs))],
        out_specs=[pl.BlockSpec((half,128),lambda b,p:(b,p)),
                   pl.BlockSpec((1,1,2,half,half),lambda b,p:(b,p,0,0,0))],
        out_shape=[jax.ShapeDtypeStruct((rows,width),jnp.bfloat16),
                   jax.ShapeDtypeStruct((2,pairs,2,half,half),jnp.bfloat16)],
        compiler_params=pltpu.CompilerParams(vmem_limit_bytes=40<<20),name="attn_fwd")(bias,proj,proj,proj)

def attn_bwd_kernel(q_ref,k_ref,v_ref,g_ref,c_ref,p_ref,dq_ref,dk_ref,dv_ref):
    q=q_ref[...]; k=k_ref[...]; v=v_ref[...]; g=g_ref[...]; c=c_ref[...]
    rows,width=q.shape
    lane=lax.broadcasted_iota(jnp.int32,(rows,width),1)
    gc=g.astype(jnp.float32)*c.astype(jnp.float32)
    dq=[];dk=[];dv=[]
    for j in range(2):
        mine=(lane>=64)==(j==1)
        zero=jnp.zeros_like(q)
        qj=jnp.where(mine,q,zero); gj=jnp.where(mine,g,zero)
        di=jnp.sum(jnp.where(mine,gc,0.0),axis=1,keepdims=True)
        p=p_ref[0,0,j]
        dp=nt(gj,v)
        ds=(p.astype(jnp.float32)*(dp-di)).astype(jnp.bfloat16)
        dq.append(nn(ds,k))
        dk.append(tn(ds,qj))
        dv.append(tn(p,gj))
    dq_ref[...]=(jnp.where(lane<64,dq[0],dq[1])*0.125).astype(jnp.bfloat16)
    dk_ref[...]=((dk[0]+dk[1])*0.125).astype(jnp.bfloat16)
    dv_ref[...]=(dv[0]+dv[1]).astype(jnp.bfloat16)

def attn_bwd(proj,gctx,ctx,p):
    rows=proj.shape[0]; half=rows//2; width=proj.shape[1]//3; pairs=width//128
    sp=lambda o: pl.BlockSpec((half,128),lambda b,p:(b,p+o*pairs))
    return pl.pallas_call(attn_bwd_kernel,grid=(2,pairs),
        in_specs=[sp(0),sp(1),sp(2),sp(0),sp(0),pl.BlockSpec((1,1,2,half,half),lambda b,p:(b,p,0,0,0))],
        out_specs=[sp(0)]*3,
        out_shape=[jax.ShapeDtypeStruct((rows,width),jnp.bfloat16)]*3,
        compiler_params=pltpu.CompilerParams(vmem_limit_bytes=40<<20),name="attn_bwd")(proj,proj,proj,gctx,ctx,p)
MESH=pl.DeviceIdType.MESH
F32=jnp.float32; BF=jnp.bfloat16

def place():
    me=lax.axis_index("dp")
    c=lax.rem(me,2); x=lax.rem(me//2,2); y=lax.rem(me//4,2); z=me//8
    return c,x,y,z
def dev(z,yx,c): return ((z*4+yx)*2+c,)

def greet():
    c,x,y,z=place(); yx=y*2+x
    bar=pltpu.get_barrier_semaphore()
    peers=[dev(z,yx,1-c),dev(z,y*2+1-x,c),dev(z,(1-y)*2+x,c)]+[dev(lax.rem(z+k,4),yx,c) for k in (1,2,3)]
    for p in peers: pl.semaphore_signal(bar,inc=1,device_id=p,device_id_type=MESH)
    pl.semaphore_wait(bar,len(peers))

class Gather:
    def __init__(self,view,ss,rs):
        self.view=view; self.ss=ss; self.rs=rs
        c,x,y,z=place()
        self.c=c; self.z=z; self.yx=y*2+x
        self.xn=y*2+1-x; self.yn=(1-y)*2+x; self.dg=(1-y)*2+1-x
        self.sends=[]
    def _cp(self,src,dst,slot,d):
        return pltpu.make_async_remote_copy(src_ref=src,dst_ref=dst,send_sem=self.ss.at[slot],recv_sem=self.rs.at[slot],device_id=d,device_id_type=MESH)
    def send(self,src,dst,slot,d):
        cp=self._cp(src,dst,slot,d); cp.start(); self.sends.append(cp)
    def got(self,dst,slot,d):
        self._cp(dst,dst,slot,d).wait_recv()
    def one(self,z): return self.view(pl.ds(z,1),self.yx,self.c)
    def z_send(self,src):
        for k in (1,2,3):
            self.send(src,self.one(self.z),k-1,dev(lax.rem(self.z+k,4),self.yx,self.c))
    def sib(self,ref,slot): self.send(ref,ref,slot,dev(self.z,self.yx,1-self.c))
    def z_recv(self):
        for k in (1,2,3):
            zz=lax.rem(self.z+4-k,4)
            self.got(self.one(zz),k-1,dev(zz,self.yx,self.c))
    def xy_send(self):
        r=self.view(pl.ds(0,4),self.yx,self.c)
        self.send(r,r,3,dev(self.z,self.xn,self.c))
        self.send(r,r,4,dev(self.z,self.yn,self.c))
        for k in (1,2,3): self.sib(self.one(lax.rem(self.z+4-k,4)),6+k)
    def xy_recv(self):
        rx=self.view(pl.ds(0,4),self.xn,self.c)
        self.got(rx,3,dev(self.z,self.xn,self.c))
        h=self.view(pl.ds(0,2),self.xn,self.c)
        self.send(h,h,5,dev(self.z,self.yn,self.c))
        ry=self.view(pl.ds(0,4),self.yn,self.c)
        self.got(ry,4,dev(self.z,self.yn,self.c))
        h=self.view(pl.ds(2,2),self.yn,self.c)
        self.send(h,h,6,dev(self.z,self.xn,self.c))
        self.sib(rx,10); self.sib(ry,11)
    def diag_recv(self):
        a=self.view(pl.ds(0,2),self.dg,self.c)
        self.got(a,5,dev(self.z,self.yn,self.c))
        self.sib(a,12)
        b=self.view(pl.ds(2,2),self.dg,self.c)
        self.got(b,6,dev(self.z,self.xn,self.c))
        self.sib(b,13)
    def finish(self):
        o=1-self.c; s=dev(self.z,self.yx,o)
        for k in (1,2,3): self.got(self.view(pl.ds(lax.rem(self.z+4-k,4),1),self.yx,o),6+k,s)
        self.got(self.view(pl.ds(0,4),self.xn,o),10,s)
        self.got(self.view(pl.ds(0,4),self.yn,o),11,s)
        self.got(self.view(pl.ds(0,2),self.dg,o),12,s)
        self.got(self.view(pl.ds(2,2),self.dg,o),13,s)
    def drain(self):
        for cp in self.sends: cp.wait_send()

def cols_view(ref):
    half=ref.shape[-1]//2
    def view(zs,yx,lane): return ref.at[zs,yx,:,pl.ds(pl.multiple_of(lane*half,128),half)]
    return view
def rows_view(ref):
    def view(zs,yx,lane): return ref.at[zs,yx,lane]
    return view

def join(c,own,sib):
    a=own.astype(F32); b=sib.astype(F32)
    return jnp.concatenate([jnp.where(c==0,a,b),jnp.where(c==0,b,a)],axis=0).astype(BF)

def gather_kernel(sm_ref,q_ref,p_ref,f1_ref,f2_ref,gs_ref,gq_ref,gp_ref,g1_ref,g2_ref,
        sq,sp,s1,bq,bp,b1,ss0,rs0,ssl,ss,rs):
    greet()
    c,x,y,z=place(); yx=y*2+x
    sibd=dev(z,yx,1-c)
    first=[]
    def swap(src,dst,i):
        cp=pltpu.make_async_remote_copy(src_ref=src,dst_ref=dst,send_sem=ss0.at[i],recv_sem=rs0.at[i],device_id=sibd,device_id_type=MESH)
        cp.start(); first.append(cp)
    swap(sm_ref,gs_ref.at[z,yx,c],0)
    swap(q_ref,sq,1); swap(p_ref,sp,2); swap(f1_ref,s1,3)
    swap(f2_ref,g2_ref.at[z,yx,c],4)
    gs=[Gather(rows_view(gs_ref),ss.at[0],rs.at[0]),Gather(cols_view(gq_ref),ss.at[1],rs.at[1]),Gather(cols_view(gp_ref),ss.at[2],rs.at[2]),
        Gather(cols_view(g1_ref),ss.at[3],rs.at[3]),Gather(rows_view(g2_ref),ss.at[4],rs.at[4])]
    local=[]
    def keep(src,dst,i):
        cp=pltpu.make_async_copy(src,dst,ssl.at[i]); cp.start(); local.append(cp)
    def half(b):
        h=b.shape[-1]//2
        return b.at[:,:,pl.ds(pl.multiple_of(c*h,128),h)]
    keep(sm_ref,gs_ref.at[z,yx,c],0)
    keep(f2_ref,g2_ref.at[z,yx,c],4)
    def begin(i):
        if i==0:
            local[0].wait(); gs[0].z_send(gs[0].one(z))
        elif i==4:
            local[1].wait(); gs[4].z_send(gs[4].one(z))
        else:
            own,sib,buf,dst={1:(q_ref,sq,bq,gq_ref),2:(p_ref,sp,bp,gp_ref),3:(f1_ref,s1,b1,g1_ref)}[i]
            first[i].wait_recv()
            buf[0]=join(c,own[...],sib[...])
            keep(buf,dst.at[pl.ds(z,1),yx],i)
            gs[i].z_send(half(buf))
    begin(0); begin(1)
    gs[0].z_recv(); gs[0].xy_send()
    begin(2)
    gs[1].z_recv(); local[2].wait(); gs[1].xy_send()
    begin(3)
    gs[0].xy_recv()
    gs[2].z_recv(); local[3].wait(); gs[2].xy_send()
    gs[0].diag_recv()
    gs[1].xy_recv()
    begin(4)
    gs[3].z_recv(); local[4].wait(); gs[3].xy_send()
    gs[2].xy_recv()
    gs[1].diag_recv()
    gs[2].diag_recv()
    gs[4].z_recv(); gs[4].xy_send()
    gs[3].xy_recv()
    gs[3].diag_recv()
    gs[4].xy_recv()
    gs[4].diag_recv()
    first[0].wait_recv(); first[4].wait_recv()
    for g in gs: g.finish()
    for cp in first: cp.wait_send()
    for g in gs: g.drain()

def gather_all(small,wq,wp,w1,w2):
    sds=jax.ShapeDtypeStruct
    nq,np_,n1,n2=wq.shape[1],wp.shape[1],w1.shape[1],w2.shape[1]
    r=wq.shape[0]; r2=w2.shape[0]
    V=pl.BlockSpec(memory_space=pltpu.VMEM); A=pl.BlockSpec(memory_space=pl.ANY)
    D=pltpu.SemaphoreType.DMA
    return pl.pallas_call(gather_kernel,
        in_specs=[V]*5,out_specs=[A]*5,
        out_shape=[sds((4,4,2)+small.shape,BF),sds((4,4,2*r,nq),BF),sds((4,4,2*r,np_),BF),sds((4,4,2*r,n1),BF),sds((4,4,2,r2,n2),BF)],
        scratch_shapes=[pltpu.VMEM((r,n),BF) for n in (nq,np_,n1)]+[pltpu.VMEM((1,2*r,n),BF) for n in (nq,np_,n1)]+
            [D((5,)),D((5,)),D((5,)),D((5,14)),D((5,14))],
        compiler_params=pltpu.CompilerParams(collective_id=0,has_side_effects=True,vmem_limit_bytes=16<<20),name="gather_all")(small,wq,wp,w1,w2)

class Scatter:
    def __init__(self,view,a,s,rxa,ryb,rx,ry,b,rz,ss,rs,ls):
        self.view=view; self.a=a; self.s=s; self.rxa=rxa; self.ryb=ryb; self.rx=rx; self.ry=ry; self.b=b; self.rz=rz
        self.ss=ss; self.rs=rs; self.ls=ls
        c,x,y,z=place()
        self.c=c; self.z=z; self.yx=y*2+x
        self.xn=y*2+1-x; self.yn=(1-y)*2+x; self.dg=(1-y)*2+1-x
        self.cps={}
    def send(self,src,dst,slot,d):
        cp=pltpu.make_async_remote_copy(src_ref=src,dst_ref=dst,send_sem=self.ss.at[slot],recv_sem=self.rs.at[slot],device_id=d,device_id_type=MESH)
        cp.start(); self.cps[slot]=cp
    def r0(self):
        self.send(self.view(1-self.c),self.s,0,dev(self.z,self.yx,1-self.c))
        self.loc=pltpu.make_async_copy(self.view(self.c),self.a,self.ls); self.loc.start()
    def r1(self):
        self.loc.wait(); self.cps[0].wait_recv()
        a,s=self.a,self.s
        def add(yx):
            def body(i,_):
                a[i,yx]=(a[i,yx].astype(F32)+s[i,yx].astype(F32)).astype(a.dtype)
                return 0
            lax.fori_loop(0,4,body,0)
        xd=dev(self.z,self.xn,self.c); yd=dev(self.z,self.yn,self.c)
        add(self.dg)
        self.send(a.at[pl.ds(0,2),self.dg],self.rxa,1,xd)
        self.send(a.at[pl.ds(2,2),self.dg],self.ryb,2,yd)
        add(self.xn)
        self.send(a.at[pl.ds(0,2),self.xn],self.rx.at[pl.ds(0,2)],3,xd)
        add(self.yn)
        self.send(a.at[pl.ds(2,2),self.yn],self.ry.at[pl.ds(2,2)],4,yd)
        add(self.yx)
    def r2(self):
        a=self.a
        xd=dev(self.z,self.xn,self.c); yd=dev(self.z,self.yn,self.c)
        self.cps[1].wait_recv()
        def body(i,_):
            a[i,self.yn]=(a[i,self.yn].astype(F32)+self.rxa[i].astype(F32)).astype(a.dtype)
            return 0
        lax.fori_loop(0,2,body,0)
        self.send(a.at[pl.ds(0,2),self.yn],self.ry.at[pl.ds(0,2)],6,yd)
        self.cps[2].wait_recv()
        def body(i,_):
            a[i+2,self.xn]=(a[i+2,self.xn].astype(F32)+self.ryb[i].astype(F32)).astype(a.dtype)
            return 0
        lax.fori_loop(0,2,body,0)
        self.send(a.at[pl.ds(2,2),self.xn],self.rx.at[pl.ds(2,2)],5,xd)
    def r3(self):
        for s in (3,4,5,6): self.cps[s].wait_recv()
        def body(i,_):
            self.b[i]=(self.a[i,self.yx].astype(F32)+self.rx[i].astype(F32)+self.ry[i].astype(F32)).astype(self.b.dtype)
            return 0
        lax.fori_loop(0,4,body,0)
        for k in (1,2,3):
            zz=lax.rem(self.z+k,4)
            self.send(self.b.at[zz],self.rz.at[k-1],6+k,dev(zz,self.yx,self.c))
    def r4(self):
        t=self.b[self.z].astype(F32)
        for k in (1,2,3):
            self.cps[6+k].wait_recv()
            t=t+self.rz[k-1].astype(F32)
        return t
    def drain(self):
        for cp in self.cps.values(): cp.wait_send()

def scatter_scratch(r,n,dt):
    V=pltpu.VMEM
    return [V((4,4,r,n),dt),V((4,4,r,n),dt),V((2,r,n),dt),V((2,r,n),dt),V((4,r,n),dt),V((4,r,n),dt),V((4,r,n),dt),V((3,r,n),dt)]

def scatter_kernel(sm_ref,q_ref,p_ref,f1_ref,f2_ref,os_ref,oq_ref,op_ref,o1_ref,o2_ref,*sc):
    bufs=[sc[8*i:8*i+8] for i in range(5)]
    fin=sc[40:46]; ss,rs,ls,fs,fr=sc[46:]
    greet()
    c,x,y,z=place(); yx=y*2+x
    def cv(ref):
        h=ref.shape[-1]//2
        return lambda lane: ref.at[:,:,:,pl.ds(pl.multiple_of(lane*h,128),h)]
    def rv(ref): return lambda lane: ref.at[:,:,lane]
    refs=[sm_ref,q_ref,p_ref,f1_ref,f2_ref]
    S=[Scatter((rv if i in (0,4) else cv)(refs[i]),*bufs[i],ss.at[i],rs.at[i],ls.at[i]) for i in range(5)]
    order=[4,3,2,1,0]
    sibd=dev(z,yx,1-c)
    ends=[]
    outs={1:oq_ref,2:op_ref,3:o1_ref}
    def end(i):
        t=S[i].r4()
        if i==0: os_ref[...]=t
        elif i==4: o2_ref[...]=t
        else:
            f,rf=fin[2*(i-1)],fin[2*(i-1)+1]
            r=t.shape[0]//2
            f[0]=t[:r]; f[1]=t[r:]
            cp=pltpu.make_async_remote_copy(src_ref=f.at[1-c],dst_ref=rf,send_sem=fs.at[i],recv_sem=fr.at[i],device_id=sibd,device_id_type=MESH)
            cp.start(); ends.append((i,cp))
    def close():
        for i,cp in ends:
            cp.wait_recv()
            f,rf=fin[2*(i-1)],fin[2*(i-1)+1]
            own=f[c]; oth=rf[...]
            o=outs[i]; h=own.shape[-1]
            o[:,:h]=jnp.where(c==0,own,oth); o[:,h:]=jnp.where(c==0,oth,own)
            cp.wait_send()
    for i in order: S[i].r0()
    n=len(order)
    stages=[lambda i:S[i].r1(),lambda i:S[i].r2(),lambda i:S[i].r3(),lambda i:end(i)]
    for t in range(n+3):
        for s in range(3,-1,-1):
            k=t-s
            if 0<=k<n: stages[s](order[k])
    close()
    for s in S: s.drain()

def scatter_all(sm,q,p,f1,f2):
    sds=jax.ShapeDtypeStruct
    V=pl.BlockSpec(memory_space=pltpu.VMEM); A=pl.BlockSpec(memory_space=pl.ANY)
    D=pltpu.SemaphoreType.DMA
    sc=[]
    for a,dt in ((sm,F32),(q,BF),(p,BF),(f1,BF),(f2,BF)):
        if a.ndim==5: sc+=scatter_scratch(a.shape[3],a.shape[4],dt)
        else: sc+=scatter_scratch(a.shape[2],a.shape[3]//2,dt)
    outs=[sds(sm.shape[3:],F32)]
    for a in (q,p,f1):
        r,n=a.shape[2]//2,a.shape[3]
        sc+=[pltpu.VMEM((2,r,n//2),F32),pltpu.VMEM((r,n//2),F32)]
        outs.append(sds((r,n),F32))
    outs.append(sds(f2.shape[3:],F32))
    return pl.pallas_call(scatter_kernel,in_specs=[A]*5,out_specs=[V]*5,out_shape=outs,
        scratch_shapes=sc+[D((5,10)),D((5,10)),D((5,)),D((5,)),D((5,))],
        compiler_params=pltpu.CompilerParams(collective_id=1,has_side_effects=True,vmem_limit_bytes=56<<20),name="scatter_all")(sm,q,p,f1,f2)
class Gather2:
    def __init__(self,view,ss,rs):
        self.view=view; self.ss=ss; self.rs=rs
        c,x,y,z=place()
        self.c=c; self.z=z; self.yx=y*2+x
        self.xn=y*2+1-x; self.yn=(1-y)*2+x; self.dg=(1-y)*2+1-x
        self.xd=dev(z,self.xn,c); self.yd=dev(z,self.yn,c); self.sd=dev(z,self.yx,1-c)
        self.sends=[]
    def at(self,k,yx,lane=None): return self.view(pl.ds(lax.rem(self.z+4-k,4),1),yx,self.c if lane is None else lane)
    def all(self,yx,lane=None): return self.view(pl.ds(0,4),yx,self.c if lane is None else lane)
    def _cp(self,src,dst,slot,d):
        return pltpu.make_async_remote_copy(src_ref=src,dst_ref=dst,send_sem=self.ss.at[slot],recv_sem=self.rs.at[slot],device_id=d,device_id_type=MESH)
    def send(self,src,dst,slot,d):
        cp=self._cp(src,dst,slot,d); cp.start(); self.sends.append(cp)
    def got(self,dst,slot,d): self._cp(dst,dst,slot,d).wait_recv()
    def near(self,src):
        self.send(src,self.at(0,self.yx),3,self.xd)
        self.send(src,self.at(0,self.yx),7,self.yd)
    def far(self,src):
        for k in (1,2,3): self.send(src,self.at(0,self.yx),k-1,dev(lax.rem(self.z+k,4),self.yx,self.c))
    def X0(self):
        r=self.at(0,self.xn); self.got(r,3,self.xd)
        self.send(r,r,11,self.yd)
        self.got(self.at(0,self.yn),7,self.yd)
    def Z(self,k):
        r=self.at(k,self.yx)
        self.got(r,k-1,dev(lax.rem(self.z+4-k,4),self.yx,self.c))
        self.send(r,r,3+k,self.xd); self.send(r,r,7+k,self.yd); self.send(r,r,14+k,self.sd)
    def X(self,k):
        a=self.at(k,self.xn); b=self.at(k,self.yn)
        self.got(a,3+k,self.xd)
        if k==1: self.send(a,a,11+k,self.yd)
        self.got(b,7+k,self.yd)
        if k!=1: self.send(b,b,11+k,self.xd)
        if k==2:
            for yx,s in ((self.xn,18),(self.yn,19)):
                r=self.all(yx); self.send(r,r,s,self.sd)
    def D(self):
        for k in (0,1,3,2):
            self.got(self.at(k,self.dg),11+k,self.yd if k<2 else self.xd)
        r=self.all(self.dg); self.send(r,r,20,self.sd)
    def F(self):
        o=1-self.c
        for k in (1,2,3): self.got(self.at(k,self.yx,o),14+k,self.sd)
        for yx,s in ((self.xn,18),(self.yn,19),(self.dg,20)): self.got(self.all(yx,o),s,self.sd)
    def drain(self):
        for cp in self.sends: cp.wait_send()

def gelu_parts(x):
    cdf=0.5+0.5*lax.erf(x*0.7071067811865476)
    e=jnp.exp2(x*x*(-0.5*1.4426950408889634))
    return x*cdf, cdf+x*e*0.3989422804014327

def row_stats(x):
    inv=1.0/x.shape[1]
    mean=jnp.sum(x,axis=1,keepdims=True)*inv
    c=x-mean
    var=jnp.sum(c*c,axis=1,keepdims=True)*inv
    return c,lax.rsqrt(var+eps_norm)

def by_sixteen(first,last,rows):
    step=next(k for k in (200,160,80) if k%16==0 and (last-first)%k==0)
    def body(i,_):
        for u in range(step//16): rows(pl.ds(pl.multiple_of(first+i*step+16*u,16),16))
        return 0
    lax.fori_loop(0,(last-first)//step,body,0)

def spread(each,total,cols):
    j=lax.broadcasted_iota(jnp.int32,(128,total),1); l=lax.broadcasted_iota(jnp.int32,(128,total),0)
    return jnp.where(j-cols*each==l,1.0,0.0).astype(BF)

def over(each,shape):
    j=lax.broadcasted_iota(jnp.int32,shape,1)
    return (j*((1<<22)//each+1))>>22

def settled(g1,r):
    return r+jnp.where(r>=400,-8*g1,jnp.where(r>=392,400*g1,0))

def segments(groups,offsets,pos):
    g=groups[0]
    length=jnp.where(g==0,P_SMALL,jnp.where(g==1,P_MID,P_LARGE))
    seg=jnp.full(pos.shape,-1,jnp.int32)
    for s in range(8):
        o=offsets[s]
        seg=jnp.where((pos>=o)&(pos<o+length),s,seg)
    return seg

def settle_rows(g1,read,write):
    def either(a,b): return [jnp.where(g1==1,u,w) for u,w in zip(a,b)]
    def body(i,_):
        r=pl.multiple_of(i*56,8)
        write(r,56,read(r,56)); return 0
    lax.fori_loop(0,7,body,0)
    write(392,8,either(read(792,8),read(392,8)))
    def body2(i,_):
        r=pl.multiple_of(400+i*40,8)
        write(r,40,either(read(pl.multiple_of(392+i*40,8),40),read(r,40))); return 0
    lax.fori_loop(0,10,body2,0)

FORWARD_ORDER=(
    96, 0, 1, 16, 32, 48, 17, 97, 200, 80, 4, 201, 98, 3, 21, 49, 5, 64, 33, 65, 99, 6, 50, 100, 2, 8, 7, 53, 20,
    81, 202, 51, 19, 203, 24, 37, 52, 9, 35, 204, 54, 36, 56, 34, 22, 40, 18, 55, 23, 10, 220, 230, 38, 39, 69,
    25, 231, 41, 26, 67, 68, 221, 72, 42, 66, 57, 232, 233, 222, 70, 71, 234, 85, 58, 83, 235, 84, 82, 73, 205,
    74, 240, 88, 241, 86, 242, 243, 87, 244, 245, 250, 251, 89, 252, 253, 90,
)

def forward_kernel(groups,offsets,v0,v1,v2,v3,v4,v5,v6,v7,v8,q_ref,p_ref,f1_ref,f2_ref,tok_r,cot_r,mask_ref,
        wq_o,wp_o,w1_o,w2_o,pr_o,n1_o,n2_o,ctx_o,pj_o,hid_o,dg_o,xa_o,xb_o,mid_o,pt2_o,gt_o,cs_o,vec_o,meta_o,
        gs,gq,gp,g1w,sq,sp,s1,bq,bp,b1,raw,mid,st,xa,xb,n1,nt_,pj,bias,ctx,n2,hid,dg,gt,cs,pt2,pst,sc,sm_ref,smf,mk,tok_ref,cot_ref,bqv,bf1,
        ss0,rs0,ssl,sss,srs,ss,rs,psem,osem,lsem):
    loads=[pltpu.make_async_copy(a,b,lsem.at[i]) for i,(a,b) in enumerate(((tok_r,tok_ref),(cot_r,cot_ref)))]
    for cp in loads: cp.start()
    smf[...]=jnp.zeros_like(smf)
    for i,r in enumerate((v0,v1,v2,v3,v4,v5,v6,v7,v8)):
        m=r.shape[0]
        smf[i:i+1,0:m]=r[...].astype(F32).reshape(1,m)
    sm_ref[...]=smf[...].astype(BF)
    greet()
    c,x,y,z=place(); yx=y*2+x
    sibd=dev(z,yx,1-c)
    first=[]
    def swap(src,dst,i):
        cp=pltpu.make_async_remote_copy(src_ref=src,dst_ref=dst,send_sem=ss0.at[i],recv_sem=rs0.at[i],device_id=sibd,device_id_type=MESH)
        cp.start(); first.append(cp)
    swap(sm_ref,gs.at[z,yx,c],0)
    swap(q_ref,sq,1); swap(p_ref,sp,2); swap(f1_ref,s1,3)
    swap(f2_ref,w2_o.at[z,yx,c],4)
    gs[z,yx,c]=sm_ref[...]
    own2=pltpu.make_async_copy(f2_ref,w2_o.at[z,yx,c],ssl.at[0]); own2.start()
    S=Gather(rows_view(gs),sss,srs)
    QA,QB,QC,Pj,F1=[Gather2(cols_view(r),ss.at[i],rs.at[i]) for i,r in enumerate((gq.at[0],gq.at[1],gq.at[2],gp,g1w))]
    F2=Gather2(rows_view(w2_o),ss.at[5],rs.at[5])
    outs=[]; lag=[]; used=[0]
    def put(src,dst):
        cp=pltpu.make_async_copy(src,dst,osem.at[used[0]]); cp.start(); outs.append(cp); used[0]+=1
    waited=set()
    def swapped(i):
        if i not in waited: waited.add(i); first[i].wait_recv()
    def build(own,sib,buf,dst):
        j=join(c,own,sib)
        buf[0]=j; dst[z,yx]=j
    def parts(ref,g): return jnp.concatenate([ref[:,o+256*g:o+256*g+256] for o in (0,768,1536)],axis=1)
    def half(b):
        h=b.shape[-1]//2
        return b.at[:,:,pl.ds(pl.multiple_of(c*h,128),h)]
    def near(n):
        if n=="F2": own2.wait(); F2.near(F2.at(0,yx)); return
        if n[0]=="Q":
            g="ABC".index(n[1]); swapped(1); build(parts(q_ref,g),parts(sq,g),bq.at[g],gq.at[g]); G[n].near(half(bq.at[g]))
        elif n=="P": swapped(2); build(p_ref[...],sp[...],bp,gp); Pj.near(half(bp))
        else: swapped(3); build(f1_ref[...],s1[...],b1,g1w); F1.near(half(b1))
    def far(n):
        if n=="F2": F2.far(F2.at(0,yx))
        elif n[0]=="Q": G[n].far(half(bq.at["ABC".index(n[1])]))
        else: G[n].far(half(bp if n=="P" else b1))
    G={"QA":QA,"QB":QB,"QC":QC,"P":Pj,"F1":F1,"F2":F2}
    def finish(n):
        if n=="F2": first[4].wait_recv()
        G[n].F()
        if n[0]=="Q": g="ABC".index(n[1]); put(gq.at[g],wq_o.at[g])
        elif n=="P": put(gp,wp_o)
        elif n=="F1": put(g1w,w1_o)
    def small(k):
        if k=="s": S.z_send(S.one(z))
        elif k=="Z": S.z_recv(); S.xy_send()
        elif k=="X": S.xy_recv()
        elif k=="D": S.diag_recv()
        else: first[0].wait_recv(); S.finish()
    g1=jnp.where(groups[0]==1,1,0)
    def setup(k):
        if k==0:
            loads[0].wait()
            raw[...]=tok_ref[...].astype(F32)
        segc=segments(groups,offsets,settled(g1,lax.broadcasted_iota(jnp.int32,(400,1),0)+400*k))
        meta_o[400*k:400*k+400,0:1]=jnp.where(segc>=0,1.0,0.0)
        segr=segments(groups,offsets,settled(g1,lax.broadcasted_iota(jnp.int32,(1,400),1)+400*k))
        bias[k]=jnp.where(segc==segr,0.0,-1e30)
    def vectors():
        X=gs[...].reshape(512,128)
        E=nn(X,spread(24,768,over(24,(128,768))))
        E=jnp.where(lax.broadcasted_iota(jnp.int32,(512,768),0)>>4==over(24,(512,768)),E,0.0).reshape(32,16,768)
        vec_o[...]=jnp.sum(E,axis=0)
        def wide(row,each,total):
            sel=jnp.where(lax.broadcasted_iota(jnp.int32,(32,512),1)==lax.broadcasted_iota(jnp.int32,(32,512),0)*16+row,1.0,0.0).astype(BF)
            e=nn(nn(sel,X).astype(BF),spread(each,total,over(each,(128,total))))
            e=jnp.where(lax.broadcasted_iota(jnp.int32,(32,total),0)==over(each,(32,total)),e,0.0)
            return jnp.sum(e,axis=0,keepdims=True)
        bqv[...]=wide(3,48,1536); bf1[...]=wide(7,96,3072)
    def norm_one():
        mask=jnp.broadcast_to(mask_ref[...].astype(F32).reshape(1,800),(8,800)).T
        mk[...]=mask[:,0:1]
        def write(r,n,v):
            t,m=v
            meta_o[pl.ds(r,n),1:2]=m
            mid[pl.ds(r,n),:]=jnp.where(m>0.0,vec_o[0:1,:],t)
        settle_rows(g1,lambda r,n:(raw[pl.ds(r,n),:],mk[pl.ds(r,n),:]),write)
        def rows(r):
            s=mid[r,:]
            st[r,:]=s.astype(BF)
            cc,rstd=row_stats(s)
            xh=cc*rstd
            xa[r,:]=xh.astype(BF); meta_o[r,2:3]=rstd
            n1[r,:]=(xh*vec_o[1:2,:]+vec_o[2:3,:]).astype(BF)
        by_sixteen(0,800,rows)
        put(xa,xa_o)
    def cotangents():
        loads[1].wait()
        raw[...]=cot_ref[...].astype(F32)
        def write2(r,n,v): mid[pl.ds(r,n),:]=v[0]
        settle_rows(g1,lambda r,n:(raw[pl.ds(r,n),:],),write2)
        def body(i,_):
            r=pl.ds(pl.multiple_of(i*80,16),80)
            v=mid[r,:]
            cs[r,:]=v.astype(BF); gt[r,:]=(v*meta_o[r,0:1]).astype(BF)
            return 0
        lax.fori_loop(0,10,body,0)
        put(cs,cs_o); put(gt,gt_o)
        nt_[...]=n1[...].T
        put(nt_,n1_o)
        lag.append(outs[-1])
    def qkv(g):
        r=nn(n1[...],gq[g].reshape(768,768))
        for k,o in enumerate((0,768,1536)):
            t=r[:,256*k:256*k+256]
            if k!=1: t=t+bqv[:,384*k+256*g:384*k+256*g+256]
            pj[:,o+256*g:o+256*g+256]=t.astype(BF)
        if g==2: put(pj,pj_o)
    lane=lax.broadcasted_iota(jnp.int32,(400,128),1)
    def where_of(t):
        return lax.rem(t,4)//2,2*(t//4)+lax.rem(t,2)
    def pcopy(t):
        b,p=where_of(t)
        return pltpu.make_async_copy(pst.at[lax.rem(t,2)],pr_o.at[b*6+p],psem.at[lax.rem(t,2)])
    def attend(t,_):
        b,p=where_of(t); s=lax.rem(t,2)
        r=pl.ds(pl.multiple_of(b*400,16),400)
        cc=lambda o: pl.ds(pl.multiple_of(o+p*128,128),128)
        @pl.when(t>=2)
        def _(): pcopy(t-2).wait()
        q=pj[r,cc(0)]; k=pj[r,cc(768)]; v=pj[r,cc(1536)]
        res=[]
        for j in range(2):
            qj=jnp.where((lane>=64)==(j==1),q,jnp.zeros_like(q))
            sc[j]=nt(qj,k)
        for j in range(2):
            for i in range(10):
                u=slice(40*i,40*i+40)
                t_=sc[j,u]*0.18033688011112042+bias[b,u]
                e=jnp.exp2(t_-jnp.max(t_,axis=1,keepdims=True))
                sc[j,u]=e*(1.0/jnp.sum(e,axis=1,keepdims=True))
        for j in range(2):
            pr=sc[j].astype(BF)
            pst[s,j]=pr
            res.append(nn(pr,v))
        ctx[r,cc(0)]=jnp.where(lane<64,res[0],res[1]).astype(BF)
        pcopy(t).start()
        return 0
    def proj():
        put(ctx,ctx_o)
        wpv=gp[...].reshape(768,768)
        def body(i,_):
            r=pl.ds(pl.multiple_of(i*400,16),400)
            mid[r,:]=st[r,:].astype(F32)+meta_o[r,0:1]*(nn(ctx[r,:],wpv)+vec_o[4:5,:])
            return 0
        lax.fori_loop(0,2,body,0)
        def rows(r):
            cc,rstd=row_stats(mid[r,:])
            xh=cc*rstd
            xb[r,:]=xh.astype(BF); meta_o[r,3:4]=rstd
            n2[r,:]=(xh*vec_o[5:6,:]+vec_o[6:7,:]).astype(BF)
        by_sixteen(0,800,rows)
        put(mid,mid_o); put(xb,xb_o)
        lag[0].wait(); outs[:]=[o for o in outs if o is not lag[0]]
        nt_[...]=n2[...].T
        put(nt_,n2_o)
    def mlp(i,_):
        cc=pl.ds(pl.multiple_of(i*512,128),512)
        a,d=gelu_parts(nn(n2[...],g1w[:,:,:,cc].reshape(768,512))+bf1[:,cc])
        hid[:,cc]=a.astype(BF); dg[:,cc]=d.astype(BF)
        return 0
    def grads(i,_):
        cc=pl.ds(pl.multiple_of(i*768,128),768)
        pt2[i]=tn(hid[:,cc],gt[...]).astype(BF).reshape(4,2,96,768)
        return 0
    chunks=("QA","QB","QC","P","F1","F2")
    k=0
    while k<len(FORWARD_ORDER):
        op=FORWARD_ORDER[k]; k+=1
        if op>=96 and op<200: small("sZXDF"[op-96])
        elif op<96:
            n=chunks[op//16]; g=G[n]; t=op%16
            if t==0: near(n)
            elif t==1: far(n)
            elif t==2: g.X0()
            elif t<6: g.Z(t-2)
            elif t<9: g.X(t-5)
            elif t==9: g.D()
            else: finish(n)
        elif op<220: (lambda:setup(0),lambda:setup(1),vectors,norm_one,cotangents,proj)[op-200]()
        elif op<230: qkv(op-220)
        else:
            a=b=op%10
            while k<len(FORWARD_ORDER) and FORWARD_ORDER[k]==op-a+b+1: b+=1; k+=1
            if op>=250:
                lax.fori_loop(a,b+1,grads,0)
                put(pt2.at[pl.ds(a,b+1-a)],pt2_o.at[pl.ds(a,b+1-a)])
            elif op<240: lax.fori_loop(2*a,2*b+2,attend,0)
            else:
                lax.fori_loop(a,b+1,mlp,0)
                if b==5:
                    put(hid,hid_o); put(dg,dg_o)
    pcopy(10).wait(); pcopy(11).wait()
    for cp in outs: cp.wait()
    for cp in first: cp.wait_send()
    for g in [S]+list(G.values()): g.drain()

def forward(groups,offsets,vectors,wq,wp,w1,w2,tok,cot,mask):
    sds=jax.ShapeDtypeStruct
    V=pl.BlockSpec(memory_space=pltpu.VMEM); A=pl.BlockSpec(memory_space=pl.ANY); M=pl.BlockSpec(memory_space=pltpu.SMEM)
    D=pltpu.SemaphoreType.DMA
    v=pltpu.VMEM
    R,W=tok.shape
    outs=[((3,4,4,48,768),BF),((4,4,48,768),BF),((4,4,48,3072),BF),((4,4,2,96,768),BF),((12,2,400,400),BF),
        ((W,R),BF),((W,R),BF),((R,W),BF),((R,3*W),BF),((R,4*W),BF),((R,4*W),BF),((R,W),BF),((R,W),BF),((R,W),F32),((4,4,2,96,768),BF),((R,W),BF),((R,W),BF),
        ((16,W),F32),((R,4),F32)]
    return pl.pallas_call(forward_kernel,
        in_specs=[M,M]+[V]*13+[A,A,V],out_specs=[A]*17+[V,V],out_shape=[sds(*o) for o in outs],
        scratch_shapes=[v((4,4,2,16,128),BF),v((3,4,4,48,768),BF),v((4,4,48,768),BF),v((4,4,48,3072),BF),
            v((24,2304),BF),v((24,768),BF),v((24,3072),BF),v((3,1,48,768),BF),v((1,48,768),BF),v((1,48,3072),BF),
            v((R,W),F32),v((R,W),F32),v((R,W),BF),v((R,W),BF),v((R,W),BF),v((R,W),BF),v((W,R),BF),v((R,3*W),BF),v((2,400,400),F32),v((R,W),BF),v((R,W),BF),
            v((R,4*W),BF),v((R,4*W),BF),v((R,W),BF),v((R,W),BF),v((4,4,2,96,768),BF),v((2,2,400,400),BF),v((2,400,400),F32),v((16,128),BF),v((16,128),F32),v((800,1),F32),v((R,W),BF),v((R,W),BF),v((1,2*W),F32),v((1,4*W),F32),
            D((5,)),D((5,)),D((1,)),D((14,)),D((14,)),D((6,21)),D((6,21)),D((2,)),D((24,)),D((2,))],
        compiler_params=pltpu.CompilerParams(collective_id=0,has_side_effects=True,vmem_limit_bytes=60<<20),name="forward")(
        groups,offsets,*vectors,wq,wp,w1,w2,tok,cot,mask)

class Reduce:
    def __init__(self,give,a,s,rxa,ryb,rx,ry,b,rz,ss,rs):
        self.give=give; self.a=a; self.s=s; self.rxa=rxa; self.ryb=ryb; self.rx=rx; self.ry=ry; self.b=b; self.rz=rz
        self.ss=ss; self.rs=rs
        c,x,y,z=place()
        self.c=c; self.z=z; self.yx=y*2+x
        self.xn=y*2+1-x; self.yn=(1-y)*2+x; self.dg=(1-y)*2+1-x
        self.xd=dev(z,self.xn,c); self.yd=dev(z,self.yn,c); self.sd=dev(z,self.yx,1-c)
        self.cps={}
    def send(self,src,dst,slot,d):
        cp=pltpu.make_async_remote_copy(src_ref=src,dst_ref=dst,send_sem=self.ss.at[slot],recv_sem=self.rs.at[slot],device_id=d,device_id_type=MESH)
        cp.start(); self.cps[slot]=cp
    def r0(self): self.send(self.give,self.s,0,self.sd)
    def add(self,n,z0,yx,other):
        t=self.a(pl.ds(z0,n),yx)
        t[...]=t[...]+other[...]
    def r1(self):
        self.cps[0].wait_recv()
        def own(yx): self.add(4,0,yx,self.s.at[:,yx])
        own(self.dg)
        self.send(self.a(pl.ds(0,2),self.dg),self.rxa,1,self.xd)
        self.send(self.a(pl.ds(2,2),self.dg),self.ryb,2,self.yd)
        own(self.xn)
        self.send(self.a(pl.ds(0,2),self.xn),self.rx.at[pl.ds(0,2)],3,self.xd)
        own(self.yn)
        self.send(self.a(pl.ds(2,2),self.yn),self.ry.at[pl.ds(2,2)],4,self.yd)
        own(self.yx)
    def r2(self):
        self.cps[1].wait_recv()
        self.add(2,0,self.yn,self.rxa)
        self.send(self.a(pl.ds(0,2),self.yn),self.ry.at[pl.ds(0,2)],6,self.yd)
        self.cps[2].wait_recv()
        self.add(2,2,self.xn,self.ryb)
        self.send(self.a(pl.ds(2,2),self.xn),self.rx.at[pl.ds(2,2)],5,self.xd)
    def r3(self):
        for s in (3,4,5,6): self.cps[s].wait_recv()
        for i in range(4):
            k=pl.ds(i,1)
            self.b[k]=(self.a(k,self.yx)[...].astype(F32)+self.rx[k].astype(F32)+self.ry[k].astype(F32)).astype(BF)
        for k in (1,2,3):
            zz=lax.rem(self.z+k,4)
            self.send(self.b.at[zz],self.rz.at[k-1],6+k,dev(zz,self.yx,self.c))
    def total(self):
        t=self.b[self.z].astype(F32)
        for k in (1,2,3):
            self.cps[6+k].wait_recv()
            t=t+self.rz[k-1].astype(F32)
        return t
    def drain(self):
        for cp in self.cps.values(): cp.wait_send()

def eights(v):
    return jnp.sum(v.reshape(v.shape[0]//8,8,v.shape[1]),axis=0)

class Total:
    def __init__(self,v,r,ss,rs):
        self.v=v; self.r=r; self.ss=ss; self.rs=rs; self.cps=[]
    def send(self,a,slot,d):
        cp=pltpu.make_async_remote_copy(src_ref=self.v.at[a],dst_ref=self.r.at[slot],send_sem=self.ss.at[slot],recv_sem=self.rs.at[slot],device_id=d,device_id_type=MESH)
        cp.start(); self.cps.append(cp)
    def stage(self,k):
        c,x,y,z=place(); yx=y*2+x
        if k==0: self.send(0,0,dev(z,yx,1-c))
        elif k==1:
            self.cps[0].wait_recv(); self.v[1]=self.v[0]+self.r[0]
            self.send(1,1,dev(z,y*2+1-x,c)); self.send(1,2,dev(z,(1-y)*2+x,c)); self.send(1,3,dev(z,(1-y)*2+1-x,c))
        elif k==2:
            for h in (1,2,3): self.cps[h].wait_recv()
            self.v[2]=self.v[1]+self.r[1]+(self.r[2]+self.r[3])
            for h in (1,2,3): self.send(2,3+h,dev(lax.rem(z+h,4),yx,c))
        else:
            for h in (1,2,3): self.cps[3+h].wait_recv()
            self.sum=self.v[2]+self.r[4]+self.r[5]+self.r[6]
    def drain(self):
        for cp in self.cps: cp.wait_send()

BACKWARD_ORDER=(
    16, 200, 240, 241, 242, 0, 17, 243, 220, 221, 222, 32, 1, 64, 223, 201, 18, 33, 202, 80, 48, 2, 203, 34, 204,
    19, 96, 81, 250, 97, 3, 49, 251, 35, 230, 252, 112, 98, 82, 50, 65, 253, 113, 99, 231, 128, 83, 254, 51, 66,
    255, 114, 232, 176, 129, 67, 115, 144, 177, 205, 130, 4, 68, 145, 100, 178, 206, 146, 131, 207, 160, 36, 84,
    161, 147, 208, 116, 162, 209, 179, 148, 52, 20, 132, 163,
)

def backward_kernel(w2_r,w1_r,wp_r,wq_r,pr_r,n1_r,n2_r,ctx_r,pj_r,hid_r,dg_r,xa_r,xb_r,mid_r,pt2_r,gt_r,cs_r,vec,meta,
        out_o,tok_o,sm_o,oq,op_,o1,o2,
        w2,w1,wp,gp,pj,mid,gf,nt_,tmp,ctx,gt,gb,pst,acc,accb,
        a2,s2,xa2,yb2,x2,y2,b2,z2,part,sb,xab,ybb,xb,yb,bb,zb,fb,frb,vs,vr,us,ur,
        lsem,psem,osem,rss,rrs,fss,frs,vss,vrs,uss,urs):
    greet()
    c,x,y,z=place(); yx=y*2+x
    sibd=dev(z,yx,1-c)
    loads={}; held=set()
    def get(name,src,dst):
        cp=pltpu.make_async_copy(src,dst,lsem.at[len(loads)]); cp.start(); loads[name]=cp
    def have(*names):
        for n in names:
            if n not in held: held.add(n); loads[n].wait()
    C2=[Reduce(pt2_r.at[:,:,1-c,h],lambda zs,q,h=h: a2.at[h,zs,q],s2.at[h],xa2.at[h],yb2.at[h],x2.at[h],y2.at[h],b2.at[h],z2.at[h],rss.at[h],rrs.at[h]) for h in range(2)]
    def sib_at(i): return sb.at[i] if i<5 else s2.at[(i-5)//2,:,:,:,pl.ds(384*((i-5)%2),384)]
    mine=pl.ds(pl.multiple_of(c*384,128),384); theirs=pl.ds(pl.multiple_of((1-c)*384,128),384)
    CH=[Reduce(part.at[i,:,:,:,theirs],lambda zs,q,i=i: part.at[i,zs,q,:,mine],sib_at(i),xab.at[i],ybb.at[i],xb.at[i],yb.at[i],bb.at[i],zb.at[i],rss.at[2+i],rrs.at[2+i]) for i in range(8)]
    F=CH[0:4]; PJ=CH[4]; QK=CH[5:8]
    get("gt",gt_r,gt)
    def tile(i):
        get("t%d"%i,w2_r.at[pl.ds(16*i,16)],w2.at[pl.ds(16*i,16)]); get("d%d"%i,dg_r.at[:,pl.ds(768*i,768)],gp.at[:,pl.ds(768*i,768)])
    tile(0); tile(1)
    ahead={240:lambda:(get("a2a",pt2_r.at[:,:,c,0],a2.at[0]),tile(2)),241:lambda:(tile(3),get("a2b",pt2_r.at[:,:,c,1],a2.at[1])),
        242:lambda:get("n2",n2_r,nt_),243:lambda:(get("cs",cs_r,tmp),get("w1",w1_r,w1)),220:lambda:(get("xb",xb_r,gb),get("wp",wp_r,wp)),
        221:lambda:get("ctx",ctx_r,ctx),222:lambda:get("pj",pj_r,pj)}
    acc[...]=jnp.zeros_like(acc)
    ends=[]
    def end(i):
        t=CH[i].total()
        fb[i,0]=t[:24]; fb[i,1]=t[24:]
        cp=pltpu.make_async_remote_copy(src_ref=fb.at[i,1-c],dst_ref=frb.at[i],send_sem=fss.at[i],recv_sem=frs.at[i],device_id=sibd,device_id_type=MESH)
        cp.start(); ends.append((i,cp))
    def end2(h): o2[48*h:48*h+48,:]=C2[h].total()
    def mlp(i,_):
        cc=pl.ds(pl.multiple_of(i*768,128),768)
        g=(nt(gt[...],w2[pl.ds(16*i,16)].reshape(768,768))*gp[:,cc].astype(F32)).astype(BF)
        gp[:,cc]=g
        accb[:,cc]=eights(g.astype(F32))
        return 0
    def w1grad(i):
        have("n2")
        if 220+i in ahead: ahead[220+i]()
        part[i]=nn(nt_[...],gp[:,768*i:768*i+768]).astype(BF).reshape(4,4,48,768)
        if i==3: get("n1",n1_r,nt_)
    def norm_back(i0,rows,col,gain,ka,kb,finish):
        def body(i,_):
            sums={}; later=[]
            def add(k,v): sums[k]=sums[k]+eights(v) if k in sums else eights(v)
            for u in range(5):
                r=pl.ds(pl.multiple_of(i0+(i*5+u)*16,16),16)
                g,xh,rstd=gf[r,:],rows[r,:].astype(F32),meta[r,col:col+1]
                add(ka,g*xh); add(kb,g)
                gx=g*gain
                m1=jnp.sum(gx,axis=1,keepdims=True)*(1.0/768); m2=jnp.sum(gx*xh,axis=1,keepdims=True)*(1.0/768)
                later+=finish(r,rstd*(gx-m1-xh*m2),add)
            for ref,r,v in later: ref[r,:]=v
            for k,v in sums.items(): acc[k]+=v
            return 0
        lax.fori_loop(0,25//5,body,0)
    def finish2(r,d,add):
        gm=tmp[r,:].astype(F32)+d
        v=(meta[r,0:1]*gm).astype(BF)
        add(4,v.astype(F32)); add(8,gt[r,:].astype(F32))
        return [(mid,r,gm),(gb,r,v)]
    def p10(k):
        have("w1","cs","xb")
        r=slice(400*k,400*k+400)
        gf[r,:]=nt(gp[r,:],w1[...].reshape(768,3072))
        norm_back(400*k,gb,3,vec[5:6,:],5,6,finish2)
        if k==1:
            get("hid",hid_r,gp); get("xa",xa_r,tmp)
            for g in range(3): get("wq%d"%g,wq_r.at[g],w1.at[:,:,:,pl.ds(768*g,768)])
    gc=gt
    def gctx():
        have("wp")
        gc[...]=nt(gb[...],wp[...].reshape(768,768)).astype(BF)
        pcopy(0).start()
    def wpgrad():
        have("ctx")
        part[4]=tn(ctx[...],gb[...]).astype(BF).reshape(4,4,48,768)
    lane=lax.broadcasted_iota(jnp.int32,(400,128),1)
    def where_of(t):
        return lax.rem(t,4)//2,2*(t//4)+lax.rem(t,2)
    def pcopy(t):
        b,p=where_of(t)
        return pltpu.make_async_copy(pr_r.at[b*6+p],pst.at[lax.rem(t,2)],psem.at[lax.rem(t,2)])
    def attend(t,_):
        b,p=where_of(t); s=lax.rem(t,2)
        r=pl.ds(pl.multiple_of(b*400,16),400)
        cc=lambda o: pl.ds(pl.multiple_of(o+p*128,128),128)
        pcopy(t).wait()
        @pl.when(t<11)
        def _(): pcopy(t+1).start()
        q=pj[r,cc(0)]; k=pj[r,cc(768)]; v=pj[r,cc(1536)]; g=gc[r,cc(0)]
        gx=g.astype(F32)*ctx[r,cc(0)].astype(F32)
        dq=[];dk=[];dv=[]
        for j in range(2):
            own=(lane>=64)==(j==1)
            zero=jnp.zeros_like(q)
            qj=jnp.where(own,q,zero); gj=jnp.where(own,g,zero)
            di=jnp.sum(jnp.where(own,gx,0.0),axis=1,keepdims=True)
            pr=pst[s,j]
            ds=(pr.astype(F32)*(nt(gj,v)-di)).astype(BF)
            dq.append(nn(ds,k)); dk.append(tn(ds,qj)); dv.append(tn(pr,gj))
        pj[r,cc(0)]=(jnp.where(lane<64,dq[0],dq[1])*0.125).astype(BF)
        pj[r,cc(768)]=((dk[0]+dk[1])*0.125).astype(BF)
        pj[r,cc(1536)]=(dv[0]+dv[1]).astype(BF)
        return 0
    def group(r,g): return jnp.concatenate([pj[r,o+256*g:o+256*g+256] for o in (0,768,1536)],axis=1)
    def qkvgrad(g):
        if g==0: have("n1")
        cols=group(slice(None),g)
        acc[3,:,256*g:256*g+256]=eights(cols[:,:256].astype(F32)); acc[7,:,256*g:256*g+256]=eights(cols[:,512:].astype(F32))
        part[5+g]=nn(nt_[...],cols).astype(BF).reshape(4,4,48,768)
        if g==2:
            for k in range(6): us[0,k:k+1,:]=jnp.sum(acc[3+k],axis=0,keepdims=True)
            for k in range(4): us[0,6+k:7+k,:]=jnp.sum(accb[:,768*k:768*k+768],axis=0,keepdims=True)
            us[0,10:16,:]=jnp.zeros((6,768),F32)
    def finish1(r,d,add):
        gs=mid[r,:]+d
        m=meta[r,1:2]>0.0
        add(0,jnp.where(m,gs,0.0))
        return [(mid,r,jnp.where(m,0.0,gs))]
    stores=[]
    def put(src,dst):
        cp=pltpu.make_async_copy(src,dst,osem.at[len(stores)]); cp.start(); stores.append(cp)
    def back(i):
        if i==0: have("xa","wq0","wq1","wq2")
        r=slice(400*i,400*i+400)
        gf[r,:]=sum(nt(group(r,g),w1[:,:,:,768*g:768*g+768].reshape(768,768)) for g in range(3))
        norm_back(400*i,tmp,2,vec[1:2,:],1,2,finish1)
        if i==1: put(mid,tok_o); get("mid2",mid_r,gf)
    def fin():
        for k in range(3): vs[0,k:k+1,:]=jnp.sum(acc[k],axis=0,keepdims=True)
        vs[0,3:8,:]=jnp.zeros((5,768),F32)
    def outp(i):
        if i==0: have("hid","mid2")
        r=slice(400*i,400*i+400)
        gf[r,:]=gf[r,:]+meta[r,0:1]*(nn(gp[r,:],w2[...].reshape(3072,768))+vec[8:9,:])
        put(gf.at[pl.ds(400*i,400)],out_o.at[pl.ds(400*i,400)])
    sums=[Total(vs,vr,vss,vrs),Total(us,ur,uss,urs)]
    plain=(lambda:None,lambda:p10(0),lambda:p10(1),gctx,wpgrad,lambda:back(0),lambda:back(1),fin,lambda:outp(0),lambda:outp(1))
    k=0
    while k<len(BACKWARD_ORDER):
        op=BACKWARD_ORDER[k]; k+=1
        i,t=op//16,op%16
        if i<10:
            if t==4:
                if i<2: end2(i)
                else: end(i-2)
            else:
                if i<2 and t==1: have(("a2a","a2b")[i])
                r=(C2+CH)[i]
                (r.r0,r.r1,r.r2,r.r3)[t]()
        elif i<12: sums[i-10].stage(t)
        elif op<220: plain[op-200]()
        elif op<230: w1grad(op-220)
        elif op<240: qkvgrad(op-230)
        else:
            a=b=op%10
            while k<len(BACKWARD_ORDER) and BACKWARD_ORDER[k]==op-a+b+1: b+=1; k+=1
            if op<250:
                have("gt")
                for i in range(a,b+1):
                    have("t%d"%i,"d%d"%i); ahead[240+i]()
                    lax.fori_loop(i,i+1,mlp,0)
            else:
                if a==0: have("pj")
                lax.fori_loop(2*a,2*b+2,attend,0)
    vt,ut=sums[0].sum,sums[1].sum
    me=lax.axis_index("dp")
    def turn(v,by): return pltpu.roll(v,lax.rem(768-by,768),1)[:,:128]
    eight=lambda v: jnp.concatenate([v]*8,axis=0)
    sm_o[0:8,:]=turn(vt,24*me)
    t=turn(ut,24*me)
    sm_o[4:7,:]=t[1:4]; sm_o[8:9,:]=t[5:6]
    sm_o[3:4,:]=turn(eight(jnp.where(me>=16,ut[4:5],ut[0:1])),48*lax.rem(me,16))[0:1]
    k8=me//8
    pick=jnp.where(k8==0,ut[6:7],jnp.where(k8==1,ut[7:8],jnp.where(k8==2,ut[8:9],ut[9:10])))
    sm_o[7:8,:]=turn(eight(pick),96*lax.rem(me,8))[0:1]
    for i,cp in ends:
        cp.wait_recv()
        own=fb[i,c]; oth=frb[i]
        lo=jnp.where(c==0,own,oth); hi=jnp.where(c==0,oth,own)
        if i<4: o1[:,768*i:768*i+384]=lo; o1[:,768*i+384:768*i+768]=hi
        elif i==4: op_[:,:384]=lo; op_[:,384:]=hi
        else:
            g=256*(i-5)
            oq[:,g:g+256]=lo[:,:256]; oq[:,768+g:768+g+128]=lo[:,256:]
            oq[:,768+g+128:768+g+256]=hi[:,:128]; oq[:,1536+g:1536+g+256]=hi[:,128:]
        cp.wait_send()
    for cp in stores: cp.wait()
    for q in C2+CH+sums: q.drain()

def backward(w2,w1,wp,wq,pr,n1,n2,ctx,pj,hid,dg,xa,xb,mid,pt2,gt,cs,vec,meta):
    sds=jax.ShapeDtypeStruct
    V=pl.BlockSpec(memory_space=pltpu.VMEM); A=pl.BlockSpec(memory_space=pl.ANY)
    D=pltpu.SemaphoreType.DMA
    v=pltpu.VMEM
    W,R=n1.shape
    scr=[v((64,48,W),BF),v((4,4,48,4*W),BF),v((4,4,48,W),BF),v((R,4*W),BF),v((R,3*W),BF),v((R,W),F32),v((R,W),F32),v((W,R),BF),
        v((R,W),BF),v((R,W),BF),v((R,W),BF),v((R,W),BF),v((2,2,400,400),BF),v((9,8,W),F32),v((8,4*W),F32)]
    def rs(n,r,w,own):
        o=[v((n,4,4,r,own),BF),v((min(n,5),4,4,r,w),BF),v((n,2,r,w),BF),v((n,2,r,w),BF),v((n,4,r,w),BF),v((n,4,r,w),BF),v((n,4,r,w),BF),v((n,3,r,w),BF)]
        return o
    scr+=rs(2,48,W,W)+rs(8,48,W//2,W)
    scr+=[v((8,2,24,W//2),F32),v((8,24,W//2),F32),v((3,8,W),F32),v((7,8,W),F32),v((3,16,W),F32),v((7,16,W),F32)]
    scr+=[D((28,)),D((2,)),D((3,)),D((10,10)),D((10,10)),D((8,)),D((8,))]+[D((7,))]*4
    outs=[((R,W),F32),((R,W),F32),((16,128),F32),((24,3*W),F32),((24,W),F32),((24,4*W),F32),((96,W),F32)]
    return pl.pallas_call(backward_kernel,in_specs=[A]*17+[V]*2,out_specs=[A,A]+[V]*5,out_shape=[sds(*o) for o in outs],scratch_shapes=scr,
        compiler_params=pltpu.CompilerParams(collective_id=1,has_side_effects=True,vmem_limit_bytes=63<<20),name="backward")(
        w2,w1,wp,wq,pr,n1,n2,ctx,pj,hid,dg,xa,xb,mid,pt2,gt,cs,vec,meta)

def settle_back_kernel(groups,out_r,tok_r,sm,q_r,p_r,w1_r,w2_r,out_o,tok_o,q_o,p_o,w1_o,w2_o,v0,v1,v2,v3,v4,v5,v6,v7,v8,buf,ob,tb,qb,pb,b1,b2,sem):
    pairs=((tok_r,tb),(out_r,buf),(w1_r,b1),(q_r,qb),(w2_r,b2),(p_r,pb))
    loads=[pltpu.make_async_copy(a,b,sem.at[i]) for i,(a,b) in enumerate(pairs)]
    for cp in loads: cp.start()
    moved=groups[0]==1
    one=[pltpu.make_async_copy(tb,tok_o,sem.at[6])]
    three=[pltpu.make_async_copy(tb.at[pl.ds(a,n)],tok_o.at[pl.ds(b,n)],sem.at[7+i]) for i,(a,b,n) in enumerate(((0,0,392),(400,392,400),(392,792,8)))]
    for i,v in enumerate((v0,v1,v2,v3,v4,v5,v6,v7,v8)):
        m=v.shape[0]
        v[...]=sm[i:i+1,0:m].reshape(m)
    loads[0].wait()
    @pl.when(moved)
    def _():
        for cp in three: cp.start()
    @pl.when(jnp.logical_not(moved))
    def _():
        for cp in one: cp.start()
    loads[1].wait()
    ob[0:384]=buf[0:384].astype(BF)
    a=buf[384:800]
    b=jnp.concatenate([buf[384:392],buf[400:800],buf[392:400]],axis=0)
    ob[384:800]=jnp.where(moved,b,a).astype(BF)
    stores=[pltpu.make_async_copy(ob,out_o,sem.at[10])]
    stores[0].start()
    for i,(b,o) in enumerate(((b1,w1_o),(qb,q_o),(b2,w2_o),(pb,p_o))):
        loads[2+i].wait()
        cp=pltpu.make_async_copy(b,o,sem.at[11+i]); cp.start(); stores.append(cp)
    for cp in stores: cp.wait()
    @pl.when(moved)
    def _():
        for cp in three: cp.wait()
    @pl.when(jnp.logical_not(moved))
    def _():
        for cp in one: cp.wait()

def settle_back(groups,sizes,out,tok,sm,q,p,w1,w2):
    sds=jax.ShapeDtypeStruct
    V=pl.BlockSpec(memory_space=pltpu.VMEM); A=pl.BlockSpec(memory_space=pl.ANY); M=pl.BlockSpec(memory_space=pltpu.SMEM)
    v=pltpu.VMEM
    return pl.pallas_call(settle_back_kernel,in_specs=[M,A,A,V,A,A,A,A],out_specs=[A]*6+[V]*len(sizes),
        out_shape=[sds(out.shape,BF)]+[sds(a.shape,F32) for a in (tok,q,p,w1,w2)]+[sds((m,),F32) for m in sizes],
        scratch_shapes=[v(out.shape,F32),v(out.shape,BF)]+[v(a.shape,F32) for a in (tok,q,p,w1,w2)]+[pltpu.SemaphoreType.DMA((15,))],
        compiler_params=pltpu.CompilerParams(vmem_limit_bytes=60<<20),name="settle_back")(groups,out,tok,sm,q,p,w1,w2)

def normalize(values, gain, shift):
    center = values - jnp.mean(values, axis=-1, keepdims=True)
    spread = jnp.mean(center * center, axis=-1, keepdims=True)
    return center * lax.rsqrt(spread + eps_norm) * gain + shift

def activate(values):
    return jax.nn.gelu(values, approximate=False)

def segment_rows(groups, offsets, rows):
    lengths = jnp.where(groups == 0, P_SMALL, jnp.where(groups == 1, P_MID, P_LARGE)).astype(jnp.int32)
    positions = jnp.arange(rows, dtype=jnp.int32)
    inside = (positions[None, :] >= offsets[:, None]) & (positions[None, :] < offsets[:, None] + lengths[:, None])
    labels = jnp.arange(1, offsets.shape[0] + 1, dtype=jnp.int32)
    return jnp.sum(jnp.where(inside, labels[:, None], 0), axis=0) - 1

def settle(mid, rows):
    half = rows.shape[0] // 2
    cut = P_MID * (half // P_MID)
    gap = half - cut
    end = rows.shape[0] - gap
    moved = jnp.concatenate([rows[:cut], rows[end:], rows[cut:end]], axis=0)
    return jnp.where(mid, moved, rows)

def unsettle(mid, rows):
    half = rows.shape[0] // 2
    cut = P_MID * (half // P_MID)
    gap = half - cut
    moved = jnp.concatenate([rows[:cut], rows[half:], rows[cut:half]], axis=0)
    return jnp.where(mid, moved, rows)

def shards(n, tokens, mask_bits, groups, offsets, mask_token, ln1_gain, ln1_bias, w_qkv, b_qv, w_proj, b_proj,
           ln2_gain, ln2_bias, w_fc1, b_fc1, w_fc2, b_fc2, cotangent):
    vectors = (mask_token, ln1_gain, ln1_bias, b_qv, b_proj, ln2_gain, ln2_bias, b_fc1, b_fc2)
    sizes = [v.shape[0] for v in vectors]
    places = [sum(sizes[:i]) for i in range(len(sizes) + 1)]
    small_all = lax.all_gather(jnp.concatenate(vectors), "dp", axis=0, tiled=False)
    full_qkv, full_proj, full_fc1, full_fc2 = [
        lax.all_gather(w, "dp", axis=0, tiled=True) for w in (w_qkv, w_proj, w_fc1, w_fc2)]
    token_mask, gain_one, shift_one, bias_qv, bias_proj, gain_two, shift_two, bias_one, bias_two = [
        small_all[:, places[i]:places[i + 1]].reshape(-1).astype(F32) for i in range(len(sizes))]
    rows, width = tokens.shape
    half = rows // 2
    mid = groups[0] == 1
    tokens = settle(mid, tokens)
    cotangent = settle(mid, cotangent)
    mask_bits = settle(mid, mask_bits)
    segment = settle(mid, segment_rows(groups, offsets, rows))
    valid_col = (segment >= 0).astype(F32)[:, None]
    halves = segment.reshape(2, half)
    bias = jnp.where(halves[:, :, None] == halves[:, None, :], 0.0, -1e30).astype(F32)
    masked_rows = (mask_bits == 1)[:, None]
    start = jnp.where(masked_rows, token_mask[None, :], tokens.astype(F32))
    normed_one = normalize(start, gain_one, shift_one).astype(BF)
    full_bias = jnp.concatenate([bias_qv[:width], jnp.zeros((width,), F32), bias_qv[width:]])
    projected = (jnp.dot(normed_one, full_qkv, preferred_element_type=F32) + full_bias).astype(BF)
    context_low, probs = attn_fwd(projected, bias)
    middle = start + valid_col * (jnp.dot(context_low, full_proj, preferred_element_type=F32) + bias_proj)
    normed_two = normalize(middle, gain_two, shift_two).astype(BF)
    hidden_pre = jnp.dot(normed_two, full_fc1, preferred_element_type=F32) + bias_one
    hidden_low = activate(hidden_pre).astype(BF)
    result = middle + valid_col * (jnp.dot(hidden_low, full_fc2, preferred_element_type=F32) + bias_two)
    output = unsettle(mid, result.astype(BF))
    upstream = cotangent.astype(F32)
    grad_two = (valid_col * upstream).astype(BF)
    grad_wfc2 = tn(hidden_low, grad_two)
    grad_bfc2 = jnp.sum(grad_two.astype(F32), axis=0)
    grad_hidden = nt(grad_two, full_fc2)
    _, gelu_back = jax.vjp(activate, hidden_pre)
    grad_pre = gelu_back(grad_hidden)[0].astype(BF)
    grad_wfc1 = tn(normed_two, grad_pre)
    grad_bfc1 = jnp.sum(grad_pre.astype(F32), axis=0)
    grad_normed_two = nt(grad_pre, full_fc1)
    _, norm_back_two = jax.vjp(normalize, middle, gain_two, shift_two)
    grad_mid_part, grad_gain_two, grad_shift_two = norm_back_two(grad_normed_two)
    grad_middle = upstream + grad_mid_part
    grad_branch = (valid_col * grad_middle).astype(BF)
    grad_wproj = tn(context_low, grad_branch)
    grad_bproj = jnp.sum(grad_branch.astype(F32), axis=0)
    grad_context = nt(grad_branch, full_proj).astype(BF)
    dq, dk, dv = attn_bwd(projected, grad_context, context_low, probs)
    grad_projected = jnp.concatenate([dq, dk, dv], axis=1)
    grad_wqkv = tn(normed_one, grad_projected)
    grad_bqv = jnp.concatenate([jnp.sum(dq.astype(F32), axis=0), jnp.sum(dv.astype(F32), axis=0)])
    grad_normed_one = nt(grad_projected, full_qkv)
    _, norm_back_one = jax.vjp(normalize, start, gain_one, shift_one)
    grad_start_part, grad_gain_one, grad_shift_one = norm_back_one(grad_normed_one)
    grad_start = grad_middle + grad_start_part
    grad_token = jnp.sum(jnp.where(masked_rows, grad_start, 0.0), axis=0)
    grad_input = unsettle(mid, jnp.where(masked_rows, 0.0, grad_start))
    grad_vectors = (grad_token, grad_gain_one, grad_shift_one, grad_bqv, grad_bproj, grad_gain_two, grad_shift_two,
                    grad_bfc1, grad_bfc2)
    grad_small = jnp.concatenate([g.reshape(n, -1) for g in grad_vectors], axis=1)
    small_share = lax.psum_scatter(grad_small, "dp", scatter_dimension=0, tiled=False)
    share_qkv, share_proj, share_fc1, share_fc2 = [
        lax.psum_scatter(g, "dp", scatter_dimension=0, tiled=True)
        for g in (grad_wqkv, grad_wproj, grad_wfc1, grad_wfc2)]
    v = [small_share[places[i]:places[i + 1]] for i in range(len(sizes))]
    return (output, grad_input, v[0], v[1], v[2], share_qkv, v[3], share_proj, v[4], v[5], v[6], share_fc1, v[7],
            share_fc2, v[8])


def shards_fast(n, tokens, mask_bits, groups, offsets, mask_token, ln1_gain, ln1_bias, w_qkv, b_qv, w_proj, b_proj,
           ln2_gain, ln2_bias, w_fc1, b_fc1, w_fc2, b_fc2, cotangent):
    vectors = (mask_token, ln1_gain, ln1_bias, b_qv, b_proj, ln2_gain, ln2_bias, b_fc1, b_fc2)
    sizes = [v.shape[0] for v in vectors]
    (gq, gp, g1, g2, probs, normed_one, normed_two, context_low, projected, hidden_low, dgelu, rows_one, rows_two, middle, part2,
     grad_two, cots, vec, meta) = forward(groups, offsets, vectors, w_qkv, w_proj, w_fc1, w_fc2, tokens, cotangent, mask_bits)
    width = tokens.shape[1]
    shares = backward(
        g2.reshape(64, 48, width), g1, gp, gq, probs, normed_one, normed_two, context_low,
        projected, hidden_low, dgelu, rows_one, rows_two, middle, part2.reshape(4, 4, 2, 2, 48, width), grad_two, cots, vec, meta)
    output, grad_input, share_qkv, share_proj, share_fc1, share_fc2, *v = settle_back(groups, sizes, *shares)
    return (output, grad_input, v[0], v[1], v[2], share_qkv, v[3], share_proj, v[4], v[5], v[6], share_fc1, v[7],
            share_fc2, v[8])

def solution(mesh):
    row, flat = P("dp", None), P("dp")
    return jax.shard_map(
        functools.partial(shards_fast if mesh.shape["dp"] == 32 else shards, mesh.shape["dp"]),
        mesh=mesh,
        in_specs=(row, flat, flat, flat, flat, flat, flat, row, flat, row, flat, flat, flat, row, flat, row, flat, row),
        out_specs=(row, row, flat, flat, flat, row, flat, row, flat, flat, flat, row, flat, row, flat),
        check_vma=False,
    )
```

```python
import functools

import jax
import jax.numpy as jnp
from jax import lax
from jax.experimental import pallas as pl
from jax.experimental.pallas import tpu as pltpu
from jax.sharding import PartitionSpec as P

P_SMALL = 100
P_MID = 196
P_LARGE = 400
eps_norm = 1e-06

def nt(a,b): return lax.dot_general(a,b,(((1,),(1,)),((),())),preferred_element_type=jnp.float32)
def nn(a,b): return lax.dot_general(a,b,(((1,),(0,)),((),())),preferred_element_type=jnp.float32)
def tn(a,b): return lax.dot_general(a,b,(((0,),(0,)),((),())),preferred_element_type=jnp.float32)

def attn_fwd_kernel(bias_ref, q_ref, k_ref, v_ref, ctx_ref, p_ref):
    q=q_ref[...]; k=k_ref[...]; v=v_ref[...]
    rows,width=q.shape
    lane=lax.broadcasted_iota(jnp.int32,(rows,width),1)
    bias=bias_ref[0]
    outs=[]
    for j in range(2):
        mine=(lane>=64)==(j==1)
        qj=jnp.where(mine,q,jnp.zeros_like(q))
        s=nt(qj,k)*0.18033688011112042+bias
        m=jnp.max(s,axis=1,keepdims=True)
        e=jnp.exp2(s-m)
        l=jnp.sum(e,axis=1,keepdims=True)
        p=(e*(1.0/l)).astype(jnp.bfloat16)
        p_ref[0,0,j]=p
        outs.append(nn(p,v))
    ctx_ref[...]=jnp.where(lane<64,outs[0],outs[1]).astype(jnp.bfloat16)

def attn_fwd(proj,bias):
    rows=proj.shape[0]; half=rows//2; width=proj.shape[1]//3; pairs=width//128
    return pl.pallas_call(attn_fwd_kernel,grid=(2,pairs),
        in_specs=[pl.BlockSpec((1,half,half),lambda b,p:(b,0,0)),
                  pl.BlockSpec((half,128),lambda b,p:(b,p)),
                  pl.BlockSpec((half,128),lambda b,p:(b,p+pairs)),
                  pl.BlockSpec((half,128),lambda b,p:(b,p+2*pairs))],
        out_specs=[pl.BlockSpec((half,128),lambda b,p:(b,p)),
                   pl.BlockSpec((1,1,2,half,half),lambda b,p:(b,p,0,0,0))],
        out_shape=[jax.ShapeDtypeStruct((rows,width),jnp.bfloat16),
                   jax.ShapeDtypeStruct((2,pairs,2,half,half),jnp.bfloat16)],
        compiler_params=pltpu.CompilerParams(vmem_limit_bytes=40<<20),name="attn_fwd")(bias,proj,proj,proj)

def attn_bwd_kernel(q_ref,k_ref,v_ref,g_ref,c_ref,p_ref,dq_ref,dk_ref,dv_ref):
    q=q_ref[...]; k=k_ref[...]; v=v_ref[...]; g=g_ref[...]; c=c_ref[...]
    rows,width=q.shape
    lane=lax.broadcasted_iota(jnp.int32,(rows,width),1)
    gc=g.astype(jnp.float32)*c.astype(jnp.float32)
    dq=[];dk=[];dv=[]
    for j in range(2):
        mine=(lane>=64)==(j==1)
        zero=jnp.zeros_like(q)
        qj=jnp.where(mine,q,zero); gj=jnp.where(mine,g,zero)
        di=jnp.sum(jnp.where(mine,gc,0.0),axis=1,keepdims=True)
        p=p_ref[0,0,j]
        dp=nt(gj,v)
        ds=(p.astype(jnp.float32)*(dp-di)).astype(jnp.bfloat16)
        dq.append(nn(ds,k))
        dk.append(tn(ds,qj))
        dv.append(tn(p,gj))
    dq_ref[...]=(jnp.where(lane<64,dq[0],dq[1])*0.125).astype(jnp.bfloat16)
    dk_ref[...]=((dk[0]+dk[1])*0.125).astype(jnp.bfloat16)
    dv_ref[...]=(dv[0]+dv[1]).astype(jnp.bfloat16)

def attn_bwd(proj,gctx,ctx,p):
    rows=proj.shape[0]; half=rows//2; width=proj.shape[1]//3; pairs=width//128
    sp=lambda o: pl.BlockSpec((half,128),lambda b,p:(b,p+o*pairs))
    return pl.pallas_call(attn_bwd_kernel,grid=(2,pairs),
        in_specs=[sp(0),sp(1),sp(2),sp(0),sp(0),pl.BlockSpec((1,1,2,half,half),lambda b,p:(b,p,0,0,0))],
        out_specs=[sp(0)]*3,
        out_shape=[jax.ShapeDtypeStruct((rows,width),jnp.bfloat16)]*3,
        compiler_params=pltpu.CompilerParams(vmem_limit_bytes=40<<20),name="attn_bwd")(proj,proj,proj,gctx,ctx,p)
MESH=pl.DeviceIdType.MESH
F32=jnp.float32; BF=jnp.bfloat16

def place():
    me=lax.axis_index("dp")
    c=lax.rem(me,2); x=lax.rem(me//2,2); y=lax.rem(me//4,2); z=me//8
    return c,x,y,z
def dev(z,yx,c): return ((z*4+yx)*2+c,)

def greet():
    c,x,y,z=place(); yx=y*2+x
    bar=pltpu.get_barrier_semaphore()
    peers=[dev(z,yx,1-c),dev(z,y*2+1-x,c),dev(z,(1-y)*2+x,c)]+[dev(lax.rem(z+k,4),yx,c) for k in (1,2,3)]
    for p in peers: pl.semaphore_signal(bar,inc=1,device_id=p,device_id_type=MESH)
    pl.semaphore_wait(bar,len(peers))

class Gather:
    def __init__(self,view,ss,rs):
        self.view=view; self.ss=ss; self.rs=rs
        c,x,y,z=place()
        self.c=c; self.z=z; self.yx=y*2+x
        self.xn=y*2+1-x; self.yn=(1-y)*2+x; self.dg=(1-y)*2+1-x
        self.sends=[]
    def _cp(self,src,dst,slot,d):
        return pltpu.make_async_remote_copy(src_ref=src,dst_ref=dst,send_sem=self.ss.at[slot],recv_sem=self.rs.at[slot],device_id=d,device_id_type=MESH)
    def send(self,src,dst,slot,d):
        cp=self._cp(src,dst,slot,d); cp.start(); self.sends.append(cp)
    def got(self,dst,slot,d):
        self._cp(dst,dst,slot,d).wait_recv()
    def one(self,z): return self.view(pl.ds(z,1),self.yx,self.c)
    def z_send(self,src):
        for k in (1,2,3):
            self.send(src,self.one(self.z),k-1,dev(lax.rem(self.z+k,4),self.yx,self.c))
    def sib(self,ref,slot): self.send(ref,ref,slot,dev(self.z,self.yx,1-self.c))
    def z_recv(self):
        for k in (1,2,3):
            zz=lax.rem(self.z+4-k,4)
            self.got(self.one(zz),k-1,dev(zz,self.yx,self.c))
    def xy_send(self):
        r=self.view(pl.ds(0,4),self.yx,self.c)
        self.send(r,r,3,dev(self.z,self.xn,self.c))
        self.send(r,r,4,dev(self.z,self.yn,self.c))
        for k in (1,2,3): self.sib(self.one(lax.rem(self.z+4-k,4)),6+k)
    def xy_recv(self):
        rx=self.view(pl.ds(0,4),self.xn,self.c)
        self.got(rx,3,dev(self.z,self.xn,self.c))
        h=self.view(pl.ds(0,2),self.xn,self.c)
        self.send(h,h,5,dev(self.z,self.yn,self.c))
        ry=self.view(pl.ds(0,4),self.yn,self.c)
        self.got(ry,4,dev(self.z,self.yn,self.c))
        h=self.view(pl.ds(2,2),self.yn,self.c)
        self.send(h,h,6,dev(self.z,self.xn,self.c))
        self.sib(rx,10); self.sib(ry,11)
    def diag_recv(self):
        a=self.view(pl.ds(0,2),self.dg,self.c)
        self.got(a,5,dev(self.z,self.yn,self.c))
        self.sib(a,12)
        b=self.view(pl.ds(2,2),self.dg,self.c)
        self.got(b,6,dev(self.z,self.xn,self.c))
        self.sib(b,13)
    def finish(self):
        o=1-self.c; s=dev(self.z,self.yx,o)
        for k in (1,2,3): self.got(self.view(pl.ds(lax.rem(self.z+4-k,4),1),self.yx,o),6+k,s)
        self.got(self.view(pl.ds(0,4),self.xn,o),10,s)
        self.got(self.view(pl.ds(0,4),self.yn,o),11,s)
        self.got(self.view(pl.ds(0,2),self.dg,o),12,s)
        self.got(self.view(pl.ds(2,2),self.dg,o),13,s)
    def drain(self):
        for cp in self.sends: cp.wait_send()

def cols_view(ref):
    half=ref.shape[-1]//2
    def view(zs,yx,lane): return ref.at[zs,yx,:,pl.ds(pl.multiple_of(lane*half,128),half)]
    return view
def rows_view(ref):
    def view(zs,yx,lane): return ref.at[zs,yx,lane]
    return view

def join(c,own,sib):
    a=own.astype(F32); b=sib.astype(F32)
    return jnp.concatenate([jnp.where(c==0,a,b),jnp.where(c==0,b,a)],axis=0).astype(BF)

def gather_kernel(sm_ref,q_ref,p_ref,f1_ref,f2_ref,gs_ref,gq_ref,gp_ref,g1_ref,g2_ref,
        sq,sp,s1,bq,bp,b1,ss0,rs0,ssl,ss,rs):
    greet()
    c,x,y,z=place(); yx=y*2+x
    sibd=dev(z,yx,1-c)
    first=[]
    def swap(src,dst,i):
        cp=pltpu.make_async_remote_copy(src_ref=src,dst_ref=dst,send_sem=ss0.at[i],recv_sem=rs0.at[i],device_id=sibd,device_id_type=MESH)
        cp.start(); first.append(cp)
    swap(sm_ref,gs_ref.at[z,yx,c],0)
    swap(q_ref,sq,1); swap(p_ref,sp,2); swap(f1_ref,s1,3)
    swap(f2_ref,g2_ref.at[z,yx,c],4)
    gs=[Gather(rows_view(gs_ref),ss.at[0],rs.at[0]),Gather(cols_view(gq_ref),ss.at[1],rs.at[1]),Gather(cols_view(gp_ref),ss.at[2],rs.at[2]),
        Gather(cols_view(g1_ref),ss.at[3],rs.at[3]),Gather(rows_view(g2_ref),ss.at[4],rs.at[4])]
    local=[]
    def keep(src,dst,i):
        cp=pltpu.make_async_copy(src,dst,ssl.at[i]); cp.start(); local.append(cp)
    def half(b):
        h=b.shape[-1]//2
        return b.at[:,:,pl.ds(pl.multiple_of(c*h,128),h)]
    keep(sm_ref,gs_ref.at[z,yx,c],0)
    keep(f2_ref,g2_ref.at[z,yx,c],4)
    def begin(i):
        if i==0:
            local[0].wait(); gs[0].z_send(gs[0].one(z))
        elif i==4:
            local[1].wait(); gs[4].z_send(gs[4].one(z))
        else:
            own,sib,buf,dst={1:(q_ref,sq,bq,gq_ref),2:(p_ref,sp,bp,gp_ref),3:(f1_ref,s1,b1,g1_ref)}[i]
            first[i].wait_recv()
            buf[0]=join(c,own[...],sib[...])
            keep(buf,dst.at[pl.ds(z,1),yx],i)
            gs[i].z_send(half(buf))
    begin(0); begin(1)
    gs[0].z_recv(); gs[0].xy_send()
    begin(2)
    gs[1].z_recv(); local[2].wait(); gs[1].xy_send()
    begin(3)
    gs[0].xy_recv()
    gs[2].z_recv(); local[3].wait(); gs[2].xy_send()
    gs[0].diag_recv()
    gs[1].xy_recv()
    begin(4)
    gs[3].z_recv(); local[4].wait(); gs[3].xy_send()
    gs[2].xy_recv()
    gs[1].diag_recv()
    gs[2].diag_recv()
    gs[4].z_recv(); gs[4].xy_send()
    gs[3].xy_recv()
    gs[3].diag_recv()
    gs[4].xy_recv()
    gs[4].diag_recv()
    first[0].wait_recv(); first[4].wait_recv()
    for g in gs: g.finish()
    for cp in first: cp.wait_send()
    for g in gs: g.drain()

def gather_all(small,wq,wp,w1,w2):
    sds=jax.ShapeDtypeStruct
    nq,np_,n1,n2=wq.shape[1],wp.shape[1],w1.shape[1],w2.shape[1]
    r=wq.shape[0]; r2=w2.shape[0]
    V=pl.BlockSpec(memory_space=pltpu.VMEM); A=pl.BlockSpec(memory_space=pl.ANY)
    D=pltpu.SemaphoreType.DMA
    return pl.pallas_call(gather_kernel,
        in_specs=[V]*5,out_specs=[A]*5,
        out_shape=[sds((4,4,2)+small.shape,BF),sds((4,4,2*r,nq),BF),sds((4,4,2*r,np_),BF),sds((4,4,2*r,n1),BF),sds((4,4,2,r2,n2),BF)],
        scratch_shapes=[pltpu.VMEM((r,n),BF) for n in (nq,np_,n1)]+[pltpu.VMEM((1,2*r,n),BF) for n in (nq,np_,n1)]+
            [D((5,)),D((5,)),D((5,)),D((5,14)),D((5,14))],
        compiler_params=pltpu.CompilerParams(collective_id=0,has_side_effects=True,vmem_limit_bytes=16<<20),name="gather_all")(small,wq,wp,w1,w2)

class Scatter:
    def __init__(self,view,a,s,rxa,ryb,rx,ry,b,rz,ss,rs,ls):
        self.view=view; self.a=a; self.s=s; self.rxa=rxa; self.ryb=ryb; self.rx=rx; self.ry=ry; self.b=b; self.rz=rz
        self.ss=ss; self.rs=rs; self.ls=ls
        c,x,y,z=place()
        self.c=c; self.z=z; self.yx=y*2+x
        self.xn=y*2+1-x; self.yn=(1-y)*2+x; self.dg=(1-y)*2+1-x
        self.cps={}
    def send(self,src,dst,slot,d):
        cp=pltpu.make_async_remote_copy(src_ref=src,dst_ref=dst,send_sem=self.ss.at[slot],recv_sem=self.rs.at[slot],device_id=d,device_id_type=MESH)
        cp.start(); self.cps[slot]=cp
    def r0(self):
        self.send(self.view(1-self.c),self.s,0,dev(self.z,self.yx,1-self.c))
        self.loc=pltpu.make_async_copy(self.view(self.c),self.a,self.ls); self.loc.start()
    def r1(self):
        self.loc.wait(); self.cps[0].wait_recv()
        a,s=self.a,self.s
        def add(yx):
            def body(i,_):
                a[i,yx]=(a[i,yx].astype(F32)+s[i,yx].astype(F32)).astype(a.dtype)
                return 0
            lax.fori_loop(0,4,body,0)
        xd=dev(self.z,self.xn,self.c); yd=dev(self.z,self.yn,self.c)
        add(self.dg)
        self.send(a.at[pl.ds(0,2),self.dg],self.rxa,1,xd)
        self.send(a.at[pl.ds(2,2),self.dg],self.ryb,2,yd)
        add(self.xn)
        self.send(a.at[pl.ds(0,2),self.xn],self.rx.at[pl.ds(0,2)],3,xd)
        add(self.yn)
        self.send(a.at[pl.ds(2,2),self.yn],self.ry.at[pl.ds(2,2)],4,yd)
        add(self.yx)
    def r2(self):
        a=self.a
        xd=dev(self.z,self.xn,self.c); yd=dev(self.z,self.yn,self.c)
        self.cps[1].wait_recv()
        def body(i,_):
            a[i,self.yn]=(a[i,self.yn].astype(F32)+self.rxa[i].astype(F32)).astype(a.dtype)
            return 0
        lax.fori_loop(0,2,body,0)
        self.send(a.at[pl.ds(0,2),self.yn],self.ry.at[pl.ds(0,2)],6,yd)
        self.cps[2].wait_recv()
        def body(i,_):
            a[i+2,self.xn]=(a[i+2,self.xn].astype(F32)+self.ryb[i].astype(F32)).astype(a.dtype)
            return 0
        lax.fori_loop(0,2,body,0)
        self.send(a.at[pl.ds(2,2),self.xn],self.rx.at[pl.ds(2,2)],5,xd)
    def r3(self):
        for s in (3,4,5,6): self.cps[s].wait_recv()
        def body(i,_):
            self.b[i]=(self.a[i,self.yx].astype(F32)+self.rx[i].astype(F32)+self.ry[i].astype(F32)).astype(self.b.dtype)
            return 0
        lax.fori_loop(0,4,body,0)
        for k in (1,2,3):
            zz=lax.rem(self.z+k,4)
            self.send(self.b.at[zz],self.rz.at[k-1],6+k,dev(zz,self.yx,self.c))
    def r4(self):
        t=self.b[self.z].astype(F32)
        for k in (1,2,3):
            self.cps[6+k].wait_recv()
            t=t+self.rz[k-1].astype(F32)
        return t
    def drain(self):
        for cp in self.cps.values(): cp.wait_send()

def scatter_scratch(r,n,dt):
    V=pltpu.VMEM
    return [V((4,4,r,n),dt),V((4,4,r,n),dt),V((2,r,n),dt),V((2,r,n),dt),V((4,r,n),dt),V((4,r,n),dt),V((4,r,n),dt),V((3,r,n),dt)]

def scatter_kernel(sm_ref,q_ref,p_ref,f1_ref,f2_ref,os_ref,oq_ref,op_ref,o1_ref,o2_ref,*sc):
    bufs=[sc[8*i:8*i+8] for i in range(5)]
    fin=sc[40:46]; ss,rs,ls,fs,fr=sc[46:]
    greet()
    c,x,y,z=place(); yx=y*2+x
    def cv(ref):
        h=ref.shape[-1]//2
        return lambda lane: ref.at[:,:,:,pl.ds(pl.multiple_of(lane*h,128),h)]
    def rv(ref): return lambda lane: ref.at[:,:,lane]
    refs=[sm_ref,q_ref,p_ref,f1_ref,f2_ref]
    S=[Scatter((rv if i in (0,4) else cv)(refs[i]),*bufs[i],ss.at[i],rs.at[i],ls.at[i]) for i in range(5)]
    order=[4,3,2,1,0]
    sibd=dev(z,yx,1-c)
    ends=[]
    outs={1:oq_ref,2:op_ref,3:o1_ref}
    def end(i):
        t=S[i].r4()
        if i==0: os_ref[...]=t
        elif i==4: o2_ref[...]=t
        else:
            f,rf=fin[2*(i-1)],fin[2*(i-1)+1]
            r=t.shape[0]//2
            f[0]=t[:r]; f[1]=t[r:]
            cp=pltpu.make_async_remote_copy(src_ref=f.at[1-c],dst_ref=rf,send_sem=fs.at[i],recv_sem=fr.at[i],device_id=sibd,device_id_type=MESH)
            cp.start(); ends.append((i,cp))
    def close():
        for i,cp in ends:
            cp.wait_recv()
            f,rf=fin[2*(i-1)],fin[2*(i-1)+1]
            own=f[c]; oth=rf[...]
            o=outs[i]; h=own.shape[-1]
            o[:,:h]=jnp.where(c==0,own,oth); o[:,h:]=jnp.where(c==0,oth,own)
            cp.wait_send()
    for i in order: S[i].r0()
    n=len(order)
    stages=[lambda i:S[i].r1(),lambda i:S[i].r2(),lambda i:S[i].r3(),lambda i:end(i)]
    for t in range(n+3):
        for s in range(3,-1,-1):
            k=t-s
            if 0<=k<n: stages[s](order[k])
    close()
    for s in S: s.drain()

def scatter_all(sm,q,p,f1,f2):
    sds=jax.ShapeDtypeStruct
    V=pl.BlockSpec(memory_space=pltpu.VMEM); A=pl.BlockSpec(memory_space=pl.ANY)
    D=pltpu.SemaphoreType.DMA
    sc=[]
    for a,dt in ((sm,F32),(q,BF),(p,BF),(f1,BF),(f2,BF)):
        if a.ndim==5: sc+=scatter_scratch(a.shape[3],a.shape[4],dt)
        else: sc+=scatter_scratch(a.shape[2],a.shape[3]//2,dt)
    outs=[sds(sm.shape[3:],F32)]
    for a in (q,p,f1):
        r,n=a.shape[2]//2,a.shape[3]
        sc+=[pltpu.VMEM((2,r,n//2),F32),pltpu.VMEM((r,n//2),F32)]
        outs.append(sds((r,n),F32))
    outs.append(sds(f2.shape[3:],F32))
    return pl.pallas_call(scatter_kernel,in_specs=[A]*5,out_specs=[V]*5,out_shape=outs,
        scratch_shapes=sc+[D((5,10)),D((5,10)),D((5,)),D((5,)),D((5,))],
        compiler_params=pltpu.CompilerParams(collective_id=1,has_side_effects=True,vmem_limit_bytes=56<<20),name="scatter_all")(sm,q,p,f1,f2)
class Gather2:
    def __init__(self,view,ss,rs):
        self.view=view; self.ss=ss; self.rs=rs
        c,x,y,z=place()
        self.c=c; self.z=z; self.yx=y*2+x
        self.xn=y*2+1-x; self.yn=(1-y)*2+x; self.dg=(1-y)*2+1-x
        self.xd=dev(z,self.xn,c); self.yd=dev(z,self.yn,c); self.sd=dev(z,self.yx,1-c)
        self.sends=[]
    def at(self,k,yx,lane=None): return self.view(pl.ds(lax.rem(self.z+4-k,4),1),yx,self.c if lane is None else lane)
    def all(self,yx,lane=None): return self.view(pl.ds(0,4),yx,self.c if lane is None else lane)
    def _cp(self,src,dst,slot,d):
        return pltpu.make_async_remote_copy(src_ref=src,dst_ref=dst,send_sem=self.ss.at[slot],recv_sem=self.rs.at[slot],device_id=d,device_id_type=MESH)
    def send(self,src,dst,slot,d):
        cp=self._cp(src,dst,slot,d); cp.start(); self.sends.append(cp)
    def got(self,dst,slot,d): self._cp(dst,dst,slot,d).wait_recv()
    def near(self,src):
        self.send(src,self.at(0,self.yx),3,self.xd)
        self.send(src,self.at(0,self.yx),7,self.yd)
    def far(self,src):
        for k in (1,2,3): self.send(src,self.at(0,self.yx),k-1,dev(lax.rem(self.z+k,4),self.yx,self.c))
    def X0(self):
        r=self.at(0,self.xn); self.got(r,3,self.xd)
        self.send(r,r,11,self.yd)
        self.got(self.at(0,self.yn),7,self.yd)
    def Z(self,k):
        r=self.at(k,self.yx)
        self.got(r,k-1,dev(lax.rem(self.z+4-k,4),self.yx,self.c))
        self.send(r,r,3+k,self.xd); self.send(r,r,7+k,self.yd); self.send(r,r,14+k,self.sd)
    def X(self,k):
        a=self.at(k,self.xn); b=self.at(k,self.yn)
        self.got(a,3+k,self.xd)
        if k==1: self.send(a,a,11+k,self.yd)
        self.got(b,7+k,self.yd)
        if k!=1: self.send(b,b,11+k,self.xd)
        if k==2:
            for yx,s in ((self.xn,18),(self.yn,19)):
                r=self.all(yx); self.send(r,r,s,self.sd)
    def D(self):
        for k in (0,1,3,2):
            self.got(self.at(k,self.dg),11+k,self.yd if k<2 else self.xd)
        r=self.all(self.dg); self.send(r,r,20,self.sd)
    def F(self):
        o=1-self.c
        for k in (1,2,3): self.got(self.at(k,self.yx,o),14+k,self.sd)
        for yx,s in ((self.xn,18),(self.yn,19),(self.dg,20)): self.got(self.all(yx,o),s,self.sd)
    def drain(self):
        for cp in self.sends: cp.wait_send()

def gelu_parts(x):
    cdf=0.5+0.5*lax.erf(x*0.7071067811865476)
    e=jnp.exp2(x*x*(-0.5*1.4426950408889634))
    return x*cdf, cdf+x*e*0.3989422804014327

def row_stats(x):
    inv=1.0/x.shape[1]
    mean=jnp.sum(x,axis=1,keepdims=True)*inv
    c=x-mean
    var=jnp.sum(c*c,axis=1,keepdims=True)*inv
    return c,lax.rsqrt(var+eps_norm)

def by_sixteen(first,last,rows):
    step=next(k for k in (200,160,80) if k%16==0 and (last-first)%k==0)
    def body(i,_):
        for u in range(step//16): rows(pl.ds(pl.multiple_of(first+i*step+16*u,16),16))
        return 0
    lax.fori_loop(0,(last-first)//step,body,0)

def spread(each,total,cols):
    j=lax.broadcasted_iota(jnp.int32,(128,total),1); l=lax.broadcasted_iota(jnp.int32,(128,total),0)
    return jnp.where(j-cols*each==l,1.0,0.0).astype(BF)

def over(each,shape):
    j=lax.broadcasted_iota(jnp.int32,shape,1)
    return (j*((1<<22)//each+1))>>22

def settled(g1,r):
    return r+jnp.where(r>=400,-8*g1,jnp.where(r>=392,400*g1,0))

def segments(groups,offsets,pos):
    g=groups[0]
    length=jnp.where(g==0,P_SMALL,jnp.where(g==1,P_MID,P_LARGE))
    seg=jnp.full(pos.shape,-1,jnp.int32)
    for s in range(8):
        o=offsets[s]
        seg=jnp.where((pos>=o)&(pos<o+length),s,seg)
    return seg

def settle_rows(g1,read,write):
    def either(a,b): return [jnp.where(g1==1,u,w) for u,w in zip(a,b)]
    def body(i,_):
        r=pl.multiple_of(i*56,8)
        write(r,56,read(r,56)); return 0
    lax.fori_loop(0,7,body,0)
    write(392,8,either(read(792,8),read(392,8)))
    def body2(i,_):
        r=pl.multiple_of(400+i*40,8)
        write(r,40,either(read(pl.multiple_of(392+i*40,8),40),read(r,40))); return 0
    lax.fori_loop(0,10,body2,0)

FORWARD_ORDER=(
    96, 0, 1, 16, 32, 48, 17, 97, 200, 80, 4, 201, 98, 3, 21, 49, 5, 64, 33, 65, 99, 6, 50, 100, 2, 8, 7, 53, 20,
    81, 202, 51, 19, 203, 24, 37, 52, 9, 35, 204, 54, 36, 56, 34, 22, 40, 18, 55, 23, 10, 220, 230, 38, 39, 69,
    25, 231, 41, 26, 67, 68, 221, 72, 42, 66, 57, 232, 233, 222, 70, 71, 234, 85, 58, 83, 235, 84, 82, 73, 205,
    74, 240, 88, 241, 86, 242, 243, 87, 244, 245, 250, 251, 89, 252, 253, 90,
)

def forward_kernel(groups,offsets,v0,v1,v2,v3,v4,v5,v6,v7,v8,q_ref,p_ref,f1_ref,f2_ref,tok_r,cot_r,mask_ref,
        wq_o,wp_o,w1_o,w2_o,pr_o,n1_o,n2_o,ctx_o,pj_o,hid_o,dg_o,xa_o,xb_o,mid_o,pt2_o,gt_o,cs_o,vec_o,meta_o,
        gs,gq,gp,g1w,sq,sp,s1,bq,bp,b1,raw,mid,st,xa,xb,n1,nt_,pj,bias,ctx,n2,hid,dg,gt,cs,pt2,pst,sc,sm_ref,smf,mk,tok_ref,cot_ref,bqv,bf1,
        ss0,rs0,ssl,sss,srs,ss,rs,psem,osem,lsem):
    loads=[pltpu.make_async_copy(a,b,lsem.at[i]) for i,(a,b) in enumerate(((tok_r,tok_ref),(cot_r,cot_ref)))]
    for cp in loads: cp.start()
    smf[...]=jnp.zeros_like(smf)
    for i,r in enumerate((v0,v1,v2,v3,v4,v5,v6,v7,v8)):
        m=r.shape[0]
        smf[i:i+1,0:m]=r[...].astype(F32).reshape(1,m)
    sm_ref[...]=smf[...].astype(BF)
    greet()
    c,x,y,z=place(); yx=y*2+x
    sibd=dev(z,yx,1-c)
    first=[]
    def swap(src,dst,i):
        cp=pltpu.make_async_remote_copy(src_ref=src,dst_ref=dst,send_sem=ss0.at[i],recv_sem=rs0.at[i],device_id=sibd,device_id_type=MESH)
        cp.start(); first.append(cp)
    swap(sm_ref,gs.at[z,yx,c],0)
    swap(q_ref,sq,1); swap(p_ref,sp,2); swap(f1_ref,s1,3)
    swap(f2_ref,w2_o.at[z,yx,c],4)
    gs[z,yx,c]=sm_ref[...]
    own2=pltpu.make_async_copy(f2_ref,w2_o.at[z,yx,c],ssl.at[0]); own2.start()
    S=Gather(rows_view(gs),sss,srs)
    QA,QB,QC,Pj,F1=[Gather2(cols_view(r),ss.at[i],rs.at[i]) for i,r in enumerate((gq.at[0],gq.at[1],gq.at[2],gp,g1w))]
    F2=Gather2(rows_view(w2_o),ss.at[5],rs.at[5])
    outs=[]; lag=[]; used=[0]
    def put(src,dst):
        cp=pltpu.make_async_copy(src,dst,osem.at[used[0]]); cp.start(); outs.append(cp); used[0]+=1
    waited=set()
    def swapped(i):
        if i not in waited: waited.add(i); first[i].wait_recv()
    def build(own,sib,buf,dst):
        j=join(c,own,sib)
        buf[0]=j; dst[z,yx]=j
    def parts(ref,g): return jnp.concatenate([ref[:,o+256*g:o+256*g+256] for o in (0,768,1536)],axis=1)
    def half(b):
        h=b.shape[-1]//2
        return b.at[:,:,pl.ds(pl.multiple_of(c*h,128),h)]
    def near(n):
        if n=="F2": own2.wait(); F2.near(F2.at(0,yx)); return
        if n[0]=="Q":
            g="ABC".index(n[1]); swapped(1); build(parts(q_ref,g),parts(sq,g),bq.at[g],gq.at[g]); G[n].near(half(bq.at[g]))
        elif n=="P": swapped(2); build(p_ref[...],sp[...],bp,gp); Pj.near(half(bp))
        else: swapped(3); build(f1_ref[...],s1[...],b1,g1w); F1.near(half(b1))
    def far(n):
        if n=="F2": F2.far(F2.at(0,yx))
        elif n[0]=="Q": G[n].far(half(bq.at["ABC".index(n[1])]))
        else: G[n].far(half(bp if n=="P" else b1))
    G={"QA":QA,"QB":QB,"QC":QC,"P":Pj,"F1":F1,"F2":F2}
    def finish(n):
        if n=="F2": first[4].wait_recv()
        G[n].F()
        if n[0]=="Q": g="ABC".index(n[1]); put(gq.at[g],wq_o.at[g])
        elif n=="P": put(gp,wp_o)
        elif n=="F1": put(g1w,w1_o)
    def small(k):
        if k=="s": S.z_send(S.one(z))
        elif k=="Z": S.z_recv(); S.xy_send()
        elif k=="X": S.xy_recv()
        elif k=="D": S.diag_recv()
        else: first[0].wait_recv(); S.finish()
    g1=jnp.where(groups[0]==1,1,0)
    def setup(k):
        if k==0:
            loads[0].wait()
            raw[...]=tok_ref[...].astype(F32)
        segc=segments(groups,offsets,settled(g1,lax.broadcasted_iota(jnp.int32,(400,1),0)+400*k))
        meta_o[400*k:400*k+400,0:1]=jnp.where(segc>=0,1.0,0.0)
        segr=segments(groups,offsets,settled(g1,lax.broadcasted_iota(jnp.int32,(1,400),1)+400*k))
        bias[k]=jnp.where(segc==segr,0.0,-1e30)
    def vectors():
        X=gs[...].reshape(512,128)
        E=nn(X,spread(24,768,over(24,(128,768))))
        E=jnp.where(lax.broadcasted_iota(jnp.int32,(512,768),0)>>4==over(24,(512,768)),E,0.0).reshape(32,16,768)
        vec_o[...]=jnp.sum(E,axis=0)
        def wide(row,each,total):
            sel=jnp.where(lax.broadcasted_iota(jnp.int32,(32,512),1)==lax.broadcasted_iota(jnp.int32,(32,512),0)*16+row,1.0,0.0).astype(BF)
            e=nn(nn(sel,X).astype(BF),spread(each,total,over(each,(128,total))))
            e=jnp.where(lax.broadcasted_iota(jnp.int32,(32,total),0)==over(each,(32,total)),e,0.0)
            return jnp.sum(e,axis=0,keepdims=True)
        bqv[...]=wide(3,48,1536); bf1[...]=wide(7,96,3072)
    def norm_one():
        mask=jnp.broadcast_to(mask_ref[...].astype(F32).reshape(1,800),(8,800)).T
        mk[...]=mask[:,0:1]
        def write(r,n,v):
            t,m=v
            meta_o[pl.ds(r,n),1:2]=m
            mid[pl.ds(r,n),:]=jnp.where(m>0.0,vec_o[0:1,:],t)
        settle_rows(g1,lambda r,n:(raw[pl.ds(r,n),:],mk[pl.ds(r,n),:]),write)
        def rows(r):
            s=mid[r,:]
            st[r,:]=s.astype(BF)
            cc,rstd=row_stats(s)
            xh=cc*rstd
            xa[r,:]=xh.astype(BF); meta_o[r,2:3]=rstd
            n1[r,:]=(xh*vec_o[1:2,:]+vec_o[2:3,:]).astype(BF)
        by_sixteen(0,800,rows)
        put(xa,xa_o)
    def cotangents():
        loads[1].wait()
        raw[...]=cot_ref[...].astype(F32)
        def write2(r,n,v): mid[pl.ds(r,n),:]=v[0]
        settle_rows(g1,lambda r,n:(raw[pl.ds(r,n),:],),write2)
        def body(i,_):
            r=pl.ds(pl.multiple_of(i*80,16),80)
            v=mid[r,:]
            cs[r,:]=v.astype(BF); gt[r,:]=(v*meta_o[r,0:1]).astype(BF)
            return 0
        lax.fori_loop(0,10,body,0)
        put(cs,cs_o); put(gt,gt_o)
        nt_[...]=n1[...].T
        put(nt_,n1_o)
        lag.append(outs[-1])
    def qkv(g):
        r=nn(n1[...],gq[g].reshape(768,768))
        for k,o in enumerate((0,768,1536)):
            t=r[:,256*k:256*k+256]
            if k!=1: t=t+bqv[:,384*k+256*g:384*k+256*g+256]
            pj[:,o+256*g:o+256*g+256]=t.astype(BF)
        if g==2: put(pj,pj_o)
    lane=lax.broadcasted_iota(jnp.int32,(400,128),1)
    def where_of(t):
        return lax.rem(t,4)//2,2*(t//4)+lax.rem(t,2)
    def pcopy(t):
        b,p=where_of(t)
        return pltpu.make_async_copy(pst.at[lax.rem(t,2)],pr_o.at[b*6+p],psem.at[lax.rem(t,2)])
    def attend(t,_):
        b,p=where_of(t); s=lax.rem(t,2)
        r=pl.ds(pl.multiple_of(b*400,16),400)
        cc=lambda o: pl.ds(pl.multiple_of(o+p*128,128),128)
        @pl.when(t>=2)
        def _(): pcopy(t-2).wait()
        q=pj[r,cc(0)]; k=pj[r,cc(768)]; v=pj[r,cc(1536)]
        res=[]
        for j in range(2):
            qj=jnp.where((lane>=64)==(j==1),q,jnp.zeros_like(q))
            sc[j]=nt(qj,k)
        for j in range(2):
            for i in range(10):
                u=slice(40*i,40*i+40)
                t_=sc[j,u]*0.18033688011112042+bias[b,u]
                e=jnp.exp2(t_-jnp.max(t_,axis=1,keepdims=True))
                sc[j,u]=e*(1.0/jnp.sum(e,axis=1,keepdims=True))
        for j in range(2):
            pr=sc[j].astype(BF)
            pst[s,j]=pr
            res.append(nn(pr,v))
        ctx[r,cc(0)]=jnp.where(lane<64,res[0],res[1]).astype(BF)
        pcopy(t).start()
        return 0
    def proj():
        put(ctx,ctx_o)
        wpv=gp[...].reshape(768,768)
        def body(i,_):
            r=pl.ds(pl.multiple_of(i*400,16),400)
            mid[r,:]=st[r,:].astype(F32)+meta_o[r,0:1]*(nn(ctx[r,:],wpv)+vec_o[4:5,:])
            return 0
        lax.fori_loop(0,2,body,0)
        def rows(r):
            cc,rstd=row_stats(mid[r,:])
            xh=cc*rstd
            xb[r,:]=xh.astype(BF); meta_o[r,3:4]=rstd
            n2[r,:]=(xh*vec_o[5:6,:]+vec_o[6:7,:]).astype(BF)
        by_sixteen(0,800,rows)
        put(mid,mid_o); put(xb,xb_o)
        lag[0].wait(); outs[:]=[o for o in outs if o is not lag[0]]
        nt_[...]=n2[...].T
        put(nt_,n2_o)
    def mlp(i,_):
        cc=pl.ds(pl.multiple_of(i*512,128),512)
        a,d=gelu_parts(nn(n2[...],g1w[:,:,:,cc].reshape(768,512))+bf1[:,cc])
        hid[:,cc]=a.astype(BF); dg[:,cc]=d.astype(BF)
        return 0
    def grads(i,_):
        cc=pl.ds(pl.multiple_of(i*768,128),768)
        pt2[i]=tn(hid[:,cc],gt[...]).astype(BF).reshape(4,2,96,768)
        return 0
    chunks=("QA","QB","QC","P","F1","F2")
    k=0
    while k<len(FORWARD_ORDER):
        op=FORWARD_ORDER[k]; k+=1
        if op>=96 and op<200: small("sZXDF"[op-96])
        elif op<96:
            n=chunks[op//16]; g=G[n]; t=op%16
            if t==0: near(n)
            elif t==1: far(n)
            elif t==2: g.X0()
            elif t<6: g.Z(t-2)
            elif t<9: g.X(t-5)
            elif t==9: g.D()
            else: finish(n)
        elif op<220: (lambda:setup(0),lambda:setup(1),vectors,norm_one,cotangents,proj)[op-200]()
        elif op<230: qkv(op-220)
        else:
            a=b=op%10
            while k<len(FORWARD_ORDER) and FORWARD_ORDER[k]==op-a+b+1: b+=1; k+=1
            if op>=250:
                lax.fori_loop(a,b+1,grads,0)
                put(pt2.at[pl.ds(a,b+1-a)],pt2_o.at[pl.ds(a,b+1-a)])
            elif op<240: lax.fori_loop(2*a,2*b+2,attend,0)
            else:
                lax.fori_loop(a,b+1,mlp,0)
                if b==5:
                    put(hid,hid_o); put(dg,dg_o)
    pcopy(10).wait(); pcopy(11).wait()
    for cp in outs: cp.wait()
    for cp in first: cp.wait_send()
    for g in [S]+list(G.values()): g.drain()

def forward(groups,offsets,vectors,wq,wp,w1,w2,tok,cot,mask):
    sds=jax.ShapeDtypeStruct
    V=pl.BlockSpec(memory_space=pltpu.VMEM); A=pl.BlockSpec(memory_space=pl.ANY); M=pl.BlockSpec(memory_space=pltpu.SMEM)
    D=pltpu.SemaphoreType.DMA
    v=pltpu.VMEM
    R,W=tok.shape
    outs=[((3,4,4,48,768),BF),((4,4,48,768),BF),((4,4,48,3072),BF),((4,4,2,96,768),BF),((12,2,400,400),BF),
        ((W,R),BF),((W,R),BF),((R,W),BF),((R,3*W),BF),((R,4*W),BF),((R,4*W),BF),((R,W),BF),((R,W),BF),((R,W),F32),((4,4,2,96,768),BF),((R,W),BF),((R,W),BF),
        ((16,W),F32),((R,4),F32)]
    return pl.pallas_call(forward_kernel,
        in_specs=[M,M]+[V]*13+[A,A,V],out_specs=[A]*17+[V,V],out_shape=[sds(*o) for o in outs],
        scratch_shapes=[v((4,4,2,16,128),BF),v((3,4,4,48,768),BF),v((4,4,48,768),BF),v((4,4,48,3072),BF),
            v((24,2304),BF),v((24,768),BF),v((24,3072),BF),v((3,1,48,768),BF),v((1,48,768),BF),v((1,48,3072),BF),
            v((R,W),F32),v((R,W),F32),v((R,W),BF),v((R,W),BF),v((R,W),BF),v((R,W),BF),v((W,R),BF),v((R,3*W),BF),v((2,400,400),F32),v((R,W),BF),v((R,W),BF),
            v((R,4*W),BF),v((R,4*W),BF),v((R,W),BF),v((R,W),BF),v((4,4,2,96,768),BF),v((2,2,400,400),BF),v((2,400,400),F32),v((16,128),BF),v((16,128),F32),v((800,1),F32),v((R,W),BF),v((R,W),BF),v((1,2*W),F32),v((1,4*W),F32),
            D((5,)),D((5,)),D((1,)),D((14,)),D((14,)),D((6,21)),D((6,21)),D((2,)),D((24,)),D((2,))],
        compiler_params=pltpu.CompilerParams(collective_id=0,has_side_effects=True,vmem_limit_bytes=60<<20),name="forward")(
        groups,offsets,*vectors,wq,wp,w1,w2,tok,cot,mask)

class Reduce:
    def __init__(self,give,a,s,rxa,ryb,rx,ry,b,rz,ss,rs):
        self.give=give; self.a=a; self.s=s; self.rxa=rxa; self.ryb=ryb; self.rx=rx; self.ry=ry; self.b=b; self.rz=rz
        self.ss=ss; self.rs=rs
        c,x,y,z=place()
        self.c=c; self.z=z; self.yx=y*2+x
        self.xn=y*2+1-x; self.yn=(1-y)*2+x; self.dg=(1-y)*2+1-x
        self.xd=dev(z,self.xn,c); self.yd=dev(z,self.yn,c); self.sd=dev(z,self.yx,1-c)
        self.cps={}
    def send(self,src,dst,slot,d):
        cp=pltpu.make_async_remote_copy(src_ref=src,dst_ref=dst,send_sem=self.ss.at[slot],recv_sem=self.rs.at[slot],device_id=d,device_id_type=MESH)
        cp.start(); self.cps[slot]=cp
    def r0(self): self.send(self.give,self.s,0,self.sd)
    def add(self,n,z0,yx,other):
        t=self.a(pl.ds(z0,n),yx)
        t[...]=t[...]+other[...]
    def r1(self):
        self.cps[0].wait_recv()
        def own(yx): self.add(4,0,yx,self.s.at[:,yx])
        own(self.dg)
        self.send(self.a(pl.ds(0,2),self.dg),self.rxa,1,self.xd)
        self.send(self.a(pl.ds(2,2),self.dg),self.ryb,2,self.yd)
        own(self.xn)
        self.send(self.a(pl.ds(0,2),self.xn),self.rx.at[pl.ds(0,2)],3,self.xd)
        own(self.yn)
        self.send(self.a(pl.ds(2,2),self.yn),self.ry.at[pl.ds(2,2)],4,self.yd)
        own(self.yx)
    def r2(self):
        self.cps[1].wait_recv()
        self.add(2,0,self.yn,self.rxa)
        self.send(self.a(pl.ds(0,2),self.yn),self.ry.at[pl.ds(0,2)],6,self.yd)
        self.cps[2].wait_recv()
        self.add(2,2,self.xn,self.ryb)
        self.send(self.a(pl.ds(2,2),self.xn),self.rx.at[pl.ds(2,2)],5,self.xd)
    def r3(self):
        for s in (3,4,5,6): self.cps[s].wait_recv()
        for i in range(4):
            k=pl.ds(i,1)
            self.b[k]=(self.a(k,self.yx)[...].astype(F32)+self.rx[k].astype(F32)+self.ry[k].astype(F32)).astype(BF)
        for k in (1,2,3):
            zz=lax.rem(self.z+k,4)
            self.send(self.b.at[zz],self.rz.at[k-1],6+k,dev(zz,self.yx,self.c))
    def total(self):
        t=self.b[self.z].astype(F32)
        for k in (1,2,3):
            self.cps[6+k].wait_recv()
            t=t+self.rz[k-1].astype(F32)
        return t
    def drain(self):
        for cp in self.cps.values(): cp.wait_send()

def eights(v):
    return jnp.sum(v.reshape(v.shape[0]//8,8,v.shape[1]),axis=0)

class Total:
    def __init__(self,v,r,ss,rs):
        self.v=v; self.r=r; self.ss=ss; self.rs=rs; self.cps=[]
    def send(self,a,slot,d):
        cp=pltpu.make_async_remote_copy(src_ref=self.v.at[a],dst_ref=self.r.at[slot],send_sem=self.ss.at[slot],recv_sem=self.rs.at[slot],device_id=d,device_id_type=MESH)
        cp.start(); self.cps.append(cp)
    def stage(self,k):
        c,x,y,z=place(); yx=y*2+x
        if k==0: self.send(0,0,dev(z,yx,1-c))
        elif k==1:
            self.cps[0].wait_recv(); self.v[1]=self.v[0]+self.r[0]
            self.send(1,1,dev(z,y*2+1-x,c)); self.send(1,2,dev(z,(1-y)*2+x,c)); self.send(1,3,dev(z,(1-y)*2+1-x,c))
        elif k==2:
            for h in (1,2,3): self.cps[h].wait_recv()
            self.v[2]=self.v[1]+self.r[1]+(self.r[2]+self.r[3])
            for h in (1,2,3): self.send(2,3+h,dev(lax.rem(z+h,4),yx,c))
        else:
            for h in (1,2,3): self.cps[3+h].wait_recv()
            self.sum=self.v[2]+self.r[4]+self.r[5]+self.r[6]
    def drain(self):
        for cp in self.cps: cp.wait_send()

BACKWARD_ORDER=(
    16, 200, 240, 241, 242, 0, 17, 243, 220, 221, 222, 32, 1, 64, 223, 201, 18, 33, 202, 80, 48, 2, 203, 34, 204,
    19, 96, 81, 250, 97, 3, 49, 251, 35, 230, 252, 112, 98, 82, 50, 65, 253, 113, 99, 231, 128, 83, 254, 51, 66,
    255, 114, 232, 176, 129, 67, 115, 144, 177, 205, 130, 4, 68, 145, 100, 178, 206, 146, 131, 207, 160, 36, 84,
    161, 147, 208, 116, 162, 209, 179, 148, 52, 20, 132, 163,
)

def backward_kernel(w2_r,w1_r,wp_r,wq_r,pr_r,n1_r,n2_r,ctx_r,pj_r,hid_r,dg_r,xa_r,xb_r,mid_r,pt2_r,gt_r,cs_r,vec,meta,
        out_o,tok_o,sm_o,oq,op_,o1,o2,
        w2,w1,wp,gp,pj,mid,gf,nt_,tmp,ctx,gt,gb,pst,acc,accb,
        a2,s2,xa2,yb2,x2,y2,b2,z2,part,sb,xab,ybb,xb,yb,bb,zb,fb,frb,vs,vr,us,ur,
        lsem,psem,osem,rss,rrs,fss,frs,vss,vrs,uss,urs):
    greet()
    c,x,y,z=place(); yx=y*2+x
    sibd=dev(z,yx,1-c)
    loads={}; held=set()
    def get(name,src,dst):
        cp=pltpu.make_async_copy(src,dst,lsem.at[len(loads)]); cp.start(); loads[name]=cp
    def have(*names):
        for n in names:
            if n not in held: held.add(n); loads[n].wait()
    C2=[Reduce(pt2_r.at[:,:,1-c,h],lambda zs,q,h=h: a2.at[h,zs,q],s2.at[h],xa2.at[h],yb2.at[h],x2.at[h],y2.at[h],b2.at[h],z2.at[h],rss.at[h],rrs.at[h]) for h in range(2)]
    def sib_at(i): return sb.at[i] if i<5 else s2.at[(i-5)//2,:,:,:,pl.ds(384*((i-5)%2),384)]
    mine=pl.ds(pl.multiple_of(c*384,128),384); theirs=pl.ds(pl.multiple_of((1-c)*384,128),384)
    CH=[Reduce(part.at[i,:,:,:,theirs],lambda zs,q,i=i: part.at[i,zs,q,:,mine],sib_at(i),xab.at[i],ybb.at[i],xb.at[i],yb.at[i],bb.at[i],zb.at[i],rss.at[2+i],rrs.at[2+i]) for i in range(8)]
    F=CH[0:4]; PJ=CH[4]; QK=CH[5:8]
    get("gt",gt_r,gt)
    def tile(i):
        get("t%d"%i,w2_r.at[pl.ds(16*i,16)],w2.at[pl.ds(16*i,16)]); get("d%d"%i,dg_r.at[:,pl.ds(768*i,768)],gp.at[:,pl.ds(768*i,768)])
    tile(0); tile(1)
    ahead={240:lambda:(get("a2a",pt2_r.at[:,:,c,0],a2.at[0]),tile(2)),241:lambda:(tile(3),get("a2b",pt2_r.at[:,:,c,1],a2.at[1])),
        242:lambda:get("n2",n2_r,nt_),243:lambda:(get("cs",cs_r,tmp),get("w1",w1_r,w1)),220:lambda:(get("xb",xb_r,gb),get("wp",wp_r,wp)),
        221:lambda:get("ctx",ctx_r,ctx),222:lambda:get("pj",pj_r,pj)}
    acc[...]=jnp.zeros_like(acc)
    ends=[]
    def end(i):
        t=CH[i].total()
        fb[i,0]=t[:24]; fb[i,1]=t[24:]
        cp=pltpu.make_async_remote_copy(src_ref=fb.at[i,1-c],dst_ref=frb.at[i],send_sem=fss.at[i],recv_sem=frs.at[i],device_id=sibd,device_id_type=MESH)
        cp.start(); ends.append((i,cp))
    def end2(h): o2[48*h:48*h+48,:]=C2[h].total()
    def mlp(i,_):
        cc=pl.ds(pl.multiple_of(i*768,128),768)
        g=(nt(gt[...],w2[pl.ds(16*i,16)].reshape(768,768))*gp[:,cc].astype(F32)).astype(BF)
        gp[:,cc]=g
        accb[:,cc]=eights(g.astype(F32))
        return 0
    def w1grad(i):
        have("n2")
        if 220+i in ahead: ahead[220+i]()
        part[i]=nn(nt_[...],gp[:,768*i:768*i+768]).astype(BF).reshape(4,4,48,768)
        if i==3: get("n1",n1_r,nt_)
    def norm_back(i0,rows,col,gain,ka,kb,finish):
        def body(i,_):
            sums={}; later=[]
            def add(k,v): sums[k]=sums[k]+eights(v) if k in sums else eights(v)
            for u in range(5):
                r=pl.ds(pl.multiple_of(i0+(i*5+u)*16,16),16)
                g,xh,rstd=gf[r,:],rows[r,:].astype(F32),meta[r,col:col+1]
                add(ka,g*xh); add(kb,g)
                gx=g*gain
                m1=jnp.sum(gx,axis=1,keepdims=True)*(1.0/768); m2=jnp.sum(gx*xh,axis=1,keepdims=True)*(1.0/768)
                later+=finish(r,rstd*(gx-m1-xh*m2),add)
            for ref,r,v in later: ref[r,:]=v
            for k,v in sums.items(): acc[k]+=v
            return 0
        lax.fori_loop(0,25//5,body,0)
    def finish2(r,d,add):
        gm=tmp[r,:].astype(F32)+d
        v=(meta[r,0:1]*gm).astype(BF)
        add(4,v.astype(F32)); add(8,gt[r,:].astype(F32))
        return [(mid,r,gm),(gb,r,v)]
    def p10(k):
        have("w1","cs","xb")
        r=slice(400*k,400*k+400)
        gf[r,:]=nt(gp[r,:],w1[...].reshape(768,3072))
        norm_back(400*k,gb,3,vec[5:6,:],5,6,finish2)
        if k==1:
            get("hid",hid_r,gp); get("xa",xa_r,tmp)
            for g in range(3): get("wq%d"%g,wq_r.at[g],w1.at[:,:,:,pl.ds(768*g,768)])
    gc=gt
    def gctx():
        have("wp")
        gc[...]=nt(gb[...],wp[...].reshape(768,768)).astype(BF)
        pcopy(0).start()
    def wpgrad():
        have("ctx")
        part[4]=tn(ctx[...],gb[...]).astype(BF).reshape(4,4,48,768)
    lane=lax.broadcasted_iota(jnp.int32,(400,128),1)
    def where_of(t):
        return lax.rem(t,4)//2,2*(t//4)+lax.rem(t,2)
    def pcopy(t):
        b,p=where_of(t)
        return pltpu.make_async_copy(pr_r.at[b*6+p],pst.at[lax.rem(t,2)],psem.at[lax.rem(t,2)])
    def attend(t,_):
        b,p=where_of(t); s=lax.rem(t,2)
        r=pl.ds(pl.multiple_of(b*400,16),400)
        cc=lambda o: pl.ds(pl.multiple_of(o+p*128,128),128)
        pcopy(t).wait()
        @pl.when(t<11)
        def _(): pcopy(t+1).start()
        q=pj[r,cc(0)]; k=pj[r,cc(768)]; v=pj[r,cc(1536)]; g=gc[r,cc(0)]
        gx=g.astype(F32)*ctx[r,cc(0)].astype(F32)
        dq=[];dk=[];dv=[]
        for j in range(2):
            own=(lane>=64)==(j==1)
            zero=jnp.zeros_like(q)
            qj=jnp.where(own,q,zero); gj=jnp.where(own,g,zero)
            di=jnp.sum(jnp.where(own,gx,0.0),axis=1,keepdims=True)
            pr=pst[s,j]
            ds=(pr.astype(F32)*(nt(gj,v)-di)).astype(BF)
            dq.append(nn(ds,k)); dk.append(tn(ds,qj)); dv.append(tn(pr,gj))
        pj[r,cc(0)]=(jnp.where(lane<64,dq[0],dq[1])*0.125).astype(BF)
        pj[r,cc(768)]=((dk[0]+dk[1])*0.125).astype(BF)
        pj[r,cc(1536)]=(dv[0]+dv[1]).astype(BF)
        return 0
    def group(r,g): return jnp.concatenate([pj[r,o+256*g:o+256*g+256] for o in (0,768,1536)],axis=1)
    def qkvgrad(g):
        if g==0: have("n1")
        cols=group(slice(None),g)
        acc[3,:,256*g:256*g+256]=eights(cols[:,:256].astype(F32)); acc[7,:,256*g:256*g+256]=eights(cols[:,512:].astype(F32))
        part[5+g]=nn(nt_[...],cols).astype(BF).reshape(4,4,48,768)
        if g==2:
            for k in range(6): us[0,k:k+1,:]=jnp.sum(acc[3+k],axis=0,keepdims=True)
            for k in range(4): us[0,6+k:7+k,:]=jnp.sum(accb[:,768*k:768*k+768],axis=0,keepdims=True)
            us[0,10:16,:]=jnp.zeros((6,768),F32)
    def finish1(r,d,add):
        gs=mid[r,:]+d
        m=meta[r,1:2]>0.0
        add(0,jnp.where(m,gs,0.0))
        return [(mid,r,jnp.where(m,0.0,gs))]
    stores=[]
    def put(src,dst):
        cp=pltpu.make_async_copy(src,dst,osem.at[len(stores)]); cp.start(); stores.append(cp)
    def back(i):
        if i==0: have("xa","wq0","wq1","wq2")
        r=slice(400*i,400*i+400)
        gf[r,:]=sum(nt(group(r,g),w1[:,:,:,768*g:768*g+768].reshape(768,768)) for g in range(3))
        norm_back(400*i,tmp,2,vec[1:2,:],1,2,finish1)
        if i==1: put(mid,tok_o); get("mid2",mid_r,gf)
    def fin():
        for k in range(3): vs[0,k:k+1,:]=jnp.sum(acc[k],axis=0,keepdims=True)
        vs[0,3:8,:]=jnp.zeros((5,768),F32)
    def outp(i):
        if i==0: have("hid","mid2")
        r=slice(400*i,400*i+400)
        gb[r,:]=(gf[r,:]+meta[r,0:1]*(nn(gp[r,:],w2[...].reshape(3072,768))+vec[8:9,:])).astype(BF)
        put(gb.at[pl.ds(400*i,400)],out_o.at[pl.ds(400*i,400)])
    sums=[Total(vs,vr,vss,vrs),Total(us,ur,uss,urs)]
    plain=(lambda:None,lambda:p10(0),lambda:p10(1),gctx,wpgrad,lambda:back(0),lambda:back(1),fin,lambda:outp(0),lambda:outp(1))
    k=0
    while k<len(BACKWARD_ORDER):
        op=BACKWARD_ORDER[k]; k+=1
        i,t=op//16,op%16
        if i<10:
            if t==4:
                if i<2: end2(i)
                else: end(i-2)
            else:
                if i<2 and t==1: have(("a2a","a2b")[i])
                r=(C2+CH)[i]
                (r.r0,r.r1,r.r2,r.r3)[t]()
        elif i<12: sums[i-10].stage(t)
        elif op<220: plain[op-200]()
        elif op<230: w1grad(op-220)
        elif op<240: qkvgrad(op-230)
        else:
            a=b=op%10
            while k<len(BACKWARD_ORDER) and BACKWARD_ORDER[k]==op-a+b+1: b+=1; k+=1
            if op<250:
                have("gt")
                for i in range(a,b+1):
                    have("t%d"%i,"d%d"%i); ahead[240+i]()
                    lax.fori_loop(i,i+1,mlp,0)
            else:
                if a==0: have("pj")
                lax.fori_loop(2*a,2*b+2,attend,0)
    vt,ut=sums[0].sum,sums[1].sum
    me=lax.axis_index("dp")
    def turn(v,by): return pltpu.roll(v,lax.rem(768-by,768),1)[:,:128]
    eight=lambda v: jnp.concatenate([v]*8,axis=0)
    sm_o[0:8,:]=turn(vt,24*me)
    t=turn(ut,24*me)
    sm_o[4:7,:]=t[1:4]; sm_o[8:9,:]=t[5:6]
    sm_o[3:4,:]=turn(eight(jnp.where(me>=16,ut[4:5],ut[0:1])),48*lax.rem(me,16))[0:1]
    k8=me//8
    pick=jnp.where(k8==0,ut[6:7],jnp.where(k8==1,ut[7:8],jnp.where(k8==2,ut[8:9],ut[9:10])))
    sm_o[7:8,:]=turn(eight(pick),96*lax.rem(me,8))[0:1]
    for i,cp in ends:
        cp.wait_recv()
        own=fb[i,c]; oth=frb[i]
        lo=jnp.where(c==0,own,oth); hi=jnp.where(c==0,oth,own)
        if i<4: o1[:,768*i:768*i+384]=lo; o1[:,768*i+384:768*i+768]=hi
        elif i==4: op_[:,:384]=lo; op_[:,384:]=hi
        else:
            g=256*(i-5)
            oq[:,g:g+256]=lo[:,:256]; oq[:,768+g:768+g+128]=lo[:,256:]
            oq[:,768+g+128:768+g+256]=hi[:,:128]; oq[:,1536+g:1536+g+256]=hi[:,128:]
        cp.wait_send()
    for cp in stores: cp.wait()
    for q in C2+CH+sums: q.drain()

def backward(w2,w1,wp,wq,pr,n1,n2,ctx,pj,hid,dg,xa,xb,mid,pt2,gt,cs,vec,meta):
    sds=jax.ShapeDtypeStruct
    V=pl.BlockSpec(memory_space=pltpu.VMEM); A=pl.BlockSpec(memory_space=pl.ANY)
    D=pltpu.SemaphoreType.DMA
    v=pltpu.VMEM
    W,R=n1.shape
    scr=[v((64,48,W),BF),v((4,4,48,4*W),BF),v((4,4,48,W),BF),v((R,4*W),BF),v((R,3*W),BF),v((R,W),F32),v((R,W),F32),v((W,R),BF),
        v((R,W),BF),v((R,W),BF),v((R,W),BF),v((R,W),BF),v((2,2,400,400),BF),v((9,8,W),F32),v((8,4*W),F32)]
    def rs(n,r,w,own):
        o=[v((n,4,4,r,own),BF),v((min(n,5),4,4,r,w),BF),v((n,2,r,w),BF),v((n,2,r,w),BF),v((n,4,r,w),BF),v((n,4,r,w),BF),v((n,4,r,w),BF),v((n,3,r,w),BF)]
        return o
    scr+=rs(2,48,W,W)+rs(8,48,W//2,W)
    scr+=[v((8,2,24,W//2),F32),v((8,24,W//2),F32),v((3,8,W),F32),v((7,8,W),F32),v((3,16,W),F32),v((7,16,W),F32)]
    scr+=[D((28,)),D((2,)),D((3,)),D((10,10)),D((10,10)),D((8,)),D((8,))]+[D((7,))]*4
    outs=[((R,W),BF),((R,W),F32),((16,128),F32),((24,3*W),F32),((24,W),F32),((24,4*W),F32),((96,W),F32)]
    return pl.pallas_call(backward_kernel,in_specs=[A]*17+[V]*2,out_specs=[A,A]+[V]*5,out_shape=[sds(*o) for o in outs],scratch_shapes=scr,
        compiler_params=pltpu.CompilerParams(collective_id=1,has_side_effects=True,vmem_limit_bytes=63<<20),name="backward")(
        w2,w1,wp,wq,pr,n1,n2,ctx,pj,hid,dg,xa,xb,mid,pt2,gt,cs,vec,meta)

def settle_back_kernel(groups,out_r,tok_r,sm,q_r,p_r,w1_r,w2_r,out_o,tok_o,q_o,p_o,w1_o,w2_o,v0,v1,v2,v3,v4,v5,v6,v7,v8,buf,ob,tb,qb,pb,b1,b2,sem):
    pairs=((tok_r,tb),(out_r,buf),(w1_r,b1),(q_r,qb),(w2_r,b2),(p_r,pb))
    loads=[pltpu.make_async_copy(a,b,sem.at[i]) for i,(a,b) in enumerate(pairs)]
    for cp in loads: cp.start()
    moved=groups[0]==1
    one=[pltpu.make_async_copy(tb,tok_o,sem.at[6])]
    three=[pltpu.make_async_copy(tb.at[pl.ds(a,n)],tok_o.at[pl.ds(b,n)],sem.at[7+i]) for i,(a,b,n) in enumerate(((0,0,392),(400,392,400),(392,792,8)))]
    for i,v in enumerate((v0,v1,v2,v3,v4,v5,v6,v7,v8)):
        m=v.shape[0]
        v[...]=sm[i:i+1,0:m].reshape(m)
    loads[0].wait()
    @pl.when(moved)
    def _():
        for cp in three: cp.start()
    @pl.when(jnp.logical_not(moved))
    def _():
        for cp in one: cp.start()
    loads[1].wait()
    ob[0:384]=buf[0:384]
    a=buf[384:800].astype(F32)
    b=jnp.concatenate([a[0:8],a[16:416],a[8:16]],axis=0)
    ob[384:800]=jnp.where(moved,b,a).astype(BF)
    stores=[pltpu.make_async_copy(ob,out_o,sem.at[10])]
    stores[0].start()
    for i,(b,o) in enumerate(((b1,w1_o),(qb,q_o),(b2,w2_o),(pb,p_o))):
        loads[2+i].wait()
        cp=pltpu.make_async_copy(b,o,sem.at[11+i]); cp.start(); stores.append(cp)
    for cp in stores: cp.wait()
    @pl.when(moved)
    def _():
        for cp in three: cp.wait()
    @pl.when(jnp.logical_not(moved))
    def _():
        for cp in one: cp.wait()

def settle_back(groups,sizes,out,tok,sm,q,p,w1,w2):
    sds=jax.ShapeDtypeStruct
    V=pl.BlockSpec(memory_space=pltpu.VMEM); A=pl.BlockSpec(memory_space=pl.ANY); M=pl.BlockSpec(memory_space=pltpu.SMEM)
    v=pltpu.VMEM
    return pl.pallas_call(settle_back_kernel,in_specs=[M,A,A,V,A,A,A,A],out_specs=[A]*6+[V]*len(sizes),
        out_shape=[sds(out.shape,BF)]+[sds(a.shape,F32) for a in (tok,q,p,w1,w2)]+[sds((m,),F32) for m in sizes],
        scratch_shapes=[v(out.shape,BF),v(out.shape,BF)]+[v(a.shape,F32) for a in (tok,q,p,w1,w2)]+[pltpu.SemaphoreType.DMA((15,))],
        compiler_params=pltpu.CompilerParams(vmem_limit_bytes=60<<20),name="settle_back")(groups,out,tok,sm,q,p,w1,w2)

def normalize(values, gain, shift):
    center = values - jnp.mean(values, axis=-1, keepdims=True)
    spread = jnp.mean(center * center, axis=-1, keepdims=True)
    return center * lax.rsqrt(spread + eps_norm) * gain + shift

def activate(values):
    return jax.nn.gelu(values, approximate=False)

def segment_rows(groups, offsets, rows):
    lengths = jnp.where(groups == 0, P_SMALL, jnp.where(groups == 1, P_MID, P_LARGE)).astype(jnp.int32)
    positions = jnp.arange(rows, dtype=jnp.int32)
    inside = (positions[None, :] >= offsets[:, None]) & (positions[None, :] < offsets[:, None] + lengths[:, None])
    labels = jnp.arange(1, offsets.shape[0] + 1, dtype=jnp.int32)
    return jnp.sum(jnp.where(inside, labels[:, None], 0), axis=0) - 1

def settle(mid, rows):
    half = rows.shape[0] // 2
    cut = P_MID * (half // P_MID)
    gap = half - cut
    end = rows.shape[0] - gap
    moved = jnp.concatenate([rows[:cut], rows[end:], rows[cut:end]], axis=0)
    return jnp.where(mid, moved, rows)

def unsettle(mid, rows):
    half = rows.shape[0] // 2
    cut = P_MID * (half // P_MID)
    gap = half - cut
    moved = jnp.concatenate([rows[:cut], rows[half:], rows[cut:half]], axis=0)
    return jnp.where(mid, moved, rows)

def shards(n, tokens, mask_bits, groups, offsets, mask_token, ln1_gain, ln1_bias, w_qkv, b_qv, w_proj, b_proj,
           ln2_gain, ln2_bias, w_fc1, b_fc1, w_fc2, b_fc2, cotangent):
    vectors = (mask_token, ln1_gain, ln1_bias, b_qv, b_proj, ln2_gain, ln2_bias, b_fc1, b_fc2)
    sizes = [v.shape[0] for v in vectors]
    places = [sum(sizes[:i]) for i in range(len(sizes) + 1)]
    small_all = lax.all_gather(jnp.concatenate(vectors), "dp", axis=0, tiled=False)
    full_qkv, full_proj, full_fc1, full_fc2 = [
        lax.all_gather(w, "dp", axis=0, tiled=True) for w in (w_qkv, w_proj, w_fc1, w_fc2)]
    token_mask, gain_one, shift_one, bias_qv, bias_proj, gain_two, shift_two, bias_one, bias_two = [
        small_all[:, places[i]:places[i + 1]].reshape(-1).astype(F32) for i in range(len(sizes))]
    rows, width = tokens.shape
    half = rows // 2
    mid = groups[0] == 1
    tokens = settle(mid, tokens)
    cotangent = settle(mid, cotangent)
    mask_bits = settle(mid, mask_bits)
    segment = settle(mid, segment_rows(groups, offsets, rows))
    valid_col = (segment >= 0).astype(F32)[:, None]
    halves = segment.reshape(2, half)
    bias = jnp.where(halves[:, :, None] == halves[:, None, :], 0.0, -1e30).astype(F32)
    masked_rows = (mask_bits == 1)[:, None]
    start = jnp.where(masked_rows, token_mask[None, :], tokens.astype(F32))
    normed_one = normalize(start, gain_one, shift_one).astype(BF)
    full_bias = jnp.concatenate([bias_qv[:width], jnp.zeros((width,), F32), bias_qv[width:]])
    projected = (jnp.dot(normed_one, full_qkv, preferred_element_type=F32) + full_bias).astype(BF)
    context_low, probs = attn_fwd(projected, bias)
    middle = start + valid_col * (jnp.dot(context_low, full_proj, preferred_element_type=F32) + bias_proj)
    normed_two = normalize(middle, gain_two, shift_two).astype(BF)
    hidden_pre = jnp.dot(normed_two, full_fc1, preferred_element_type=F32) + bias_one
    hidden_low = activate(hidden_pre).astype(BF)
    result = middle + valid_col * (jnp.dot(hidden_low, full_fc2, preferred_element_type=F32) + bias_two)
    output = unsettle(mid, result.astype(BF))
    upstream = cotangent.astype(F32)
    grad_two = (valid_col * upstream).astype(BF)
    grad_wfc2 = tn(hidden_low, grad_two)
    grad_bfc2 = jnp.sum(grad_two.astype(F32), axis=0)
    grad_hidden = nt(grad_two, full_fc2)
    _, gelu_back = jax.vjp(activate, hidden_pre)
    grad_pre = gelu_back(grad_hidden)[0].astype(BF)
    grad_wfc1 = tn(normed_two, grad_pre)
    grad_bfc1 = jnp.sum(grad_pre.astype(F32), axis=0)
    grad_normed_two = nt(grad_pre, full_fc1)
    _, norm_back_two = jax.vjp(normalize, middle, gain_two, shift_two)
    grad_mid_part, grad_gain_two, grad_shift_two = norm_back_two(grad_normed_two)
    grad_middle = upstream + grad_mid_part
    grad_branch = (valid_col * grad_middle).astype(BF)
    grad_wproj = tn(context_low, grad_branch)
    grad_bproj = jnp.sum(grad_branch.astype(F32), axis=0)
    grad_context = nt(grad_branch, full_proj).astype(BF)
    dq, dk, dv = attn_bwd(projected, grad_context, context_low, probs)
    grad_projected = jnp.concatenate([dq, dk, dv], axis=1)
    grad_wqkv = tn(normed_one, grad_projected)
    grad_bqv = jnp.concatenate([jnp.sum(dq.astype(F32), axis=0), jnp.sum(dv.astype(F32), axis=0)])
    grad_normed_one = nt(grad_projected, full_qkv)
    _, norm_back_one = jax.vjp(normalize, start, gain_one, shift_one)
    grad_start_part, grad_gain_one, grad_shift_one = norm_back_one(grad_normed_one)
    grad_start = grad_middle + grad_start_part
    grad_token = jnp.sum(jnp.where(masked_rows, grad_start, 0.0), axis=0)
    grad_input = unsettle(mid, jnp.where(masked_rows, 0.0, grad_start))
    grad_vectors = (grad_token, grad_gain_one, grad_shift_one, grad_bqv, grad_bproj, grad_gain_two, grad_shift_two,
                    grad_bfc1, grad_bfc2)
    grad_small = jnp.concatenate([g.reshape(n, -1) for g in grad_vectors], axis=1)
    small_share = lax.psum_scatter(grad_small, "dp", scatter_dimension=0, tiled=False)
    share_qkv, share_proj, share_fc1, share_fc2 = [
        lax.psum_scatter(g, "dp", scatter_dimension=0, tiled=True)
        for g in (grad_wqkv, grad_wproj, grad_wfc1, grad_wfc2)]
    v = [small_share[places[i]:places[i + 1]] for i in range(len(sizes))]
    return (output, grad_input, v[0], v[1], v[2], share_qkv, v[3], share_proj, v[4], v[5], v[6], share_fc1, v[7],
            share_fc2, v[8])


def shards_fast(n, tokens, mask_bits, groups, offsets, mask_token, ln1_gain, ln1_bias, w_qkv, b_qv, w_proj, b_proj,
           ln2_gain, ln2_bias, w_fc1, b_fc1, w_fc2, b_fc2, cotangent):
    vectors = (mask_token, ln1_gain, ln1_bias, b_qv, b_proj, ln2_gain, ln2_bias, b_fc1, b_fc2)
    sizes = [v.shape[0] for v in vectors]
    (gq, gp, g1, g2, probs, normed_one, normed_two, context_low, projected, hidden_low, dgelu, rows_one, rows_two, middle, part2,
     grad_two, cots, vec, meta) = forward(groups, offsets, vectors, w_qkv, w_proj, w_fc1, w_fc2, tokens, cotangent, mask_bits)
    width = tokens.shape[1]
    shares = backward(
        g2.reshape(64, 48, width), g1, gp, gq, probs, normed_one, normed_two, context_low,
        projected, hidden_low, dgelu, rows_one, rows_two, middle, part2.reshape(4, 4, 2, 2, 48, width), grad_two, cots, vec, meta)
    output, grad_input, share_qkv, share_proj, share_fc1, share_fc2, *v = settle_back(groups, sizes, *shares)
    return (output, grad_input, v[0], v[1], v[2], share_qkv, v[3], share_proj, v[4], v[5], v[6], share_fc1, v[7],
            share_fc2, v[8])

def solution(mesh):
    row, flat = P("dp", None), P("dp")
    return jax.shard_map(
        functools.partial(shards_fast if mesh.shape["dp"] == 32 else shards, mesh.shape["dp"]),
        mesh=mesh,
        in_specs=(row, flat, flat, flat, flat, flat, flat, row, flat, row, flat, flat, flat, row, flat, row, flat, row),
        out_specs=(row, row, flat, flat, flat, row, flat, row, flat, flat, flat, row, flat, row, flat),
        check_vma=False,
    )
```
